32 devices in a mesh: dp: 4 (over y, x), side: 2 (over core), blk: 4 (over z).
Axes of the slice: x: 2, y: 2, z: 4, core: 2. Of those that a mesh axis runs over, the one named last changes fastest.
Arguments:
- feats: bfloat16 [1024, 8, 8, 512], P(('dp', 'side', 'blk')), may hold values from -8 to 8
- size_group: int32 [1024], P(('dp', 'side', 'blk')), may hold values from 0 to 1
- labels: int32 [1024], P(('dp', 'side', 'blk')), may hold values from 0 to 9
- class_wt: int32 [10], replicated, may hold values from 1 to 5
- owners: int32 [18], replicated, may hold values from 0 to 3, as said below
- basis_in: bfloat16 [2, 512, 512], replicated, may hold values from -2 to 2
- basis_out: bfloat16 [2, 512, 512], replicated, may hold values from -2 to 2
- scales: float32 [9216, 512], P(('dp', 'blk'), 'side'), may hold values from 3e-06 to 3e-05
- master: float32 [40, 512, 512], P('blk', 'side'), may hold values from -0.09375 to 0.09375
- moment1: float32 [40, 512, 512], P('blk', 'side'), may hold values from -1.25 to 1.25
- moment2: float32 [40, 512, 512], P('blk', 'side'), may hold values from 0.0001953125 to 0.001953125
- norm_params: float32 [2, 2, 512], replicated, may hold values from 0.5 to 1.5
- norm_m: float32 [2, 2, 512], replicated, may hold values from -0.0009765625 to 0.0009765625
- norm_v: float32 [2, 2, 512], replicated, may hold values from 1.953125e-10 to 1.171875e-09
- head: float32 [513, 10], replicated, may hold values from -0.25 to 0.25
- head_m: float32 [513, 10], replicated, may hold values from -0.009765625 to 0.009765625
- head_v: float32 [513, 10], replicated, may hold values from 1.953125e-08 to 1.171875e-07
Outputs:
- loss_sum: float32 [], replicated
- weight_total: float32 [], replicated
- new_scales: float32 [9216, 512], P(('dp', 'blk'), 'side')
- new_master: float32 [40, 512, 512], P('blk', 'side')
- new_moment1: float32 [40, 512, 512], P('blk', 'side')
- new_moment2: float32 [40, 512, 512], P('blk', 'side')
- new_norm: float32 [2, 2, 512], replicated
- new_norm_m: float32 [2, 2, 512], replicated
- new_norm_v: float32 [2, 2, 512], replicated
- new_head: float32 [513, 10], replicated
- new_head_m: float32 [513, 10], replicated
- new_head_v: float32 [513, 10], replicated
The draws below stay inside these ranges and needn't reach their ends.
Inputs may be any that keep to these rules, and one draw needn't show every extreme that they name: Each of the 4 owners holds at most 10 of the 18 matrices, and one owner holds exactly 10.
All inputs are finite; a program needn't handle non-finite values.
Results may differ from the reference program's by a relative error of at most 0.0067.
Values may be sent and summed in bfloat16 or wider, within the bound.
A program may use at most 256 MiB of HBM per device.

```python
import math
import jax
import jax.numpy as jnp
from jax import lax

C = 512
K = 10
SIDE = 8
L = 2
TAPS = 9
CAP = 10
STEP = 10
IMAGES = 1024
ROWS = 9216
N_BLK = 4


def shared_classes(key):
    return jax.random.randint(jax.random.fold_in(key, 101), (IMAGES,), 0, K).astype(jnp.int32)


def local_basis(key):
    first, second = jax.random.split(key)
    diagonal = jax.random.uniform(first, (L, C), minval=0.8, maxval=1.4)
    spread = jnp.clip(jax.random.normal(second, (L, C, C)), -2.5, 2.5) * (0.3 * C ** (-0.5))
    identity = jnp.eye(C, dtype=jnp.float32)
    return spread * (1.0 - identity)[None] + identity[None] * diagonal[:, None, :]


def draw_owners(key, part):
    first, second, third = jax.random.split(key, 3)
    busiest = jax.random.randint(first, (), 0, N_BLK)
    order = jax.random.permutation(second, L * TAPS)
    others = jax.random.randint(third, (L * TAPS,), 0, N_BLK - 1)
    others = others + (others >= busiest).astype(jnp.int32)
    return jnp.where(order < CAP, busiest, others).astype(jnp.int32)


def draw_labels(key, part):
    return shared_classes(key)


def draw_feats(key, part):
    classes = shared_classes(key)
    key = jax.random.fold_in(key, 2)
    first, second, third = jax.random.split(key, 3)
    image_level = jax.random.uniform(first, (IMAGES,), minval=-0.75, maxval=0.75)
    class_level = jax.random.uniform(second, (K, C), minval=-1.0, maxval=1.0)
    levels = jnp.exp(image_level[:, None] + class_level[classes])
    noise = jax.random.normal(third, (IMAGES, SIDE, SIDE, C))
    values = jnp.clip(noise * levels[:, None, None, :], -8.0, 8.0)
    return values.astype(jnp.bfloat16)


def draw_basis_in(key, part):
    key = jax.random.fold_in(key, 3)
    return local_basis(key).astype(jnp.bfloat16)


def draw_basis_out(key, part):
    key = jax.random.fold_in(key, 4)
    return local_basis(key).astype(jnp.bfloat16)


def plant(entries, stream_key, smallest, largest):
    extent = entries.shape
    place = [jax.random.randint(jax.random.fold_in(stream_key, axis), (), 0, extent[axis]) for axis in range(len(extent))]
    entries = entries.at[tuple(place)].set(smallest)
    longest = extent.index(max(extent))
    place[longest] = (place[longest] + 1) % extent[longest]
    return entries.at[tuple(place)].set(largest)


def block_scale(own_key, shape, cuts, smallest, top_value):
    def one(dim, blocks):
        draws = jax.random.uniform(jax.random.fold_in(jax.random.fold_in(own_key, 6), dim), (blocks,), jnp.float32, smallest / len(cuts), top_value / len(cuts))
        return jnp.repeat(jnp.exp(draws), shape[dim] // blocks).reshape((-1,) + (1,) * (len(shape) - dim - 1))

    gain = one(*cuts[0])
    for cut in cuts[1:]:
        gain = gain * one(*cut)
    return gain


def gaussian(key, shape, deviation, most, pieces=(), kind=jnp.bfloat16):
    entries = deviation * jax.random.normal(key, shape, jnp.float32)
    if pieces:
        entries = entries * block_scale(key, shape, pieces, -0.22, 0.18)
    return jnp.clip(entries, -most, most).astype(kind)


def setup_inputs(seed: int = 0) -> dict:
    key_of = jax.random.split(jax.random.key(seed), 18)
    feats = draw_feats(jax.random.fold_in(key_of[17], 71), 0)
    size_group = plant(jax.random.randint(key_of[1], (IMAGES,), 0, 2), jax.random.fold_in(key_of[1], 1), 0, 1).astype(jnp.int32)
    labels = draw_labels(jax.random.fold_in(key_of[17], 71), 0)
    class_wt = plant(jax.random.randint(key_of[3], (K,), 1, 6), jax.random.fold_in(key_of[3], 1), 1, 5).astype(jnp.int32)
    owners = draw_owners(jax.random.fold_in(key_of[17], 71), 0)
    basis_in = draw_basis_in(jax.random.fold_in(key_of[17], 71), 0)
    basis_out = draw_basis_out(jax.random.fold_in(key_of[17], 71), 0)
    scales = jnp.clip(jnp.exp(math.log(2.9999999242136255e-05) - 2.30258503 * jax.random.uniform(key_of[7], (ROWS, C), jnp.float32) ** block_scale(key_of[7], (ROWS, C), ((0, 16), (1, 2)), -0.2, 0.2)), 3.000000106112566e-06, 2.9999999242136255e-05)
    master = gaussian(key_of[8], (N_BLK * CAP, C, C), (TAPS * C) ** -0.5, 0.09375, ((0, 4), (1, 2)), jnp.float32)
    moment1 = gaussian(key_of[9], (N_BLK * CAP, C, C), (2.6 * IMAGES ** -0.5), 1.25, ((0, 4), (1, 2)), jnp.float32)
    moment2 = jnp.clip(jnp.exp(math.log(0.001953125) - 2.3025851 * jax.random.uniform(key_of[10], (N_BLK * CAP, C, C), jnp.float32) ** block_scale(key_of[10], (N_BLK * CAP, C, C), ((0, 4), (1, 2)), -0.2, 0.2)), 0.0001953125, 0.001953125)
    norm_params = jnp.clip(1.0 + 0.1 * jax.random.normal(key_of[11], (L, 2, C), jnp.float32), 0.5, 1.5)
    norm_m = gaussian(key_of[12], (L, 2, C), (0.002 * IMAGES ** -0.5), 0.0009765625, (), jnp.float32)
    norm_v = jnp.clip(jnp.exp(jax.random.uniform(key_of[13], (L, 2, C), jnp.float32, math.log(1.953125022824409e-10), math.log(1.171875041450221e-09))), 1.953125022824409e-10, 1.171875041450221e-09)
    head = gaussian(key_of[14], (C + 1, K), C ** -0.5, 0.25, (), jnp.float32)
    head_m = gaussian(key_of[15], (C + 1, K), (0.02 * IMAGES ** -0.5), 0.009765625, (), jnp.float32)
    head_v = jnp.clip(jnp.exp(jax.random.uniform(key_of[16], (C + 1, K), jnp.float32, math.log(1.9531249506599124e-08), math.log(1.1718749703959475e-07))), 1.9531249506599124e-08, 1.1718749703959475e-07)
    return {"feats": feats, "size_group": size_group, "labels": labels, "class_wt": class_wt, "owners": owners, "basis_in": basis_in, "basis_out": basis_out, "scales": scales, "master": master, "moment1": moment1, "moment2": moment2, "norm_params": norm_params, "norm_m": norm_m, "norm_v": norm_v, "head": head, "head_m": head_m, "head_v": head_v}


EPS_NORM = 1e-05
DAMPING = 0.001
DECAY = 0.95
BETA_ONE = 0.9
BETA_TWO = 0.999
ADAM_EPS = 1e-08
WEIGHT_DECAY = 0.01
RATE_CONV = 0.01
RATE_NORM = 0.5
RATE_HEAD = 0.02
HIGHEST = lax.Precision.HIGHEST

@jax.custom_vjp
def low(v):
    return lax.optimization_barrier(v.astype(jnp.bfloat16)).astype(jnp.float32)

@jax.custom_vjp
def low_back(v):
    return v

def low_keep(v):
    return (low(v), None)

def low_pass(kept, grad):
    return (grad,)

def back_keep(v):
    return (v, None)

def back_low(kept, grad):
    return (low(grad),)
low.defvjp(low_keep, low_pass)
low_back.defvjp(back_keep, back_low)

def adamw(weight_now, first_now, second_now, gradient, rate):
    first_new = BETA_ONE * first_now + (1.0 - BETA_ONE) * gradient
    second_new = BETA_TWO * second_now + (1.0 - BETA_TWO) * gradient * gradient
    first_hat = first_new / (1.0 - BETA_ONE ** STEP)
    second_hat = second_new / (1.0 - BETA_TWO ** STEP)
    weight_new = weight_now - rate * (first_hat / (jnp.sqrt(second_hat) + ADAM_EPS) + WEIGHT_DECAY * weight_now)
    return (weight_new, first_new, second_new)

def pad_cells(values):
    return jnp.pad(values, ((0, 0), (1, 1), (1, 1), (0, 0)))

def conv_ref(inputs, kernel):
    side_len = inputs.shape[1]
    padded = pad_cells(inputs)
    total = None
    for tap in range(TAPS):
        shifted = padded[:, tap // 3:tap // 3 + side_len, tap % 3:tap % 3 + side_len]
        term = jnp.einsum('npqc,co->npqo', shifted, kernel[tap], precision=HIGHEST)
        total = term if total is None else total + term
    return total

def image_sums(act_proj, grad_proj):
    side_len = act_proj.shape[1]
    blocks = act_proj.shape[0] // 32
    padded = pad_cells(act_proj)
    part_act = padded.reshape((blocks, 32) + padded.shape[1:])
    part_grad = grad_proj.reshape((blocks, 32) + grad_proj.shape[1:])

    def advance(carry, item):
        first, second = carry
        block_act, block_grad = item
        firsts, seconds = ([], [])
        for tap in range(TAPS):
            shifted = block_act[:, tap // 3:tap // 3 + side_len, tap % 3:tap % 3 + side_len]
            each = jnp.einsum('npqi,npqj->nij', shifted, block_grad, precision=HIGHEST)
            firsts.append(lax.optimization_barrier(jnp.sum(each, axis=0)))
            seconds.append(lax.optimization_barrier(jnp.sum(each * each, axis=0)))
        return ((first + jnp.stack(firsts), second + jnp.stack(seconds)), None)
    zero = jnp.zeros((TAPS, C, C), jnp.float32)
    (first, second), unused = lax.scan(advance, (zero, zero), (part_act, part_grad))
    return (first, second)

def reference(feats, size_group, labels, class_wt, owners, basis_in, basis_out, scales, master, moment1, moment2, norm_params, norm_m, norm_v, head, head_m, head_v):
    line = jnp.arange(SIDE)
    inner = (line[:, None] < SIDE // 2) & (line[None, :] < SIDE // 2)
    cell_mask = jnp.where((size_group == 1)[:, None, None], True, inner[None]).astype(jnp.float32)
    mask_four = cell_mask[..., None]
    pixels = lax.optimization_barrier(jnp.sum(cell_mask, axis=(1, 2)))
    count_all = jnp.sum(pixels)
    class_hot = (labels[:, None] == jnp.arange(K)[None, :]).astype(jnp.float32)
    weight = lax.optimization_barrier(jnp.sum(class_hot * class_wt[None, :].astype(jnp.float32), axis=1))
    weight_total = jnp.sum(weight)
    index = jnp.arange(L * TAPS)
    earlier = (owners[:, None] == owners[None, :]) & (index[None, :] < index[:, None])
    slot = owners * CAP + lax.optimization_barrier(jnp.sum(earlier.astype(jnp.int32), axis=1))
    kernels = low(master[slot]).reshape(L, TAPS, C, C)
    errors = jnp.zeros((L,) + feats.shape, jnp.float32)
    start = low(feats.astype(jnp.float32) * mask_four)

    def forward(norms, head_now, errs):
        current = start
        inputs = []
        for layer in range(L):
            inputs.append(current)
            conv_out = low_back(conv_ref(current, kernels[layer]) + errs[layer])
            masked = conv_out * mask_four
            average = lax.optimization_barrier(jnp.sum(masked, axis=(0, 1, 2))) / count_all
            square = lax.optimization_barrier(jnp.sum(masked * conv_out, axis=(0, 1, 2))) / count_all
            inv_std = lax.rsqrt(square - average * average + EPS_NORM)
            normed = (conv_out - average) * inv_std
            act_out = jax.nn.silu(norms[layer, 0] * normed + norms[layer, 1]) * mask_four
            current = low(act_out) if layer < L - 1 else act_out
        pooled = lax.optimization_barrier(jnp.sum(current, axis=(1, 2))) / pixels[:, None]
        logits = jnp.dot(low(pooled), low(head_now[:C]), precision=HIGHEST) + head_now[C]
        log_prob = jax.nn.log_softmax(logits, axis=-1)
        return (-jnp.sum(weight * lax.optimization_barrier(jnp.sum(class_hot * log_prob, axis=1))), inputs)
    loss_sum, pull, inputs = jax.vjp(forward, norm_params, head, errors, has_aux=True)
    grad_norm, grad_head, grad_out = pull(jnp.ones_like(loss_sum))
    firsts, seconds = ([], [])
    for layer in range(L):
        act_proj = low(jnp.einsum('npqc,ci->npqi', inputs[layer], basis_in[layer].astype(jnp.float32), precision=HIGHEST))
        grad_proj = low(jnp.einsum('npqo,oj->npqj', grad_out[layer], basis_out[layer].astype(jnp.float32), precision=HIGHEST))
        first, second = image_sums(act_proj, grad_proj)
        firsts.append(first)
        seconds.append(second)
    proj_sum = jnp.stack(firsts).reshape(L * TAPS * C, C)
    proj_square = jnp.stack(seconds).reshape(L * TAPS * C, C)
    new_scales = DECAY * scales + (1.0 - DECAY) * proj_square / IMAGES
    precond = low(proj_sum / weight_total / (new_scales + DAMPING)).reshape(L * TAPS, C, C)
    basis_rows = jnp.repeat(basis_in.astype(jnp.float32), TAPS, axis=0)
    basis_cols = jnp.repeat(basis_out.astype(jnp.float32), TAPS, axis=0)
    turned = low(jnp.einsum('mci,mij->mcj', basis_rows, precond, precision=HIGHEST))
    update = jnp.einsum('mcj,moj->mco', turned, basis_cols, precision=HIGHEST)
    slot_grad = jnp.zeros(master.shape, jnp.float32).at[slot].set(update)
    new_master, new_moment1, new_moment2 = adamw(master, moment1, moment2, slot_grad, RATE_CONV)
    new_norm, new_norm_m, new_norm_v = adamw(norm_params, norm_m, norm_v, grad_norm / weight_total, RATE_NORM)
    new_head, new_head_m, new_head_v = adamw(head, head_m, head_v, grad_head / weight_total, RATE_HEAD)
    return (loss_sum, weight_total, new_scales, new_master, new_moment1, new_moment2, new_norm, new_norm_m, new_norm_v, new_head, new_head_m, new_head_v)
```

```python
import functools

import jax
import jax.numpy as jnp
from jax import lax
from jax.experimental import pallas as pl
from jax.experimental.pallas import tpu as pltpu
from jax.sharding import PartitionSpec as P

L = 2
TAPS = 9
STEP = 10


EPS_NORM = 1e-05
DAMPING = 0.001
DECAY = 0.95
BETA_ONE = 0.9
BETA_TWO = 0.999
ADAM_EPS = 1e-08
WEIGHT_DECAY = 0.01
RATE_CONV = 0.01
RATE_NORM = 0.5
RATE_HEAD = 0.02


def adamw(weight_now, first_now, second_now, gradient, rate):
    first_new = BETA_ONE * first_now + (1.0 - BETA_ONE) * gradient
    second_new = BETA_TWO * second_now + (1.0 - BETA_TWO) * gradient * gradient
    first_hat = first_new / (1.0 - BETA_ONE**STEP)
    second_hat = second_new / (1.0 - BETA_TWO**STEP)
    weight_new = weight_now - rate * (
        first_hat / (jnp.sqrt(second_hat) + ADAM_EPS) + WEIGHT_DECAY * weight_now
    )
    return (weight_new, first_new, second_new)


def pad_cells(values):
    return jnp.pad(values, ((0, 0), (1, 1), (1, 1), (0, 0)))


def conv_forward(inputs, kernel):
    side_len = inputs.shape[1]
    padded = pad_cells(inputs)
    total = None
    for tap in range(TAPS):
        shifted = padded[:, tap // 3 : tap // 3 + side_len, tap % 3 : tap % 3 + side_len]
        term = jnp.einsum("npqc,co->npqo", shifted, kernel[tap], preferred_element_type=jnp.float32)
        total = term if total is None else total + term
    return total


def conv_backward(grads, kernel):
    side_len = grads.shape[1]
    total = None
    for tap in range(TAPS):
        offset_row = tap // 3
        offset_col = tap % 3
        term = jnp.einsum("npqo,co->npqc", grads, kernel[tap], preferred_element_type=jnp.float32)
        term = jnp.pad(
            term, ((0, 0), (offset_row, 2 - offset_row), (offset_col, 2 - offset_col), (0, 0))
        )
        total = term if total is None else total + term
    return total[:, 1 : side_len + 1, 1 : side_len + 1]


def tap_sums(act_proj, grad_proj):
    side_len = act_proj.shape[1]
    padded = pad_cells(act_proj)
    firsts, seconds = ([], [])
    for tap in range(TAPS):
        shifted = padded[:, tap // 3 : tap // 3 + side_len, tap % 3 : tap % 3 + side_len]
        each = jnp.einsum("npqi,npqj->nij", shifted, grad_proj, preferred_element_type=jnp.float32)
        firsts.append(jnp.sum(each, axis=0))
        seconds.append(jnp.sum(each * each, axis=0))
    return jnp.concatenate([jnp.stack(firsts), jnp.stack(seconds)], axis=-1)


MESH = pl.DeviceIdType.MESH
SUB = 64
UNIT = 256


def _id(dp, side, blk):
    return (dp, side, blk)


def statistics_kernel(
    images,
    at_hbm,
    gr_hbm,
    out_ref,
    at_v,
    gr_v,
    side_send,
    side_recv,
    own,
    x_send,
    x_recv,
    x_keep,
    z1_send,
    z1_recv,
    z2_send,
    z2_recv,
    z2_keep,
    y_send,
    y_recv,
    y_keep,
    load_sem,
    side_ss,
    side_rs,
    x_ss,
    x_rs,
    z1_ss,
    z1_rs,
    z2_ss,
    z2_rs,
    y_ss,
    y_rs,
):
    dp, me_side, me_z = lax.axis_index("dp"), lax.axis_index("side"), lax.axis_index("blk")
    me_y, me_x = dp // 2, lax.rem(dp, 2)
    to_side = (dp, 1 - me_side, me_z)
    to_x = (me_y * 2 + 1 - me_x, me_side, me_z)
    to_y = ((1 - me_y) * 2 + me_x, me_side, me_z)
    z_low, z_high = lax.rem(me_z, 2), me_z // 2
    to_z1 = (dp, me_side, z_high * 2 + 1 - z_low)
    to_z2 = (dp, me_side, (1 - z_high) * 2 + z_low)
    steps = 2 * 9

    def loads():
        items = []
        for li in range(2):
            items.append((at_hbm.at[li], at_v.at[li], li * 4 + 3))
            for b in range(3):
                slot = b if li == 0 or b != 1 else 3
                items.append(
                    (
                        gr_hbm.at[li, pl.ds(b * images, images)],
                        gr_v.at[pl.ds(slot * images, images)],
                        li * 4 + b,
                    )
                )
        return {key: pltpu.make_async_copy(s, d, load_sem.at[key]) for s, d, key in items}

    load = loads()
    load[3].start()
    load[0].start()
    load[1].start()
    load[2].start()
    load[7].start()
    load[5].start()

    barrier = pltpu.get_barrier_semaphore()
    for target in (to_side, to_x, to_y, to_z1, to_z2):
        pl.semaphore_signal(barrier, inc=1, device_id=target, device_id_type=MESH)
    pl.semaphore_wait(barrier, 5)

    def remote(src, dst, ss, rs, target):
        return pltpu.make_async_remote_copy(
            src_ref=src, dst_ref=dst, send_sem=ss, recv_sem=rs, device_id=target,
            device_id_type=MESH,
        )

    def side_copy(k, j):
        ring = lax.rem(k, 2)
        return remote(
            side_send.at[ring, j], side_recv.at[ring, j], side_ss.at[ring, j],
            side_rs.at[ring, j], to_side,
        )

    def x_copy(k):
        ring = lax.rem(k, 4)
        return remote(x_send.at[ring], x_recv.at[k], x_ss.at[ring], x_rs.at[k], to_x)

    def z1_copy(k, w, slot):
        ring = lax.rem(k, 4)
        return remote(
            z1_send.at[ring, w], z1_recv.at[slot], z1_ss.at[ring, w], z1_rs.at[slot], to_z1
        )

    def z2_copy(k, w, slot):
        ring = lax.rem(k, 4)
        return remote(
            z2_send.at[ring, w], z2_recv.at[slot], z2_ss.at[ring, w], z2_rs.at[slot], to_z2
        )

    def y_copy(k, w, slot):
        ring = lax.rem(k, 4)
        return remote(
            y_send.at[ring, w], y_recv.at[slot], y_ss.at[ring, w], y_rs.at[slot], to_y
        )

    def product(k, j, half, store):
        li = k // 9
        unit = 9 * j + lax.rem(k, 9)
        tap = unit // 2
        base = lax.rem(unit, 2) * UNIT
        a, b = tap // 3, lax.rem(tap, 3)
        slot = jnp.where((b == 1) & (li == 1), 3, b)
        first_row = pl.multiple_of((2 - a) * 16, 16)
        cols = pl.ds(pl.multiple_of(half * 256, 256), 256)

        def tile(r, carry):
            rows = pl.ds(pl.multiple_of(base + r * 128, 128), 128)
            square = total = None
            for n in range(images):
                p = jnp.dot(
                    at_v[li, rows, n * 128 : (n + 1) * 128],
                    gr_v[slot * images + n, pl.ds(first_row, 128), cols],
                    preferred_element_type=jnp.float32,
                )
                square = p * p if square is None else square + p * p
                total = p if total is None else total + p
            store(r, total, square)
            return carry

        lax.fori_loop(0, 2, tile, 0)

    def subunits(k):
        li = k // 9
        i = lax.rem(k, 9)
        for w in range(4):
            v = 4 * i + w
            owner = v // 9
            yield w, li, owner, lax.rem(v, 9)

    def step(k, carry):
        @pl.when(k == 0)
        def _():
            load[3].wait()
            load[0].wait()
            load[1].wait()

        @pl.when(k == 1)
        def _():
            load[2].wait()

        @pl.when(k == 8)
        def _():
            load[4].start()

        @pl.when(k == 9)
        def _():
            load[6].start()
            load[7].wait()
            load[4].wait()
            load[5].wait()

        @pl.when(k == 10)
        def _():
            load[6].wait()

        @pl.when(k < steps)
        def _():
            ring = lax.rem(k, 2)
            for j in range(2):
                @pl.when(k >= 2)
                def _():
                    side_copy(k - 2, j).wait_send()

                def store(r, total, square, j=j):
                    rows = pl.ds(pl.multiple_of(r * 128, 128), 128)
                    side_send[ring, j, 0, rows, :] = total.astype(jnp.bfloat16)
                    side_send[ring, j, 1, rows, :] = square.astype(jnp.bfloat16)

                product(k, j, 1 - me_side, store)
                side_copy(k, j).start()
            for j in range(2):
                def store(r, total, square, j=j):
                    rows = pl.ds(pl.multiple_of(r * 128, 128), 128)
                    own[j, 0, rows, :] = total
                    own[j, 1, rows, :] = square

                product(k, j, me_side, store)
            for j in range(2):
                side_copy(k, j).wait_recv()
            @pl.when(k >= 4)
            def _():
                x_copy(k - 4).wait_send()
            mine = own[me_x] + side_recv[ring, me_x].astype(jnp.float32)
            x_keep[lax.rem(k, 4)] = mine
            other = own[1 - me_x] + side_recv[ring, 1 - me_x].astype(jnp.float32)
            x_send[lax.rem(k, 4)] = other.astype(jnp.bfloat16)
            x_copy(k).start()

        kx = k - 2

        @pl.when((kx >= 0) & (kx < steps))
        def _():
            ring = lax.rem(kx, 4)
            x_copy(kx).wait_recv()
            both = x_keep[ring] + x_recv[kx].astype(jnp.float32)
            x_keep[ring] = both
            for w, li, owner, q in subunits(kx):
                leaves = lax.rem(owner, 2) != z_low
                slot = li * 18 + (owner // 2) * 9 + q

                @pl.when(leaves)
                def _():
                    z1_send[ring, w] = x_keep[ring, :, w * SUB : (w + 1) * SUB, :].astype(
                        jnp.bfloat16
                    )
                    z1_copy(kx, w, slot).start()

        kz = k - 3

        @pl.when((kz >= 0) & (kz < steps))
        def _():
            ring = lax.rem(kz, 4)
            for w, li, owner, q in subunits(kz):
                slot = li * 18 + (owner // 2) * 9 + q
                stays = lax.rem(owner, 2) == z_low

                @pl.when(lax.rem(owner, 2) != z_low)
                def _():
                    z1_copy(kz, w, slot).wait_send()

                @pl.when(stays & (owner // 2 == z_high))
                def _():
                    z1_copy(kz, w, slot).wait_recv()
                    z2_keep[ring, w] = x_keep[ring, :, w * SUB : (w + 1) * SUB, :] + z1_recv[
                        slot
                    ].astype(jnp.float32)

                @pl.when(stays & (owner // 2 != z_high))
                def _():
                    z1_copy(kz, w, slot).wait_recv()
                    z2_send[ring, w] = (
                        x_keep[ring, :, w * SUB : (w + 1) * SUB, :]
                        + z1_recv[slot].astype(jnp.float32)
                    ).astype(jnp.bfloat16)
                    z2_copy(kz, w, li * 9 + q).start()

        kt = k - 4

        @pl.when((kt >= 0) & (kt < steps))
        def _():
            ring = lax.rem(kt, 4)
            for w, li, owner, q in subunits(kt):
                low_same = lax.rem(owner, 2) == z_low

                @pl.when(low_same & (owner // 2 != z_high))
                def _():
                    z2_copy(kt, w, li * 9 + q).wait_send()

                here = owner == me_z

                @pl.when(here & (me_y == 1 - li))
                def _():
                    z2_copy(kt, w, li * 9 + q).wait_recv()
                    y_keep[ring, w] = z2_keep[ring, w] + z2_recv[li * 9 + q].astype(jnp.float32)

                @pl.when(here & (me_y != 1 - li))
                def _():
                    z2_copy(kt, w, li * 9 + q).wait_recv()
                    y_send[ring, w] = (
                        z2_keep[ring, w] + z2_recv[li * 9 + q].astype(jnp.float32)
                    ).astype(jnp.bfloat16)
                    y_copy(kt, w, q).start()

        ky = k - 5

        @pl.when(ky >= 0)
        def _():
            ring = lax.rem(ky, 4)
            for w, li, owner, q in subunits(ky):
                here = owner == me_z

                @pl.when(here & (me_y == 1 - li))
                def _():
                    y_copy(ky, w, q).wait_recv()
                    value = y_keep[ring, w] + y_recv[q].astype(jnp.float32)
                    rows = pl.ds(pl.multiple_of(q * SUB, SUB), SUB)
                    out_ref[0, rows, :] = value[0]
                    out_ref[1, rows, :] = value[1]

                @pl.when(here & (me_y != 1 - li))
                def _():
                    y_copy(ky, w, q).wait_send()

        return carry

    lax.fori_loop(0, steps + 5, step, 0)
    for j in range(2):
        side_copy(steps - 2, j).wait_send()
        side_copy(steps - 1, j).wait_send()
    for k in range(steps - 4, steps):
        x_copy(k).wait_send()


def statistics(act_turned, grad_turned):
    images = act_turned.shape[2] // 128
    dma = pltpu.SemaphoreType.DMA
    low, full = jnp.bfloat16, jnp.float32
    pair = (2, UNIT, 256)
    small = (2, SUB, 256)
    return pl.pallas_call(
        functools.partial(statistics_kernel, images),
        out_shape=jax.ShapeDtypeStruct((2, 576, 256), full),
        in_specs=[pl.BlockSpec(memory_space=pl.ANY)] * 2,
        out_specs=pl.BlockSpec(memory_space=pltpu.VMEM),
        scratch_shapes=[
            pltpu.VMEM((2, 512, images * 128), low),
            pltpu.VMEM((4 * images, 160, 512), low),
            pltpu.VMEM((2, 2) + pair, low),
            pltpu.VMEM((2, 2) + pair, low),
            pltpu.VMEM((2,) + pair, full),
            pltpu.VMEM((4,) + pair, low),
            pltpu.VMEM((18,) + pair, low),
            pltpu.VMEM((4,) + pair, full),
            pltpu.VMEM((4, 4) + small, low),
            pltpu.VMEM((36,) + small, low),
            pltpu.VMEM((4, 4) + small, low),
            pltpu.VMEM((18,) + small, low),
            pltpu.VMEM((4, 4) + small, full),
            pltpu.VMEM((4, 4) + small, low),
            pltpu.VMEM((9,) + small, low),
            pltpu.VMEM((4, 4) + small, full),
            dma((8,)),
            dma((2, 2)),
            dma((2, 2)),
            dma((4,)),
            dma((18,)),
            dma((4, 4)),
            dma((36,)),
            dma((4, 4)),
            dma((18,)),
            dma((4, 4)),
            dma((9,)),
        ],
        name="statistics",
        compiler_params=pltpu.CompilerParams(
            collective_id=0, has_side_effects=True, vmem_limit_bytes=62 * 2**20
        ),
    )(act_turned, grad_turned)


def turned_operands(inputs, grad_low, basis_in, basis_out):
    images, side_len, _, width = inputs.shape
    wide = jnp.pad(inputs, ((0, 0), (0, 0), (0, 8), (0, 0))).reshape(images * 128, width)
    act = lax.dot_general(
        basis_in, wide, (((0,), (1,)), ((), ())), preferred_element_type=jnp.float32
    ).astype(jnp.bfloat16)
    grad = jnp.einsum(
        "npqo,oj->npqj", grad_low, basis_out, preferred_element_type=jnp.float32
    ).astype(jnp.bfloat16)
    zero = ((0, 0), (1, 1))
    shifts = [
        jnp.pad(grad[:, :, 1:], zero + ((0, 9), (0, 0))),
        jnp.pad(grad, zero + ((0, 8), (0, 0))),
        jnp.pad(grad[:, :, :7], zero + ((1, 8), (0, 0))),
    ]
    return act, jnp.concatenate([s.reshape(images, 160, width) for s in shifts], axis=0)


def shards(
    feats,
    size_group,
    labels,
    class_wt,
    owners,
    basis_in,
    basis_out,
    scales,
    master,
    moment1,
    moment2,
    norm_params,
    norm_m,
    norm_v,
    head,
    head_m,
    head_v,
):
    count_img = feats.shape[0]
    side_len = feats.shape[1]
    width = feats.shape[3]
    half = width // 2
    n_dp = lax.axis_size("dp")
    n_side = lax.axis_size("side")
    n_blk = lax.axis_size("blk")
    slots_dev = master.shape[0]
    matrices = owners.shape[0]
    block_rows = scales.shape[0]
    images_all = count_img * n_dp * n_side * n_blk
    index = jnp.arange(matrices)
    earlier = (owners[:, None] == owners[None, :]) & (index[None, :] < index[:, None])
    slot = owners * slots_dev + jnp.sum(earlier.astype(jnp.int32), axis=1)
    pieces = lax.all_gather(master.astype(jnp.bfloat16), ("side", "blk"), axis=0, tiled=True)
    pieces = pieces.reshape(n_side, n_blk * slots_dev, master.shape[1], width)
    pick = (slot[:, None] == jnp.arange(n_blk * slots_dev)[None, :]).astype(jnp.bfloat16)
    kernels = jnp.einsum("ms,hsrc->mhrc", pick, pieces, preferred_element_type=jnp.float32)
    kernels = kernels.astype(jnp.bfloat16).reshape(L, TAPS, width, width)
    line = jnp.arange(side_len)
    inner = (line[:, None] < side_len // 2) & (line[None, :] < side_len // 2)
    cell_mask = jnp.where((size_group == 1)[:, None, None], True, inner[None]).astype(jnp.float32)
    mask_four = cell_mask[..., None]
    pixels = jnp.sum(cell_mask, axis=(1, 2))
    class_hot = labels[:, None] == jnp.arange(class_wt.shape[0])[None, :]
    weight = jnp.sum(jnp.where(class_hot, class_wt[None, :], 0), axis=1).astype(jnp.float32)
    hot_float = class_hot.astype(jnp.float32)
    count_all, weight_all = lax.psum((jnp.sum(pixels), jnp.sum(weight)), ("dp", "side", "blk"))
    current = (feats.astype(jnp.float32) * mask_four).astype(jnp.bfloat16)
    kept = []
    act_out = None
    for layer in range(L):
        conv_out = conv_forward(current, kernels[layer])
        masked = conv_out * mask_four
        col_sum, sq_sum = lax.psum(
            (jnp.sum(masked, axis=(0, 1, 2)), jnp.sum(masked * conv_out, axis=(0, 1, 2))),
            ("dp", "side", "blk"),
        )
        average = col_sum / count_all
        inv_std = lax.rsqrt(sq_sum / count_all - average * average + EPS_NORM)
        normed = (conv_out - average) * inv_std
        pre_act = norm_params[layer, 0] * normed + norm_params[layer, 1]
        act_out = jax.nn.silu(pre_act) * mask_four
        kept.append((current, normed, pre_act, inv_std))
        current = act_out.astype(jnp.bfloat16)
    pooled = jnp.sum(act_out, axis=(1, 2)) / pixels[:, None]
    pooled_low = pooled.astype(jnp.bfloat16)
    head_low = head[:width].astype(jnp.bfloat16)
    logits = jnp.dot(pooled_low, head_low, preferred_element_type=jnp.float32) + head[width]
    log_prob = jax.nn.log_softmax(logits, axis=-1)
    loss_local = -jnp.sum(weight * jnp.sum(hot_float * log_prob, axis=1))
    d_logits = weight[:, None] * (jnp.exp(log_prob) - hot_float)
    grad_weights = jnp.dot(
        pooled_low.astype(jnp.float32).T, d_logits, precision=lax.Precision.HIGHEST
    )
    grad_head = jnp.concatenate([grad_weights, jnp.sum(d_logits, axis=0)[None]], axis=0)
    loss_all, head_all = lax.psum((loss_local, grad_head), ("dp", "side", "blk"))
    d_pooled = jnp.dot(d_logits, head_low.astype(jnp.float32).T, precision=lax.Precision.HIGHEST)
    d_act = d_pooled[:, None, None, :] / pixels[:, None, None, None] * mask_four
    fast = (n_dp, n_side, n_blk) == (4, 2, 4) and block_rows == 576
    terms = [None] * L
    grad_norm = [None] * L
    for layer in reversed(range(L)):
        inputs, normed, pre_act, inv_std = kept[layer]
        sigma = jax.nn.sigmoid(pre_act)
        d_pre = d_act * mask_four * sigma * (1.0 + pre_act * (1.0 - sigma))
        gamma_sum, beta_sum = lax.psum(
            (jnp.sum(d_pre * normed, axis=(0, 1, 2)), jnp.sum(d_pre, axis=(0, 1, 2))),
            ("dp", "side", "blk"),
        )
        grad_norm[layer] = jnp.stack([gamma_sum, beta_sum])
        gamma = norm_params[layer, 0]
        d_conv = (
            mask_four
            * inv_std
            * (
                gamma * d_pre
                - gamma * beta_sum / count_all
                - normed * gamma * gamma_sum / count_all
            )
        )
        grad_low = d_conv.astype(jnp.bfloat16)
        if layer > 0:
            d_act = conv_backward(grad_low, kernels[layer])
        if fast:
            terms[layer] = turned_operands(inputs, grad_low, basis_in[layer], basis_out[layer])
            continue
        act_proj = jnp.einsum(
            "npqc,ci->npqi", inputs, basis_in[layer], preferred_element_type=jnp.float32
        ).astype(jnp.bfloat16)
        grad_proj = jnp.einsum(
            "npqo,oj->npqj", grad_low, basis_out[layer], preferred_element_type=jnp.float32
        ).astype(jnp.bfloat16)
        terms[layer] = tap_sums(act_proj, grad_proj)
    if fast:
        proj_sum, proj_square = statistics(
            jnp.stack([terms[1][0], terms[0][0]]), jnp.stack([terms[1][1], terms[0][1]])
        )
    else:
        whole = jnp.stack(terms).reshape(n_dp, n_blk, block_rows, 2, 2, half)
        whole = whole.transpose(0, 4, 1, 2, 3, 5).reshape(n_dp * 2 * n_blk * block_rows, 2 * half)
        reduced = lax.psum_scatter(whole, ("dp", "side", "blk"), scatter_dimension=0, tiled=True)
        proj_sum = reduced[:, :half]
        proj_square = reduced[:, half:]
    new_scales = DECAY * scales + (1.0 - DECAY) * proj_square / images_all
    divided = (proj_sum / weight_all / (new_scales + DAMPING)).astype(jnp.bfloat16)
    spread = lax.all_gather(divided, ("dp", "side", "blk"), axis=0, tiled=True)
    spread = spread.reshape(n_dp, 2, n_blk, block_rows, half).transpose(0, 2, 3, 1, 4)
    precond_all = spread.reshape(matrices, width, width)
    slot_ids = lax.axis_index("blk") * slots_dev + jnp.arange(slots_dev)
    owned = (slot[None, :] == slot_ids[:, None]).astype(jnp.bfloat16)
    chosen = jnp.einsum(
        "qm,mij->qij", owned, precond_all, preferred_element_type=jnp.float32
    ).astype(jnp.bfloat16)
    layer_hot = (index[:, None] // TAPS == jnp.arange(L)[None, :]).astype(jnp.bfloat16)
    slot_layer = jnp.dot(owned, layer_hot, preferred_element_type=jnp.float32).astype(jnp.bfloat16)
    half_rows = lax.dynamic_slice_in_dim(
        basis_in, lax.axis_index("side") * master.shape[1], master.shape[1], 1
    )
    rows_slot = jnp.einsum(
        "ql,lci->qci", slot_layer, half_rows, preferred_element_type=jnp.float32
    ).astype(jnp.bfloat16)
    cols_slot = jnp.einsum(
        "ql,loj->qoj", slot_layer, basis_out, preferred_element_type=jnp.float32
    ).astype(jnp.bfloat16)
    turned = jnp.einsum(
        "qci,qij->qcj", rows_slot, chosen, preferred_element_type=jnp.float32
    ).astype(jnp.bfloat16)
    slot_grad = jnp.einsum("qcj,qoj->qco", turned, cols_slot, preferred_element_type=jnp.float32)
    new_master, new_moment1, new_moment2 = adamw(master, moment1, moment2, slot_grad, RATE_CONV)
    new_norm, new_norm_m, new_norm_v = adamw(
        norm_params, norm_m, norm_v, jnp.stack(grad_norm) / weight_all, RATE_NORM
    )
    new_head, new_head_m, new_head_v = adamw(head, head_m, head_v, head_all / weight_all, RATE_HEAD)
    return (
        loss_all,
        weight_all,
        new_scales,
        new_master,
        new_moment1,
        new_moment2,
        new_norm,
        new_norm_m,
        new_norm_v,
        new_head,
        new_head_m,
        new_head_v,
    )


def solution(mesh):
    return jax.shard_map(
        shards,
        mesh=mesh,
        in_specs=(
            P(("dp", "side", "blk"), None, None, None),
            P(("dp", "side", "blk")),
            P(("dp", "side", "blk")),
            P(),
            P(),
            P(),
            P(),
            P(("dp", "blk"), "side"),
            P("blk", "side", None),
            P("blk", "side", None),
            P("blk", "side", None),
            P(),
            P(),
            P(),
            P(),
            P(),
            P(),
        ),
        out_specs=(
            P(),
            P(),
            P(("dp", "blk"), "side"),
            P("blk", "side", None),
            P("blk", "side", None),
            P("blk", "side", None),
            P(),
            P(),
            P(),
            P(),
            P(),
            P(),
        ),
        check_vma=False,
    )
```

```python
import functools

import jax
import jax.numpy as jnp
from jax import lax
from jax.experimental import pallas as pl
from jax.experimental.pallas import tpu as pltpu
from jax.sharding import PartitionSpec as P

L = 2
TAPS = 9
STEP = 10


EPS_NORM = 1e-05
DAMPING = 0.001
DECAY = 0.95
BETA_ONE = 0.9
BETA_TWO = 0.999
ADAM_EPS = 1e-08
WEIGHT_DECAY = 0.01
RATE_CONV = 0.01
RATE_NORM = 0.5
RATE_HEAD = 0.02


def adamw(weight_now, first_now, second_now, gradient, rate):
    first_new = BETA_ONE * first_now + (1.0 - BETA_ONE) * gradient
    second_new = BETA_TWO * second_now + (1.0 - BETA_TWO) * gradient * gradient
    first_hat = first_new / (1.0 - BETA_ONE**STEP)
    second_hat = second_new / (1.0 - BETA_TWO**STEP)
    weight_new = weight_now - rate * (
        first_hat / (jnp.sqrt(second_hat) + ADAM_EPS) + WEIGHT_DECAY * weight_now
    )
    return (weight_new, first_new, second_new)


def pad_cells(values):
    return jnp.pad(values, ((0, 0), (1, 1), (1, 1), (0, 0)))


def conv_forward(inputs, kernel):
    side_len = inputs.shape[1]
    padded = pad_cells(inputs)
    total = None
    for tap in range(TAPS):
        shifted = padded[:, tap // 3 : tap // 3 + side_len, tap % 3 : tap % 3 + side_len]
        term = jnp.einsum("npqc,co->npqo", shifted, kernel[tap], preferred_element_type=jnp.float32)
        total = term if total is None else total + term
    return total


def conv_backward(grads, kernel):
    side_len = grads.shape[1]
    total = None
    for tap in range(TAPS):
        offset_row = tap // 3
        offset_col = tap % 3
        term = jnp.einsum("npqo,co->npqc", grads, kernel[tap], preferred_element_type=jnp.float32)
        term = jnp.pad(
            term, ((0, 0), (offset_row, 2 - offset_row), (offset_col, 2 - offset_col), (0, 0))
        )
        total = term if total is None else total + term
    return total[:, 1 : side_len + 1, 1 : side_len + 1]


def tap_sums(act_proj, grad_proj):
    side_len = act_proj.shape[1]
    padded = pad_cells(act_proj)
    firsts, seconds = ([], [])
    for tap in range(TAPS):
        shifted = padded[:, tap // 3 : tap // 3 + side_len, tap % 3 : tap % 3 + side_len]
        each = jnp.einsum("npqi,npqj->nij", shifted, grad_proj, preferred_element_type=jnp.float32)
        firsts.append(jnp.sum(each, axis=0))
        seconds.append(jnp.sum(each * each, axis=0))
    return jnp.concatenate([jnp.stack(firsts), jnp.stack(seconds)], axis=-1)


MESH = pl.DeviceIdType.MESH


def statistics_kernel(
    images,
    images_all,
    at_hbm,
    gr_hbm,
    scales_hbm,
    weight_ref,
    out,
    ns_out,
    at_v,
    gr_v,
    sc_v,
    ns_v,
    div_v,
    s_send,
    s_recv,
    x1_send,
    x1_recv,
    x1_keep,
    y1_send,
    y1_recv,
    y1_keep,
    x2_send,
    x2_recv,
    y2_send,
    y2_recv,
    two_keep,
    z_send,
    z_recv,
    z_keep,
    load_sem,
    misc_sem,
    local_sem,
    ss,
    s_rs,
    rs,
    z_ss,
    z_rs,
    gz_ss,
    gz_rs,
):
    low, full = jnp.bfloat16, jnp.float32
    dp, me_s, me_z = lax.axis_index("dp"), lax.axis_index("side"), lax.axis_index("blk")
    me_y, me_x = dp // 2, lax.rem(dp, 2)
    to_s = (dp, 1 - me_s, me_z)
    to_x = (me_y * 2 + 1 - me_x, me_s, me_z)
    to_y = ((1 - me_y) * 2 + me_x, me_s, me_z)
    steps = 2 * 9

    def remote(src, dst, send, recv, target):
        return pltpu.make_async_remote_copy(
            src_ref=src,
            dst_ref=dst,
            send_sem=send,
            recv_sem=recv,
            device_id=target,
            device_id_type=MESH,
        )

    def load(li, what):
        if what == 3:
            return pltpu.make_async_copy(at_hbm.at[li], at_v.at[li], load_sem.at[li, 3])
        at = pl.ds(what * images, images)
        return pltpu.make_async_copy(gr_hbm.at[li, at], gr_v.at[li, at], load_sem.at[li, what])

    for what in (3, 0, 1, 2):
        load(0, what).start()

    barrier = pltpu.get_barrier_semaphore()
    away = [(dp, me_s, lax.rem(me_z + d, 4)) for d in (1, 2, 3)]
    for target in [to_s, to_x, to_y] + away:
        pl.semaphore_signal(barrier, inc=1, device_id=target, device_id_type=MESH)
    pl.semaphore_wait(barrier, 6)

    sc_local = pltpu.make_async_copy(scales_hbm.at[:, me_y], sc_v.at[1 - me_y], misc_sem.at[0])
    sc_remote = remote(
        scales_hbm.at[:, 1 - me_y], sc_v.at[1 - me_y], misc_sem.at[1], misc_sem.at[2], to_y
    )
    sc_local.start()
    sc_remote.start()

    def side_copy(k):
        return remote(
            s_send.at[lax.rem(k, 2)],
            s_recv.at[lax.rem(k, 4)],
            ss.at[0, lax.rem(k, 2)],
            s_rs.at[lax.rem(k, 4)],
            to_s,
        )

    def x1_copy(j):
        ring = lax.rem(j, 2)
        return remote(x1_send.at[ring], x1_recv.at[j], ss.at[1, ring], rs.at[0, j], to_x)

    def y1_copy(j):
        ring = lax.rem(j, 2)
        return remote(
            y1_send.at[ring, 1 - me_y], y1_recv.at[j], ss.at[2, ring], rs.at[1, j], to_y
        )

    def x2_copy(j):
        ring = lax.rem(j, 2)
        return remote(x2_send.at[ring], x2_recv.at[j], ss.at[3, ring], rs.at[2, j], to_x)

    def y2_copy(j):
        ring = lax.rem(j, 2)
        return remote(y2_send.at[ring], y2_recv.at[j], ss.at[4, ring], rs.at[3, j], to_y)

    def z_copy(j, d):
        ring, other = lax.rem(j, 2), lax.rem(me_z + d, 4)
        return remote(
            z_send.at[ring, other],
            z_recv.at[j, d - 1],
            z_ss.at[ring, d - 1],
            z_rs.at[j, d - 1],
            (dp, me_s, other),
        )

    def place(j):
        return 1 - j // 9, lax.rem(j, 9)

    def local_copy(j):
        layer, i = place(j)
        ring = lax.rem(j, 2)
        return pltpu.make_async_copy(
            div_v.at[ring], out.at[me_s, layer, me_x, me_z, i, me_y], local_sem.at[ring]
        )

    def gz_copy(j, d):
        layer, i = place(j)
        ring, other = lax.rem(j, 2), lax.rem(me_z + d, 4)
        return remote(
            div_v.at[ring],
            out.at[me_s, layer, me_x, me_z, i, me_y],
            gz_ss.at[ring, d - 1],
            gz_rs.at[j, d - 1],
            (dp, me_s, other),
        )

    lower, upper = pl.ds(0, 2), pl.ds(2, 2)

    def spread(j, which, kind, target):
        part = out.at[which]
        return remote(part, part, ss.at[kind, lax.rem(j, 2)], rs.at[kind - 1, j], target)

    def g1y_copy(j):
        layer, i = place(j)
        return spread(j, (me_s, layer, me_x, lower, i, me_y), 5, to_y)

    def g1x_copy(j):
        layer, i = place(j)
        return spread(j, (me_s, layer, me_x, upper, i, me_y), 6, to_x)

    def g2x_copy(j):
        layer, i = place(j)
        return spread(j, (me_s, layer, me_x, lower, i), 7, to_x)

    def g2y_copy(j):
        layer, i = place(j)
        return spread(j, (me_s, layer, pl.ds(0, 2), upper, i, me_y), 8, to_y)

    def gs_copy(j):
        layer, i = place(j)
        return spread(j, (me_s, layer, pl.ds(0, 2), pl.ds(0, 4), i), 9, to_s)

    def products(j, half, ahead, store):
        li, i = j // 9, lax.rem(j, 9)
        cols = pl.ds(pl.multiple_of(half * 256, 256), 256)
        for u in range(8):
            x_to = ahead if u < 4 else 1 - ahead
            row = x_to * 2304 + (u % 4) * 576 + 64 * i
            tap = row // 512
            rows = pl.ds(pl.multiple_of(lax.rem(row, 512), 64), 64)
            near = pl.ds(pl.multiple_of((2 - tap // 3) * 16, 16), 128)
            shift = lax.rem(tap, 3) * images
            square = total = None
            for n in range(images):
                p = jnp.dot(
                    at_v[li, rows, n * 128 : (n + 1) * 128],
                    gr_v[li, shift + n, near, cols],
                    preferred_element_type=full,
                )
                square = p * p if square is None else square + p * p
                total = p if total is None else total + p
            store(u, x_to, u % 4, total, square)

    def step(k, carry):
        for at, needs in ((0, (0, 1, 2, 3)), (9, (0, 1, 2, 3))):
            @pl.when(k == at)
            def _():
                for what in needs:
                    load(at // 9, what).wait()

        @pl.when(k == 1)
        def _():
            for what in range(4):
                load(1, what).start()

        @pl.when((k >= 2) & (k < steps))
        def _():
            side_copy(k - 2).wait_send()

        @pl.when(k < steps)
        def _():
            ring = lax.rem(k, 2)

            def store(u, x_to, z_to, total, square):
                s_send[ring, u, 0] = total.astype(low)
                s_send[ring, u, 1] = square.astype(low)

            products(k, 1 - me_s, 0, store)
            side_copy(k).start()

        j = k - 1

        @pl.when((j >= 2) & (j < steps))
        def _():
            x1_copy(j - 2).wait_send()
            y1_copy(j - 2).wait_send()

        @pl.when((j >= 0) & (j < steps))
        def _():
            ring, four = lax.rem(j, 2), lax.rem(j, 4)
            side_copy(j).wait_recv()

            def store(u, x_to, z_to, total, square):
                got = s_recv[four, x_to * 4 + z_to].astype(full)
                both = (total + got[0], square + got[1])
                for c in range(2):
                    if z_to < 2 and u < 4:
                        x1_send[ring, z_to, c] = both[c].astype(low)
                    elif z_to < 2:
                        x1_keep[ring, z_to, c] = both[c]
                    else:
                        for y_to in range(2):
                            piece = both[c][y_to * 32 : y_to * 32 + 32]
                            y1_send[ring, y_to, x_to, z_to - 2, c] = piece.astype(low)
                            y1_keep[ring, y_to, x_to, z_to - 2, c] = piece

            products(j, me_s, 1 - me_x, store)
            x1_copy(j).start()
            y1_copy(j).start()

        j2 = k - 2

        @pl.when((j2 >= 0) & (j2 < steps))
        def _():
            ring = lax.rem(j2, 2)

            @pl.when(j2 >= 2)
            def _():
                x2_copy(j2 - 2).wait_send()
                y2_copy(j2 - 2).wait_send()

            x1_copy(j2).wait_recv()
            here = pl.ds(pl.multiple_of(me_y * 32, 32), 32)
            there = pl.ds(pl.multiple_of((1 - me_y) * 32, 32), 32)
            for z_to in range(2):
                for c in range(2):
                    two_keep[ring, z_to, c] = x1_keep[ring, z_to, c, here, :] + x1_recv[
                        j2, z_to, c, here, :
                    ].astype(full)
                    y2_send[ring, z_to, c] = (
                        x1_keep[ring, z_to, c, there, :]
                        + x1_recv[j2, z_to, c, there, :].astype(full)
                    ).astype(low)
            y2_copy(j2).start()
            y1_copy(j2).wait_recv()
            for z_to in range(2):
                two_keep[ring, 2 + z_to] = y1_keep[ring, me_y, me_x, z_to] + y1_recv[
                    j2, me_x, z_to
                ].astype(full)
                x2_send[ring, z_to] = (
                    y1_keep[ring, me_y, 1 - me_x, z_to]
                    + y1_recv[j2, 1 - me_x, z_to].astype(full)
                ).astype(low)
            x2_copy(j2).start()

        j3 = k - 3

        @pl.when((j3 >= 0) & (j3 < steps))
        def _():
            ring = lax.rem(j3, 2)

            @pl.when(j3 >= 2)
            def _():
                for d in (1, 2, 3):
                    z_copy(j3 - 2, d).wait_send()

            y2_copy(j3).wait_recv()
            x2_copy(j3).wait_recv()
            for z_to in range(4):
                got = y2_recv[j3, z_to] if z_to < 2 else x2_recv[j3, z_to - 2]
                both = two_keep[ring, z_to] + got.astype(full)
                z_keep[ring, z_to] = both
                z_send[ring, z_to] = both.astype(low)
            for d in (1, 2, 3):
                z_copy(j3, d).start()

        j4 = k - 4

        @pl.when(j4 == 0)
        def _():
            sc_local.wait()
            sc_remote.wait_recv()

        @pl.when((j4 >= 0) & (j4 < steps))
        def _():
            ring, li, i = lax.rem(j4, 2), j4 // 9, lax.rem(j4, 9)

            @pl.when(j4 >= 2)
            def _():
                for d in (1, 2, 3):
                    gz_copy(j4 - 2, d).wait_send()

            for d in (1, 2, 3):
                z_copy(j4, d).wait_recv()
            got = z_recv[j4].astype(full)
            both = z_keep[ring, me_z] + got[0] + got[1] + got[2]
            scale = DECAY * sc_v[li, i] + (1.0 - DECAY) * both[1] / images_all
            ns_v[li, i] = scale
            div_v[ring] = (both[0] / weight_ref[...] / (scale + DAMPING)).astype(low)
            local_copy(j4).start()
            for d in (1, 2, 3):
                gz_copy(j4, d).start()

        for li in range(2):
            @pl.when((j4 == 9 * li + 8) & (me_y == 1 - li))
            def _():
                pltpu.make_async_copy(ns_v.at[li], ns_out.at[:, me_y], misc_sem.at[3]).start()

            @pl.when((j4 == 9 * li + 8) & (me_y == li))
            def _():
                remote(
                    ns_v.at[li], ns_out.at[:, me_y], misc_sem.at[4], misc_sem.at[5], to_y
                ).start()

        j5 = k - 5

        @pl.when((j5 >= 0) & (j5 < steps))
        def _():
            @pl.when(j5 >= 2)
            def _():
                g1y_copy(j5 - 2).wait_send()
                g1x_copy(j5 - 2).wait_send()

            local_copy(j5).wait()
            for d in (1, 2, 3):
                gz_copy(j5, d).wait_recv()
            g1y_copy(j5).start()
            g1x_copy(j5).start()

        j6 = k - 6

        @pl.when((j6 >= 0) & (j6 < steps))
        def _():
            @pl.when(j6 >= 2)
            def _():
                g2y_copy(j6 - 2).wait_send()
                g2x_copy(j6 - 2).wait_send()

            g1y_copy(j6).wait_recv()
            g2x_copy(j6).start()
            g1x_copy(j6).wait_recv()
            g2y_copy(j6).start()

        j7 = k - 7

        @pl.when(j7 >= 0)
        def _():
            @pl.when(j7 >= 2)
            def _():
                gs_copy(j7 - 2).wait_send()

            g2x_copy(j7).wait_recv()
            g2y_copy(j7).wait_recv()
            gs_copy(j7).start()

        return carry

    lax.fori_loop(0, steps + 7, step, 0)

    def finish(j, carry):
        gs_copy(j).wait_recv()
        return carry

    lax.fori_loop(0, steps, finish, 0)
    sc_remote.wait_send()
    li = 1 - me_y
    pltpu.make_async_copy(ns_v.at[li], ns_out.at[:, me_y], misc_sem.at[3]).wait()
    ns_remote = remote(ns_v.at[0], ns_out.at[:, 0], misc_sem.at[4], misc_sem.at[5], to_y)
    ns_remote.wait_send()
    ns_remote.wait_recv()
    for j in (steps - 2, steps - 1):
        for copy in (side_copy, x1_copy, y1_copy, x2_copy, y2_copy):
            copy(j).wait_send()
        for copy in (g1y_copy, g1x_copy, g2y_copy, g2x_copy, gs_copy):
            copy(j).wait_send()
        for d in (1, 2, 3):
            z_copy(j, d).wait_send()
            gz_copy(j, d).wait_send()


def statistics(act_turned, grad_turned, scales, weight_all, images_all):
    images = act_turned.shape[2] // 128
    dma = pltpu.SemaphoreType.DMA
    low, full = jnp.bfloat16, jnp.float32
    tile, piece = (2, 64, 256), (2, 32, 256)
    any_spec = pl.BlockSpec(memory_space=pl.ANY)
    divided, new_scales = pl.pallas_call(
        functools.partial(statistics_kernel, images, images_all),
        out_shape=[
            jax.ShapeDtypeStruct((2, 2, 2, 4, 9, 2, 32, 256), low),
            jax.ShapeDtypeStruct((9, 2, 32, 256), full),
        ],
        in_specs=[any_spec, any_spec, any_spec, pl.BlockSpec(memory_space=pltpu.VMEM)],
        out_specs=[any_spec, any_spec],
        scratch_shapes=[
            pltpu.VMEM((2, 512, images * 128), low),
            pltpu.VMEM((2, 3 * images, 160, 512), low),
            pltpu.VMEM((2, 9, 32, 256), full),
            pltpu.VMEM((2, 9, 32, 256), full),
            pltpu.VMEM((2, 32, 256), low),
            pltpu.VMEM((2, 8) + tile, low),
            pltpu.VMEM((4, 8) + tile, low),
            pltpu.VMEM((2, 2) + tile, low),
            pltpu.VMEM((18, 2) + tile, low),
            pltpu.VMEM((2, 2) + tile, full),
            pltpu.VMEM((2, 2, 2, 2) + piece, low),
            pltpu.VMEM((18, 2, 2) + piece, low),
            pltpu.VMEM((2, 2, 2, 2) + piece, full),
            pltpu.VMEM((2, 2) + piece, low),
            pltpu.VMEM((18, 2) + piece, low),
            pltpu.VMEM((2, 2) + piece, low),
            pltpu.VMEM((18, 2) + piece, low),
            pltpu.VMEM((2, 4) + piece, full),
            pltpu.VMEM((2, 4) + piece, low),
            pltpu.VMEM((18, 3) + piece, low),
            pltpu.VMEM((2, 4) + piece, full),
            dma((2, 4)),
            dma((6,)),
            dma((2,)),
            dma((10, 2)),
            dma((4,)),
            dma((9, 18)),
            dma((2, 3)),
            dma((18, 3)),
            dma((2, 3)),
            dma((18, 3)),
        ],
        name="statistics",
        compiler_params=pltpu.CompilerParams(
            collective_id=0, has_side_effects=True, vmem_limit_bytes=63 * 2**20
        ),
    )(
        act_turned,
        grad_turned,
        scales.reshape(9, 2, 32, 256),
        jnp.full((1, 256), weight_all, full),
    )
    return divided.reshape(2, 18, 512, 256), new_scales.reshape(576, 256)


def turned_operands(inputs, grad_low, basis_in, basis_out):
    images, side_len, _, width = inputs.shape
    wide = jnp.pad(inputs, ((0, 0), (0, 0), (0, 8), (0, 0))).reshape(images * 128, width)
    act = lax.dot_general(
        basis_in, wide, (((0,), (1,)), ((), ())), preferred_element_type=jnp.float32
    ).astype(jnp.bfloat16)
    grad = jnp.einsum(
        "npqo,oj->npqj", grad_low, basis_out, preferred_element_type=jnp.float32
    ).astype(jnp.bfloat16)
    zero = ((0, 0), (1, 1))
    shifts = [
        jnp.pad(grad[:, :, 1:], zero + ((0, 9), (0, 0))),
        jnp.pad(grad, zero + ((0, 8), (0, 0))),
        jnp.pad(grad[:, :, :7], zero + ((1, 8), (0, 0))),
    ]
    return act, jnp.concatenate([s.reshape(images, 160, width) for s in shifts], axis=0)


def owned_kernel(
    which, divided, rows_ref, cols_ref, w_ref, m_ref, v_ref, new_w, new_m, new_v
):
    low, full = jnp.bfloat16, jnp.float32
    held = which[1, pl.program_id(0)].astype(full)
    rows = rows_ref[0]
    turned = [
        jnp.dot(rows, divided[s, 0], preferred_element_type=full).astype(low) for s in range(2)
    ]
    gradient = lax.dot_general(
        jnp.concatenate(turned, axis=1),
        cols_ref[0],
        (((1,), (1,)), ((), ())),
        preferred_element_type=full,
    )
    new_w[0], new_m[0], new_v[0] = adamw(
        w_ref[0], m_ref[0], v_ref[0], gradient * held, RATE_CONV
    )


def owned_update(divided, basis_in, basis_out, master, moment1, moment2, which):
    slots, half, width = master.shape
    block = pl.BlockSpec((1, half, width), lambda q, which: (q, 0, 0))
    return pl.pallas_call(
        owned_kernel,
        grid_spec=pltpu.PrefetchScalarGridSpec(
            num_scalar_prefetch=1,
            grid=(slots,),
            in_specs=[
                pl.BlockSpec((2, 1, width, half), lambda q, which: (0, which[0, q], 0, 0)),
                pl.BlockSpec((1, half, width), lambda q, which: (which[0, q] // TAPS, which[2, q], 0)),
                pl.BlockSpec((1, width, width), lambda q, which: (which[0, q] // TAPS, 0, 0)),
                block,
                block,
                block,
            ],
            out_specs=[block, block, block],
        ),
        out_shape=[jax.ShapeDtypeStruct(master.shape, jnp.float32)] * 3,
        name="owned_update",
        compiler_params=pltpu.CompilerParams(vmem_limit_bytes=32 * 2**20),
    )(which, divided, basis_in, basis_out, master, moment1, moment2)


def shards(
    feats,
    size_group,
    labels,
    class_wt,
    owners,
    basis_in,
    basis_out,
    scales,
    master,
    moment1,
    moment2,
    norm_params,
    norm_m,
    norm_v,
    head,
    head_m,
    head_v,
):
    count_img = feats.shape[0]
    side_len = feats.shape[1]
    width = feats.shape[3]
    half = width // 2
    n_dp = lax.axis_size("dp")
    n_side = lax.axis_size("side")
    n_blk = lax.axis_size("blk")
    slots_dev = master.shape[0]
    matrices = owners.shape[0]
    block_rows = scales.shape[0]
    images_all = count_img * n_dp * n_side * n_blk
    index = jnp.arange(matrices)
    earlier = (owners[:, None] == owners[None, :]) & (index[None, :] < index[:, None])
    slot = owners * slots_dev + jnp.sum(earlier.astype(jnp.int32), axis=1)
    pieces = lax.all_gather(master.astype(jnp.bfloat16), ("side", "blk"), axis=0, tiled=True)
    pieces = pieces.reshape(n_side, n_blk * slots_dev, master.shape[1], width)
    pick = (slot[:, None] == jnp.arange(n_blk * slots_dev)[None, :]).astype(jnp.bfloat16)
    kernels = jnp.einsum("ms,hsrc->mhrc", pick, pieces, preferred_element_type=jnp.float32)
    kernels = kernels.astype(jnp.bfloat16).reshape(L, TAPS, width, width)
    line = jnp.arange(side_len)
    inner = (line[:, None] < side_len // 2) & (line[None, :] < side_len // 2)
    cell_mask = jnp.where((size_group == 1)[:, None, None], True, inner[None]).astype(jnp.float32)
    mask_four = cell_mask[..., None]
    pixels = jnp.sum(cell_mask, axis=(1, 2))
    class_hot = labels[:, None] == jnp.arange(class_wt.shape[0])[None, :]
    weight = jnp.sum(jnp.where(class_hot, class_wt[None, :], 0), axis=1).astype(jnp.float32)
    hot_float = class_hot.astype(jnp.float32)
    count_all, weight_all = lax.psum((jnp.sum(pixels), jnp.sum(weight)), ("dp", "side", "blk"))
    current = (feats.astype(jnp.float32) * mask_four).astype(jnp.bfloat16)
    kept = []
    act_out = None
    for layer in range(L):
        conv_out = conv_forward(current, kernels[layer])
        masked = conv_out * mask_four
        col_sum, sq_sum = lax.psum(
            (jnp.sum(masked, axis=(0, 1, 2)), jnp.sum(masked * conv_out, axis=(0, 1, 2))),
            ("dp", "side", "blk"),
        )
        average = col_sum / count_all
        inv_std = lax.rsqrt(sq_sum / count_all - average * average + EPS_NORM)
        normed = (conv_out - average) * inv_std
        pre_act = norm_params[layer, 0] * normed + norm_params[layer, 1]
        act_out = jax.nn.silu(pre_act) * mask_four
        kept.append((current, normed, pre_act, inv_std))
        current = act_out.astype(jnp.bfloat16)
    pooled = jnp.sum(act_out, axis=(1, 2)) / pixels[:, None]
    pooled_low = pooled.astype(jnp.bfloat16)
    head_low = head[:width].astype(jnp.bfloat16)
    logits = jnp.dot(pooled_low, head_low, preferred_element_type=jnp.float32) + head[width]
    log_prob = jax.nn.log_softmax(logits, axis=-1)
    loss_local = -jnp.sum(weight * jnp.sum(hot_float * log_prob, axis=1))
    d_logits = weight[:, None] * (jnp.exp(log_prob) - hot_float)
    grad_weights = jnp.dot(
        pooled_low.astype(jnp.float32).T, d_logits, precision=lax.Precision.HIGHEST
    )
    grad_head = jnp.concatenate([grad_weights, jnp.sum(d_logits, axis=0)[None]], axis=0)
    loss_all, head_all = lax.psum((loss_local, grad_head), ("dp", "side", "blk"))
    d_pooled = jnp.dot(d_logits, head_low.astype(jnp.float32).T, precision=lax.Precision.HIGHEST)
    d_act = d_pooled[:, None, None, :] / pixels[:, None, None, None] * mask_four
    fast = (n_dp, n_side, n_blk) == (4, 2, 4) and block_rows == 576
    terms = [None] * L
    grad_norm = [None] * L
    for layer in reversed(range(L)):
        inputs, normed, pre_act, inv_std = kept[layer]
        sigma = jax.nn.sigmoid(pre_act)
        d_pre = d_act * mask_four * sigma * (1.0 + pre_act * (1.0 - sigma))
        gamma_sum, beta_sum = lax.psum(
            (jnp.sum(d_pre * normed, axis=(0, 1, 2)), jnp.sum(d_pre, axis=(0, 1, 2))),
            ("dp", "side", "blk"),
        )
        grad_norm[layer] = jnp.stack([gamma_sum, beta_sum])
        gamma = norm_params[layer, 0]
        d_conv = (
            mask_four
            * inv_std
            * (
                gamma * d_pre
                - gamma * beta_sum / count_all
                - normed * gamma * gamma_sum / count_all
            )
        )
        grad_low = d_conv.astype(jnp.bfloat16)
        if layer > 0:
            d_act = conv_backward(grad_low, kernels[layer])
        if fast:
            terms[layer] = turned_operands(inputs, grad_low, basis_in[layer], basis_out[layer])
            continue
        act_proj = jnp.einsum(
            "npqc,ci->npqi", inputs, basis_in[layer], preferred_element_type=jnp.float32
        ).astype(jnp.bfloat16)
        grad_proj = jnp.einsum(
            "npqo,oj->npqj", grad_low, basis_out[layer], preferred_element_type=jnp.float32
        ).astype(jnp.bfloat16)
        terms[layer] = tap_sums(act_proj, grad_proj)
    slot_ids = lax.axis_index("blk") * slots_dev + jnp.arange(slots_dev)
    hits = slot[None, :] == slot_ids[:, None]
    which = jnp.stack(
        [
            jnp.sum(jnp.where(hits, index[None, :], 0), axis=1),
            jnp.sum(hits.astype(jnp.int32), axis=1),
            jnp.full((slots_dev,), lax.axis_index("side"), jnp.int32),
        ]
    ).astype(jnp.int32)
    if fast:
        divided, new_scales = statistics(
            jnp.stack([terms[1][0], terms[0][0]]),
            jnp.stack([terms[1][1], terms[0][1]]),
            scales,
            weight_all,
            images_all,
        )
        new_master, new_moment1, new_moment2 = owned_update(
            divided, basis_in, basis_out, master, moment1, moment2, which
        )
    else:
        whole = jnp.stack(terms).reshape(n_dp, n_blk, block_rows, 2, 2, half)
        whole = whole.transpose(0, 4, 1, 2, 3, 5).reshape(n_dp * 2 * n_blk * block_rows, 2 * half)
        reduced = lax.psum_scatter(whole, ("dp", "side", "blk"), scatter_dimension=0, tiled=True)
        proj_sum = reduced[:, :half]
        proj_square = reduced[:, half:]
        new_scales = DECAY * scales + (1.0 - DECAY) * proj_square / images_all
        divided = (proj_sum / weight_all / (new_scales + DAMPING)).astype(jnp.bfloat16)
        spread = lax.all_gather(divided, ("dp", "side", "blk"), axis=0, tiled=True)
        spread = spread.reshape(n_dp, 2, n_blk, block_rows, half).transpose(0, 2, 3, 1, 4)
        precond_all = spread.reshape(matrices, width, width)
        slot_ids = lax.axis_index("blk") * slots_dev + jnp.arange(slots_dev)
        owned = (slot[None, :] == slot_ids[:, None]).astype(jnp.bfloat16)
        chosen = jnp.einsum(
            "qm,mij->qij", owned, precond_all, preferred_element_type=jnp.float32
        ).astype(jnp.bfloat16)
        layer_hot = (index[:, None] // TAPS == jnp.arange(L)[None, :]).astype(jnp.bfloat16)
        slot_layer = jnp.dot(owned, layer_hot, preferred_element_type=jnp.float32).astype(jnp.bfloat16)
        half_rows = lax.dynamic_slice_in_dim(
            basis_in, lax.axis_index("side") * master.shape[1], master.shape[1], 1
        )
        rows_slot = jnp.einsum(
            "ql,lci->qci", slot_layer, half_rows, preferred_element_type=jnp.float32
        ).astype(jnp.bfloat16)
        cols_slot = jnp.einsum(
            "ql,loj->qoj", slot_layer, basis_out, preferred_element_type=jnp.float32
        ).astype(jnp.bfloat16)
        turned = jnp.einsum(
            "qci,qij->qcj", rows_slot, chosen, preferred_element_type=jnp.float32
        ).astype(jnp.bfloat16)
        slot_grad = jnp.einsum("qcj,qoj->qco", turned, cols_slot, preferred_element_type=jnp.float32)
        new_master, new_moment1, new_moment2 = adamw(master, moment1, moment2, slot_grad, RATE_CONV)
    new_norm, new_norm_m, new_norm_v = adamw(
        norm_params, norm_m, norm_v, jnp.stack(grad_norm) / weight_all, RATE_NORM
    )
    new_head, new_head_m, new_head_v = adamw(head, head_m, head_v, head_all / weight_all, RATE_HEAD)
    return (
        loss_all,
        weight_all,
        new_scales,
        new_master,
        new_moment1,
        new_moment2,
        new_norm,
        new_norm_m,
        new_norm_v,
        new_head,
        new_head_m,
        new_head_v,
    )


def solution(mesh):
    return jax.shard_map(
        shards,
        mesh=mesh,
        in_specs=(
            P(("dp", "side", "blk"), None, None, None),
            P(("dp", "side", "blk")),
            P(("dp", "side", "blk")),
            P(),
            P(),
            P(),
            P(),
            P(("dp", "blk"), "side"),
            P("blk", "side", None),
            P("blk", "side", None),
            P("blk", "side", None),
            P(),
            P(),
            P(),
            P(),
            P(),
            P(),
        ),
        out_specs=(
            P(),
            P(),
            P(("dp", "blk"), "side"),
            P("blk", "side", None),
            P("blk", "side", None),
            P("blk", "side", None),
            P(),
            P(),
            P(),
            P(),
            P(),
            P(),
        ),
        check_vma=False,
    )
```

```python
import functools

import jax
import jax.numpy as jnp
from jax import lax
from jax.experimental import pallas as pl
from jax.experimental.pallas import tpu as pltpu
from jax.sharding import PartitionSpec as P

L = 2
TAPS = 9
STEP = 10


EPS_NORM = 1e-05
DAMPING = 0.001
DECAY = 0.95
BETA_ONE = 0.9
BETA_TWO = 0.999
ADAM_EPS = 1e-08
WEIGHT_DECAY = 0.01
RATE_CONV = 0.01
RATE_NORM = 0.5
RATE_HEAD = 0.02


def adamw(weight_now, first_now, second_now, gradient, rate):
    first_new = BETA_ONE * first_now + (1.0 - BETA_ONE) * gradient
    second_new = BETA_TWO * second_now + (1.0 - BETA_TWO) * gradient * gradient
    first_hat = first_new / (1.0 - BETA_ONE**STEP)
    second_hat = second_new / (1.0 - BETA_TWO**STEP)
    weight_new = weight_now - rate * (
        first_hat / (jnp.sqrt(second_hat) + ADAM_EPS) + WEIGHT_DECAY * weight_now
    )
    return (weight_new, first_new, second_new)


def pad_cells(values):
    return jnp.pad(values, ((0, 0), (1, 1), (1, 1), (0, 0)))


def conv_forward(inputs, kernel):
    side_len = inputs.shape[1]
    padded = pad_cells(inputs)
    total = None
    for tap in range(TAPS):
        shifted = padded[:, tap // 3 : tap // 3 + side_len, tap % 3 : tap % 3 + side_len]
        term = jnp.einsum("npqc,co->npqo", shifted, kernel[tap], preferred_element_type=jnp.float32)
        total = term if total is None else total + term
    return total


def conv_backward(grads, kernel):
    side_len = grads.shape[1]
    total = None
    for tap in range(TAPS):
        offset_row = tap // 3
        offset_col = tap % 3
        term = jnp.einsum("npqo,co->npqc", grads, kernel[tap], preferred_element_type=jnp.float32)
        term = jnp.pad(
            term, ((0, 0), (offset_row, 2 - offset_row), (offset_col, 2 - offset_col), (0, 0))
        )
        total = term if total is None else total + term
    return total[:, 1 : side_len + 1, 1 : side_len + 1]


def tap_sums(act_proj, grad_proj):
    side_len = act_proj.shape[1]
    padded = pad_cells(act_proj)
    firsts, seconds = ([], [])
    for tap in range(TAPS):
        shifted = padded[:, tap // 3 : tap // 3 + side_len, tap % 3 : tap % 3 + side_len]
        each = jnp.einsum("npqi,npqj->nij", shifted, grad_proj, preferred_element_type=jnp.float32)
        firsts.append(jnp.sum(each, axis=0))
        seconds.append(jnp.sum(each * each, axis=0))
    return jnp.concatenate([jnp.stack(firsts), jnp.stack(seconds)], axis=-1)


MESH = pl.DeviceIdType.MESH


def sweep_kernel(
    classes,
    feats_ref,
    group_ref,
    own_slot,
    own_flag,
    master_hbm,
    params_ref,
    head_ref,
    bias_ref,
    hot_ref,
    weight_ref,
    image_group,
    basis_in_ref,
    basis_out_ref,
    at_out,
    gr_out,
    total_out,
    norm_out,
    head_out,
    w_full,
    xpad,
    conv_a,
    conv_b,
    d_buf,
    at_v,
    n_pad,
    gr_v,
    piece,
    w_own,
    w_left,
    w_right,
    w_back,
    basis_t,
    small_one,
    small_two,
    head_one,
    head_two,
    out_sem,
    g_ss,
    g_rs,
    one_ss,
    one_rs,
    two_ss,
    two_rs,
):
    low, full = jnp.bfloat16, jnp.float32
    highest = lax.Precision.HIGHEST
    dp, me_s, me_z = lax.axis_index("dp"), lax.axis_index("side"), lax.axis_index("blk")
    me_y, me_x = dp // 2, lax.rem(dp, 2)
    to_s = (dp, 1 - me_s, me_z)
    to_x = (me_y * 2 + 1 - me_x, me_s, me_z)
    to_y = ((1 - me_y) * 2 + me_x, me_s, me_z)
    dp_x, dp_y = me_y * 2 + 1 - me_x, (1 - me_y) * 2 + me_x
    dp_xy = (1 - me_y) * 2 + 1 - me_x
    to_right = (dp, me_s, lax.rem(me_z + 1, 4))
    to_left = (dp, me_s, lax.rem(me_z + 3, 4))
    images, width = 32, 512
    matrices = 2 * TAPS

    def remote(src, dst, send, recv, target):
        return pltpu.make_async_remote_copy(
            src_ref=src,
            dst_ref=dst,
            send_sem=send,
            recv_sem=recv,
            device_id=target,
            device_id_type=MESH,
        )

    piece_copy = pltpu.make_async_copy(
        master_hbm.at[:, pl.ds(pl.multiple_of(dp * 64, 64), 64)], piece, out_sem.at[0]
    )
    piece_copy.start()

    near = [(a, b) for a in range(4) for b in range(2) if a or b]
    barrier = pltpu.get_barrier_semaphore()

    def near_id(a, b):
        return lax.rem(dp + a, 4), lax.rem(me_s + b, 2)

    for a, b in near:
        other, core = near_id(a, b)
        pl.semaphore_signal(barrier, inc=1, device_id=(other, core, me_z), device_id_type=MESH)
    for d in (1, 2, 3):
        pl.semaphore_signal(
            barrier, inc=1, device_id=(dp, me_s, lax.rem(me_z + d, 4)), device_id_type=MESH
        )

    piece_copy.wait()

    def own(m, carry):
        value = piece[own_slot[m]] * own_flag[m].astype(full)
        w_own[m] = value.astype(low)
        return carry

    lax.fori_loop(0, matrices, own, 0)

    @pl.when(me_z == 0)
    def _():
        w_left[...] = jnp.zeros_like(w_left)

    @pl.when(me_z == 3)
    def _():
        w_right[...] = jnp.zeros_like(w_right)

    pl.semaphore_wait(barrier, 10)

    def right_copy(m):
        return remote(w_left.at[m], w_left.at[m], g_ss.at[0, m], g_rs.at[0, m], to_right)

    def left_copy(m):
        return remote(w_back.at[m], w_right.at[m], g_ss.at[1, m], g_rs.at[1, m], to_left)

    def x_copy(m):
        part = w_full.at[m, me_s, dp]
        return remote(part, part, g_ss.at[2, m], g_rs.at[2, m], to_x)

    def y_copy(m):
        part = w_full.at[m, me_s, dp]
        return remote(part, part, g_ss.at[3, m], g_rs.at[3, m], to_y)

    def even_copy(m):
        part = w_full.at[m, me_s, dp_x]
        return remote(part, part, g_ss.at[4, m], g_rs.at[4, m], to_y)

    def odd_copy(m):
        part = w_full.at[m, me_s, dp_y]
        return remote(part, part, g_ss.at[4, m], g_rs.at[4, m], to_x)

    def core_copy(m):
        part = w_full.at[m, me_s]
        return remote(part, part, g_ss.at[5, m], g_rs.at[5, m], to_s)

    def flow_right(m):
        @pl.when((m >= 0) & (m < matrices))
        def _():
            @pl.when(me_z > 0)
            def _():
                right_copy(m).wait_recv()

            w_left[m] = w_left[m] + w_own[m]

            @pl.when(me_z < 3)
            def _():
                right_copy(m).start()

    def flow_left(m):
        @pl.when((m >= 0) & (m < matrices))
        def _():
            @pl.when(me_z < 3)
            def _():
                left_copy(m).wait_recv()

            w_back[m] = w_right[m] + w_own[m]

            @pl.when(me_z > 0)
            def _():
                left_copy(m).start()

    early_right = me_z < 2

    def gather(t):
        flow_right(jnp.where(early_right, t, t - 2))
        flow_left(jnp.where(early_right, t - 2, t))
        m = t - 2

        @pl.when((m >= 0) & (m < matrices))
        def _():
            w_full[m, me_s, dp] = w_left[m] + w_right[m]
            x_copy(m).start()
            y_copy(m).start()

        m4 = t - 4

        @pl.when((m4 >= 0) & (m4 < matrices))
        def _():
            x_copy(m4).wait_recv()
            y_copy(m4).wait_recv()

            @pl.when(lax.rem(m4, 2) == 0)
            def _():
                even_copy(m4).start()

            @pl.when(lax.rem(m4, 2) == 1)
            def _():
                odd_copy(m4).start()

        m6 = t - 6

        @pl.when((m6 >= 0) & (m6 < matrices))
        def _():
            even_copy(m6).wait_recv()
            core_copy(m6).start()

    def weights(m):
        return w_full[m].reshape(width, width)

    def inner(p, q):
        return jnp.where((p < 4) & (q < 4), 1.0, 0.0).astype(full)

    def mask_of(p, q, rows=slice(None)):
        return jnp.maximum(group_ref[rows, :], inner(p, q))

    def cell(i):
        return pl.ds(pl.multiple_of(i * images, images), images)

    def half_cell(i, g):
        return pl.ds(pl.multiple_of(i * images + g * 16, 16), 16)

    def prepare(t):
        for g in range(2):
            block = feats_ref[g * 16 : g * 16 + 16, t].astype(full)
            turned = jnp.swapaxes(block, 0, 1)
            for q in range(8):
                value = turned[q] * mask_of(t, q, slice(g * 16, g * 16 + 16))
                xpad[t + 1, q + 1, g * 16 : g * 16 + 16, :] = value.astype(low)
        line = lax.broadcasted_iota(jnp.int32, (8, 8, width), 0)
        column = lax.broadcasted_iota(jnp.int32, (8, 8, width), 1)
        core = jnp.where((line < 4) & (column < 4), 1.0, 0.0).astype(full)
        wide = []
        for k in range(4):
            n = t * 4 + k
            value = feats_ref[n].astype(full) * jnp.maximum(core, image_group[n].astype(full))
            value = jnp.concatenate([value, jnp.zeros_like(value)], axis=1)
            wide.append(value.reshape(128, width).astype(low))
        project(0, t, jnp.concatenate(wide, axis=0))

    def project(layer, t, rows):
        at_v[:, pl.ds(pl.multiple_of(t * 512, 512), 512)] = lax.dot_general(
            basis_t[layer], rows, (((1,), (1,)), ((), ())), preferred_element_type=full
        ).astype(low)

    def at_copy(li):
        return pltpu.make_async_copy(at_v, at_out.at[li], out_sem.at[1 + li])

    def gr_copy(li):
        return pltpu.make_async_copy(gr_v, gr_out.at[li], out_sem.at[3 + li])

    def conv_tap(tap, m, acc):
        a, b = tap // 3, lax.rem(tap, 3)
        kernel = weights(m)
        for p in range(8):
            rows = xpad[p + a, pl.ds(b, 8)].reshape(8 * images, width)
            acc[p * 256 : p * 256 + 256, :] += jnp.dot(rows, kernel, preferred_element_type=full)

    xpad[...] = jnp.zeros_like(xpad)
    conv_a[...] = jnp.zeros_like(conv_a)
    conv_b[...] = jnp.zeros_like(conv_b)
    for layer in range(2):
        basis_t[layer] = basis_in_ref[layer].T

    def first(t, carry):
        gather(t)

        @pl.when(t < 8)
        def _():
            prepare(t)

        tap = t - 8

        @pl.when(tap >= 0)
        def _():
            core_copy(tap).wait_recv()
            conv_tap(tap, tap, conv_a)

        return carry

    lax.fori_loop(0, 17, first, 0)
    at_copy(1).start()

    mine = dp * 2 + me_s

    def sum_one(buf, sems, n, a, b):
        other, core = near_id(a, b)
        return remote(
            buf.at[mine], buf.at[mine], sems[0].at[n, a * 2 + b], sems[1].at[n, mine],
            (other, core, me_z),
        )

    def sum_one_wait(buf, n, a, b):
        other, core = near_id(a, b)
        slot = other * 2 + core
        remote(
            buf.at[slot], buf.at[slot], one_ss.at[n, a * 2 + b], one_rs.at[n, slot],
            (other, core, me_z),
        ).wait_recv()

    def sum_two(buf, n, d):
        other = lax.rem(me_z + d, 4)
        return remote(
            buf.at[me_z], buf.at[me_z], two_ss.at[n, d], two_rs.at[n, me_z], (dp, me_s, other)
        )

    def sum_start(n, buf):
        for a, b in near:
            sum_one(buf, (one_ss, one_rs), n, a, b).start()

    def sum_middle(n, buf, buf_two):
        for a, b in near:
            sum_one_wait(buf, n, a, b)
        total = buf[0]
        for slot in range(1, 8):
            total = total + buf[slot]
        buf_two[me_z] = total
        for d in (1, 2, 3):
            sum_two(buf_two, n, d).start()

    def sum_end(n, buf_two):
        for d in (1, 2, 3):
            other = lax.rem(me_z + d, 4)
            remote(
                buf_two.at[other], buf_two.at[other], two_ss.at[n, d], two_rs.at[n, other],
                (dp, me_s, other),
            ).wait_recv()
        return buf_two[0] + buf_two[1] + buf_two[2] + buf_two[3]

    def sum_sent(n, buf, buf_two):
        for a, b in near:
            sum_one(buf, (one_ss, one_rs), n, a, b).wait_send()
        for d in (1, 2, 3):
            sum_two(buf_two, n, d).wait_send()

    def column(value):
        return jnp.sum(value, axis=0, keepdims=True)

    zero = jnp.zeros((images, width), full)

    def channel_sums(acc):
        def line(p, carry):
            sums, squares = carry
            for q in range(8):
                value = acc[cell(p * 8 + q), :]
                masked = value * mask_of(p, q)
                sums = sums + masked
                squares = squares + masked * value
            return sums, squares

        sums, squares = lax.fori_loop(0, 8, line, (zero, zero))
        return column(sums), column(squares)

    sums, squares = channel_sums(conv_a)
    group = group_ref[...]
    pixels = 16.0 + 48.0 * group
    small_one[0, mine, 0:1, :] = sums
    small_one[0, mine, 1:2, :] = squares
    small_one[0, mine, 2:3, :] = column(pixels)
    small_one[0, mine, 3:4, :] = jnp.broadcast_to(column(weight_ref[...])[:, 0:1], (1, width))
    sum_start(0, small_one.at[0])

    def later(t, carry):
        gather(t)
        return carry

    lax.fori_loop(17, 20, later, 0)
    sum_middle(0, small_one.at[0], small_two.at[0])
    lax.fori_loop(20, 22, later, 0)
    total = sum_end(0, small_two.at[0])
    total_out[...] = total
    count = total[2:3]

    def moments(total):
        average = total[0:1] / count
        return average, lax.rsqrt(total[1:2] / count - average * average + EPS_NORM)

    average_a, inv_a = moments(total)

    def activation(value, layer, average, inv):
        normed = (value - average) * inv
        pre = params_ref[layer, 0:1, :] * normed + params_ref[layer, 1:2, :]
        return normed, pre, jax.nn.sigmoid(pre)

    def images_first(values):
        return jnp.swapaxes(jnp.stack(values), 0, 1)

    def act_line(p, carry):
        for g in range(2):
            acts = []
            for q in range(8):
                value = conv_a[half_cell(p * 8 + q, g), :]
                normed, pre, sigma = activation(value, 0, average_a, inv_a)
                act = pre * sigma * mask_of(p, q, slice(g * 16, g * 16 + 16))
                xpad[p + 1, q + 1, g * 16 : g * 16 + 16, :] = act.astype(low)
                acts.append(act)
            turned = images_first(acts)
            turned = jnp.concatenate([turned, jnp.zeros_like(turned)], axis=1).astype(low)
            n_pad[g * 16 : g * 16 + 16, pl.ds(pl.multiple_of(p * 16, 16), 16), :] = turned
        return carry

    lax.fori_loop(0, 8, act_line, 0)
    lax.fori_loop(22, 24, later, 0)

    def second(tap, carry):
        core_copy(TAPS + tap).wait_recv()
        conv_tap(tap, TAPS + tap, conv_b)
        return carry

    lax.fori_loop(0, TAPS, second, 0)
    sums, squares = channel_sums(conv_b)
    small_one[1, mine, 0:1, :] = sums
    small_one[1, mine, 1:2, :] = squares
    small_one[1, mine, 2:4, :] = jnp.zeros((2, width), full)
    sum_start(1, small_one.at[1])
    at_copy(1).wait()

    def project_one(t, carry):
        project(1, t, n_pad[pl.ds(t * 4, 4)].reshape(512, width))
        return carry

    lax.fori_loop(0, 4, project_one, 0)
    sum_middle(1, small_one.at[1], small_two.at[1])
    lax.fori_loop(4, 8, project_one, 0)
    at_copy(0).start()
    total = sum_end(1, small_two.at[1])
    average_b, inv_b = moments(total)

    def pool_line(p, carry):
        for q in range(8):
            normed, pre, sigma = activation(conv_b[cell(p * 8 + q), :], 1, average_b, inv_b)
            carry = carry + pre * sigma * mask_of(p, q)
        return carry

    pooled = lax.fori_loop(0, 8, pool_line, zero) / pixels
    pooled_low = pooled.astype(low)
    head_low = head_ref[...].astype(low)
    logits = jnp.dot(pooled_low, head_low, preferred_element_type=full) + bias_ref[...]
    valid = lax.broadcasted_iota(jnp.int32, logits.shape, 1) < classes
    top = jnp.max(jnp.where(valid, logits, -1e30), axis=1, keepdims=True)
    shifted = logits - top
    spread = jnp.sum(jnp.where(valid, jnp.exp(shifted), 0.0), axis=1, keepdims=True)
    log_prob = jnp.where(valid, shifted - jnp.log(spread), 0.0)
    hot = hot_ref[...]
    image_weight = weight_ref[...]
    picked = jnp.sum(hot * log_prob, axis=1, keepdims=True)
    loss = -column(image_weight * picked)[:, 0:1]
    d_logits = jnp.where(valid, image_weight * (jnp.exp(log_prob) - hot), 0.0)
    grad_head = lax.dot_general(
        d_logits,
        pooled_low.astype(full),
        (((0,), (0,)), ((), ())),
        precision=highest,
        preferred_element_type=full,
    )
    head_one[mine, 0:16, :] = grad_head[0:16]
    head_one[mine, 16:24, :] = jnp.zeros((8, width), full)
    head_one[mine, 16:17, 0:128] = column(d_logits)
    head_one[mine, 17:18, :] = jnp.broadcast_to(loss, (1, width))
    d_pooled = (
        lax.dot_general(
            d_logits,
            head_low.astype(full),
            (((1,), (1,)), ((), ())),
            precision=highest,
            preferred_element_type=full,
        )
        / pixels
    )

    def d_line_top(p, carry):
        gammas, betas = carry
        for q in range(8):
            at = cell(p * 8 + q)
            normed, pre, sigma = activation(conv_b[at, :], 1, average_b, inv_b)
            d_pre = d_pooled * mask_of(p, q) * sigma * (1.0 + pre * (1.0 - sigma))
            d_buf[at, :] = d_pre
            gammas = gammas + d_pre * normed
            betas = betas + d_pre
        return gammas, betas

    gammas, betas = lax.fori_loop(0, 8, d_line_top, (zero, zero))

    def put_sums(n, gammas, betas):
        small_one[n, mine, 0:1, :] = column(gammas)
        small_one[n, mine, 1:2, :] = column(betas)
        small_one[n, mine, 2:4, :] = jnp.zeros((2, width), full)
        sum_start(n, small_one.at[n])

    put_sums(2, gammas, betas)
    sum_start(4, head_one)

    def clear(n, carry):
        gr_v[n, 0:16, :] = jnp.zeros((16, width), low)
        gr_v[n, 144:160, :] = jnp.zeros((16, width), low)
        return carry

    lax.fori_loop(0, 3 * images, clear, 0)
    sum_middle(2, small_one.at[2], small_two.at[2])
    total_b = sum_end(2, small_two.at[2])
    norm_out[1] = total_b

    def grad_lines(layer, acc, average, inv, total):
        gamma = params_ref[layer, 0:1, :]
        beta_part = gamma * total[1:2] / count
        gamma_part = gamma * total[0:1] / count

        def line(p, carry):
            for q in range(8):
                at = cell(p * 8 + q)
                normed = (acc[at, :] - average) * inv
                value = mask_of(p, q) * (
                    inv * (gamma * d_buf[at, :] - beta_part - normed * gamma_part)
                )
                xpad[p + 1, q + 1, :, :] = value.astype(low)
            return carry

        lax.fori_loop(0, 8, line, 0)

    grad_lines(1, conv_b, average_b, inv_b, total_b)
    d_buf[...] = jnp.zeros_like(d_buf)

    def back(tap, carry):
        a, b = tap // 3, lax.rem(tap, 3)
        kernel = weights(TAPS + tap)
        for p in range(8):
            rows = xpad[p + 2 - a, pl.ds(2 - b, 8)].reshape(8 * images, width)
            d_buf[p * 256 : p * 256 + 256, :] += lax.dot_general(
                rows, kernel, (((1,), (1,)), ((), ())), preferred_element_type=full
            )
        return carry

    lax.fori_loop(0, TAPS, back, 0)
    sum_middle(4, head_one, head_two)

    def d_line(p, carry):
        gammas, betas = carry
        for q in range(8):
            at = cell(p * 8 + q)
            normed, pre, sigma = activation(conv_a[at, :], 0, average_a, inv_a)
            d_pre = d_buf[at, :] * mask_of(p, q) * sigma * (1.0 + pre * (1.0 - sigma))
            d_buf[at, :] = d_pre
            gammas = gammas + d_pre * normed
            betas = betas + d_pre
        return gammas, betas

    gammas, betas = lax.fori_loop(0, 8, d_line, (zero, zero))
    put_sums(3, gammas, betas)

    def turn_grads(layer):
        def line(p, carry):
            rows = xpad[p + 1, 1:9].reshape(8 * images, width)
            value = jnp.dot(rows, basis_out_ref[layer], preferred_element_type=full)
            value = value.reshape(8, images, width)
            lines = pl.ds(pl.multiple_of(p * 16 + 16, 16), 16)
            for g in range(4):
                turned = jnp.swapaxes(value[:, g * 8 : g * 8 + 8], 0, 1)
                gap = jnp.zeros((8, 1, width), full)
                rest = jnp.zeros((8, 8, width), full)
                shifts = (
                    jnp.concatenate([turned[:, 1:], gap], axis=1),
                    turned,
                    jnp.concatenate([gap, turned[:, :7]], axis=1),
                )
                for b in range(3):
                    wide = jnp.concatenate([shifts[b], rest], axis=1).astype(low)
                    gr_v[b * images + g * 8 : b * images + g * 8 + 8, lines, :] = wide
            return carry

        return line

    lax.fori_loop(0, 4, turn_grads(1), 0)
    sum_middle(3, small_one.at[3], small_two.at[3])
    lax.fori_loop(4, 8, turn_grads(1), 0)
    gr_copy(0).start()
    total_a = sum_end(3, small_two.at[3])
    norm_out[0] = total_a
    grad_lines(0, conv_a, average_a, inv_a, total_a)
    head_out[...] = sum_end(4, head_two)
    gr_copy(0).wait()
    lax.fori_loop(0, 8, turn_grads(0), 0)
    gr_copy(1).start()
    at_copy(0).wait()

    def sent(m, carry):
        @pl.when(me_z < 3)
        def _():
            right_copy(m).wait_send()

        @pl.when(me_z > 0)
        def _():
            left_copy(m).wait_send()

        x_copy(m).wait_send()
        y_copy(m).wait_send()
        even_copy(m).wait_send()
        core_copy(m).wait_send()
        return carry

    lax.fori_loop(0, matrices, sent, 0)
    for n in range(4):
        sum_sent(n, small_one.at[n], small_two.at[n])
    sum_sent(4, head_one, head_two)
    gr_copy(1).wait()


def sweep(
    feats, size_group, labels, class_wt, slot, owners, basis_in, basis_out, master, norm_params, head
):
    count_img, side_len, _, width = feats.shape
    classes = class_wt.shape[0]
    low, full, dma = jnp.bfloat16, jnp.float32, pltpu.SemaphoreType.DMA
    held = owners == lax.axis_index("blk")
    own_slot = jnp.where(held, slot - lax.axis_index("blk") * master.shape[0], 0)
    hot = (labels[:, None] == jnp.arange(128)[None, :]).astype(full)
    weight = jnp.sum(
        jnp.where(labels[:, None] == jnp.arange(classes)[None, :], class_wt[None, :], 0), axis=1
    ).astype(full)
    group = jnp.broadcast_to((size_group == 1).astype(full)[:, None], (count_img, width))
    vmem, any_spec = pl.BlockSpec(memory_space=pltpu.VMEM), pl.BlockSpec(memory_space=pl.ANY)
    smem = pl.BlockSpec(memory_space=pltpu.SMEM)
    rows = count_img * side_len * side_len
    return pl.pallas_call(
        functools.partial(sweep_kernel, classes),
        out_shape=[
            jax.ShapeDtypeStruct((2, width, count_img * 128), low),
            jax.ShapeDtypeStruct((2, 3 * count_img, 160, width), low),
            jax.ShapeDtypeStruct((4, width), full),
            jax.ShapeDtypeStruct((2, 4, width), full),
            jax.ShapeDtypeStruct((24, width), full),
        ],
        in_specs=[vmem, vmem, smem, smem, any_spec, vmem, vmem, vmem, vmem, vmem, smem, vmem, vmem],
        out_specs=[any_spec, any_spec, vmem, vmem, vmem],
        scratch_shapes=[
            pltpu.VMEM((18, 2, 4, 64, 512), low),
            pltpu.VMEM((10, 10, 32, 512), low),
            pltpu.VMEM((rows, 512), full),
            pltpu.VMEM((rows, 512), full),
            pltpu.VMEM((rows, 512), full),
            pltpu.VMEM((512, 4096), low),
            pltpu.VMEM((32, 128, 512), low),
            pltpu.VMEM((96, 160, 512), low),
            pltpu.VMEM((10, 64, 512), full),
            pltpu.VMEM((18, 64, 512), low),
            pltpu.VMEM((18, 64, 512), low),
            pltpu.VMEM((18, 64, 512), low),
            pltpu.VMEM((18, 64, 512), low),
            pltpu.VMEM((2, 512, 512), low),
            pltpu.VMEM((4, 8, 4, 512), full),
            pltpu.VMEM((4, 4, 4, 512), full),
            pltpu.VMEM((8, 24, 512), full),
            pltpu.VMEM((4, 24, 512), full),
            dma((5,)),
            dma((6, 18)),
            dma((6, 18)),
            dma((5, 8)),
            dma((5, 8)),
            dma((5, 4)),
            dma((5, 4)),
        ],
        name="sweep",
        compiler_params=pltpu.CompilerParams(
            collective_id=1, has_side_effects=True, vmem_limit_bytes=63 * 2**20
        ),
    )(
        feats,
        group,
        own_slot.astype(jnp.int32),
        held.astype(jnp.int32),
        master,
        norm_params,
        jnp.pad(head[:width], ((0, 0), (0, 128 - classes))),
        jnp.pad(head[width:], ((0, 0), (0, 128 - classes))),
        hot,
        jnp.broadcast_to(weight[:, None], (count_img, 128)),
        (size_group == 1).astype(jnp.int32),
        basis_in,
        basis_out,
    )


def statistics_kernel(
    images,
    images_all,
    at_hbm,
    gr_hbm,
    scales_hbm,
    weight_ref,
    out,
    ns_out,
    at_v,
    gr_v,
    sc_v,
    ns_v,
    div_v,
    s_send,
    s_recv,
    x1_send,
    x1_recv,
    x1_keep,
    y1_send,
    y1_recv,
    y1_keep,
    x2_send,
    x2_recv,
    y2_send,
    y2_recv,
    two_keep,
    z_send,
    z_recv,
    z_keep,
    load_sem,
    misc_sem,
    local_sem,
    ss,
    s_rs,
    rs,
    z_ss,
    z_rs,
    gz_ss,
    gz_rs,
):
    low, full = jnp.bfloat16, jnp.float32
    dp, me_s, me_z = lax.axis_index("dp"), lax.axis_index("side"), lax.axis_index("blk")
    me_y, me_x = dp // 2, lax.rem(dp, 2)
    to_s = (dp, 1 - me_s, me_z)
    to_x = (me_y * 2 + 1 - me_x, me_s, me_z)
    to_y = ((1 - me_y) * 2 + me_x, me_s, me_z)
    steps = 2 * 9

    def remote(src, dst, send, recv, target):
        return pltpu.make_async_remote_copy(
            src_ref=src,
            dst_ref=dst,
            send_sem=send,
            recv_sem=recv,
            device_id=target,
            device_id_type=MESH,
        )

    def load(li, what):
        if what == 3:
            return pltpu.make_async_copy(at_hbm.at[li], at_v.at[li], load_sem.at[li, 3])
        at = pl.ds(what * images, images)
        return pltpu.make_async_copy(gr_hbm.at[li, at], gr_v.at[li, at], load_sem.at[li, what])

    for what in (3, 0, 1, 2):
        load(0, what).start()

    barrier = pltpu.get_barrier_semaphore()
    away = [(dp, me_s, lax.rem(me_z + d, 4)) for d in (1, 2, 3)]
    for target in [to_s, to_x, to_y] + away:
        pl.semaphore_signal(barrier, inc=1, device_id=target, device_id_type=MESH)
    pl.semaphore_wait(barrier, 6)

    sc_local = pltpu.make_async_copy(scales_hbm.at[:, me_y], sc_v.at[1 - me_y], misc_sem.at[0])
    sc_remote = remote(
        scales_hbm.at[:, 1 - me_y], sc_v.at[1 - me_y], misc_sem.at[1], misc_sem.at[2], to_y
    )
    sc_local.start()
    sc_remote.start()

    def side_copy(k):
        return remote(
            s_send.at[lax.rem(k, 2)],
            s_recv.at[lax.rem(k, 4)],
            ss.at[0, lax.rem(k, 2)],
            s_rs.at[lax.rem(k, 4)],
            to_s,
        )

    def x1_copy(j):
        ring = lax.rem(j, 2)
        return remote(x1_send.at[ring], x1_recv.at[j], ss.at[1, ring], rs.at[0, j], to_x)

    def y1_copy(j):
        ring = lax.rem(j, 2)
        return remote(
            y1_send.at[ring, 1 - me_y], y1_recv.at[j], ss.at[2, ring], rs.at[1, j], to_y
        )

    def x2_copy(j):
        ring = lax.rem(j, 2)
        return remote(x2_send.at[ring], x2_recv.at[j], ss.at[3, ring], rs.at[2, j], to_x)

    def y2_copy(j):
        ring = lax.rem(j, 2)
        return remote(y2_send.at[ring], y2_recv.at[j], ss.at[4, ring], rs.at[3, j], to_y)

    def z_copy(j, d):
        ring, other = lax.rem(j, 2), lax.rem(me_z + d, 4)
        return remote(
            z_send.at[ring, other],
            z_recv.at[j, d - 1],
            z_ss.at[ring, d - 1],
            z_rs.at[j, d - 1],
            (dp, me_s, other),
        )

    def place(j):
        return 1 - j // 9, lax.rem(j, 9)

    def local_copy(j):
        layer, i = place(j)
        ring = lax.rem(j, 2)
        return pltpu.make_async_copy(
            div_v.at[ring], out.at[me_s, layer, me_x, me_z, i, me_y], local_sem.at[ring]
        )

    def gz_copy(j, d):
        layer, i = place(j)
        ring, other = lax.rem(j, 2), lax.rem(me_z + d, 4)
        return remote(
            div_v.at[ring],
            out.at[me_s, layer, me_x, me_z, i, me_y],
            gz_ss.at[ring, d - 1],
            gz_rs.at[j, d - 1],
            (dp, me_s, other),
        )

    lower, upper = pl.ds(0, 2), pl.ds(2, 2)

    def spread(j, which, kind, target):
        part = out.at[which]
        return remote(part, part, ss.at[kind, lax.rem(j, 2)], rs.at[kind - 1, j], target)

    def g1y_copy(j):
        layer, i = place(j)
        return spread(j, (me_s, layer, me_x, lower, i, me_y), 5, to_y)

    def g1x_copy(j):
        layer, i = place(j)
        return spread(j, (me_s, layer, me_x, upper, i, me_y), 6, to_x)

    def g2x_copy(j):
        layer, i = place(j)
        return spread(j, (me_s, layer, me_x, lower, i), 7, to_x)

    def g2y_copy(j):
        layer, i = place(j)
        return spread(j, (me_s, layer, pl.ds(0, 2), upper, i, me_y), 8, to_y)

    def gs_copy(j):
        layer, i = place(j)
        return spread(j, (me_s, layer, pl.ds(0, 2), pl.ds(0, 4), i), 9, to_s)

    def products(j, half, ahead, store):
        li, i = j // 9, lax.rem(j, 9)
        cols = pl.ds(pl.multiple_of(half * 256, 256), 256)
        for u in range(8):
            x_to = ahead if u < 4 else 1 - ahead
            row = x_to * 2304 + (u % 4) * 576 + 64 * i
            tap = row // 512
            rows = pl.ds(pl.multiple_of(lax.rem(row, 512), 64), 64)
            near = pl.ds(pl.multiple_of((2 - tap // 3) * 16, 16), 128)
            shift = lax.rem(tap, 3) * images
            square = total = None
            for n in range(images):
                p = jnp.dot(
                    at_v[li, rows, n * 128 : (n + 1) * 128],
                    gr_v[li, shift + n, near, cols],
                    preferred_element_type=full,
                )
                square = p * p if square is None else square + p * p
                total = p if total is None else total + p
            store(u, x_to, u % 4, total, square)

    def step(k, carry):
        for at, needs in ((0, (0, 1, 2, 3)), (9, (0, 1, 2, 3))):
            @pl.when(k == at)
            def _():
                for what in needs:
                    load(at // 9, what).wait()

        @pl.when(k == 1)
        def _():
            for what in range(4):
                load(1, what).start()

        @pl.when((k >= 2) & (k < steps))
        def _():
            side_copy(k - 2).wait_send()

        @pl.when(k < steps)
        def _():
            ring = lax.rem(k, 2)

            def store(u, x_to, z_to, total, square):
                s_send[ring, u, 0] = total.astype(low)
                s_send[ring, u, 1] = square.astype(low)

            products(k, 1 - me_s, 0, store)
            side_copy(k).start()

        j = k - 1

        @pl.when((j >= 2) & (j < steps))
        def _():
            x1_copy(j - 2).wait_send()
            y1_copy(j - 2).wait_send()

        @pl.when((j >= 0) & (j < steps))
        def _():
            ring, four = lax.rem(j, 2), lax.rem(j, 4)
            side_copy(j).wait_recv()

            def store(u, x_to, z_to, total, square):
                got = s_recv[four, x_to * 4 + z_to].astype(full)
                both = (total + got[0], square + got[1])
                for c in range(2):
                    if z_to < 2 and u < 4:
                        x1_send[ring, z_to, c] = both[c].astype(low)
                    elif z_to < 2:
                        x1_keep[ring, z_to, c] = both[c]
                    else:
                        for y_to in range(2):
                            piece = both[c][y_to * 32 : y_to * 32 + 32]
                            y1_send[ring, y_to, x_to, z_to - 2, c] = piece.astype(low)
                            y1_keep[ring, y_to, x_to, z_to - 2, c] = piece

            products(j, me_s, 1 - me_x, store)
            x1_copy(j).start()
            y1_copy(j).start()

        j2 = k - 2

        @pl.when((j2 >= 0) & (j2 < steps))
        def _():
            ring = lax.rem(j2, 2)

            @pl.when(j2 >= 2)
            def _():
                x2_copy(j2 - 2).wait_send()
                y2_copy(j2 - 2).wait_send()

            x1_copy(j2).wait_recv()
            here = pl.ds(pl.multiple_of(me_y * 32, 32), 32)
            there = pl.ds(pl.multiple_of((1 - me_y) * 32, 32), 32)
            for z_to in range(2):
                for c in range(2):
                    two_keep[ring, z_to, c] = x1_keep[ring, z_to, c, here, :] + x1_recv[
                        j2, z_to, c, here, :
                    ].astype(full)
                    y2_send[ring, z_to, c] = (
                        x1_keep[ring, z_to, c, there, :]
                        + x1_recv[j2, z_to, c, there, :].astype(full)
                    ).astype(low)
            y2_copy(j2).start()
            y1_copy(j2).wait_recv()
            for z_to in range(2):
                two_keep[ring, 2 + z_to] = y1_keep[ring, me_y, me_x, z_to] + y1_recv[
                    j2, me_x, z_to
                ].astype(full)
                x2_send[ring, z_to] = (
                    y1_keep[ring, me_y, 1 - me_x, z_to]
                    + y1_recv[j2, 1 - me_x, z_to].astype(full)
                ).astype(low)
            x2_copy(j2).start()

        j3 = k - 3

        @pl.when((j3 >= 0) & (j3 < steps))
        def _():
            ring = lax.rem(j3, 2)

            @pl.when(j3 >= 2)
            def _():
                for d in (1, 2, 3):
                    z_copy(j3 - 2, d).wait_send()

            y2_copy(j3).wait_recv()
            x2_copy(j3).wait_recv()
            for z_to in range(4):
                got = y2_recv[j3, z_to] if z_to < 2 else x2_recv[j3, z_to - 2]
                both = two_keep[ring, z_to] + got.astype(full)
                z_keep[ring, z_to] = both
                z_send[ring, z_to] = both.astype(low)
            for d in (1, 2, 3):
                z_copy(j3, d).start()

        j4 = k - 4

        @pl.when(j4 == 0)
        def _():
            sc_local.wait()
            sc_remote.wait_recv()

        @pl.when((j4 >= 0) & (j4 < steps))
        def _():
            ring, li, i = lax.rem(j4, 2), j4 // 9, lax.rem(j4, 9)

            @pl.when(j4 >= 2)
            def _():
                for d in (1, 2, 3):
                    gz_copy(j4 - 2, d).wait_send()

            for d in (1, 2, 3):
                z_copy(j4, d).wait_recv()
            got = z_recv[j4].astype(full)
            both = z_keep[ring, me_z] + got[0] + got[1] + got[2]
            scale = DECAY * sc_v[li, i] + (1.0 - DECAY) * both[1] / images_all
            ns_v[li, i] = scale
            div_v[ring] = (both[0] / weight_ref[...] / (scale + DAMPING)).astype(low)
            local_copy(j4).start()
            for d in (1, 2, 3):
                gz_copy(j4, d).start()

        for li in range(2):
            @pl.when((j4 == 9 * li + 8) & (me_y == 1 - li))
            def _():
                pltpu.make_async_copy(ns_v.at[li], ns_out.at[:, me_y], misc_sem.at[3]).start()

            @pl.when((j4 == 9 * li + 8) & (me_y == li))
            def _():
                remote(
                    ns_v.at[li], ns_out.at[:, me_y], misc_sem.at[4], misc_sem.at[5], to_y
                ).start()

        j5 = k - 5

        @pl.when((j5 >= 0) & (j5 < steps))
        def _():
            @pl.when(j5 >= 2)
            def _():
                g1y_copy(j5 - 2).wait_send()
                g1x_copy(j5 - 2).wait_send()

            local_copy(j5).wait()
            for d in (1, 2, 3):
                gz_copy(j5, d).wait_recv()
            g1y_copy(j5).start()
            g1x_copy(j5).start()

        j6 = k - 6

        @pl.when((j6 >= 0) & (j6 < steps))
        def _():
            @pl.when(j6 >= 2)
            def _():
                g2y_copy(j6 - 2).wait_send()
                g2x_copy(j6 - 2).wait_send()

            g1y_copy(j6).wait_recv()
            g2x_copy(j6).start()
            g1x_copy(j6).wait_recv()
            g2y_copy(j6).start()

        j7 = k - 7

        @pl.when(j7 >= 0)
        def _():
            @pl.when(j7 >= 2)
            def _():
                gs_copy(j7 - 2).wait_send()

            g2x_copy(j7).wait_recv()
            g2y_copy(j7).wait_recv()
            gs_copy(j7).start()

        return carry

    lax.fori_loop(0, steps + 7, step, 0)

    def finish(j, carry):
        gs_copy(j).wait_recv()
        return carry

    lax.fori_loop(0, steps, finish, 0)
    sc_remote.wait_send()
    li = 1 - me_y
    pltpu.make_async_copy(ns_v.at[li], ns_out.at[:, me_y], misc_sem.at[3]).wait()
    ns_remote = remote(ns_v.at[0], ns_out.at[:, 0], misc_sem.at[4], misc_sem.at[5], to_y)
    ns_remote.wait_send()
    ns_remote.wait_recv()
    for j in (steps - 2, steps - 1):
        for copy in (side_copy, x1_copy, y1_copy, x2_copy, y2_copy):
            copy(j).wait_send()
        for copy in (g1y_copy, g1x_copy, g2y_copy, g2x_copy, gs_copy):
            copy(j).wait_send()
        for d in (1, 2, 3):
            z_copy(j, d).wait_send()
            gz_copy(j, d).wait_send()


def statistics(act_turned, grad_turned, scales, weight_all, images_all):
    images = act_turned.shape[2] // 128
    dma = pltpu.SemaphoreType.DMA
    low, full = jnp.bfloat16, jnp.float32
    tile, piece = (2, 64, 256), (2, 32, 256)
    any_spec = pl.BlockSpec(memory_space=pl.ANY)
    divided, new_scales = pl.pallas_call(
        functools.partial(statistics_kernel, images, images_all),
        out_shape=[
            jax.ShapeDtypeStruct((2, 2, 2, 4, 9, 2, 32, 256), low),
            jax.ShapeDtypeStruct((9, 2, 32, 256), full),
        ],
        in_specs=[any_spec, any_spec, any_spec, pl.BlockSpec(memory_space=pltpu.VMEM)],
        out_specs=[any_spec, any_spec],
        scratch_shapes=[
            pltpu.VMEM((2, 512, images * 128), low),
            pltpu.VMEM((2, 3 * images, 160, 512), low),
            pltpu.VMEM((2, 9, 32, 256), full),
            pltpu.VMEM((2, 9, 32, 256), full),
            pltpu.VMEM((2, 32, 256), low),
            pltpu.VMEM((2, 8) + tile, low),
            pltpu.VMEM((4, 8) + tile, low),
            pltpu.VMEM((2, 2) + tile, low),
            pltpu.VMEM((18, 2) + tile, low),
            pltpu.VMEM((2, 2) + tile, full),
            pltpu.VMEM((2, 2, 2, 2) + piece, low),
            pltpu.VMEM((18, 2, 2) + piece, low),
            pltpu.VMEM((2, 2, 2, 2) + piece, full),
            pltpu.VMEM((2, 2) + piece, low),
            pltpu.VMEM((18, 2) + piece, low),
            pltpu.VMEM((2, 2) + piece, low),
            pltpu.VMEM((18, 2) + piece, low),
            pltpu.VMEM((2, 4) + piece, full),
            pltpu.VMEM((2, 4) + piece, low),
            pltpu.VMEM((18, 3) + piece, low),
            pltpu.VMEM((2, 4) + piece, full),
            dma((2, 4)),
            dma((6,)),
            dma((2,)),
            dma((10, 2)),
            dma((4,)),
            dma((9, 18)),
            dma((2, 3)),
            dma((18, 3)),
            dma((2, 3)),
            dma((18, 3)),
        ],
        name="statistics",
        compiler_params=pltpu.CompilerParams(
            collective_id=0, has_side_effects=True, vmem_limit_bytes=63 * 2**20
        ),
    )(
        act_turned,
        grad_turned,
        scales.reshape(9, 2, 32, 256),
        jnp.full((1, 256), weight_all, full),
    )
    return divided.reshape(2, 18, 512, 256), new_scales.reshape(576, 256)


def owned_kernel(
    which, divided, rows_ref, cols_ref, w_ref, m_ref, v_ref, new_w, new_m, new_v
):
    low, full = jnp.bfloat16, jnp.float32
    held = which[1, pl.program_id(0)].astype(full)
    rows = rows_ref[0]
    turned = [
        jnp.dot(rows, divided[s, 0], preferred_element_type=full).astype(low) for s in range(2)
    ]
    gradient = lax.dot_general(
        jnp.concatenate(turned, axis=1),
        cols_ref[0],
        (((1,), (1,)), ((), ())),
        preferred_element_type=full,
    )
    new_w[0], new_m[0], new_v[0] = adamw(
        w_ref[0], m_ref[0], v_ref[0], gradient * held, RATE_CONV
    )


def owned_update(divided, basis_in, basis_out, master, moment1, moment2, which):
    slots, half, width = master.shape
    block = pl.BlockSpec((1, half, width), lambda q, which: (q, 0, 0))
    return pl.pallas_call(
        owned_kernel,
        grid_spec=pltpu.PrefetchScalarGridSpec(
            num_scalar_prefetch=1,
            grid=(slots,),
            in_specs=[
                pl.BlockSpec((2, 1, width, half), lambda q, which: (0, which[0, q], 0, 0)),
                pl.BlockSpec((1, half, width), lambda q, which: (which[0, q] // TAPS, which[2, q], 0)),
                pl.BlockSpec((1, width, width), lambda q, which: (which[0, q] // TAPS, 0, 0)),
                block,
                block,
                block,
            ],
            out_specs=[block, block, block],
        ),
        out_shape=[jax.ShapeDtypeStruct(master.shape, jnp.float32)] * 3,
        name="owned_update",
        compiler_params=pltpu.CompilerParams(vmem_limit_bytes=32 * 2**20),
    )(which, divided, basis_in, basis_out, master, moment1, moment2)


def shards_general(
    feats,
    size_group,
    labels,
    class_wt,
    owners,
    basis_in,
    basis_out,
    scales,
    master,
    moment1,
    moment2,
    norm_params,
    norm_m,
    norm_v,
    head,
    head_m,
    head_v,
):
    count_img = feats.shape[0]
    side_len = feats.shape[1]
    width = feats.shape[3]
    half = width // 2
    n_dp = lax.axis_size("dp")
    n_side = lax.axis_size("side")
    n_blk = lax.axis_size("blk")
    slots_dev = master.shape[0]
    matrices = owners.shape[0]
    block_rows = scales.shape[0]
    images_all = count_img * n_dp * n_side * n_blk
    index = jnp.arange(matrices)
    earlier = (owners[:, None] == owners[None, :]) & (index[None, :] < index[:, None])
    slot = owners * slots_dev + jnp.sum(earlier.astype(jnp.int32), axis=1)
    pieces = lax.all_gather(master.astype(jnp.bfloat16), ("side", "blk"), axis=0, tiled=True)
    pieces = pieces.reshape(n_side, n_blk * slots_dev, master.shape[1], width)
    pick = (slot[:, None] == jnp.arange(n_blk * slots_dev)[None, :]).astype(jnp.bfloat16)
    kernels = jnp.einsum("ms,hsrc->mhrc", pick, pieces, preferred_element_type=jnp.float32)
    kernels = kernels.astype(jnp.bfloat16).reshape(L, TAPS, width, width)
    line = jnp.arange(side_len)
    inner = (line[:, None] < side_len // 2) & (line[None, :] < side_len // 2)
    cell_mask = jnp.where((size_group == 1)[:, None, None], True, inner[None]).astype(jnp.float32)
    mask_four = cell_mask[..., None]
    pixels = jnp.sum(cell_mask, axis=(1, 2))
    class_hot = labels[:, None] == jnp.arange(class_wt.shape[0])[None, :]
    weight = jnp.sum(jnp.where(class_hot, class_wt[None, :], 0), axis=1).astype(jnp.float32)
    hot_float = class_hot.astype(jnp.float32)
    count_all, weight_all = lax.psum((jnp.sum(pixels), jnp.sum(weight)), ("dp", "side", "blk"))
    current = (feats.astype(jnp.float32) * mask_four).astype(jnp.bfloat16)
    kept = []
    act_out = None
    for layer in range(L):
        conv_out = conv_forward(current, kernels[layer])
        masked = conv_out * mask_four
        col_sum, sq_sum = lax.psum(
            (jnp.sum(masked, axis=(0, 1, 2)), jnp.sum(masked * conv_out, axis=(0, 1, 2))),
            ("dp", "side", "blk"),
        )
        average = col_sum / count_all
        inv_std = lax.rsqrt(sq_sum / count_all - average * average + EPS_NORM)
        normed = (conv_out - average) * inv_std
        pre_act = norm_params[layer, 0] * normed + norm_params[layer, 1]
        act_out = jax.nn.silu(pre_act) * mask_four
        kept.append((current, normed, pre_act, inv_std))
        current = act_out.astype(jnp.bfloat16)
    pooled = jnp.sum(act_out, axis=(1, 2)) / pixels[:, None]
    pooled_low = pooled.astype(jnp.bfloat16)
    head_low = head[:width].astype(jnp.bfloat16)
    logits = jnp.dot(pooled_low, head_low, preferred_element_type=jnp.float32) + head[width]
    log_prob = jax.nn.log_softmax(logits, axis=-1)
    loss_local = -jnp.sum(weight * jnp.sum(hot_float * log_prob, axis=1))
    d_logits = weight[:, None] * (jnp.exp(log_prob) - hot_float)
    grad_weights = jnp.dot(
        pooled_low.astype(jnp.float32).T, d_logits, precision=lax.Precision.HIGHEST
    )
    grad_head = jnp.concatenate([grad_weights, jnp.sum(d_logits, axis=0)[None]], axis=0)
    loss_all, head_all = lax.psum((loss_local, grad_head), ("dp", "side", "blk"))
    d_pooled = jnp.dot(d_logits, head_low.astype(jnp.float32).T, precision=lax.Precision.HIGHEST)
    d_act = d_pooled[:, None, None, :] / pixels[:, None, None, None] * mask_four
    terms = [None] * L
    grad_norm = [None] * L
    for layer in reversed(range(L)):
        inputs, normed, pre_act, inv_std = kept[layer]
        sigma = jax.nn.sigmoid(pre_act)
        d_pre = d_act * mask_four * sigma * (1.0 + pre_act * (1.0 - sigma))
        gamma_sum, beta_sum = lax.psum(
            (jnp.sum(d_pre * normed, axis=(0, 1, 2)), jnp.sum(d_pre, axis=(0, 1, 2))),
            ("dp", "side", "blk"),
        )
        grad_norm[layer] = jnp.stack([gamma_sum, beta_sum])
        gamma = norm_params[layer, 0]
        d_conv = (
            mask_four
            * inv_std
            * (
                gamma * d_pre
                - gamma * beta_sum / count_all
                - normed * gamma * gamma_sum / count_all
            )
        )
        grad_low = d_conv.astype(jnp.bfloat16)
        if layer > 0:
            d_act = conv_backward(grad_low, kernels[layer])
        act_proj = jnp.einsum(
            "npqc,ci->npqi", inputs, basis_in[layer], preferred_element_type=jnp.float32
        ).astype(jnp.bfloat16)
        grad_proj = jnp.einsum(
            "npqo,oj->npqj", grad_low, basis_out[layer], preferred_element_type=jnp.float32
        ).astype(jnp.bfloat16)
        terms[layer] = tap_sums(act_proj, grad_proj)
    whole = jnp.stack(terms).reshape(n_dp, n_blk, block_rows, 2, 2, half)
    whole = whole.transpose(0, 4, 1, 2, 3, 5).reshape(n_dp * 2 * n_blk * block_rows, 2 * half)
    reduced = lax.psum_scatter(whole, ("dp", "side", "blk"), scatter_dimension=0, tiled=True)
    proj_sum = reduced[:, :half]
    proj_square = reduced[:, half:]
    new_scales = DECAY * scales + (1.0 - DECAY) * proj_square / images_all
    divided = (proj_sum / weight_all / (new_scales + DAMPING)).astype(jnp.bfloat16)
    spread = lax.all_gather(divided, ("dp", "side", "blk"), axis=0, tiled=True)
    spread = spread.reshape(n_dp, 2, n_blk, block_rows, half).transpose(0, 2, 3, 1, 4)
    precond_all = spread.reshape(matrices, width, width)
    slot_ids = lax.axis_index("blk") * slots_dev + jnp.arange(slots_dev)
    owned = (slot[None, :] == slot_ids[:, None]).astype(jnp.bfloat16)
    chosen = jnp.einsum(
        "qm,mij->qij", owned, precond_all, preferred_element_type=jnp.float32
    ).astype(jnp.bfloat16)
    layer_hot = (index[:, None] // TAPS == jnp.arange(L)[None, :]).astype(jnp.bfloat16)
    slot_layer = jnp.dot(owned, layer_hot, preferred_element_type=jnp.float32).astype(jnp.bfloat16)
    half_rows = lax.dynamic_slice_in_dim(
        basis_in, lax.axis_index("side") * master.shape[1], master.shape[1], 1
    )
    rows_slot = jnp.einsum(
        "ql,lci->qci", slot_layer, half_rows, preferred_element_type=jnp.float32
    ).astype(jnp.bfloat16)
    cols_slot = jnp.einsum(
        "ql,loj->qoj", slot_layer, basis_out, preferred_element_type=jnp.float32
    ).astype(jnp.bfloat16)
    turned = jnp.einsum(
        "qci,qij->qcj", rows_slot, chosen, preferred_element_type=jnp.float32
    ).astype(jnp.bfloat16)
    slot_grad = jnp.einsum("qcj,qoj->qco", turned, cols_slot, preferred_element_type=jnp.float32)
    new_master, new_moment1, new_moment2 = adamw(master, moment1, moment2, slot_grad, RATE_CONV)
    new_norm, new_norm_m, new_norm_v = adamw(
        norm_params, norm_m, norm_v, jnp.stack(grad_norm) / weight_all, RATE_NORM
    )
    new_head, new_head_m, new_head_v = adamw(head, head_m, head_v, head_all / weight_all, RATE_HEAD)
    return (
        loss_all,
        weight_all,
        new_scales,
        new_master,
        new_moment1,
        new_moment2,
        new_norm,
        new_norm_m,
        new_norm_v,
        new_head,
        new_head_m,
        new_head_v,
    )


def shards_fast(
    feats,
    size_group,
    labels,
    class_wt,
    owners,
    basis_in,
    basis_out,
    scales,
    master,
    moment1,
    moment2,
    norm_params,
    norm_m,
    norm_v,
    head,
    head_m,
    head_v,
):
    classes = class_wt.shape[0]
    width = feats.shape[3]
    slots_dev = master.shape[0]
    index = jnp.arange(owners.shape[0])
    earlier = (owners[:, None] == owners[None, :]) & (index[None, :] < index[:, None])
    slot = owners * slots_dev + jnp.sum(earlier.astype(jnp.int32), axis=1)
    act_turned, grad_turned, total, norm_sums, head_sums = sweep(
        feats,
        size_group,
        labels,
        class_wt,
        slot,
        owners,
        basis_in,
        basis_out,
        master,
        norm_params,
        head,
    )
    weight_all = total[3, 0]
    images_all = feats.shape[0] * lax.axis_size("dp") * lax.axis_size("side") * lax.axis_size("blk")
    slot_ids = lax.axis_index("blk") * slots_dev + jnp.arange(slots_dev)
    hits = slot[None, :] == slot_ids[:, None]
    which = jnp.stack(
        [
            jnp.sum(jnp.where(hits, index[None, :], 0), axis=1),
            jnp.sum(hits.astype(jnp.int32), axis=1),
            jnp.full((slots_dev,), lax.axis_index("side"), jnp.int32),
        ]
    ).astype(jnp.int32)
    divided, new_scales = statistics(act_turned, grad_turned, scales, weight_all, images_all)
    new_master, new_moment1, new_moment2 = owned_update(
        divided, basis_in, basis_out, master, moment1, moment2, which
    )
    new_norm, new_norm_m, new_norm_v = adamw(
        norm_params, norm_m, norm_v, norm_sums[:, :2] / weight_all, RATE_NORM
    )
    head_all = jnp.concatenate([head_sums[:classes].T, head_sums[16:17, :classes]], axis=0)
    new_head, new_head_m, new_head_v = adamw(head, head_m, head_v, head_all / weight_all, RATE_HEAD)
    return (
        head_sums[17, 0],
        weight_all,
        new_scales,
        new_master,
        new_moment1,
        new_moment2,
        new_norm,
        new_norm_m,
        new_norm_v,
        new_head,
        new_head_m,
        new_head_v,
    )


def shards(*args):
    feats, class_wt, scales, master = args[0], args[3], args[7], args[8]
    mesh_shape = tuple(lax.axis_size(name) for name in ("dp", "side", "blk"))
    fits = (
        mesh_shape == (4, 2, 4)
        and scales.shape == (576, 256)
        and feats.shape == (32, 8, 8, 512)
        and master.shape == (10, 256, 512)
        and class_wt.shape[0] <= 16
    )
    return shards_fast(*args) if fits else shards_general(*args)


def solution(mesh):
    return jax.shard_map(
        shards,
        mesh=mesh,
        in_specs=(
            P(("dp", "side", "blk"), None, None, None),
            P(("dp", "side", "blk")),
            P(("dp", "side", "blk")),
            P(),
            P(),
            P(),
            P(),
            P(("dp", "blk"), "side"),
            P("blk", "side", None),
            P("blk", "side", None),
            P("blk", "side", None),
            P(),
            P(),
            P(),
            P(),
            P(),
            P(),
        ),
        out_specs=(
            P(),
            P(),
            P(("dp", "blk"), "side"),
            P("blk", "side", None),
            P("blk", "side", None),
            P("blk", "side", None),
            P(),
            P(),
            P(),
            P(),
            P(),
            P(),
        ),
        check_vma=False,
    )
```

```python
import functools

import jax
import jax.numpy as jnp
from jax import lax
from jax.experimental import pallas as pl
from jax.experimental.pallas import tpu as pltpu
from jax.sharding import PartitionSpec as P

L = 2
TAPS = 9
STEP = 10


EPS_NORM = 1e-05
DAMPING = 0.001
DECAY = 0.95
BETA_ONE = 0.9
BETA_TWO = 0.999
ADAM_EPS = 1e-08
WEIGHT_DECAY = 0.01
RATE_CONV = 0.01
RATE_NORM = 0.5
RATE_HEAD = 0.02


def adamw(weight_now, first_now, second_now, gradient, rate):
    first_new = BETA_ONE * first_now + (1.0 - BETA_ONE) * gradient
    second_new = BETA_TWO * second_now + (1.0 - BETA_TWO) * gradient * gradient
    first_hat = first_new / (1.0 - BETA_ONE**STEP)
    second_hat = second_new / (1.0 - BETA_TWO**STEP)
    weight_new = weight_now - rate * (
        first_hat / (jnp.sqrt(second_hat) + ADAM_EPS) + WEIGHT_DECAY * weight_now
    )
    return (weight_new, first_new, second_new)


def pad_cells(values):
    return jnp.pad(values, ((0, 0), (1, 1), (1, 1), (0, 0)))


def conv_forward(inputs, kernel):
    side_len = inputs.shape[1]
    padded = pad_cells(inputs)
    total = None
    for tap in range(TAPS):
        shifted = padded[:, tap // 3 : tap // 3 + side_len, tap % 3 : tap % 3 + side_len]
        term = jnp.einsum("npqc,co->npqo", shifted, kernel[tap], preferred_element_type=jnp.float32)
        total = term if total is None else total + term
    return total


def conv_backward(grads, kernel):
    side_len = grads.shape[1]
    total = None
    for tap in range(TAPS):
        offset_row = tap // 3
        offset_col = tap % 3
        term = jnp.einsum("npqo,co->npqc", grads, kernel[tap], preferred_element_type=jnp.float32)
        term = jnp.pad(
            term, ((0, 0), (offset_row, 2 - offset_row), (offset_col, 2 - offset_col), (0, 0))
        )
        total = term if total is None else total + term
    return total[:, 1 : side_len + 1, 1 : side_len + 1]


def tap_sums(act_proj, grad_proj):
    side_len = act_proj.shape[1]
    padded = pad_cells(act_proj)
    firsts, seconds = ([], [])
    for tap in range(TAPS):
        shifted = padded[:, tap // 3 : tap // 3 + side_len, tap % 3 : tap % 3 + side_len]
        each = jnp.einsum("npqi,npqj->nij", shifted, grad_proj, preferred_element_type=jnp.float32)
        firsts.append(jnp.sum(each, axis=0))
        seconds.append(jnp.sum(each * each, axis=0))
    return jnp.concatenate([jnp.stack(firsts), jnp.stack(seconds)], axis=-1)


MESH = pl.DeviceIdType.MESH


def sweep_kernel(
    feats_ref,
    image_group,
    labels_ref,
    class_ref,
    owners_ref,
    master_hbm,
    params_ref,
    head_ref,
    basis_in_ref,
    basis_out_ref,
    at_out,
    gr_out,
    total_out,
    norm_out,
    head_out,
    w_full,
    xpad,
    conv_a,
    conv_b,
    d_buf,
    at_v,
    n_pad,
    gr_v,
    group_ref,
    hot_ref,
    weight_ref,
    piece,
    w_own,
    w_left,
    w_right,
    w_back,
    basis_t,
    small_one,
    small_two,
    head_one,
    head_two,
    out_sem,
    g_ss,
    g_rs,
    one_ss,
    one_rs,
    two_ss,
    two_rs,
):
    low, full = jnp.bfloat16, jnp.float32
    highest = lax.Precision.HIGHEST
    dp, me_s, me_z = lax.axis_index("dp"), lax.axis_index("side"), lax.axis_index("blk")
    me_y, me_x = dp // 2, lax.rem(dp, 2)
    to_s = (dp, 1 - me_s, me_z)
    to_x = (me_y * 2 + 1 - me_x, me_s, me_z)
    to_y = ((1 - me_y) * 2 + me_x, me_s, me_z)
    dp_x, dp_y = me_y * 2 + 1 - me_x, (1 - me_y) * 2 + me_x
    dp_xy = (1 - me_y) * 2 + 1 - me_x
    to_right = (dp, me_s, lax.rem(me_z + 1, 4))
    to_left = (dp, me_s, lax.rem(me_z + 3, 4))
    images, width = 32, 512
    matrices = 2 * TAPS

    def remote(src, dst, send, recv, target):
        return pltpu.make_async_remote_copy(
            src_ref=src,
            dst_ref=dst,
            send_sem=send,
            recv_sem=recv,
            device_id=target,
            device_id_type=MESH,
        )

    piece_copy = pltpu.make_async_copy(
        master_hbm.at[:, pl.ds(pl.multiple_of(dp * 64, 64), 64)], piece, out_sem.at[0]
    )
    piece_copy.start()

    near = [(a, b) for a in range(4) for b in range(2) if a or b]
    barrier = pltpu.get_barrier_semaphore()

    def near_id(a, b):
        return lax.rem(dp + a, 4), lax.rem(me_s + b, 2)

    for a, b in near:
        other, core = near_id(a, b)
        pl.semaphore_signal(barrier, inc=1, device_id=(other, core, me_z), device_id_type=MESH)
    for d in (1, 2, 3):
        pl.semaphore_signal(
            barrier, inc=1, device_id=(dp, me_s, lax.rem(me_z + d, 4)), device_id_type=MESH
        )

    piece_copy.wait()

    mine_is = [jnp.where(owners_ref[m] == me_z, 1, 0) for m in range(matrices)]
    before = jnp.zeros((), jnp.int32)
    for m in range(matrices):
        value = piece[jnp.minimum(before, piece.shape[0] - 1)] * mine_is[m].astype(full)
        w_own[m] = value.astype(low)
        before = before + mine_is[m]

    @pl.when(me_z == 0)
    def _():
        w_left[...] = jnp.zeros_like(w_left)

    @pl.when(me_z == 3)
    def _():
        w_right[...] = jnp.zeros_like(w_right)

    pl.semaphore_wait(barrier, 10)

    def right_copy(m):
        return remote(w_left.at[m], w_left.at[m], g_ss.at[0, m], g_rs.at[0, m], to_right)

    def left_copy(m):
        return remote(w_back.at[m], w_right.at[m], g_ss.at[1, m], g_rs.at[1, m], to_left)

    def x_copy(m):
        part = w_full.at[m, me_s, dp]
        return remote(part, part, g_ss.at[2, m], g_rs.at[2, m], to_x)

    def y_copy(m):
        part = w_full.at[m, me_s, dp]
        return remote(part, part, g_ss.at[3, m], g_rs.at[3, m], to_y)

    def even_copy(m):
        part = w_full.at[m, me_s, dp_x]
        return remote(part, part, g_ss.at[4, m], g_rs.at[4, m], to_y)

    def odd_copy(m):
        part = w_full.at[m, me_s, dp_y]
        return remote(part, part, g_ss.at[4, m], g_rs.at[4, m], to_x)

    def core_copy(m):
        part = w_full.at[m, me_s]
        return remote(part, part, g_ss.at[5, m], g_rs.at[5, m], to_s)

    def flow_right(m):
        @pl.when((m >= 0) & (m < matrices))
        def _():
            @pl.when(me_z > 0)
            def _():
                right_copy(m).wait_recv()

            w_left[m] = w_left[m] + w_own[m]

            @pl.when(me_z < 3)
            def _():
                right_copy(m).start()

    def flow_left(m):
        @pl.when((m >= 0) & (m < matrices))
        def _():
            @pl.when(me_z < 3)
            def _():
                left_copy(m).wait_recv()

            w_back[m] = w_right[m] + w_own[m]

            @pl.when(me_z > 0)
            def _():
                left_copy(m).start()

    def gather(t):
        flow_right(t - 2 * me_z)
        flow_left(t - 2 * (3 - me_z))
        m = t - 6

        @pl.when((m >= 0) & (m < matrices))
        def _():
            w_full[m, me_s, dp] = w_left[m] + w_right[m]
            x_copy(m).start()
            y_copy(m).start()

        m4 = t - 8

        @pl.when((m4 >= 0) & (m4 < matrices))
        def _():
            x_copy(m4).wait_recv()
            y_copy(m4).wait_recv()

            @pl.when(lax.rem(m4, 2) == 0)
            def _():
                even_copy(m4).start()

            @pl.when(lax.rem(m4, 2) == 1)
            def _():
                odd_copy(m4).start()

        m6 = t - 10

        @pl.when((m6 >= 0) & (m6 < matrices))
        def _():
            even_copy(m6).wait_recv()
            core_copy(m6).start()

    def weights(m):
        return w_full[m].reshape(width, width)

    def inner(p, q):
        return jnp.where((p < 4) & (q < 4), 1.0, 0.0).astype(full)

    def mask_of(p, q, rows=slice(None)):
        return jnp.maximum(group_ref[rows, :], inner(p, q))

    def cell(i):
        return pl.ds(pl.multiple_of(i * images, images), images)

    def half_cell(i, g):
        return pl.ds(pl.multiple_of(i * images + g * 16, 16), 16)

    def full_map(n):
        return jnp.where(image_group[n] == 1, 1.0, 0.0).astype(full)

    def prepare(t):
        for g in range(2):
            block = feats_ref[g * 16 : g * 16 + 16, t].astype(full)
            turned = jnp.swapaxes(block, 0, 1)
            for q in range(8):
                value = turned[q] * mask_of(t, q, slice(g * 16, g * 16 + 16))
                xpad[t + 1, q + 1, g * 16 : g * 16 + 16, :] = value.astype(low)
        line = lax.broadcasted_iota(jnp.int32, (8, 8, width), 0)
        column = lax.broadcasted_iota(jnp.int32, (8, 8, width), 1)
        core = jnp.where((line < 4) & (column < 4), 1.0, 0.0).astype(full)
        wide = []
        for k in range(4):
            n = t * 4 + k
            value = feats_ref[n].astype(full) * jnp.maximum(core, full_map(n))
            value = jnp.concatenate([value, jnp.zeros_like(value)], axis=1)
            wide.append(value.reshape(128, width).astype(low))
        project(0, t, jnp.concatenate(wide, axis=0))

    def project(layer, t, rows):
        at_v[:, pl.ds(pl.multiple_of(t * 512, 512), 512)] = lax.dot_general(
            basis_t[layer], rows, (((1,), (1,)), ((), ())), preferred_element_type=full
        ).astype(low)

    def at_copy(li):
        return pltpu.make_async_copy(at_v, at_out.at[li], out_sem.at[1 + li])

    def gr_copy(li):
        return pltpu.make_async_copy(gr_v, gr_out.at[li], out_sem.at[3 + li])

    def conv_tap(tap, m, acc):
        a, b = tap // 3, lax.rem(tap, 3)
        kernel = weights(m)
        for p in range(8):
            rows = xpad[p + a, pl.ds(b, 8)].reshape(8 * images, width)
            acc[p * 256 : p * 256 + 256, :] += jnp.dot(rows, kernel, preferred_element_type=full)

    for t in range(3):
        gather(t)
    xpad[...] = jnp.zeros_like(xpad)
    basis_t[0] = basis_in_ref[0].T
    place = lax.broadcasted_iota(jnp.int32, (1, 128), 1)
    for n in range(images):
        group_ref[n : n + 1, :] = jnp.full((1, width), full_map(n), full)
        hot_ref[n : n + 1, :] = jnp.where(place == labels_ref[n], 1.0, 0.0).astype(full)
        weight_ref[n : n + 1, :] = jnp.full((1, 128), class_ref[labels_ref[n]].astype(full), full)

    def first(t, carry):
        gather(t)

        @pl.when(t < 11)
        def _():
            prepare(t - 3)

        @pl.when(t == 11)
        def _():
            conv_a[...] = jnp.zeros_like(conv_a)
            conv_b[...] = jnp.zeros_like(conv_b)
            basis_t[1] = basis_in_ref[1].T

        tap = t - 12

        @pl.when(tap >= 0)
        def _():
            core_copy(tap).wait_recv()
            conv_tap(tap, tap, conv_a)

        return carry

    lax.fori_loop(3, 21, first, 0)
    at_copy(1).start()

    mine = dp * 2 + me_s

    def sum_one(buf, sems, n, a, b):
        other, core = near_id(a, b)
        return remote(
            buf.at[mine], buf.at[mine], sems[0].at[n, a * 2 + b], sems[1].at[n, mine],
            (other, core, me_z),
        )

    def sum_one_wait(buf, n, a, b):
        other, core = near_id(a, b)
        slot = other * 2 + core
        remote(
            buf.at[slot], buf.at[slot], one_ss.at[n, a * 2 + b], one_rs.at[n, slot],
            (other, core, me_z),
        ).wait_recv()

    def sum_two(buf, n, d):
        other = lax.rem(me_z + d, 4)
        return remote(
            buf.at[me_z], buf.at[me_z], two_ss.at[n, d], two_rs.at[n, me_z], (dp, me_s, other)
        )

    def sum_start(n, buf):
        for a, b in near:
            sum_one(buf, (one_ss, one_rs), n, a, b).start()

    def sum_middle(n, buf, buf_two):
        for a, b in near:
            sum_one_wait(buf, n, a, b)
        total = buf[0]
        for slot in range(1, 8):
            total = total + buf[slot]
        buf_two[me_z] = total
        for d in (1, 2, 3):
            sum_two(buf_two, n, d).start()

    def sum_end(n, buf_two):
        for d in (1, 2, 3):
            other = lax.rem(me_z + d, 4)
            remote(
                buf_two.at[other], buf_two.at[other], two_ss.at[n, d], two_rs.at[n, other],
                (dp, me_s, other),
            ).wait_recv()
        return buf_two[0] + buf_two[1] + buf_two[2] + buf_two[3]

    def sum_sent(n, buf, buf_two):
        for a, b in near:
            sum_one(buf, (one_ss, one_rs), n, a, b).wait_send()
        for d in (1, 2, 3):
            sum_two(buf_two, n, d).wait_send()

    def column(value):
        return jnp.sum(value, axis=0, keepdims=True)

    zero = jnp.zeros((images, width), full)

    def channel_sums(acc):
        def line(p, carry):
            sums, squares = carry
            for q in range(8):
                value = acc[cell(p * 8 + q), :]
                masked = value * mask_of(p, q)
                sums = sums + masked
                squares = squares + masked * value
            return sums, squares

        sums, squares = lax.fori_loop(0, 8, line, (zero, zero))
        return column(sums), column(squares)

    sums, squares = channel_sums(conv_a)
    group = group_ref[...]
    pixels = 16.0 + 48.0 * group
    small_one[0, mine, 0:1, :] = sums
    small_one[0, mine, 1:2, :] = squares
    small_one[0, mine, 2:3, :] = column(pixels)
    small_one[0, mine, 3:4, :] = jnp.broadcast_to(column(weight_ref[...])[:, 0:1], (1, width))
    sum_start(0, small_one.at[0])

    def later(t, carry):
        gather(t)
        return carry

    lax.fori_loop(21, 23, later, 0)
    sum_middle(0, small_one.at[0], small_two.at[0])
    lax.fori_loop(23, 24, later, 0)
    total = sum_end(0, small_two.at[0])
    total_out[...] = total
    count = total[2:3]

    def moments(total):
        average = total[0:1] / count
        return average, lax.rsqrt(total[1:2] / count - average * average + EPS_NORM)

    average_a, inv_a = moments(total)

    def activation(value, layer, average, inv):
        normed = (value - average) * inv
        pre = params_ref[layer, 0:1, :] * normed + params_ref[layer, 1:2, :]
        return normed, pre, jax.nn.sigmoid(pre)

    def images_first(values):
        return jnp.swapaxes(jnp.stack(values), 0, 1)

    def act_line(p, carry):
        for g in range(2):
            acts = []
            for q in range(8):
                value = conv_a[half_cell(p * 8 + q, g), :]
                normed, pre, sigma = activation(value, 0, average_a, inv_a)
                act = pre * sigma * mask_of(p, q, slice(g * 16, g * 16 + 16))
                xpad[p + 1, q + 1, g * 16 : g * 16 + 16, :] = act.astype(low)
                acts.append(act)
            turned = images_first(acts)
            turned = jnp.concatenate([turned, jnp.zeros_like(turned)], axis=1).astype(low)
            n_pad[g * 16 : g * 16 + 16, pl.ds(pl.multiple_of(p * 16, 16), 16), :] = turned
        return carry

    lax.fori_loop(0, 8, act_line, 0)

    def second(tap, carry):
        core_copy(TAPS + tap).wait_recv()
        conv_tap(tap, TAPS + tap, conv_b)

        @pl.when(tap < 4)
        def _():
            gather(24 + tap)

        return carry

    lax.fori_loop(0, TAPS, second, 0)
    sums, squares = channel_sums(conv_b)
    small_one[1, mine, 0:1, :] = sums
    small_one[1, mine, 1:2, :] = squares
    small_one[1, mine, 2:4, :] = jnp.zeros((2, width), full)
    sum_start(1, small_one.at[1])
    at_copy(1).wait()

    def project_one(t, carry):
        project(1, t, n_pad[pl.ds(t * 4, 4)].reshape(512, width))
        return carry

    lax.fori_loop(0, 4, project_one, 0)
    sum_middle(1, small_one.at[1], small_two.at[1])
    lax.fori_loop(4, 8, project_one, 0)
    at_copy(0).start()
    total = sum_end(1, small_two.at[1])
    average_b, inv_b = moments(total)

    def pool_line(p, carry):
        for q in range(8):
            normed, pre, sigma = activation(conv_b[cell(p * 8 + q), :], 1, average_b, inv_b)
            carry = carry + pre * sigma * mask_of(p, q)
        return carry

    pooled = lax.fori_loop(0, 8, pool_line, zero) / pixels
    pooled_low = pooled.astype(low)
    classes = head_ref.shape[1]
    head_low = head_ref[0:width, :].astype(low)
    logits = jnp.dot(pooled_low, head_low, preferred_element_type=full) + head_ref[width:, :]
    shifted = logits - jnp.max(logits, axis=1, keepdims=True)
    log_prob = shifted - jnp.log(jnp.sum(jnp.exp(shifted), axis=1, keepdims=True))
    hot = hot_ref[:, 0:classes]
    image_weight = weight_ref[:, 0:classes]
    picked = jnp.sum(hot * log_prob, axis=1, keepdims=True)
    loss = -column(weight_ref[:, 0:1] * picked)
    d_logits = image_weight * (jnp.exp(log_prob) - hot)
    grad_head = lax.dot_general(
        d_logits,
        pooled_low.astype(full),
        (((0,), (0,)), ((), ())),
        precision=highest,
        preferred_element_type=full,
    )
    head_one[mine, :, :] = jnp.zeros((24, width), full)
    head_one[mine, 0:classes, :] = grad_head
    head_one[mine, 16:17, 0:classes] = column(d_logits)
    head_one[mine, 17:18, :] = jnp.broadcast_to(loss, (1, width))
    d_pooled = (
        lax.dot_general(
            d_logits,
            head_low.astype(full),
            (((1,), (1,)), ((), ())),
            precision=highest,
            preferred_element_type=full,
        )
        / pixels
    )

    def d_line_top(p, carry):
        gammas, betas = carry
        for q in range(8):
            at = cell(p * 8 + q)
            normed, pre, sigma = activation(conv_b[at, :], 1, average_b, inv_b)
            d_pre = d_pooled * mask_of(p, q) * sigma * (1.0 + pre * (1.0 - sigma))
            d_buf[at, :] = d_pre
            gammas = gammas + d_pre * normed
            betas = betas + d_pre
        return gammas, betas

    gammas, betas = lax.fori_loop(0, 8, d_line_top, (zero, zero))

    def put_sums(n, gammas, betas):
        small_one[n, mine, 0:1, :] = column(gammas)
        small_one[n, mine, 1:2, :] = column(betas)
        small_one[n, mine, 2:4, :] = jnp.zeros((2, width), full)
        sum_start(n, small_one.at[n])

    put_sums(2, gammas, betas)

    sum_middle(2, small_one.at[2], small_two.at[2])
    total_b = sum_end(2, small_two.at[2])
    norm_out[1] = total_b
    sum_start(4, head_one)

    def grad_lines(layer, acc, average, inv, total):
        gamma = params_ref[layer, 0:1, :]
        beta_part = gamma * total[1:2] / count
        gamma_part = gamma * total[0:1] / count

        def line(p, carry):
            for q in range(8):
                at = cell(p * 8 + q)
                normed = (acc[at, :] - average) * inv
                value = mask_of(p, q) * (
                    inv * (gamma * d_buf[at, :] - beta_part - normed * gamma_part)
                )
                xpad[p + 1, q + 1, :, :] = value.astype(low)
            return carry

        lax.fori_loop(0, 8, line, 0)

    grad_lines(1, conv_b, average_b, inv_b, total_b)
    d_buf[...] = jnp.zeros_like(d_buf)

    def back(tap, carry):
        a, b = tap // 3, lax.rem(tap, 3)
        kernel = weights(TAPS + tap)
        for p in range(8):
            rows = xpad[p + 2 - a, pl.ds(2 - b, 8)].reshape(8 * images, width)
            d_buf[p * 256 : p * 256 + 256, :] += lax.dot_general(
                rows, kernel, (((1,), (1,)), ((), ())), preferred_element_type=full
            )
        return carry

    lax.fori_loop(0, TAPS, back, 0)
    sum_middle(4, head_one, head_two)

    def d_line(p, carry):
        gammas, betas = carry
        for q in range(8):
            at = cell(p * 8 + q)
            normed, pre, sigma = activation(conv_a[at, :], 0, average_a, inv_a)
            d_pre = d_buf[at, :] * mask_of(p, q) * sigma * (1.0 + pre * (1.0 - sigma))
            d_buf[at, :] = d_pre
            gammas = gammas + d_pre * normed
            betas = betas + d_pre
        return gammas, betas

    gammas, betas = lax.fori_loop(0, 8, d_line, (zero, zero))
    put_sums(3, gammas, betas)

    def turn_grads(layer):
        def line(p, carry):
            rows = xpad[p + 1, 1:9].reshape(8 * images, width)
            value = jnp.dot(rows, basis_out_ref[layer], preferred_element_type=full)
            value = value.reshape(8, images, width)
            lines = pl.ds(pl.multiple_of(p * 16, 16), 16)
            for g in range(4):
                turned = jnp.swapaxes(value[:, g * 8 : g * 8 + 8], 0, 1)
                turned = jnp.concatenate([turned, jnp.zeros_like(turned)], axis=1).astype(low)
                gr_v[g * 8 : g * 8 + 8, lines, :] = turned
            return carry

        return line

    lax.fori_loop(0, 4, turn_grads(1), 0)
    sum_middle(3, small_one.at[3], small_two.at[3])
    lax.fori_loop(4, 8, turn_grads(1), 0)
    gr_copy(0).start()
    total_a = sum_end(3, small_two.at[3])
    norm_out[0] = total_a
    grad_lines(0, conv_a, average_a, inv_a, total_a)
    head_out[...] = sum_end(4, head_two)
    gr_copy(0).wait()
    lax.fori_loop(0, 8, turn_grads(0), 0)
    gr_copy(1).start()
    at_copy(0).wait()

    def sent(m, carry):
        @pl.when(me_z < 3)
        def _():
            right_copy(m).wait_send()

        @pl.when(me_z > 0)
        def _():
            left_copy(m).wait_send()

        x_copy(m).wait_send()
        y_copy(m).wait_send()
        even_copy(m).wait_send()
        core_copy(m).wait_send()
        return carry

    lax.fori_loop(0, matrices, sent, 0)
    for n in range(4):
        sum_sent(n, small_one.at[n], small_two.at[n])
    sum_sent(4, head_one, head_two)
    gr_copy(1).wait()


def sweep(
    feats, size_group, labels, class_wt, owners, basis_in, basis_out, master, norm_params, head
):
    count_img, side_len, _, width = feats.shape
    low, full, dma = jnp.bfloat16, jnp.float32, pltpu.SemaphoreType.DMA
    vmem, any_spec = pl.BlockSpec(memory_space=pltpu.VMEM), pl.BlockSpec(memory_space=pl.ANY)
    smem = pl.BlockSpec(memory_space=pltpu.SMEM)
    rows = count_img * side_len * side_len
    return pl.pallas_call(
        sweep_kernel,
        out_shape=[
            jax.ShapeDtypeStruct((2, width, count_img * 128), low),
            jax.ShapeDtypeStruct((2, count_img, 128, width), low),
            jax.ShapeDtypeStruct((4, width), full),
            jax.ShapeDtypeStruct((2, 4, width), full),
            jax.ShapeDtypeStruct((24, width), full),
        ],
        in_specs=[vmem, smem, smem, smem, smem, any_spec, vmem, vmem, vmem, vmem],
        out_specs=[any_spec, any_spec, vmem, vmem, vmem],
        scratch_shapes=[
            pltpu.VMEM((18, 2, 4, 64, 512), low),
            pltpu.VMEM((10, 10, 32, 512), low),
            pltpu.VMEM((rows, 512), full),
            pltpu.VMEM((rows, 512), full),
            pltpu.VMEM((rows, 512), full),
            pltpu.VMEM((512, 4096), low),
            pltpu.VMEM((32, 128, 512), low),
            pltpu.VMEM((32, 128, 512), low),
            pltpu.VMEM((32, 512), full),
            pltpu.VMEM((32, 128), full),
            pltpu.VMEM((32, 128), full),
            pltpu.VMEM((10, 64, 512), full),
            pltpu.VMEM((18, 64, 512), low),
            pltpu.VMEM((18, 64, 512), low),
            pltpu.VMEM((18, 64, 512), low),
            pltpu.VMEM((18, 64, 512), low),
            pltpu.VMEM((2, 512, 512), low),
            pltpu.VMEM((4, 8, 4, 512), full),
            pltpu.VMEM((4, 4, 4, 512), full),
            pltpu.VMEM((8, 24, 512), full),
            pltpu.VMEM((4, 24, 512), full),
            dma((5,)),
            dma((6, 18)),
            dma((6, 18)),
            dma((5, 8)),
            dma((5, 8)),
            dma((5, 4)),
            dma((5, 4)),
        ],
        name="sweep",
        compiler_params=pltpu.CompilerParams(
            collective_id=1, has_side_effects=True, vmem_limit_bytes=63 * 2**20
        ),
    )(
        feats,
        size_group,
        labels,
        class_wt,
        owners,
        master,
        norm_params,
        head,
        basis_in,
        basis_out,
    )


def statistics_kernel(
    images,
    images_all,
    at_hbm,
    gr_hbm,
    scales_hbm,
    weight_ref,
    out,
    ns_out,
    at_v,
    gc_v,
    gr_v,
    sc_v,
    ns_v,
    div_v,
    s_send,
    s_recv,
    x1_send,
    x1_recv,
    x1_keep,
    y1_send,
    y1_recv,
    y1_keep,
    x2_send,
    x2_recv,
    y2_send,
    y2_recv,
    two_keep,
    z_send,
    z_recv,
    z_keep,
    load_sem,
    misc_sem,
    local_sem,
    ss,
    s_rs,
    rs,
    z_ss,
    z_rs,
    gz_ss,
    gz_rs,
):
    low, full = jnp.bfloat16, jnp.float32
    dp, me_s, me_z = lax.axis_index("dp"), lax.axis_index("side"), lax.axis_index("blk")
    me_y, me_x = dp // 2, lax.rem(dp, 2)
    to_s = (dp, 1 - me_s, me_z)
    to_x = (me_y * 2 + 1 - me_x, me_s, me_z)
    to_y = ((1 - me_y) * 2 + me_x, me_s, me_z)
    steps = 2 * 9

    def remote(src, dst, send, recv, target):
        return pltpu.make_async_remote_copy(
            src_ref=src,
            dst_ref=dst,
            send_sem=send,
            recv_sem=recv,
            device_id=target,
            device_id_type=MESH,
        )

    def load_act(li):
        return pltpu.make_async_copy(at_hbm.at[li], at_v.at[li], load_sem.at[li])

    def load_grad(li):
        return pltpu.make_async_copy(gr_hbm.at[li], gc_v, load_sem.at[2 + li])

    load_grad(0).start()
    load_act(0).start()

    def shifted(li, n):
        lines = gc_v[n].astype(full).reshape(8, 16, 512)[:, 0:8]
        gap, rest = jnp.zeros((8, 1, 512), full), jnp.zeros((8, 8, 512), full)
        for b, value in enumerate(
            (
                jnp.concatenate([lines[:, 1:], gap], axis=1),
                lines,
                jnp.concatenate([gap, lines[:, :7]], axis=1),
            )
        ):
            wide = jnp.concatenate([value, rest], axis=1).reshape(128, 512).astype(low)
            at = b * images + n
            gr_v[li, at, 0:16, :] = jnp.zeros((16, 512), low)
            gr_v[li, at, 16:144, :] = wide
            gr_v[li, at, 144:160, :] = jnp.zeros((16, 512), low)

    barrier = pltpu.get_barrier_semaphore()
    away = [(dp, me_s, lax.rem(me_z + d, 4)) for d in (1, 2, 3)]
    for target in [to_s, to_x, to_y] + away:
        pl.semaphore_signal(barrier, inc=1, device_id=target, device_id_type=MESH)
    pl.semaphore_wait(barrier, 6)

    sc_local = pltpu.make_async_copy(scales_hbm.at[:, me_y], sc_v.at[1 - me_y], misc_sem.at[0])
    sc_remote = remote(
        scales_hbm.at[:, 1 - me_y], sc_v.at[1 - me_y], misc_sem.at[1], misc_sem.at[2], to_y
    )
    sc_local.start()
    sc_remote.start()

    def side_copy(k):
        return remote(
            s_send.at[lax.rem(k, 2)],
            s_recv.at[lax.rem(k, 4)],
            ss.at[0, lax.rem(k, 2)],
            s_rs.at[lax.rem(k, 4)],
            to_s,
        )

    def x1_copy(j):
        ring = lax.rem(j, 2)
        return remote(x1_send.at[ring], x1_recv.at[j], ss.at[1, ring], rs.at[0, j], to_x)

    def y1_copy(j):
        ring = lax.rem(j, 2)
        return remote(
            y1_send.at[ring, 1 - me_y], y1_recv.at[j], ss.at[2, ring], rs.at[1, j], to_y
        )

    def x2_copy(j):
        ring = lax.rem(j, 2)
        return remote(x2_send.at[ring], x2_recv.at[j], ss.at[3, ring], rs.at[2, j], to_x)

    def y2_copy(j):
        ring = lax.rem(j, 2)
        return remote(y2_send.at[ring], y2_recv.at[j], ss.at[4, ring], rs.at[3, j], to_y)

    def z_copy(j, d):
        ring, other = lax.rem(j, 2), lax.rem(me_z + d, 4)
        return remote(
            z_send.at[ring, other],
            z_recv.at[j, d - 1],
            z_ss.at[ring, d - 1],
            z_rs.at[j, d - 1],
            (dp, me_s, other),
        )

    def place(j):
        return 1 - j // 9, lax.rem(j, 9)

    def local_copy(j):
        layer, i = place(j)
        ring = lax.rem(j, 2)
        return pltpu.make_async_copy(
            div_v.at[ring], out.at[me_s, layer, me_x, me_z, i, me_y], local_sem.at[ring]
        )

    def gz_copy(j, d):
        layer, i = place(j)
        ring, other = lax.rem(j, 2), lax.rem(me_z + d, 4)
        return remote(
            div_v.at[ring],
            out.at[me_s, layer, me_x, me_z, i, me_y],
            gz_ss.at[ring, d - 1],
            gz_rs.at[j, d - 1],
            (dp, me_s, other),
        )

    lower, upper = pl.ds(0, 2), pl.ds(2, 2)

    def spread(j, which, kind, target):
        part = out.at[which]
        return remote(part, part, ss.at[kind, lax.rem(j, 2)], rs.at[kind - 1, j], target)

    def g1y_copy(j):
        layer, i = place(j)
        return spread(j, (me_s, layer, me_x, lower, i, me_y), 5, to_y)

    def g1x_copy(j):
        layer, i = place(j)
        return spread(j, (me_s, layer, me_x, upper, i, me_y), 6, to_x)

    def g2x_copy(j):
        layer, i = place(j)
        return spread(j, (me_s, layer, me_x, lower, i), 7, to_x)

    def g2y_copy(j):
        layer, i = place(j)
        return spread(j, (me_s, layer, pl.ds(0, 2), upper, i, me_y), 8, to_y)

    def gs_copy(j):
        layer, i = place(j)
        return spread(j, (me_s, layer, pl.ds(0, 2), pl.ds(0, 4), i), 9, to_s)

    def products(j, half, ahead, store):
        li, i = j // 9, lax.rem(j, 9)
        cols = pl.ds(pl.multiple_of(half * 256, 256), 256)
        for u in range(8):
            x_to = ahead if u < 4 else 1 - ahead
            row = x_to * 2304 + (u % 4) * 576 + 64 * i
            tap = row // 512
            rows = pl.ds(pl.multiple_of(lax.rem(row, 512), 64), 64)
            near = pl.ds(pl.multiple_of((2 - tap // 3) * 16, 16), 128)
            shift = lax.rem(tap, 3) * images
            square = total = None
            for n in range(images):
                p = jnp.dot(
                    at_v[li, rows, n * 128 : (n + 1) * 128],
                    gr_v[li, shift + n, near, cols],
                    preferred_element_type=full,
                )
                square = p * p if square is None else square + p * p
                total = p if total is None else total + p
            store(u, x_to, u % 4, total, square)

    def step(k, carry):
        @pl.when(k == 1)
        def _():
            load_grad(1).wait()

        @pl.when((k >= 1) & (k < 9))
        def _():
            def few(n, carry):
                shifted(1, (k - 1) * 4 + n)
                return carry

            lax.fori_loop(0, 4, few, 0)

        @pl.when(k == 9)
        def _():
            load_act(1).wait()

        @pl.when((k >= 2) & (k < steps))
        def _():
            side_copy(k - 2).wait_send()

        @pl.when(k < steps)
        def _():
            ring = lax.rem(k, 2)

            def store(u, x_to, z_to, total, square):
                s_send[ring, u, 0] = total.astype(low)
                s_send[ring, u, 1] = square.astype(low)

            products(k, 1 - me_s, 0, store)
            side_copy(k).start()

        j = k - 1

        @pl.when((j >= 2) & (j < steps))
        def _():
            x1_copy(j - 2).wait_send()
            y1_copy(j - 2).wait_send()

        @pl.when((j >= 0) & (j < steps))
        def _():
            ring, four = lax.rem(j, 2), lax.rem(j, 4)
            side_copy(j).wait_recv()

            def store(u, x_to, z_to, total, square):
                got = s_recv[four, x_to * 4 + z_to].astype(full)
                both = (total + got[0], square + got[1])
                for c in range(2):
                    if z_to < 2 and u < 4:
                        x1_send[ring, z_to, c] = both[c].astype(low)
                    elif z_to < 2:
                        x1_keep[ring, z_to, c] = both[c]
                    else:
                        for y_to in range(2):
                            piece = both[c][y_to * 32 : y_to * 32 + 32]
                            y1_send[ring, y_to, x_to, z_to - 2, c] = piece.astype(low)
                            y1_keep[ring, y_to, x_to, z_to - 2, c] = piece

            products(j, me_s, 1 - me_x, store)
            x1_copy(j).start()
            y1_copy(j).start()

        j2 = k - 2

        @pl.when((j2 >= 0) & (j2 < steps))
        def _():
            ring = lax.rem(j2, 2)

            @pl.when(j2 >= 2)
            def _():
                x2_copy(j2 - 2).wait_send()
                y2_copy(j2 - 2).wait_send()

            x1_copy(j2).wait_recv()
            here = pl.ds(pl.multiple_of(me_y * 32, 32), 32)
            there = pl.ds(pl.multiple_of((1 - me_y) * 32, 32), 32)
            for z_to in range(2):
                for c in range(2):
                    two_keep[ring, z_to, c] = x1_keep[ring, z_to, c, here, :] + x1_recv[
                        j2, z_to, c, here, :
                    ].astype(full)
                    y2_send[ring, z_to, c] = (
                        x1_keep[ring, z_to, c, there, :]
                        + x1_recv[j2, z_to, c, there, :].astype(full)
                    ).astype(low)
            y2_copy(j2).start()
            y1_copy(j2).wait_recv()
            for z_to in range(2):
                two_keep[ring, 2 + z_to] = y1_keep[ring, me_y, me_x, z_to] + y1_recv[
                    j2, me_x, z_to
                ].astype(full)
                x2_send[ring, z_to] = (
                    y1_keep[ring, me_y, 1 - me_x, z_to]
                    + y1_recv[j2, 1 - me_x, z_to].astype(full)
                ).astype(low)
            x2_copy(j2).start()

        j3 = k - 3

        @pl.when((j3 >= 0) & (j3 < steps))
        def _():
            ring = lax.rem(j3, 2)

            @pl.when(j3 >= 2)
            def _():
                for d in (1, 2, 3):
                    z_copy(j3 - 2, d).wait_send()

            y2_copy(j3).wait_recv()
            x2_copy(j3).wait_recv()
            for z_to in range(4):
                got = y2_recv[j3, z_to] if z_to < 2 else x2_recv[j3, z_to - 2]
                both = two_keep[ring, z_to] + got.astype(full)
                z_keep[ring, z_to] = both
                z_send[ring, z_to] = both.astype(low)
            for d in (1, 2, 3):
                z_copy(j3, d).start()

        j4 = k - 4

        @pl.when(j4 == 0)
        def _():
            sc_local.wait()
            sc_remote.wait_recv()

        @pl.when((j4 >= 0) & (j4 < steps))
        def _():
            ring, li, i = lax.rem(j4, 2), j4 // 9, lax.rem(j4, 9)

            @pl.when(j4 >= 2)
            def _():
                for d in (1, 2, 3):
                    gz_copy(j4 - 2, d).wait_send()

            for d in (1, 2, 3):
                z_copy(j4, d).wait_recv()
            got = z_recv[j4].astype(full)
            both = z_keep[ring, me_z] + got[0] + got[1] + got[2]
            scale = DECAY * sc_v[li, i] + (1.0 - DECAY) * both[1] / images_all
            ns_v[li, i] = scale
            div_v[ring] = (both[0] / weight_ref[3:4, 0:256] / (scale + DAMPING)).astype(low)
            local_copy(j4).start()
            for d in (1, 2, 3):
                gz_copy(j4, d).start()

        for li in range(2):
            @pl.when((j4 == 9 * li + 8) & (me_y == 1 - li))
            def _():
                pltpu.make_async_copy(ns_v.at[li], ns_out.at[:, me_y], misc_sem.at[3]).start()

            @pl.when((j4 == 9 * li + 8) & (me_y == li))
            def _():
                remote(
                    ns_v.at[li], ns_out.at[:, me_y], misc_sem.at[4], misc_sem.at[5], to_y
                ).start()

        j5 = k - 5

        @pl.when((j5 >= 0) & (j5 < steps))
        def _():
            @pl.when(j5 >= 2)
            def _():
                g1y_copy(j5 - 2).wait_send()
                g1x_copy(j5 - 2).wait_send()

            local_copy(j5).wait()
            for d in (1, 2, 3):
                gz_copy(j5, d).wait_recv()
            g1y_copy(j5).start()
            g1x_copy(j5).start()

        j6 = k - 6

        @pl.when((j6 >= 0) & (j6 < steps))
        def _():
            @pl.when(j6 >= 2)
            def _():
                g2y_copy(j6 - 2).wait_send()
                g2x_copy(j6 - 2).wait_send()

            g1y_copy(j6).wait_recv()
            g2x_copy(j6).start()
            g1x_copy(j6).wait_recv()
            g2y_copy(j6).start()

        j7 = k - 7

        @pl.when(j7 >= 0)
        def _():
            @pl.when(j7 >= 2)
            def _():
                gs_copy(j7 - 2).wait_send()

            g2x_copy(j7).wait_recv()
            g2y_copy(j7).wait_recv()
            gs_copy(j7).start()

        return carry

    load_grad(0).wait()

    def build(n, carry):
        shifted(0, n)
        return carry

    lax.fori_loop(0, images, build, 0)
    load_grad(1).start()
    load_act(0).wait()
    load_act(1).start()
    lax.fori_loop(0, steps + 7, step, 0)

    def finish(j, carry):
        gs_copy(j).wait_recv()
        return carry

    lax.fori_loop(0, steps, finish, 0)
    sc_remote.wait_send()
    li = 1 - me_y
    pltpu.make_async_copy(ns_v.at[li], ns_out.at[:, me_y], misc_sem.at[3]).wait()
    ns_remote = remote(ns_v.at[0], ns_out.at[:, 0], misc_sem.at[4], misc_sem.at[5], to_y)
    ns_remote.wait_send()
    ns_remote.wait_recv()
    for j in (steps - 2, steps - 1):
        for copy in (side_copy, x1_copy, y1_copy, x2_copy, y2_copy):
            copy(j).wait_send()
        for copy in (g1y_copy, g1x_copy, g2y_copy, g2x_copy, gs_copy):
            copy(j).wait_send()
        for d in (1, 2, 3):
            z_copy(j, d).wait_send()
            gz_copy(j, d).wait_send()


def statistics(act_turned, grad_turned, scales, total, images_all):
    images = act_turned.shape[2] // 128
    dma = pltpu.SemaphoreType.DMA
    low, full = jnp.bfloat16, jnp.float32
    tile, piece = (2, 64, 256), (2, 32, 256)
    any_spec = pl.BlockSpec(memory_space=pl.ANY)
    divided, new_scales = pl.pallas_call(
        functools.partial(statistics_kernel, images, images_all),
        out_shape=[
            jax.ShapeDtypeStruct((2, 2, 2, 4, 9, 2, 32, 256), low),
            jax.ShapeDtypeStruct((9, 2, 32, 256), full),
        ],
        in_specs=[any_spec, any_spec, any_spec, pl.BlockSpec(memory_space=pltpu.VMEM)],
        out_specs=[any_spec, any_spec],
        scratch_shapes=[
            pltpu.VMEM((2, 512, images * 128), low),
            pltpu.VMEM((images, 128, 512), low),
            pltpu.VMEM((2, 3 * images, 160, 512), low),
            pltpu.VMEM((2, 9, 32, 256), full),
            pltpu.VMEM((2, 9, 32, 256), full),
            pltpu.VMEM((2, 32, 256), low),
            pltpu.VMEM((2, 8) + tile, low),
            pltpu.VMEM((4, 8) + tile, low),
            pltpu.VMEM((2, 2) + tile, low),
            pltpu.VMEM((18, 2) + tile, low),
            pltpu.VMEM((2, 2) + tile, full),
            pltpu.VMEM((2, 2, 2, 2) + piece, low),
            pltpu.VMEM((18, 2, 2) + piece, low),
            pltpu.VMEM((2, 2, 2, 2) + piece, full),
            pltpu.VMEM((2, 2) + piece, low),
            pltpu.VMEM((18, 2) + piece, low),
            pltpu.VMEM((2, 2) + piece, low),
            pltpu.VMEM((18, 2) + piece, low),
            pltpu.VMEM((2, 4) + piece, full),
            pltpu.VMEM((2, 4) + piece, low),
            pltpu.VMEM((18, 3) + piece, low),
            pltpu.VMEM((2, 4) + piece, full),
            dma((4,)),
            dma((6,)),
            dma((2,)),
            dma((10, 2)),
            dma((4,)),
            dma((9, 18)),
            dma((2, 3)),
            dma((18, 3)),
            dma((2, 3)),
            dma((18, 3)),
        ],
        name="statistics",
        compiler_params=pltpu.CompilerParams(
            collective_id=0, has_side_effects=True, vmem_limit_bytes=63 * 2**20
        ),
    )(
        act_turned,
        grad_turned,
        scales.reshape(9, 2, 32, 256),
        total,
    )
    return divided.reshape(2, 18, 512, 256), new_scales.reshape(576, 256)


def owned_kernel(
    which, divided, rows_ref, cols_ref, w_ref, m_ref, v_ref, new_w, new_m, new_v
):
    low, full = jnp.bfloat16, jnp.float32
    held = which[1, pl.program_id(0)].astype(full)
    rows = rows_ref[0]
    turned = [
        jnp.dot(rows, divided[s, 0], preferred_element_type=full).astype(low) for s in range(2)
    ]
    gradient = lax.dot_general(
        jnp.concatenate(turned, axis=1),
        cols_ref[0],
        (((1,), (1,)), ((), ())),
        preferred_element_type=full,
    )
    new_w[0], new_m[0], new_v[0] = adamw(
        w_ref[0], m_ref[0], v_ref[0], gradient * held, RATE_CONV
    )


def owned_update(divided, basis_in, basis_out, master, moment1, moment2, which):
    slots, half, width = master.shape
    block = pl.BlockSpec((1, half, width), lambda q, which: (q, 0, 0))
    return pl.pallas_call(
        owned_kernel,
        grid_spec=pltpu.PrefetchScalarGridSpec(
            num_scalar_prefetch=1,
            grid=(slots,),
            in_specs=[
                pl.BlockSpec((2, 1, width, half), lambda q, which: (0, which[0, q], 0, 0)),
                pl.BlockSpec((1, half, width), lambda q, which: (which[0, q] // TAPS, which[2, q], 0)),
                pl.BlockSpec((1, width, width), lambda q, which: (which[0, q] // TAPS, 0, 0)),
                block,
                block,
                block,
            ],
            out_specs=[block, block, block],
        ),
        out_shape=[jax.ShapeDtypeStruct(master.shape, jnp.float32)] * 3,
        name="owned_update",
        compiler_params=pltpu.CompilerParams(vmem_limit_bytes=63 * 2**20),
    )(which, divided, basis_in, basis_out, master, moment1, moment2)


def shards_general(
    feats,
    size_group,
    labels,
    class_wt,
    owners,
    basis_in,
    basis_out,
    scales,
    master,
    moment1,
    moment2,
    norm_params,
    norm_m,
    norm_v,
    head,
    head_m,
    head_v,
):
    count_img = feats.shape[0]
    side_len = feats.shape[1]
    width = feats.shape[3]
    half = width // 2
    n_dp = lax.axis_size("dp")
    n_side = lax.axis_size("side")
    n_blk = lax.axis_size("blk")
    slots_dev = master.shape[0]
    matrices = owners.shape[0]
    block_rows = scales.shape[0]
    images_all = count_img * n_dp * n_side * n_blk
    index = jnp.arange(matrices)
    earlier = (owners[:, None] == owners[None, :]) & (index[None, :] < index[:, None])
    slot = owners * slots_dev + jnp.sum(earlier.astype(jnp.int32), axis=1)
    pieces = lax.all_gather(master.astype(jnp.bfloat16), ("side", "blk"), axis=0, tiled=True)
    pieces = pieces.reshape(n_side, n_blk * slots_dev, master.shape[1], width)
    pick = (slot[:, None] == jnp.arange(n_blk * slots_dev)[None, :]).astype(jnp.bfloat16)
    kernels = jnp.einsum("ms,hsrc->mhrc", pick, pieces, preferred_element_type=jnp.float32)
    kernels = kernels.astype(jnp.bfloat16).reshape(L, TAPS, width, width)
    line = jnp.arange(side_len)
    inner = (line[:, None] < side_len // 2) & (line[None, :] < side_len // 2)
    cell_mask = jnp.where((size_group == 1)[:, None, None], True, inner[None]).astype(jnp.float32)
    mask_four = cell_mask[..., None]
    pixels = jnp.sum(cell_mask, axis=(1, 2))
    class_hot = labels[:, None] == jnp.arange(class_wt.shape[0])[None, :]
    weight = jnp.sum(jnp.where(class_hot, class_wt[None, :], 0), axis=1).astype(jnp.float32)
    hot_float = class_hot.astype(jnp.float32)
    count_all, weight_all = lax.psum((jnp.sum(pixels), jnp.sum(weight)), ("dp", "side", "blk"))
    current = (feats.astype(jnp.float32) * mask_four).astype(jnp.bfloat16)
    kept = []
    act_out = None
    for layer in range(L):
        conv_out = conv_forward(current, kernels[layer])
        masked = conv_out * mask_four
        col_sum, sq_sum = lax.psum(
            (jnp.sum(masked, axis=(0, 1, 2)), jnp.sum(masked * conv_out, axis=(0, 1, 2))),
            ("dp", "side", "blk"),
        )
        average = col_sum / count_all
        inv_std = lax.rsqrt(sq_sum / count_all - average * average + EPS_NORM)
        normed = (conv_out - average) * inv_std
        pre_act = norm_params[layer, 0] * normed + norm_params[layer, 1]
        act_out = jax.nn.silu(pre_act) * mask_four
        kept.append((current, normed, pre_act, inv_std))
        current = act_out.astype(jnp.bfloat16)
    pooled = jnp.sum(act_out, axis=(1, 2)) / pixels[:, None]
    pooled_low = pooled.astype(jnp.bfloat16)
    head_low = head[:width].astype(jnp.bfloat16)
    logits = jnp.dot(pooled_low, head_low, preferred_element_type=jnp.float32) + head[width]
    log_prob = jax.nn.log_softmax(logits, axis=-1)
    loss_local = -jnp.sum(weight * jnp.sum(hot_float * log_prob, axis=1))
    d_logits = weight[:, None] * (jnp.exp(log_prob) - hot_float)
    grad_weights = jnp.dot(
        pooled_low.astype(jnp.float32).T, d_logits, precision=lax.Precision.HIGHEST
    )
    grad_head = jnp.concatenate([grad_weights, jnp.sum(d_logits, axis=0)[None]], axis=0)
    loss_all, head_all = lax.psum((loss_local, grad_head), ("dp", "side", "blk"))
    d_pooled = jnp.dot(d_logits, head_low.astype(jnp.float32).T, precision=lax.Precision.HIGHEST)
    d_act = d_pooled[:, None, None, :] / pixels[:, None, None, None] * mask_four
    terms = [None] * L
    grad_norm = [None] * L
    for layer in reversed(range(L)):
        inputs, normed, pre_act, inv_std = kept[layer]
        sigma = jax.nn.sigmoid(pre_act)
        d_pre = d_act * mask_four * sigma * (1.0 + pre_act * (1.0 - sigma))
        gamma_sum, beta_sum = lax.psum(
            (jnp.sum(d_pre * normed, axis=(0, 1, 2)), jnp.sum(d_pre, axis=(0, 1, 2))),
            ("dp", "side", "blk"),
        )
        grad_norm[layer] = jnp.stack([gamma_sum, beta_sum])
        gamma = norm_params[layer, 0]
        d_conv = (
            mask_four
            * inv_std
            * (
                gamma * d_pre
                - gamma * beta_sum / count_all
                - normed * gamma * gamma_sum / count_all
            )
        )
        grad_low = d_conv.astype(jnp.bfloat16)
        if layer > 0:
            d_act = conv_backward(grad_low, kernels[layer])
        act_proj = jnp.einsum(
            "npqc,ci->npqi", inputs, basis_in[layer], preferred_element_type=jnp.float32
        ).astype(jnp.bfloat16)
        grad_proj = jnp.einsum(
            "npqo,oj->npqj", grad_low, basis_out[layer], preferred_element_type=jnp.float32
        ).astype(jnp.bfloat16)
        terms[layer] = tap_sums(act_proj, grad_proj)
    whole = jnp.stack(terms).reshape(n_dp, n_blk, block_rows, 2, 2, half)
    whole = whole.transpose(0, 4, 1, 2, 3, 5).reshape(n_dp * 2 * n_blk * block_rows, 2 * half)
    reduced = lax.psum_scatter(whole, ("dp", "side", "blk"), scatter_dimension=0, tiled=True)
    proj_sum = reduced[:, :half]
    proj_square = reduced[:, half:]
    new_scales = DECAY * scales + (1.0 - DECAY) * proj_square / images_all
    divided = (proj_sum / weight_all / (new_scales + DAMPING)).astype(jnp.bfloat16)
    spread = lax.all_gather(divided, ("dp", "side", "blk"), axis=0, tiled=True)
    spread = spread.reshape(n_dp, 2, n_blk, block_rows, half).transpose(0, 2, 3, 1, 4)
    precond_all = spread.reshape(matrices, width, width)
    slot_ids = lax.axis_index("blk") * slots_dev + jnp.arange(slots_dev)
    owned = (slot[None, :] == slot_ids[:, None]).astype(jnp.bfloat16)
    chosen = jnp.einsum(
        "qm,mij->qij", owned, precond_all, preferred_element_type=jnp.float32
    ).astype(jnp.bfloat16)
    layer_hot = (index[:, None] // TAPS == jnp.arange(L)[None, :]).astype(jnp.bfloat16)
    slot_layer = jnp.dot(owned, layer_hot, preferred_element_type=jnp.float32).astype(jnp.bfloat16)
    half_rows = lax.dynamic_slice_in_dim(
        basis_in, lax.axis_index("side") * master.shape[1], master.shape[1], 1
    )
    rows_slot = jnp.einsum(
        "ql,lci->qci", slot_layer, half_rows, preferred_element_type=jnp.float32
    ).astype(jnp.bfloat16)
    cols_slot = jnp.einsum(
        "ql,loj->qoj", slot_layer, basis_out, preferred_element_type=jnp.float32
    ).astype(jnp.bfloat16)
    turned = jnp.einsum(
        "qci,qij->qcj", rows_slot, chosen, preferred_element_type=jnp.float32
    ).astype(jnp.bfloat16)
    slot_grad = jnp.einsum("qcj,qoj->qco", turned, cols_slot, preferred_element_type=jnp.float32)
    new_master, new_moment1, new_moment2 = adamw(master, moment1, moment2, slot_grad, RATE_CONV)
    new_norm, new_norm_m, new_norm_v = adamw(
        norm_params, norm_m, norm_v, jnp.stack(grad_norm) / weight_all, RATE_NORM
    )
    new_head, new_head_m, new_head_v = adamw(head, head_m, head_v, head_all / weight_all, RATE_HEAD)
    return (
        loss_all,
        weight_all,
        new_scales,
        new_master,
        new_moment1,
        new_moment2,
        new_norm,
        new_norm_m,
        new_norm_v,
        new_head,
        new_head_m,
        new_head_v,
    )


def shards_fast(
    feats,
    size_group,
    labels,
    class_wt,
    owners,
    basis_in,
    basis_out,
    scales,
    master,
    moment1,
    moment2,
    norm_params,
    norm_m,
    norm_v,
    head,
    head_m,
    head_v,
):
    classes = class_wt.shape[0]
    width = feats.shape[3]
    slots_dev = master.shape[0]
    index = jnp.arange(owners.shape[0])
    earlier = (owners[:, None] == owners[None, :]) & (index[None, :] < index[:, None])
    slot = owners * slots_dev + jnp.sum(earlier.astype(jnp.int32), axis=1)
    act_turned, grad_turned, total, norm_sums, head_sums = sweep(
        feats,
        size_group,
        labels,
        class_wt,
        owners,
        basis_in,
        basis_out,
        master,
        norm_params,
        head,
    )
    weight_all = total[3, 0]
    images_all = feats.shape[0] * lax.axis_size("dp") * lax.axis_size("side") * lax.axis_size("blk")
    slot_ids = lax.axis_index("blk") * slots_dev + jnp.arange(slots_dev)
    hits = slot[None, :] == slot_ids[:, None]
    which = jnp.stack(
        [
            jnp.sum(jnp.where(hits, index[None, :], 0), axis=1),
            jnp.sum(hits.astype(jnp.int32), axis=1),
            jnp.full((slots_dev,), lax.axis_index("side"), jnp.int32),
        ]
    ).astype(jnp.int32)
    divided, new_scales = statistics(act_turned, grad_turned, scales, total, images_all)
    new_master, new_moment1, new_moment2 = owned_update(
        divided, basis_in, basis_out, master, moment1, moment2, which
    )
    new_norm, new_norm_m, new_norm_v = adamw(
        norm_params, norm_m, norm_v, norm_sums[:, :2] / weight_all, RATE_NORM
    )
    head_all = jnp.concatenate([head_sums[:classes].T, head_sums[16:17, :classes]], axis=0)
    new_head, new_head_m, new_head_v = adamw(head, head_m, head_v, head_all / weight_all, RATE_HEAD)
    return (
        head_sums[17, 0],
        weight_all,
        new_scales,
        new_master,
        new_moment1,
        new_moment2,
        new_norm,
        new_norm_m,
        new_norm_v,
        new_head,
        new_head_m,
        new_head_v,
    )


def shards(*args):
    feats, class_wt, scales, master = args[0], args[3], args[7], args[8]
    mesh_shape = tuple(lax.axis_size(name) for name in ("dp", "side", "blk"))
    fits = (
        mesh_shape == (4, 2, 4)
        and scales.shape == (576, 256)
        and feats.shape == (32, 8, 8, 512)
        and master.shape == (10, 256, 512)
        and class_wt.shape[0] <= 16
    )
    return shards_fast(*args) if fits else shards_general(*args)


def solution(mesh):
    return jax.shard_map(
        shards,
        mesh=mesh,
        in_specs=(
            P(("dp", "side", "blk"), None, None, None),
            P(("dp", "side", "blk")),
            P(("dp", "side", "blk")),
            P(),
            P(),
            P(),
            P(),
            P(("dp", "blk"), "side"),
            P("blk", "side", None),
            P("blk", "side", None),
            P("blk", "side", None),
            P(),
            P(),
            P(),
            P(),
            P(),
            P(),
        ),
        out_specs=(
            P(),
            P(),
            P(("dp", "blk"), "side"),
            P("blk", "side", None),
            P("blk", "side", None),
            P("blk", "side", None),
            P(),
            P(),
            P(),
            P(),
            P(),
            P(),
        ),
        check_vma=False,
    )
```

```python
import functools

import jax
import jax.numpy as jnp
from jax import lax
from jax.experimental import pallas as pl
from jax.experimental.pallas import tpu as pltpu
from jax.sharding import PartitionSpec as P

L = 2
TAPS = 9
STEP = 10


EPS_NORM = 1e-05
DAMPING = 0.001
DECAY = 0.95
BETA_ONE = 0.9
BETA_TWO = 0.999
ADAM_EPS = 1e-08
WEIGHT_DECAY = 0.01
RATE_CONV = 0.01
RATE_NORM = 0.5
RATE_HEAD = 0.02


def adamw(weight_now, first_now, second_now, gradient, rate):
    first_new = BETA_ONE * first_now + (1.0 - BETA_ONE) * gradient
    second_new = BETA_TWO * second_now + (1.0 - BETA_TWO) * gradient * gradient
    first_hat = first_new * (1.0 / (1.0 - BETA_ONE**STEP))
    second_hat = second_new * (1.0 / (1.0 - BETA_TWO**STEP))
    weight_new = weight_now - rate * (
        first_hat / (jnp.sqrt(second_hat) + ADAM_EPS) + WEIGHT_DECAY * weight_now
    )
    return (weight_new, first_new, second_new)


def pad_cells(values):
    return jnp.pad(values, ((0, 0), (1, 1), (1, 1), (0, 0)))


def conv_forward(inputs, kernel):
    side_len = inputs.shape[1]
    padded = pad_cells(inputs)
    total = None
    for tap in range(TAPS):
        shifted = padded[:, tap // 3 : tap // 3 + side_len, tap % 3 : tap % 3 + side_len]
        term = jnp.einsum("npqc,co->npqo", shifted, kernel[tap], preferred_element_type=jnp.float32)
        total = term if total is None else total + term
    return total


def conv_backward(grads, kernel):
    side_len = grads.shape[1]
    total = None
    for tap in range(TAPS):
        offset_row = tap // 3
        offset_col = tap % 3
        term = jnp.einsum("npqo,co->npqc", grads, kernel[tap], preferred_element_type=jnp.float32)
        term = jnp.pad(
            term, ((0, 0), (offset_row, 2 - offset_row), (offset_col, 2 - offset_col), (0, 0))
        )
        total = term if total is None else total + term
    return total[:, 1 : side_len + 1, 1 : side_len + 1]


def tap_sums(act_proj, grad_proj):
    side_len = act_proj.shape[1]
    padded = pad_cells(act_proj)
    firsts, seconds = ([], [])
    for tap in range(TAPS):
        shifted = padded[:, tap // 3 : tap // 3 + side_len, tap % 3 : tap % 3 + side_len]
        each = jnp.einsum("npqi,npqj->nij", shifted, grad_proj, preferred_element_type=jnp.float32)
        firsts.append(jnp.sum(each, axis=0))
        seconds.append(jnp.sum(each * each, axis=0))
    return jnp.concatenate([jnp.stack(firsts), jnp.stack(seconds)], axis=-1)


MESH = pl.DeviceIdType.MESH


def step_kernel(
    images_all,
    feats_ref,
    image_group,
    labels_ref,
    class_ref,
    owners_ref,
    master_hbm,
    params_ref,
    head_ref,
    basis_in_ref,
    basis_out_ref,
    scales_hbm,
    out,
    ns_out,
    total_out,
    norm_out,
    head_out,
    w_full,
    xpad,
    conv_a,
    conv_b,
    at_v,
    gr_v,
    group_ref,
    hot_ref,
    weight_ref,
    piece,
    basis_t,
    small_one,
    small_two,
    head_one,
    head_two,
    sc_v,
    ns_v,
    div_v,
    s_send,
    s_recv,
    x1_send,
    x1_keep,
    y1_send,
    y1_keep,
    x2_send,
    y2_send,
    two_keep,
    z_send,
    z_keep,
    out_sem,
    g_ss,
    g_rs,
    one_ss,
    one_rs,
    two_ss,
    two_rs,
    misc_sem,
    local_sem,
    ss,
    s_ss,
    s_rs,
    rs,
    z_ss,
    z_rs,
    gz_ss,
    gz_rs,
):
    low, full = jnp.bfloat16, jnp.float32
    highest = lax.Precision.HIGHEST
    dp, me_s, me_z = lax.axis_index("dp"), lax.axis_index("side"), lax.axis_index("blk")
    me_y, me_x = dp // 2, lax.rem(dp, 2)
    to_s = (dp, 1 - me_s, me_z)
    to_x = (me_y * 2 + 1 - me_x, me_s, me_z)
    to_y = ((1 - me_y) * 2 + me_x, me_s, me_z)
    dp_x, dp_y = me_y * 2 + 1 - me_x, (1 - me_y) * 2 + me_x
    dp_xy = (1 - me_y) * 2 + 1 - me_x
    to_right = (dp, me_s, lax.rem(me_z + 1, 4))
    to_left = (dp, me_s, lax.rem(me_z + 3, 4))
    images, width = 32, 512
    matrices = 2 * TAPS
    steps = 2 * 9

    def w_left(m):
        return gr_v.at[m, 0:64]

    def w_right(m):
        return gr_v.at[m, 64:128]

    def w_own(m):
        return gr_v.at[18 + m, 0:64]

    def w_back(m):
        return gr_v.at[18 + m, 64:128]

    first_map = 40

    def remote(src, dst, send, recv, target):
        return pltpu.make_async_remote_copy(
            src_ref=src,
            dst_ref=dst,
            send_sem=send,
            recv_sem=recv,
            device_id=target,
            device_id_type=MESH,
        )

    piece_copy = pltpu.make_async_copy(
        master_hbm.at[:, pl.ds(pl.multiple_of(dp * 64, 64), 64)], piece, out_sem.at[0]
    )
    piece_copy.start()

    near = [(a, b) for a in range(4) for b in range(2) if a or b]
    barrier = pltpu.get_barrier_semaphore()

    def near_id(a, b):
        return lax.rem(dp + a, 4), lax.rem(me_s + b, 2)

    for a, b in near:
        other, core = near_id(a, b)
        pl.semaphore_signal(barrier, inc=1, device_id=(other, core, me_z), device_id_type=MESH)
    for d in (1, 2, 3):
        pl.semaphore_signal(
            barrier, inc=1, device_id=(dp, me_s, lax.rem(me_z + d, 4)), device_id_type=MESH
        )

    piece_copy.wait()

    mine_is = [jnp.where(owners_ref[m] == me_z, 1, 0) for m in range(matrices)]
    before = jnp.zeros((), jnp.int32)
    for m in range(matrices):
        value = piece[jnp.minimum(before, piece.shape[0] - 1)] * mine_is[m].astype(full)
        w_own(m)[...] = value.astype(low)
        before = before + mine_is[m]

    @pl.when(me_z == 0)
    def _():
        gr_v[0:18, 0:64, :] = jnp.zeros((18, 64, width), low)

    @pl.when(me_z == 3)
    def _():
        gr_v[0:18, 64:128, :] = jnp.zeros((18, 64, width), low)

    pl.semaphore_wait(barrier, 10)

    sc_local = pltpu.make_async_copy(scales_hbm.at[:, me_y], sc_v.at[1 - me_y], misc_sem.at[0])
    sc_remote = remote(
        scales_hbm.at[:, 1 - me_y], sc_v.at[1 - me_y], misc_sem.at[1], misc_sem.at[2], to_y
    )
    sc_local.start()
    sc_remote.start()

    def right_copy(m):
        return remote(w_left(m), w_left(m), g_ss.at[0, m], g_rs.at[0, m], to_right)

    def left_copy(m):
        return remote(w_back(m), w_right(m), g_ss.at[1, m], g_rs.at[1, m], to_left)

    def x_copy(m):
        part = w_full.at[m, me_s, dp]
        return remote(part, part, g_ss.at[2, m], g_rs.at[2, m], to_x)

    def y_copy(m):
        part = w_full.at[m, me_s, dp]
        return remote(part, part, g_ss.at[3, m], g_rs.at[3, m], to_y)

    def even_copy(m):
        part = w_full.at[m, me_s, dp_x]
        return remote(part, part, g_ss.at[4, m], g_rs.at[4, m], to_y)

    def odd_copy(m):
        part = w_full.at[m, me_s, dp_y]
        return remote(part, part, g_ss.at[4, m], g_rs.at[4, m], to_x)

    def core_copy(m):
        part = w_full.at[m, me_s]
        return remote(part, part, g_ss.at[5, m], g_rs.at[5, m], to_s)

    def flow_right(m):
        @pl.when((m >= 0) & (m < matrices))
        def _():
            @pl.when(me_z > 0)
            def _():
                right_copy(m).wait_recv()

            w_left(m)[...] = w_left(m)[...] + w_own(m)[...]

            @pl.when(me_z < 3)
            def _():
                right_copy(m).start()

    def flow_left(m):
        @pl.when((m >= 0) & (m < matrices))
        def _():
            @pl.when(me_z < 3)
            def _():
                left_copy(m).wait_recv()

            w_back(m)[...] = w_right(m)[...] + w_own(m)[...]

            @pl.when(me_z > 0)
            def _():
                left_copy(m).start()

    def gather(t):
        flow_right(t - 2 * me_z)
        flow_left(t - 2 * (3 - me_z))
        m = t - 6

        @pl.when((m >= 0) & (m < matrices))
        def _():
            w_full[m, me_s, dp] = w_left(m)[...] + w_right(m)[...]
            x_copy(m).start()
            y_copy(m).start()

        m4 = t - 8

        @pl.when((m4 >= 0) & (m4 < matrices))
        def _():
            x_copy(m4).wait_recv()
            y_copy(m4).wait_recv()

            @pl.when(lax.rem(m4, 2) == 0)
            def _():
                even_copy(m4).start()

            @pl.when(lax.rem(m4, 2) == 1)
            def _():
                odd_copy(m4).start()

        m6 = t - 10

        @pl.when((m6 >= 0) & (m6 < matrices))
        def _():
            even_copy(m6).wait_recv()
            core_copy(m6).start()

    def weights(m):
        return w_full[m].reshape(width, width)

    def inner(p, q):
        return jnp.where((p < 4) & (q < 4), 1.0, 0.0).astype(full)

    def mask_of(p, q, rows=slice(None)):
        return jnp.maximum(group_ref[rows, :], inner(p, q))

    def cell(i):
        return pl.ds(pl.multiple_of(i * images, images), images)

    def half_cell(i, g):
        return pl.ds(pl.multiple_of(i * images + g * 16, 16), 16)

    def full_map(n):
        return jnp.where(image_group[n] == 1, 1.0, 0.0).astype(full)

    def prepare(t):
        for g in range(2):
            block = feats_ref[g * 16 : g * 16 + 16, t].astype(full)
            turned = jnp.swapaxes(block, 0, 1)
            for q in range(8):
                value = turned[q] * mask_of(t, q, slice(g * 16, g * 16 + 16))
                xpad[t + 1, q + 1, g * 16 : g * 16 + 16, :] = value.astype(low)
        line = lax.broadcasted_iota(jnp.int32, (8, 8, width), 0)
        column = lax.broadcasted_iota(jnp.int32, (8, 8, width), 1)
        core = jnp.where((line < 4) & (column < 4), 1.0, 0.0).astype(full)
        wide = []
        for k in range(4):
            n = t * 4 + k
            value = feats_ref[n].astype(full) * jnp.maximum(core, full_map(n))
            value = jnp.concatenate([value, jnp.zeros_like(value)], axis=1)
            wide.append(value.reshape(128, width).astype(low))
        project(0, t, jnp.concatenate(wide, axis=0))

    def project(layer, t, rows):
        at_v[1 - layer, :, pl.ds(pl.multiple_of(t * 512, 512), 512)] = lax.dot_general(
            basis_t[layer], rows, (((1,), (1,)), ((), ())), preferred_element_type=full
        ).astype(low)

    def conv_tap(tap, m, acc):
        a, b = tap // 3, lax.rem(tap, 3)
        kernel = weights(m)
        for p in range(8):
            rows = xpad[p + a, pl.ds(b, 8)].reshape(8 * images, width)
            acc[p * 256 : p * 256 + 256, :] += jnp.dot(rows, kernel, preferred_element_type=full)

    for t in range(3):
        gather(t)
    xpad[...] = jnp.zeros_like(xpad)
    basis_t[0] = basis_in_ref[0].T
    place = lax.broadcasted_iota(jnp.int32, (1, 128), 1)
    for n in range(images):
        group_ref[n : n + 1, :] = jnp.full((1, width), full_map(n), full)
        hot_ref[n : n + 1, :] = jnp.where(place == labels_ref[n], 1.0, 0.0).astype(full)
        weight_ref[n : n + 1, :] = jnp.full((1, 128), class_ref[labels_ref[n]].astype(full), full)

    def first(t, carry):
        gather(t)

        @pl.when(t < 11)
        def _():
            prepare(t - 3)

        @pl.when(t == 11)
        def _():
            conv_a[...] = jnp.zeros_like(conv_a)
            conv_b[...] = jnp.zeros_like(conv_b)
            basis_t[1] = basis_in_ref[1].T

        tap = t - 12

        @pl.when(tap >= 0)
        def _():
            core_copy(tap).wait_recv()
            conv_tap(tap, tap, conv_a)

        return carry

    lax.fori_loop(3, 21, first, 0)

    mine = dp * 2 + me_s

    def sum_one(buf, sems, n, a, b):
        other, core = near_id(a, b)
        return remote(
            buf.at[mine], buf.at[mine], sems[0].at[n, a * 2 + b], sems[1].at[n, mine],
            (other, core, me_z),
        )

    def sum_one_wait(buf, n, a, b):
        other, core = near_id(a, b)
        slot = other * 2 + core
        remote(
            buf.at[slot], buf.at[slot], one_ss.at[n, a * 2 + b], one_rs.at[n, slot],
            (other, core, me_z),
        ).wait_recv()

    def sum_two(buf, n, d):
        other = lax.rem(me_z + d, 4)
        return remote(
            buf.at[me_z], buf.at[me_z], two_ss.at[n, d], two_rs.at[n, me_z], (dp, me_s, other)
        )

    def sum_start(n, buf):
        for a, b in near:
            sum_one(buf, (one_ss, one_rs), n, a, b).start()

    def sum_middle(n, buf, buf_two):
        for a, b in near:
            sum_one_wait(buf, n, a, b)
        total = buf[0]
        for slot in range(1, 8):
            total = total + buf[slot]
        buf_two[me_z] = total
        for d in (1, 2, 3):
            sum_two(buf_two, n, d).start()

    def sum_arrived(n, buf_two):
        for d in (1, 2, 3):
            other = lax.rem(me_z + d, 4)
            remote(
                buf_two.at[other], buf_two.at[other], two_ss.at[n, d], two_rs.at[n, other],
                (dp, me_s, other),
            ).wait_recv()

    def sum_total(buf_two):
        return buf_two[0] + buf_two[1] + buf_two[2] + buf_two[3]

    def sum_end(n, buf_two):
        sum_arrived(n, buf_two)
        return sum_total(buf_two)

    def sum_sent(n, buf, buf_two):
        for a, b in near:
            sum_one(buf, (one_ss, one_rs), n, a, b).wait_send()
        for d in (1, 2, 3):
            sum_two(buf_two, n, d).wait_send()

    def column(value):
        return jnp.sum(value, axis=0, keepdims=True)

    zero = jnp.zeros((images, width), full)

    def channel_sums(acc):
        def line(p, carry):
            sums, squares = carry
            for q in range(8):
                value = acc[cell(p * 8 + q), :]
                masked = value * mask_of(p, q)
                sums = sums + masked
                squares = squares + masked * value
            return sums, squares

        sums, squares = lax.fori_loop(0, 8, line, (zero, zero))
        return column(sums), column(squares)

    sums, squares = channel_sums(conv_a)
    group = group_ref[...]
    pixels = 16.0 + 48.0 * group
    small_one[0, mine, 0:1, :] = sums
    small_one[0, mine, 1:2, :] = squares
    small_one[0, mine, 2:3, :] = column(pixels)
    small_one[0, mine, 3:4, :] = jnp.broadcast_to(column(weight_ref[...])[:, 0:1], (1, width))
    sum_start(0, small_one.at[0])

    def later(t, carry):
        gather(t)
        return carry

    lax.fori_loop(21, 23, later, 0)
    sum_middle(0, small_one.at[0], small_two.at[0])
    lax.fori_loop(23, 24, later, 0)
    total = sum_end(0, small_two.at[0])
    total_out[...] = total
    count = total[2:3]

    def moments(total):
        average = total[0:1] / count
        return average, lax.rsqrt(total[1:2] / count - average * average + EPS_NORM)

    average_a, inv_a = moments(total)

    def activation(value, layer, average, inv):
        normed = (value - average) * inv
        pre = params_ref[layer, 0:1, :] * normed + params_ref[layer, 1:2, :]
        return normed, pre, jax.nn.sigmoid(pre)

    def images_first(values):
        return jnp.swapaxes(jnp.stack(values), 0, 1)

    def act_line(p, carry):
        for g in range(2):
            acts = []
            for q in range(8):
                value = conv_a[half_cell(p * 8 + q, g), :]
                normed, pre, sigma = activation(value, 0, average_a, inv_a)
                act = pre * sigma * mask_of(p, q, slice(g * 16, g * 16 + 16))
                xpad[p + 1, q + 1, g * 16 : g * 16 + 16, :] = act.astype(low)
                acts.append(act)
            turned = images_first(acts)
            turned = jnp.concatenate([turned, jnp.zeros_like(turned)], axis=1).astype(low)
            gr_v[first_map + g * 16 : first_map + g * 16 + 16, pl.ds(pl.multiple_of(p * 16, 16), 16), :] = turned
        return carry

    lax.fori_loop(0, 8, act_line, 0)

    def second(tap, carry):
        core_copy(TAPS + tap).wait_recv()
        conv_tap(tap, TAPS + tap, conv_b)

        @pl.when(tap < 4)
        def _():
            gather(24 + tap)

        return carry

    lax.fori_loop(0, TAPS, second, 0)
    sums, squares = channel_sums(conv_b)
    small_one[1, mine, 0:1, :] = sums
    small_one[1, mine, 1:2, :] = squares
    small_one[1, mine, 2:4, :] = jnp.zeros((2, width), full)
    sum_start(1, small_one.at[1])

    def project_one(t, carry):
        project(1, t, gr_v[pl.ds(first_map + t * 4, 4), 0:128, :].reshape(512, width))
        return carry

    lax.fori_loop(0, 4, project_one, 0)
    sum_middle(1, small_one.at[1], small_two.at[1])
    lax.fori_loop(4, 8, project_one, 0)
    total = sum_end(1, small_two.at[1])
    average_b, inv_b = moments(total)

    def pool_line(p, carry):
        for q in range(8):
            normed, pre, sigma = activation(conv_b[cell(p * 8 + q), :], 1, average_b, inv_b)
            carry = carry + pre * sigma * mask_of(p, q)
        return carry

    pooled = lax.fori_loop(0, 8, pool_line, zero) / pixels
    pooled_low = pooled.astype(low)
    classes = head_ref.shape[0]
    head_low = head_ref[:, 0:width].astype(low)
    bias = jnp.broadcast_to(head_ref[:, width : width + 1], (classes, classes))
    across = lax.broadcasted_iota(jnp.int32, (classes, classes), 0)
    along = lax.broadcasted_iota(jnp.int32, (classes, classes), 1)
    logits = lax.dot_general(
        pooled_low, head_low, (((1,), (1,)), ((), ())), preferred_element_type=full
    ) + column(jnp.where(across == along, bias, 0.0))
    shifted = logits - jnp.max(logits, axis=1, keepdims=True)
    log_prob = shifted - jnp.log(jnp.sum(jnp.exp(shifted), axis=1, keepdims=True))
    hot = hot_ref[:, 0:classes]
    image_weight = weight_ref[:, 0:classes]
    picked = jnp.sum(hot * log_prob, axis=1, keepdims=True)
    loss = -column(weight_ref[:, 0:1] * picked)
    d_logits = image_weight * (jnp.exp(log_prob) - hot)
    grad_head = lax.dot_general(
        d_logits,
        pooled_low.astype(full),
        (((0,), (0,)), ((), ())),
        precision=highest,
        preferred_element_type=full,
    )
    head_one[mine, :, :] = jnp.zeros((24, width), full)
    head_one[mine, 0:classes, :] = grad_head
    head_one[mine, 16:17, 0:classes] = column(d_logits)
    head_one[mine, 17:18, :] = jnp.broadcast_to(loss, (1, width))
    d_pooled = (
        lax.dot_general(
            d_logits,
            head_low.astype(full),
            (((1,), (0,)), ((), ())),
            precision=highest,
            preferred_element_type=full,
        )
        / pixels
    )

    def d_line_top(p, carry):
        gammas, betas = carry
        for q in range(8):
            at = cell(p * 8 + q)
            normed, pre, sigma = activation(conv_b[at, :], 1, average_b, inv_b)
            d_pre = d_pooled * mask_of(p, q) * sigma * (1.0 + pre * (1.0 - sigma))
            gammas = gammas + d_pre * normed
            betas = betas + d_pre
        return gammas, betas

    gammas, betas = lax.fori_loop(0, 8, d_line_top, (zero, zero))

    def put_sums(n, gammas, betas):
        small_one[n, mine, 0:1, :] = column(gammas)
        small_one[n, mine, 1:2, :] = column(betas)
        small_one[n, mine, 2:4, :] = jnp.zeros((2, width), full)
        sum_start(n, small_one.at[n])

    def sent(m, carry):
        @pl.when(me_z < 3)
        def _():
            right_copy(m).wait_send()

        @pl.when(me_z > 0)
        def _():
            left_copy(m).wait_send()

        x_copy(m).wait_send()
        y_copy(m).wait_send()
        even_copy(m).wait_send()
        core_copy(m).wait_send()
        return carry

    lax.fori_loop(0, matrices, sent, 0)
    put_sums(2, gammas, betas)

    sum_middle(2, small_one.at[2], small_two.at[2])
    total_b = sum_end(2, small_two.at[2])
    norm_out[1] = total_b
    sum_start(4, head_one)

    def grad_of(layer, normed, d_pre, inv, total):
        gamma = params_ref[layer, 0:1, :]
        return inv * (
            gamma * d_pre
            - gamma * total[1:2] / count
            - normed * (gamma * total[0:1] / count)
        )

    def grad_top(p, carry):
        for q in range(8):
            normed, pre, sigma = activation(conv_b[cell(p * 8 + q), :], 1, average_b, inv_b)
            mask = mask_of(p, q)
            d_pre = d_pooled * mask * sigma * (1.0 + pre * (1.0 - sigma))
            value = mask * grad_of(1, normed, d_pre, inv_b, total_b)
            xpad[p + 1, q + 1, :, :] = value.astype(low)
        return carry

    lax.fori_loop(0, 8, grad_top, 0)
    conv_b[...] = jnp.zeros_like(conv_b)

    def back(tap, carry):
        a, b = tap // 3, lax.rem(tap, 3)
        kernel = weights(TAPS + tap)
        for p in range(8):
            rows = xpad[p + 2 - a, pl.ds(2 - b, 8)].reshape(8 * images, width)
            conv_b[p * 256 : p * 256 + 256, :] += lax.dot_general(
                rows, kernel, (((1,), (1,)), ((), ())), preferred_element_type=full
            )
        return carry

    def d_line(p, carry):
        gammas, betas = carry
        for q in range(8):
            at = cell(p * 8 + q)
            normed, pre, sigma = activation(conv_a[at, :], 0, average_a, inv_a)
            d_pre = conv_b[at, :] * mask_of(p, q) * sigma * (1.0 + pre * (1.0 - sigma))
            conv_b[at, :] = d_pre
            gammas = gammas + d_pre * normed
            betas = betas + d_pre
        return gammas, betas

    def turn_grads(layer):
        def line(p, carry):
            rows = xpad[p + 1, 1:9].reshape(8 * images, width)
            value = jnp.dot(rows, basis_out_ref[layer], preferred_element_type=full)
            value = value.reshape(8, images, width)
            lines = pl.ds(pl.multiple_of(p * 16 + 16, 16), 16)
            gap = jnp.zeros((8, 1, width), full)
            rest = jnp.zeros((8, 8, width), full)
            for g in range(4):
                turned = jnp.swapaxes(value[:, g * 8 : g * 8 + 8], 0, 1)
                shifts = (
                    jnp.concatenate([turned[:, 1:], gap], axis=1),
                    turned,
                    jnp.concatenate([gap, turned[:, :7]], axis=1),
                )
                for b in range(3):
                    wide = jnp.concatenate([shifts[b], rest], axis=1).astype(low)
                    gr_v[b * images + g * 8 : b * images + g * 8 + 8, lines, :] = wide
            return carry

        return line

    def clear(n, carry):
        gr_v[n, 0:16, :] = jnp.zeros((16, width), low)
        gr_v[n, 144:160, :] = jnp.zeros((16, width), low)
        return carry

    lax.fori_loop(0, 3 * images, clear, 0)
    lax.fori_loop(0, 8, turn_grads(1), 0)

    def bottom():
        total_a = sum_total(small_two.at[3])
        norm_out[0] = total_a

        def line(p, carry):
            for q in range(8):
                at = cell(p * 8 + q)
                normed = (conv_a[at, :] - average_a) * inv_a
                value = mask_of(p, q) * grad_of(0, normed, conv_b[at, :], inv_a, total_a)
                xpad[p + 1, q + 1, :, :] = value.astype(low)
            return carry

        lax.fori_loop(0, 8, line, 0)
        lax.fori_loop(0, 8, turn_grads(0), 0)
        head_out[...] = sum_end(4, head_two)

    def x1_recv(j):
        return w_full.at[j, 0, :, :, 0:256]

    def y1_recv(j):
        return w_full.at[j, 0, :, :, 256:512]

    def x2_recv(j):
        return w_full.at[j, 1, 0:2, :, 0:256]

    def y2_recv(j):
        return w_full.at[j, 1, 2:4, :, 0:256]

    def z_recv(j, d):
        return w_full.at[j, 1, d - 1, :, 256:512]

    def side_copy(j):
        ring, four = lax.rem(j, 2), lax.rem(j, 4)
        return remote(s_send.at[ring], s_recv.at[four], s_ss.at[ring], s_rs.at[four], to_s)

    def x1_copy(j):
        ring = lax.rem(j, 2)
        return remote(x1_send.at[ring], x1_recv(j), ss.at[1, ring], rs.at[0, j], to_x)

    def y1_copy(j):
        ring = lax.rem(j, 2)
        return remote(y1_send.at[ring, 1 - me_y], y1_recv(j), ss.at[2, ring], rs.at[1, j], to_y)

    def x2_copy(j):
        ring = lax.rem(j, 2)
        return remote(x2_send.at[ring], x2_recv(j), ss.at[3, ring], rs.at[2, j], to_x)

    def y2_copy(j):
        ring = lax.rem(j, 2)
        return remote(y2_send.at[ring], y2_recv(j), ss.at[4, ring], rs.at[3, j], to_y)

    def z_copy(j, d):
        ring, other = lax.rem(j, 2), lax.rem(me_z + d, 4)
        return remote(
            z_send.at[ring, other],
            z_recv(j, d),
            z_ss.at[ring, d - 1],
            z_rs.at[j, d - 1],
            (dp, me_s, other),
        )

    def place(j):
        return 1 - j // 9, lax.rem(j, 9)

    def local_copy(j):
        layer, i = place(j)
        ring = lax.rem(j, 2)
        return pltpu.make_async_copy(
            div_v.at[ring], out.at[me_s, layer, me_x, me_z, i, me_y], local_sem.at[ring]
        )

    def gz_copy(j, d):
        layer, i = place(j)
        ring, other = lax.rem(j, 2), lax.rem(me_z + d, 4)
        return remote(
            div_v.at[ring],
            out.at[me_s, layer, me_x, me_z, i, me_y],
            gz_ss.at[ring, d - 1],
            gz_rs.at[j, d - 1],
            (dp, me_s, other),
        )

    lower, upper = pl.ds(0, 2), pl.ds(2, 2)

    def spread(j, which, kind, target):
        part = out.at[which]
        return remote(part, part, ss.at[kind, lax.rem(j, 2)], rs.at[kind - 1, j], target)

    def g1y_copy(j):
        layer, i = place(j)
        return spread(j, (me_s, layer, me_x, lower, i, me_y), 5, to_y)

    def g1x_copy(j):
        layer, i = place(j)
        return spread(j, (me_s, layer, me_x, upper, i, me_y), 6, to_x)

    def g2x_copy(j):
        layer, i = place(j)
        return spread(j, (me_s, layer, me_x, lower, i), 7, to_x)

    def g2y_copy(j):
        layer, i = place(j)
        return spread(j, (me_s, layer, pl.ds(0, 2), upper, i, me_y), 8, to_y)

    def gs_copy(j):
        layer, i = place(j)
        return spread(j, (me_s, layer, pl.ds(0, 2), pl.ds(0, 4), i), 9, to_s)

    def products(j, half, store):
        li, i = j // 9, lax.rem(j, 9)
        cols = pl.ds(pl.multiple_of(half * 256, 256), 256)
        for u in range(8):
            x_to = 1 - me_x if u < 4 else me_x
            row = x_to * 2304 + (u % 4) * 576 + 64 * i
            tap = row // 512
            rows = pl.ds(pl.multiple_of(lax.rem(row, 512), 64), 64)
            near = pl.ds(pl.multiple_of((2 - tap // 3) * 16, 16), 128)
            shift = lax.rem(tap, 3) * images
            square = total = None
            for n in range(images):
                p = jnp.dot(
                    at_v[li, rows, n * 128 : (n + 1) * 128],
                    gr_v[shift + n, near, cols],
                    preferred_element_type=full,
                )
                square = p * p if square is None else square + p * p
                total = p if total is None else total + p
            store(u, x_to, u % 4, total, square)

    def at_step(x):
        j = jnp.where(x < 10, x, jnp.where(x < 14, x - 4, x - 5))
        due = ((x >= 0) & (x < 6)) | ((x >= 10) & (x < 13)) | ((x >= 14) & (x < 23))
        return j, due

    def step(k, carry):
        ja, due = at_step(k)

        @pl.when(due & (ja >= 2))
        def _():
            side_copy(ja - 2).wait_send()

        @pl.when(due)
        def _():
            ring = lax.rem(ja, 2)

            def store(u, x_to, z_to, total, square):
                s_send[ring, u, 0] = total.astype(low)
                s_send[ring, u, 1] = square.astype(low)

            products(ja, 1 - me_s, store)
            side_copy(ja).start()

        jb, due = at_step(k - 1)

        @pl.when(due & (jb >= 2))
        def _():
            x1_copy(jb - 2).wait_send()
            y1_copy(jb - 2).wait_send()

        @pl.when(due)
        def _():
            ring, four = lax.rem(jb, 2), lax.rem(jb, 4)
            side_copy(jb).wait_recv()

            def store(u, x_to, z_to, total, square):
                got = s_recv[four, u].astype(full)
                both = (total + got[0], square + got[1])
                for c in range(2):
                    if z_to < 2 and u < 4:
                        x1_send[ring, z_to * 2 + c] = both[c].astype(low)
                    elif z_to < 2:
                        x1_keep[ring, z_to * 2 + c] = both[c]
                    else:
                        at = x_to * 2 + z_to - 2
                        for y_to in range(2):
                            value = both[c][y_to * 32 : y_to * 32 + 32]
                            y1_send[ring, y_to, at, c * 32 : c * 32 + 32, :] = value.astype(low)
                            y1_keep[ring, y_to, at, c * 32 : c * 32 + 32, :] = value

            products(jb, me_s, store)
            x1_copy(jb).start()
            y1_copy(jb).start()

        j7, due = at_step(k - 12)

        @pl.when(due)
        def _():
            @pl.when(j7 >= 2)
            def _():
                gs_copy(j7 - 2).wait_send()

            g2x_copy(j7).wait_recv()
            g2y_copy(j7).wait_recv()
            gs_copy(j7).start()

        j6, due = at_step(k - 10)

        @pl.when(due)
        def _():
            @pl.when(j6 >= 2)
            def _():
                g2y_copy(j6 - 2).wait_send()
                g2x_copy(j6 - 2).wait_send()

            g1y_copy(j6).wait_recv()
            g2x_copy(j6).start()
            g1x_copy(j6).wait_recv()
            g2y_copy(j6).start()

        j5, due = at_step(k - 8)

        @pl.when(due)
        def _():
            @pl.when(j5 >= 2)
            def _():
                g1y_copy(j5 - 2).wait_send()
                g1x_copy(j5 - 2).wait_send()

            local_copy(j5).wait()
            for d in (1, 2, 3):
                gz_copy(j5, d).wait_recv()
            g1y_copy(j5).start()
            g1x_copy(j5).start()

        j4, due = at_step(k - 6)

        @pl.when(due & (j4 == 0))
        def _():
            sc_local.wait()
            sc_remote.wait_recv()

        @pl.when(due)
        def _():
            ring, li, i = lax.rem(j4, 2), j4 // 9, lax.rem(j4, 9)

            @pl.when(j4 >= 2)
            def _():
                for d in (1, 2, 3):
                    gz_copy(j4 - 2, d).wait_send()

            for d in (1, 2, 3):
                z_copy(j4, d).wait_recv()
            both = z_keep[ring, me_z]
            for d in (1, 2, 3):
                both = both + z_recv(j4, d)[...].astype(full)
            scale = DECAY * sc_v[li, i] + (1.0 - DECAY) * both[32:64] / images_all
            ns_v[li, i] = scale
            div_v[ring] = (both[0:32] / total_out[3:4, 0:256] / (scale + DAMPING)).astype(low)
            local_copy(j4).start()
            for d in (1, 2, 3):
                gz_copy(j4, d).start()

        for li in range(2):
            @pl.when(due & (j4 == 9 * li + 8) & (me_y == 1 - li))
            def _():
                pltpu.make_async_copy(ns_v.at[li], ns_out.at[:, me_y], misc_sem.at[3]).start()

            @pl.when(due & (j4 == 9 * li + 8) & (me_y == li))
            def _():
                remote(
                    ns_v.at[li], ns_out.at[:, me_y], misc_sem.at[4], misc_sem.at[5], to_y
                ).start()

        j3, due = at_step(k - 4)

        @pl.when(due)
        def _():
            ring = lax.rem(j3, 2)

            @pl.when(j3 >= 2)
            def _():
                for d in (1, 2, 3):
                    z_copy(j3 - 2, d).wait_send()

            y2_copy(j3).wait_recv()
            x2_copy(j3).wait_recv()
            for z_to in range(4):
                got = y2_recv(j3)[z_to] if z_to < 2 else x2_recv(j3)[z_to - 2]
                both = two_keep[ring, z_to] + got.astype(full)
                z_keep[ring, z_to] = both
                z_send[ring, z_to] = both.astype(low)
            for d in (1, 2, 3):
                z_copy(j3, d).start()

        j2, due = at_step(k - 2)

        @pl.when(due)
        def _():
            ring = lax.rem(j2, 2)

            @pl.when(j2 >= 2)
            def _():
                x2_copy(j2 - 2).wait_send()
                y2_copy(j2 - 2).wait_send()

            x1_copy(j2).wait_recv()
            here = pl.ds(pl.multiple_of(me_y * 32, 32), 32)
            there = pl.ds(pl.multiple_of((1 - me_y) * 32, 32), 32)
            got = x1_recv(j2)
            for z_to in range(2):
                for c in range(2):
                    at, lines = z_to * 2 + c, slice(c * 32, c * 32 + 32)
                    two_keep[ring, z_to, lines, :] = x1_keep[ring, at, here, :] + got[
                        at, here, :
                    ].astype(full)
                    y2_send[ring, z_to, lines, :] = (
                        x1_keep[ring, at, there, :] + got[at, there, :].astype(full)
                    ).astype(low)
            y2_copy(j2).start()
            y1_copy(j2).wait_recv()
            got = y1_recv(j2)
            for z_to in range(2):
                mine_at, other_at = me_x * 2 + z_to, (1 - me_x) * 2 + z_to
                two_keep[ring, 2 + z_to] = y1_keep[ring, me_y, mine_at] + got[mine_at].astype(full)
                x2_send[ring, z_to] = (
                    y1_keep[ring, me_y, other_at] + got[other_at].astype(full)
                ).astype(low)
            x2_copy(j2).start()

        @pl.when((k >= 6) & (k < 9))
        def _():
            lax.fori_loop(0, 3, lambda t, carry: back((k - 6) * 3 + t, carry), 0)

        @pl.when(k == 8)
        def _():
            sum_middle(4, head_one, head_two)

        @pl.when(k == 9)
        def _():
            gammas, betas = lax.fori_loop(0, 8, d_line, (zero, zero))
            put_sums(3, gammas, betas)

        @pl.when(k == 10)
        def _():
            sum_middle(3, small_one.at[3], small_two.at[3])

        @pl.when(k == 13)
        def _():
            sum_arrived(3, small_two.at[3])
            bottom()

        return carry

    lax.fori_loop(0, steps + 5 + 12, step, 0)

    def finish(j, carry):
        gs_copy(j).wait_recv()
        return carry

    lax.fori_loop(0, steps, finish, 0)
    sc_remote.wait_send()
    li = 1 - me_y
    pltpu.make_async_copy(ns_v.at[li], ns_out.at[:, me_y], misc_sem.at[3]).wait()
    ns_remote = remote(ns_v.at[0], ns_out.at[:, 0], misc_sem.at[4], misc_sem.at[5], to_y)
    ns_remote.wait_send()
    ns_remote.wait_recv()
    for j in (steps - 2, steps - 1):
        for copy in (side_copy, x1_copy, y1_copy, x2_copy, y2_copy):
            copy(j).wait_send()
        for copy in (g1y_copy, g1x_copy, g2y_copy, g2x_copy, gs_copy):
            copy(j).wait_send()
        for d in (1, 2, 3):
            z_copy(j, d).wait_send()
            gz_copy(j, d).wait_send()
    for n in range(4):
        sum_sent(n, small_one.at[n], small_two.at[n])
    sum_sent(4, head_one, head_two)


def whole_step(
    feats, size_group, labels, class_wt, owners, basis_in, basis_out, master, norm_params, head, scales
):
    count_img, side_len, _, width = feats.shape
    images_all = count_img * lax.axis_size("dp") * lax.axis_size("side") * lax.axis_size("blk")
    low, full, dma = jnp.bfloat16, jnp.float32, pltpu.SemaphoreType.DMA
    vmem, any_spec = pl.BlockSpec(memory_space=pltpu.VMEM), pl.BlockSpec(memory_space=pl.ANY)
    smem = pl.BlockSpec(memory_space=pltpu.SMEM)
    rows = count_img * side_len * side_len
    divided, new_scales, total, norm_sums, head_sums = pl.pallas_call(
        functools.partial(step_kernel, images_all),
        out_shape=[
            jax.ShapeDtypeStruct((2, 2, 2, 4, 9, 2, 32, 256), low),
            jax.ShapeDtypeStruct((9, 2, 32, 256), full),
            jax.ShapeDtypeStruct((4, width), full),
            jax.ShapeDtypeStruct((2, 4, width), full),
            jax.ShapeDtypeStruct((24, width), full),
        ],
        in_specs=[vmem, smem, smem, smem, smem, any_spec, vmem, vmem, vmem, vmem, any_spec],
        out_specs=[any_spec, any_spec, vmem, vmem, vmem],
        scratch_shapes=[
            pltpu.VMEM((18, 2, 4, 64, 512), low),
            pltpu.VMEM((10, 10, 32, 512), low),
            pltpu.VMEM((rows, 512), full),
            pltpu.VMEM((rows, 512), full),
            pltpu.VMEM((2, 512, 4096), low),
            pltpu.VMEM((96, 160, 512), low),
            pltpu.VMEM((32, 512), full),
            pltpu.VMEM((32, 128), full),
            pltpu.VMEM((32, 128), full),
            pltpu.VMEM((10, 64, 512), full),
            pltpu.VMEM((2, 512, 512), low),
            pltpu.VMEM((4, 8, 4, 512), full),
            pltpu.VMEM((4, 4, 4, 512), full),
            pltpu.VMEM((8, 24, 512), full),
            pltpu.VMEM((4, 24, 512), full),
            pltpu.VMEM((2, 9, 32, 256), full),
            pltpu.VMEM((2, 9, 32, 256), full),
            pltpu.VMEM((2, 32, 256), low),
            pltpu.VMEM((2, 8, 2, 64, 256), low),
            pltpu.VMEM((4, 8, 2, 64, 256), low),
            pltpu.VMEM((2, 4, 64, 256), low),
            pltpu.VMEM((2, 4, 64, 256), full),
            pltpu.VMEM((2, 2, 4, 64, 256), low),
            pltpu.VMEM((2, 2, 4, 64, 256), full),
            pltpu.VMEM((2, 2, 64, 256), low),
            pltpu.VMEM((2, 2, 64, 256), low),
            pltpu.VMEM((2, 4, 64, 256), full),
            pltpu.VMEM((2, 4, 64, 256), low),
            pltpu.VMEM((2, 4, 64, 256), full),
            dma((1,)),
            dma((6, 18)),
            dma((6, 18)),
            dma((5, 8)),
            dma((5, 8)),
            dma((5, 4)),
            dma((5, 4)),
            dma((6,)),
            dma((2,)),
            dma((10, 2)),
            dma((2,)),
            dma((4,)),
            dma((9, 18)),
            dma((2, 3)),
            dma((18, 3)),
            dma((2, 3)),
            dma((18, 3)),
        ],
        name="whole_step",
        compiler_params=pltpu.CompilerParams(
            collective_id=0, has_side_effects=True, vmem_limit_bytes=63 * 2**20
        ),
    )(
        feats,
        size_group,
        labels,
        class_wt,
        owners,
        master,
        norm_params,
        head,
        basis_in,
        basis_out,
        scales.reshape(9, 2, 32, 256),
    )
    return (
        divided.reshape(2, 18, 512, 256),
        new_scales.reshape(576, 256),
        total,
        norm_sums,
        head_sums,
    )


def update_kernel(
    owners_ref,
    divided,
    basis_in,
    basis_out,
    w_hbm,
    m_hbm,
    v_hbm,
    total_ref,
    norm_sums,
    head_sums,
    norm_w,
    norm_m,
    norm_v,
    head_w,
    head_m,
    head_v,
    w_out,
    m_out,
    v_out,
    norm_w_out,
    norm_m_out,
    norm_v_out,
    head_w_out,
    head_m_out,
    head_v_out,
    loss_out,
    weight_out,
    matrix,
    p_v,
    rows_v,
    cols_v,
    w_v,
    m_v,
    v_v,
    gradients,
    in_sem,
    out_sem,
):
    low, full = jnp.bfloat16, jnp.float32
    slots, half, width = w_v.shape
    blk, side = lax.axis_index("blk"), lax.axis_index("side")

    def state_in(q):
        return [
            pltpu.make_async_copy(src.at[q], dst.at[q], in_sem.at[n, q])
            for n, (src, dst) in enumerate(((w_hbm, w_v), (m_hbm, m_v), (v_hbm, v_v)))
        ]

    def state_out(q):
        return [
            pltpu.make_async_copy(src.at[q], dst.at[q], out_sem.at[n, q])
            for n, (src, dst) in enumerate(((w_v, w_out), (m_v, m_out), (v_v, v_out)))
        ]

    rows_in = pltpu.make_async_copy(
        basis_in.at[:, pl.ds(pl.multiple_of(side * half, half), half)], rows_v, in_sem.at[4, 0]
    )
    cols_in = pltpu.make_async_copy(basis_out, cols_v, in_sem.at[4, 1])
    rows_in.start()
    cols_in.start()

    for q in range(slots):
        matrix[q] = 0
    count = jnp.zeros((), jnp.int32)
    for m in range(owners_ref.shape[0]):
        mine = owners_ref[m] == blk

        @pl.when(mine)
        def _():
            matrix[count] = m

        count = count + jnp.where(mine, 1, 0)

    def part_in(q):
        return pltpu.make_async_copy(divided.at[:, matrix[q]], p_v.at[q], in_sem.at[3, q])

    for q in range(slots):
        part_in(q).start()
        for copy in state_in(q):
            copy.start()
    weight = total_ref[3:4, 0:1]
    weight_out[0, 0] = total_ref[3, 0]
    loss_out[0, 0] = head_sums[17, 0]
    for layer in range(2):
        norm_w_out[layer], norm_m_out[layer], norm_v_out[layer] = adamw(
            norm_w[layer],
            norm_m[layer],
            norm_v[layer],
            norm_sums[layer, 0:2, :] / weight,
            RATE_NORM,
        )
    classes = head_w.shape[0]
    here = lax.broadcasted_iota(jnp.int32, (classes, classes), 0)
    there = lax.broadcasted_iota(jnp.int32, (classes, classes), 1)
    line = jnp.broadcast_to(head_sums[16:17, 0:classes], (classes, classes))
    bias = jnp.sum(jnp.where(here == there, line, 0.0), axis=1, keepdims=True)
    for at, gradient in (
        (slice(0, width), head_sums[0:classes, :]),
        (slice(width, width + 1), bias),
    ):
        head_w_out[:, at], head_m_out[:, at], head_v_out[:, at] = adamw(
            head_w[:, at], head_m[:, at], head_v[:, at], gradient / weight, RATE_HEAD
        )
    rows_in.wait()
    cols_in.wait()

    def gradient(q):
        layer = matrix[q] // TAPS
        held = jnp.where(q < count, 1.0, 0.0).astype(full)
        both = [
            jnp.dot(rows_v[layer], p_v[q, s], preferred_element_type=full).astype(low)
            for s in range(2)
        ]
        return held * lax.dot_general(
            jnp.concatenate(both, axis=1),
            cols_v[layer],
            (((1,), (1,)), ((), ())),
            preferred_element_type=full,
        )

    part_in(0).wait()
    gradients[0] = gradient(0)
    for q in range(slots):
        for copy in state_in(q):
            copy.wait()
        if q + 1 < slots:
            part_in(q + 1).wait()
            gradients[(q + 1) % 2] = gradient(q + 1)
        w_v[q], m_v[q], v_v[q] = adamw(w_v[q], m_v[q], v_v[q], gradients[q % 2], RATE_CONV)
        for copy in state_out(q):
            copy.start()
    for q in range(slots):
        for copy in state_out(q):
            copy.wait()


def update(
    owners, divided, basis_in, basis_out, states, total, norm_sums, head_sums, norm_states, head_states
):
    full, dma = jnp.float32, pltpu.SemaphoreType.DMA
    slots, half, width = states[0].shape
    vmem, any_spec = pl.BlockSpec(memory_space=pltpu.VMEM), pl.BlockSpec(memory_space=pl.ANY)
    smem = pl.BlockSpec(memory_space=pltpu.SMEM)
    like = [jax.ShapeDtypeStruct(x.shape, full) for x in (*states, *norm_states, *head_states)]
    one = jax.ShapeDtypeStruct((1, 1), full)
    return pl.pallas_call(
        update_kernel,
        out_shape=like + [one, one],
        in_specs=[smem] + [any_spec] * 6 + [vmem] * 9,
        out_specs=[any_spec] * 3 + [vmem] * 6 + [smem] * 2,
        scratch_shapes=[
            pltpu.SMEM((slots,), jnp.int32),
            pltpu.VMEM((slots, 2, width, half), jnp.bfloat16),
            pltpu.VMEM((2, half, width), jnp.bfloat16),
            pltpu.VMEM((2, width, width), jnp.bfloat16),
            pltpu.VMEM(states[0].shape, full),
            pltpu.VMEM(states[0].shape, full),
            pltpu.VMEM(states[0].shape, full),
            pltpu.VMEM((2, half, width), full),
            dma((5, slots)),
            dma((3, slots)),
        ],
        name="update",
        compiler_params=pltpu.CompilerParams(vmem_limit_bytes=63 * 2**20),
    )(
        owners,
        divided,
        basis_in,
        basis_out,
        *states,
        total,
        norm_sums,
        head_sums,
        *norm_states,
        *head_states,
    )


def shards_general(
    feats,
    size_group,
    labels,
    class_wt,
    owners,
    basis_in,
    basis_out,
    scales,
    master,
    moment1,
    moment2,
    norm_params,
    norm_m,
    norm_v,
    head,
    head_m,
    head_v,
):
    count_img = feats.shape[0]
    side_len = feats.shape[1]
    width = feats.shape[3]
    half = width // 2
    n_dp = lax.axis_size("dp")
    n_side = lax.axis_size("side")
    n_blk = lax.axis_size("blk")
    slots_dev = master.shape[0]
    matrices = owners.shape[0]
    block_rows = scales.shape[0]
    images_all = count_img * n_dp * n_side * n_blk
    index = jnp.arange(matrices)
    earlier = (owners[:, None] == owners[None, :]) & (index[None, :] < index[:, None])
    slot = owners * slots_dev + jnp.sum(earlier.astype(jnp.int32), axis=1)
    pieces = lax.all_gather(master.astype(jnp.bfloat16), ("side", "blk"), axis=0, tiled=True)
    pieces = pieces.reshape(n_side, n_blk * slots_dev, master.shape[1], width)
    pick = (slot[:, None] == jnp.arange(n_blk * slots_dev)[None, :]).astype(jnp.bfloat16)
    kernels = jnp.einsum("ms,hsrc->mhrc", pick, pieces, preferred_element_type=jnp.float32)
    kernels = kernels.astype(jnp.bfloat16).reshape(L, TAPS, width, width)
    line = jnp.arange(side_len)
    inner = (line[:, None] < side_len // 2) & (line[None, :] < side_len // 2)
    cell_mask = jnp.where((size_group == 1)[:, None, None], True, inner[None]).astype(jnp.float32)
    mask_four = cell_mask[..., None]
    pixels = jnp.sum(cell_mask, axis=(1, 2))
    class_hot = labels[:, None] == jnp.arange(class_wt.shape[0])[None, :]
    weight = jnp.sum(jnp.where(class_hot, class_wt[None, :], 0), axis=1).astype(jnp.float32)
    hot_float = class_hot.astype(jnp.float32)
    count_all, weight_all = lax.psum((jnp.sum(pixels), jnp.sum(weight)), ("dp", "side", "blk"))
    current = (feats.astype(jnp.float32) * mask_four).astype(jnp.bfloat16)
    kept = []
    act_out = None
    for layer in range(L):
        conv_out = conv_forward(current, kernels[layer])
        masked = conv_out * mask_four
        col_sum, sq_sum = lax.psum(
            (jnp.sum(masked, axis=(0, 1, 2)), jnp.sum(masked * conv_out, axis=(0, 1, 2))),
            ("dp", "side", "blk"),
        )
        average = col_sum / count_all
        inv_std = lax.rsqrt(sq_sum / count_all - average * average + EPS_NORM)
        normed = (conv_out - average) * inv_std
        pre_act = norm_params[layer, 0] * normed + norm_params[layer, 1]
        act_out = jax.nn.silu(pre_act) * mask_four
        kept.append((current, normed, pre_act, inv_std))
        current = act_out.astype(jnp.bfloat16)
    pooled = jnp.sum(act_out, axis=(1, 2)) / pixels[:, None]
    pooled_low = pooled.astype(jnp.bfloat16)
    head_low = head[:width].astype(jnp.bfloat16)
    logits = jnp.dot(pooled_low, head_low, preferred_element_type=jnp.float32) + head[width]
    log_prob = jax.nn.log_softmax(logits, axis=-1)
    loss_local = -jnp.sum(weight * jnp.sum(hot_float * log_prob, axis=1))
    d_logits = weight[:, None] * (jnp.exp(log_prob) - hot_float)
    grad_weights = jnp.dot(
        pooled_low.astype(jnp.float32).T, d_logits, precision=lax.Precision.HIGHEST
    )
    grad_head = jnp.concatenate([grad_weights, jnp.sum(d_logits, axis=0)[None]], axis=0)
    loss_all, head_all = lax.psum((loss_local, grad_head), ("dp", "side", "blk"))
    d_pooled = jnp.dot(d_logits, head_low.astype(jnp.float32).T, precision=lax.Precision.HIGHEST)
    d_act = d_pooled[:, None, None, :] / pixels[:, None, None, None] * mask_four
    terms = [None] * L
    grad_norm = [None] * L
    for layer in reversed(range(L)):
        inputs, normed, pre_act, inv_std = kept[layer]
        sigma = jax.nn.sigmoid(pre_act)
        d_pre = d_act * mask_four * sigma * (1.0 + pre_act * (1.0 - sigma))
        gamma_sum, beta_sum = lax.psum(
            (jnp.sum(d_pre * normed, axis=(0, 1, 2)), jnp.sum(d_pre, axis=(0, 1, 2))),
            ("dp", "side", "blk"),
        )
        grad_norm[layer] = jnp.stack([gamma_sum, beta_sum])
        gamma = norm_params[layer, 0]
        d_conv = (
            mask_four
            * inv_std
            * (
                gamma * d_pre
                - gamma * beta_sum / count_all
                - normed * gamma * gamma_sum / count_all
            )
        )
        grad_low = d_conv.astype(jnp.bfloat16)
        if layer > 0:
            d_act = conv_backward(grad_low, kernels[layer])
        act_proj = jnp.einsum(
            "npqc,ci->npqi", inputs, basis_in[layer], preferred_element_type=jnp.float32
        ).astype(jnp.bfloat16)
        grad_proj = jnp.einsum(
            "npqo,oj->npqj", grad_low, basis_out[layer], preferred_element_type=jnp.float32
        ).astype(jnp.bfloat16)
        terms[layer] = tap_sums(act_proj, grad_proj)
    whole = jnp.stack(terms).reshape(n_dp, n_blk, block_rows, 2, 2, half)
    whole = whole.transpose(0, 4, 1, 2, 3, 5).reshape(n_dp * 2 * n_blk * block_rows, 2 * half)
    reduced = lax.psum_scatter(whole, ("dp", "side", "blk"), scatter_dimension=0, tiled=True)
    proj_sum = reduced[:, :half]
    proj_square = reduced[:, half:]
    new_scales = DECAY * scales + (1.0 - DECAY) * proj_square / images_all
    divided = (proj_sum / weight_all / (new_scales + DAMPING)).astype(jnp.bfloat16)
    spread = lax.all_gather(divided, ("dp", "side", "blk"), axis=0, tiled=True)
    spread = spread.reshape(n_dp, 2, n_blk, block_rows, half).transpose(0, 2, 3, 1, 4)
    precond_all = spread.reshape(matrices, width, width)
    slot_ids = lax.axis_index("blk") * slots_dev + jnp.arange(slots_dev)
    owned = (slot[None, :] == slot_ids[:, None]).astype(jnp.bfloat16)
    chosen = jnp.einsum(
        "qm,mij->qij", owned, precond_all, preferred_element_type=jnp.float32
    ).astype(jnp.bfloat16)
    layer_hot = (index[:, None] // TAPS == jnp.arange(L)[None, :]).astype(jnp.bfloat16)
    slot_layer = jnp.dot(owned, layer_hot, preferred_element_type=jnp.float32).astype(jnp.bfloat16)
    half_rows = lax.dynamic_slice_in_dim(
        basis_in, lax.axis_index("side") * master.shape[1], master.shape[1], 1
    )
    rows_slot = jnp.einsum(
        "ql,lci->qci", slot_layer, half_rows, preferred_element_type=jnp.float32
    ).astype(jnp.bfloat16)
    cols_slot = jnp.einsum(
        "ql,loj->qoj", slot_layer, basis_out, preferred_element_type=jnp.float32
    ).astype(jnp.bfloat16)
    turned = jnp.einsum(
        "qci,qij->qcj", rows_slot, chosen, preferred_element_type=jnp.float32
    ).astype(jnp.bfloat16)
    slot_grad = jnp.einsum("qcj,qoj->qco", turned, cols_slot, preferred_element_type=jnp.float32)
    new_master, new_moment1, new_moment2 = adamw(master, moment1, moment2, slot_grad, RATE_CONV)
    new_norm, new_norm_m, new_norm_v = adamw(
        norm_params, norm_m, norm_v, jnp.stack(grad_norm) / weight_all, RATE_NORM
    )
    new_head, new_head_m, new_head_v = adamw(head, head_m, head_v, head_all / weight_all, RATE_HEAD)
    return (
        loss_all,
        weight_all,
        new_scales,
        new_master,
        new_moment1,
        new_moment2,
        new_norm,
        new_norm_m,
        new_norm_v,
        new_head,
        new_head_m,
        new_head_v,
    )


def shards_fast(
    feats,
    size_group,
    labels,
    class_wt,
    owners,
    basis_in,
    basis_out,
    scales,
    master,
    moment1,
    moment2,
    norm_params,
    norm_m,
    norm_v,
    head,
    head_m,
    head_v,
):
    divided, new_scales, total, norm_sums, head_sums = whole_step(
        feats,
        size_group,
        labels,
        class_wt,
        owners,
        basis_in,
        basis_out,
        master,
        norm_params,
        head.T,
        scales,
    )
    results = update(
        owners,
        divided,
        basis_in,
        basis_out,
        (master, moment1, moment2),
        total,
        norm_sums,
        head_sums,
        (norm_params, norm_m, norm_v),
        (head.T, head_m.T, head_v.T),
    )
    loss_all, weight_all = results[9][0, 0], results[10][0, 0]
    return (loss_all, weight_all, new_scales, *results[:6], *(x.T for x in results[6:9]))


def shards(*args):
    feats, class_wt, scales, master = args[0], args[3], args[7], args[8]
    mesh_shape = tuple(lax.axis_size(name) for name in ("dp", "side", "blk"))
    fits = (
        mesh_shape == (4, 2, 4)
        and scales.shape == (576, 256)
        and feats.shape == (32, 8, 8, 512)
        and master.shape == (10, 256, 512)
        and class_wt.shape[0] <= 16
    )
    return shards_fast(*args) if fits else shards_general(*args)


def solution(mesh):
    return jax.shard_map(
        shards,
        mesh=mesh,
        in_specs=(
            P(("dp", "side", "blk"), None, None, None),
            P(("dp", "side", "blk")),
            P(("dp", "side", "blk")),
            P(),
            P(),
            P(),
            P(),
            P(("dp", "blk"), "side"),
            P("blk", "side", None),
            P("blk", "side", None),
            P("blk", "side", None),
            P(),
            P(),
            P(),
            P(),
            P(),
            P(),
        ),
        out_specs=(
            P(),
            P(),
            P(("dp", "blk"), "side"),
            P("blk", "side", None),
            P("blk", "side", None),
            P("blk", "side", None),
            P(),
            P(),
            P(),
            P(),
            P(),
            P(),
        ),
        check_vma=False,
    )
```

```python
import functools

import jax
import jax.numpy as jnp
from jax import lax
from jax.experimental import pallas as pl
from jax.experimental.pallas import tpu as pltpu
from jax.sharding import PartitionSpec as P

L = 2
TAPS = 9
STEP = 10


EPS_NORM = 1e-05
DAMPING = 0.001
DECAY = 0.95
BETA_ONE = 0.9
BETA_TWO = 0.999
ADAM_EPS = 1e-08
WEIGHT_DECAY = 0.01
RATE_CONV = 0.01
RATE_NORM = 0.5
RATE_HEAD = 0.02


def adamw(weight_now, first_now, second_now, gradient, rate):
    first_new = BETA_ONE * first_now + (1.0 - BETA_ONE) * gradient
    second_new = BETA_TWO * second_now + (1.0 - BETA_TWO) * gradient * gradient
    first_hat = first_new * (1.0 / (1.0 - BETA_ONE**STEP))
    second_hat = second_new * (1.0 / (1.0 - BETA_TWO**STEP))
    weight_new = weight_now - rate * (
        first_hat / (jnp.sqrt(second_hat) + ADAM_EPS) + WEIGHT_DECAY * weight_now
    )
    return (weight_new, first_new, second_new)


def pad_cells(values):
    return jnp.pad(values, ((0, 0), (1, 1), (1, 1), (0, 0)))


def conv_forward(inputs, kernel):
    side_len = inputs.shape[1]
    padded = pad_cells(inputs)
    total = None
    for tap in range(TAPS):
        shifted = padded[:, tap // 3 : tap // 3 + side_len, tap % 3 : tap % 3 + side_len]
        term = jnp.einsum("npqc,co->npqo", shifted, kernel[tap], preferred_element_type=jnp.float32)
        total = term if total is None else total + term
    return total


def conv_backward(grads, kernel):
    side_len = grads.shape[1]
    total = None
    for tap in range(TAPS):
        offset_row = tap // 3
        offset_col = tap % 3
        term = jnp.einsum("npqo,co->npqc", grads, kernel[tap], preferred_element_type=jnp.float32)
        term = jnp.pad(
            term, ((0, 0), (offset_row, 2 - offset_row), (offset_col, 2 - offset_col), (0, 0))
        )
        total = term if total is None else total + term
    return total[:, 1 : side_len + 1, 1 : side_len + 1]


def tap_sums(act_proj, grad_proj):
    side_len = act_proj.shape[1]
    padded = pad_cells(act_proj)
    firsts, seconds = ([], [])
    for tap in range(TAPS):
        shifted = padded[:, tap // 3 : tap // 3 + side_len, tap % 3 : tap % 3 + side_len]
        each = jnp.einsum("npqi,npqj->nij", shifted, grad_proj, preferred_element_type=jnp.float32)
        firsts.append(jnp.sum(each, axis=0))
        seconds.append(jnp.sum(each * each, axis=0))
    return jnp.concatenate([jnp.stack(firsts), jnp.stack(seconds)], axis=-1)


MESH = pl.DeviceIdType.MESH


def step_kernel(
    images_all,
    feats_ref,
    image_group,
    labels_ref,
    class_ref,
    owners_ref,
    master_hbm,
    params_ref,
    head_ref,
    basis_in_ref,
    basis_out_ref,
    scales_hbm,
    out,
    ns_out,
    total_out,
    norm_out,
    head_out,
    w_full,
    xpad,
    conv_a,
    conv_b,
    at_v,
    gr_v,
    group_ref,
    hot_ref,
    weight_ref,
    piece,
    basis_t,
    small_one,
    small_two,
    head_one,
    head_two,
    sc_v,
    ns_v,
    div_v,
    s_send,
    s_recv,
    x1_send,
    x1_keep,
    y1_send,
    y1_keep,
    x2_send,
    y2_send,
    two_keep,
    z_send,
    z_keep,
    out_sem,
    g_ss,
    g_rs,
    one_ss,
    one_rs,
    two_ss,
    two_rs,
    misc_sem,
    local_sem,
    ss,
    s_ss,
    s_rs,
    rs,
    z_ss,
    z_rs,
    gz_ss,
    gz_rs,
):
    low, full = jnp.bfloat16, jnp.float32
    highest = lax.Precision.HIGHEST
    dp, me_s, me_z = lax.axis_index("dp"), lax.axis_index("side"), lax.axis_index("blk")
    me_y, me_x = dp // 2, lax.rem(dp, 2)
    to_s = (dp, 1 - me_s, me_z)
    to_x = (me_y * 2 + 1 - me_x, me_s, me_z)
    to_y = ((1 - me_y) * 2 + me_x, me_s, me_z)
    dp_x, dp_y = me_y * 2 + 1 - me_x, (1 - me_y) * 2 + me_x
    dp_xy = (1 - me_y) * 2 + 1 - me_x
    to_right = (dp, me_s, lax.rem(me_z + 1, 4))
    to_left = (dp, me_s, lax.rem(me_z + 3, 4))
    images, width = 32, 512
    matrices = 2 * TAPS
    steps = 2 * 9

    def w_left(m):
        return gr_v.at[m, 0:64]

    def w_right(m):
        return gr_v.at[m, 64:128]

    def w_own(m):
        return gr_v.at[18 + m, 0:64]

    def w_back(m):
        return gr_v.at[18 + m, 64:128]

    first_map = 40

    def remote(src, dst, send, recv, target):
        return pltpu.make_async_remote_copy(
            src_ref=src,
            dst_ref=dst,
            send_sem=send,
            recv_sem=recv,
            device_id=target,
            device_id_type=MESH,
        )

    piece_copy = pltpu.make_async_copy(
        master_hbm.at[:, pl.ds(pl.multiple_of(dp * 64, 64), 64)], piece, out_sem.at[0]
    )
    piece_copy.start()

    near = [(a, b) for a in range(4) for b in range(2) if a or b]
    barrier = pltpu.get_barrier_semaphore()

    def near_id(a, b):
        return lax.rem(dp + a, 4), lax.rem(me_s + b, 2)

    for a, b in near:
        other, core = near_id(a, b)
        pl.semaphore_signal(barrier, inc=1, device_id=(other, core, me_z), device_id_type=MESH)
    for d in (1, 2, 3):
        pl.semaphore_signal(
            barrier, inc=1, device_id=(dp, me_s, lax.rem(me_z + d, 4)), device_id_type=MESH
        )

    piece_copy.wait()

    mine_is = [jnp.where(owners_ref[m] == me_z, 1, 0) for m in range(matrices)]
    before = jnp.zeros((), jnp.int32)
    for m in range(matrices):
        value = piece[jnp.minimum(before, piece.shape[0] - 1)] * mine_is[m].astype(full)
        w_own(m)[...] = value.astype(low)
        before = before + mine_is[m]

    @pl.when(me_z == 0)
    def _():
        gr_v[0:18, 0:64, :] = jnp.zeros((18, 64, width), low)

    @pl.when(me_z == 3)
    def _():
        gr_v[0:18, 64:128, :] = jnp.zeros((18, 64, width), low)

    pl.semaphore_wait(barrier, 10)

    sc_local = pltpu.make_async_copy(scales_hbm.at[:, me_y], sc_v.at[1 - me_y], misc_sem.at[0])
    sc_remote = remote(
        scales_hbm.at[:, 1 - me_y], sc_v.at[1 - me_y], misc_sem.at[1], misc_sem.at[2], to_y
    )
    sc_local.start()
    sc_remote.start()

    def right_copy(m):
        return remote(w_left(m), w_left(m), g_ss.at[0, m], g_rs.at[0, m], to_right)

    def left_copy(m):
        return remote(w_back(m), w_right(m), g_ss.at[1, m], g_rs.at[1, m], to_left)

    def x_copy(m):
        part = w_full.at[m, me_s, dp]
        return remote(part, part, g_ss.at[2, m], g_rs.at[2, m], to_x)

    def y_copy(m):
        part = w_full.at[m, me_s, dp]
        return remote(part, part, g_ss.at[3, m], g_rs.at[3, m], to_y)

    def even_copy(m):
        part = w_full.at[m, me_s, dp_x]
        return remote(part, part, g_ss.at[4, m], g_rs.at[4, m], to_y)

    def odd_copy(m):
        part = w_full.at[m, me_s, dp_y]
        return remote(part, part, g_ss.at[4, m], g_rs.at[4, m], to_x)

    def core_copy(m):
        part = w_full.at[m, me_s]
        return remote(part, part, g_ss.at[5, m], g_rs.at[5, m], to_s)

    def flow_right(m):
        @pl.when((m >= 0) & (m < matrices))
        def _():
            @pl.when(me_z > 0)
            def _():
                right_copy(m).wait_recv()

            w_left(m)[...] = w_left(m)[...] + w_own(m)[...]

            @pl.when(me_z < 3)
            def _():
                right_copy(m).start()

    def flow_left(m):
        @pl.when((m >= 0) & (m < matrices))
        def _():
            @pl.when(me_z < 3)
            def _():
                left_copy(m).wait_recv()

            w_back(m)[...] = w_right(m)[...] + w_own(m)[...]

            @pl.when(me_z > 0)
            def _():
                left_copy(m).start()

    def gather(t):
        flow_right(t - 2 * me_z)
        flow_left(t - 2 * (3 - me_z))
        m = t - 6

        @pl.when((m >= 0) & (m < matrices))
        def _():
            w_full[m, me_s, dp] = w_left(m)[...] + w_right(m)[...]
            x_copy(m).start()
            y_copy(m).start()

        m4 = t - 8

        @pl.when((m4 >= 0) & (m4 < matrices))
        def _():
            x_copy(m4).wait_recv()
            y_copy(m4).wait_recv()

            @pl.when(lax.rem(m4, 2) == 0)
            def _():
                even_copy(m4).start()

            @pl.when(lax.rem(m4, 2) == 1)
            def _():
                odd_copy(m4).start()

        m6 = t - 11

        @pl.when((m6 >= 0) & (m6 < matrices))
        def _():
            even_copy(m6).wait_recv()
            core_copy(m6).start()

    def weights(m):
        return w_full[m].reshape(width, width)

    def inner(p, q):
        return jnp.where((p < 4) & (q < 4), 1.0, 0.0).astype(full)

    def mask_of(p, q, rows=slice(None)):
        return jnp.maximum(group_ref[rows, :], inner(p, q))

    def cell(i):
        return pl.ds(pl.multiple_of(i * images, images), images)

    def half_cell(i, g):
        return pl.ds(pl.multiple_of(i * images + g * 16, 16), 16)

    def full_map(n):
        return jnp.where(image_group[n] == 1, 1.0, 0.0).astype(full)

    def prepare(t):
        for g in range(2):
            block = feats_ref[g * 16 : g * 16 + 16, t].astype(full)
            turned = jnp.swapaxes(block, 0, 1)
            for q in range(8):
                value = turned[q] * mask_of(t, q, slice(g * 16, g * 16 + 16))
                xpad[t + 1, q + 1, g * 16 : g * 16 + 16, :] = value.astype(low)
        line = lax.broadcasted_iota(jnp.int32, (8, 8, width), 0)
        column = lax.broadcasted_iota(jnp.int32, (8, 8, width), 1)
        core = jnp.where((line < 4) & (column < 4), 1.0, 0.0).astype(full)
        wide = []
        for k in range(4):
            n = t * 4 + k
            value = feats_ref[n].astype(full) * jnp.maximum(core, full_map(n))
            value = jnp.concatenate([value, jnp.zeros_like(value)], axis=1)
            wide.append(value.reshape(128, width).astype(low))
        project(0, t, jnp.concatenate(wide, axis=0))

    def project(layer, t, rows):
        at_v[1 - layer, :, pl.ds(pl.multiple_of(t * 512, 512), 512)] = lax.dot_general(
            basis_t[layer], rows, (((1,), (1,)), ((), ())), preferred_element_type=full
        ).astype(low)

    def conv_tap(tap, m, acc):
        a, b = tap // 3, lax.rem(tap, 3)
        kernel = weights(m)
        for p in range(8):
            rows = xpad[p + a, pl.ds(b, 8)].reshape(8 * images, width)
            acc[p * 256 : p * 256 + 256, :] += jnp.dot(rows, kernel, preferred_element_type=full)

    for t in range(3):
        gather(t)
    xpad[...] = jnp.zeros_like(xpad)
    basis_t[0] = basis_in_ref[0].T
    place = lax.broadcasted_iota(jnp.int32, (1, 128), 1)
    for n in range(images):
        group_ref[n : n + 1, :] = jnp.full((1, width), full_map(n), full)
        hot_ref[n : n + 1, :] = jnp.where(place == labels_ref[n], 1.0, 0.0).astype(full)
        weight_ref[n : n + 1, :] = jnp.full((1, 128), class_ref[labels_ref[n]].astype(full), full)

    def first(t, carry):
        gather(t)

        @pl.when(t < 11)
        def _():
            prepare(t - 3)

        @pl.when(t == 11)
        def _():
            conv_a[...] = jnp.zeros_like(conv_a)
            conv_b[...] = jnp.zeros_like(conv_b)
            basis_t[1] = basis_in_ref[1].T

        tap = t - 12

        @pl.when(tap >= 0)
        def _():
            core_copy(tap).wait_recv()
            conv_tap(tap, tap, conv_a)

        return carry

    lax.fori_loop(3, 21, first, 0)

    mine = dp * 2 + me_s

    def sum_one(buf, sems, n, a, b):
        other, core = near_id(a, b)
        return remote(
            buf.at[mine], buf.at[mine], sems[0].at[n, a * 2 + b], sems[1].at[n, mine],
            (other, core, me_z),
        )

    def sum_one_wait(buf, n, a, b):
        other, core = near_id(a, b)
        slot = other * 2 + core
        remote(
            buf.at[slot], buf.at[slot], one_ss.at[n, a * 2 + b], one_rs.at[n, slot],
            (other, core, me_z),
        ).wait_recv()

    def sum_two(buf, n, d):
        other = lax.rem(me_z + d, 4)
        return remote(
            buf.at[me_z], buf.at[me_z], two_ss.at[n, d], two_rs.at[n, me_z], (dp, me_s, other)
        )

    def sum_start(n, buf):
        for a, b in near:
            sum_one(buf, (one_ss, one_rs), n, a, b).start()

    def sum_middle(n, buf, buf_two):
        for a, b in near:
            sum_one_wait(buf, n, a, b)
        total = buf[0]
        for slot in range(1, 8):
            total = total + buf[slot]
        buf_two[me_z] = total
        for d in (1, 2, 3):
            sum_two(buf_two, n, d).start()

    def sum_arrived(n, buf_two):
        for d in (1, 2, 3):
            other = lax.rem(me_z + d, 4)
            remote(
                buf_two.at[other], buf_two.at[other], two_ss.at[n, d], two_rs.at[n, other],
                (dp, me_s, other),
            ).wait_recv()

    def sum_total(buf_two):
        return buf_two[0] + buf_two[1] + buf_two[2] + buf_two[3]

    def sum_end(n, buf_two):
        sum_arrived(n, buf_two)
        return sum_total(buf_two)

    def sum_sent(n, buf, buf_two):
        for a, b in near:
            sum_one(buf, (one_ss, one_rs), n, a, b).wait_send()
        for d in (1, 2, 3):
            sum_two(buf_two, n, d).wait_send()

    def column(value):
        return jnp.sum(value, axis=0, keepdims=True)

    zero = jnp.zeros((images, width), full)

    def channel_sums(acc):
        def line(p, carry):
            sums, squares = carry
            for q in range(8):
                value = acc[cell(p * 8 + q), :]
                masked = value * mask_of(p, q)
                sums = sums + masked
                squares = squares + masked * value
            return sums, squares

        sums, squares = lax.fori_loop(0, 8, line, (zero, zero))
        return column(sums), column(squares)

    sums, squares = channel_sums(conv_a)
    group = group_ref[...]
    pixels = 16.0 + 48.0 * group
    small_one[0, mine, 0:1, :] = sums
    small_one[0, mine, 1:2, :] = squares
    small_one[0, mine, 2:3, :] = column(pixels)
    small_one[0, mine, 3:4, :] = jnp.broadcast_to(column(weight_ref[...])[:, 0:1], (1, width))
    sum_start(0, small_one.at[0])

    def later(t, carry):
        gather(t)
        return carry

    lax.fori_loop(21, 23, later, 0)
    sum_middle(0, small_one.at[0], small_two.at[0])
    lax.fori_loop(23, 24, later, 0)
    total = sum_end(0, small_two.at[0])
    total_out[...] = total
    count = total[2:3]

    def moments(total):
        average = total[0:1] / count
        return average, lax.rsqrt(total[1:2] / count - average * average + EPS_NORM)

    average_a, inv_a = moments(total)

    def activation(value, layer, average, inv):
        normed = (value - average) * inv
        pre = params_ref[layer, 0:1, :] * normed + params_ref[layer, 1:2, :]
        return normed, pre, jax.nn.sigmoid(pre)

    def images_first(values):
        return jnp.swapaxes(jnp.stack(values), 0, 1)

    def act_line(p, carry):
        for g in range(2):
            acts = []
            for q in range(8):
                value = conv_a[half_cell(p * 8 + q, g), :]
                normed, pre, sigma = activation(value, 0, average_a, inv_a)
                act = pre * sigma * mask_of(p, q, slice(g * 16, g * 16 + 16))
                xpad[p + 1, q + 1, g * 16 : g * 16 + 16, :] = act.astype(low)
                acts.append(act)
            turned = images_first(acts)
            turned = jnp.concatenate([turned, jnp.zeros_like(turned)], axis=1).astype(low)
            gr_v[first_map + g * 16 : first_map + g * 16 + 16, pl.ds(pl.multiple_of(p * 16, 16), 16), :] = turned
        return carry

    lax.fori_loop(0, 8, act_line, 0)

    def second(tap, carry):
        core_copy(TAPS + tap).wait_recv()
        conv_tap(tap, TAPS + tap, conv_b)

        @pl.when(tap < 5)
        def _():
            gather(24 + tap)

        return carry

    lax.fori_loop(0, TAPS, second, 0)
    sums, squares = channel_sums(conv_b)
    small_one[1, mine, 0:1, :] = sums
    small_one[1, mine, 1:2, :] = squares
    small_one[1, mine, 2:4, :] = jnp.zeros((2, width), full)
    sum_start(1, small_one.at[1])

    def project_one(t, carry):
        project(1, t, gr_v[pl.ds(first_map + t * 4, 4), 0:128, :].reshape(512, width))
        return carry

    lax.fori_loop(0, 4, project_one, 0)
    sum_middle(1, small_one.at[1], small_two.at[1])
    lax.fori_loop(4, 8, project_one, 0)
    total = sum_end(1, small_two.at[1])
    average_b, inv_b = moments(total)

    def pool_line(p, carry):
        for q in range(8):
            normed, pre, sigma = activation(conv_b[cell(p * 8 + q), :], 1, average_b, inv_b)
            carry = carry + pre * sigma * mask_of(p, q)
        return carry

    pooled = lax.fori_loop(0, 8, pool_line, zero) / pixels
    pooled_low = pooled.astype(low)
    classes = head_ref.shape[0]
    head_low = head_ref[:, 0:width].astype(low)
    bias = jnp.broadcast_to(head_ref[:, width : width + 1], (classes, classes))
    across = lax.broadcasted_iota(jnp.int32, (classes, classes), 0)
    along = lax.broadcasted_iota(jnp.int32, (classes, classes), 1)
    logits = lax.dot_general(
        pooled_low, head_low, (((1,), (1,)), ((), ())), preferred_element_type=full
    ) + column(jnp.where(across == along, bias, 0.0))
    shifted = logits - jnp.max(logits, axis=1, keepdims=True)
    log_prob = shifted - jnp.log(jnp.sum(jnp.exp(shifted), axis=1, keepdims=True))
    hot = hot_ref[:, 0:classes]
    image_weight = weight_ref[:, 0:classes]
    picked = jnp.sum(hot * log_prob, axis=1, keepdims=True)
    loss = -column(weight_ref[:, 0:1] * picked)
    d_logits = image_weight * (jnp.exp(log_prob) - hot)
    d_pooled = (
        lax.dot_general(
            d_logits,
            head_low.astype(full),
            (((1,), (0,)), ((), ())),
            precision=highest,
            preferred_element_type=full,
        )
        / pixels
    )

    def d_line_top(p, carry):
        gammas, betas = carry
        for q in range(8):
            at = cell(p * 8 + q)
            normed, pre, sigma = activation(conv_b[at, :], 1, average_b, inv_b)
            d_pre = d_pooled * mask_of(p, q) * sigma * (1.0 + pre * (1.0 - sigma))
            gammas = gammas + d_pre * normed
            betas = betas + d_pre
        return gammas, betas

    gammas, betas = lax.fori_loop(0, 8, d_line_top, (zero, zero))

    def put_sums(n, gammas, betas):
        small_one[n, mine, 0:1, :] = column(gammas)
        small_one[n, mine, 1:2, :] = column(betas)
        small_one[n, mine, 2:4, :] = jnp.zeros((2, width), full)
        sum_start(n, small_one.at[n])

    def sent(m, carry):
        @pl.when(me_z < 3)
        def _():
            right_copy(m).wait_send()

        @pl.when(me_z > 0)
        def _():
            left_copy(m).wait_send()

        x_copy(m).wait_send()
        y_copy(m).wait_send()
        even_copy(m).wait_send()
        core_copy(m).wait_send()
        return carry

    lax.fori_loop(0, matrices, sent, 0)
    put_sums(2, gammas, betas)
    grad_head = lax.dot_general(
        d_logits,
        pooled_low.astype(full),
        (((0,), (0,)), ((), ())),
        precision=highest,
        preferred_element_type=full,
    )
    head_one[mine, :, :] = jnp.zeros((24, width), full)
    head_one[mine, 0:classes, :] = grad_head
    head_one[mine, 16:17, 0:classes] = column(d_logits)
    head_one[mine, 17:18, :] = jnp.broadcast_to(loss, (1, width))

    def clear(n, carry):
        gr_v[n, 0:16, :] = jnp.zeros((16, width), low)
        gr_v[n, 144:160, :] = jnp.zeros((16, width), low)
        return carry

    lax.fori_loop(0, 3 * images, clear, 0)

    sum_middle(2, small_one.at[2], small_two.at[2])
    total_b = sum_end(2, small_two.at[2])
    norm_out[1] = total_b
    sum_start(4, head_one)

    def grad_of(layer, normed, d_pre, inv, total):
        gamma = params_ref[layer, 0:1, :]
        return inv * (
            gamma * d_pre
            - gamma * total[1:2] / count
            - normed * (gamma * total[0:1] / count)
        )

    def grad_top(p, carry):
        for q in range(8):
            normed, pre, sigma = activation(conv_b[cell(p * 8 + q), :], 1, average_b, inv_b)
            mask = mask_of(p, q)
            d_pre = d_pooled * mask * sigma * (1.0 + pre * (1.0 - sigma))
            value = mask * grad_of(1, normed, d_pre, inv_b, total_b)
            xpad[p + 1, q + 1, :, :] = value.astype(low)
        return carry

    lax.fori_loop(0, 8, grad_top, 0)
    conv_b[...] = jnp.zeros_like(conv_b)

    def back(tap, carry):
        a, b = tap // 3, lax.rem(tap, 3)
        kernel = weights(TAPS + tap)
        for p in range(8):
            rows = xpad[p + 2 - a, pl.ds(2 - b, 8)].reshape(8 * images, width)
            conv_b[p * 256 : p * 256 + 256, :] += lax.dot_general(
                rows, kernel, (((1,), (1,)), ((), ())), preferred_element_type=full
            )
        return carry

    def d_line(p, carry):
        gammas, betas = carry
        for q in range(8):
            at = cell(p * 8 + q)
            normed, pre, sigma = activation(conv_a[at, :], 0, average_a, inv_a)
            d_pre = conv_b[at, :] * mask_of(p, q) * sigma * (1.0 + pre * (1.0 - sigma))
            conv_b[at, :] = d_pre
            gammas = gammas + d_pre * normed
            betas = betas + d_pre
        return gammas, betas

    def turn_grads(layer):
        def line(p, carry):
            rows = xpad[p + 1, 1:9].reshape(8 * images, width)
            value = jnp.dot(rows, basis_out_ref[layer], preferred_element_type=full)
            value = value.reshape(8, images, width)
            lines = pl.ds(pl.multiple_of(p * 16 + 16, 16), 16)
            gap = jnp.zeros((8, 1, width), full)
            rest = jnp.zeros((8, 8, width), full)
            for g in range(4):
                turned = jnp.swapaxes(value[:, g * 8 : g * 8 + 8], 0, 1)
                shifts = (
                    jnp.concatenate([turned[:, 1:], gap], axis=1),
                    turned,
                    jnp.concatenate([gap, turned[:, :7]], axis=1),
                )
                for b in range(3):
                    wide = jnp.concatenate([shifts[b], rest], axis=1).astype(low)
                    gr_v[b * images + g * 8 : b * images + g * 8 + 8, lines, :] = wide
            return carry

        return line

    lax.fori_loop(0, 8, turn_grads(1), 0)

    def bottom():
        total_a = sum_total(small_two.at[3])
        norm_out[0] = total_a

        def line(p, carry):
            for q in range(8):
                at = cell(p * 8 + q)
                normed = (conv_a[at, :] - average_a) * inv_a
                value = mask_of(p, q) * grad_of(0, normed, conv_b[at, :], inv_a, total_a)
                xpad[p + 1, q + 1, :, :] = value.astype(low)
            return carry

        lax.fori_loop(0, 8, line, 0)
        lax.fori_loop(0, 8, turn_grads(0), 0)

    def x1_recv(j):
        return w_full.at[j, 0, :, :, 0:256]

    def y1_recv(j):
        return w_full.at[j, 0, :, :, 256:512]

    def x2_recv(j):
        return w_full.at[j, 1, 0:2, :, 0:256]

    def y2_recv(j):
        return w_full.at[j, 1, 2:4, :, 0:256]

    def z_recv(j, d):
        return w_full.at[j, 1, d - 1, :, 256:512]

    def side_copy(j):
        ring, four = lax.rem(j, 2), lax.rem(j, 4)
        return remote(s_send.at[ring], s_recv.at[four], s_ss.at[ring], s_rs.at[four], to_s)

    def x1_copy(j):
        ring = lax.rem(j, 2)
        return remote(x1_send.at[ring], x1_recv(j), ss.at[1, ring], rs.at[0, j], to_x)

    def y1_copy(j):
        ring = lax.rem(j, 2)
        return remote(y1_send.at[ring, 1 - me_y], y1_recv(j), ss.at[2, ring], rs.at[1, j], to_y)

    def x2_copy(j):
        ring = lax.rem(j, 2)
        return remote(x2_send.at[ring], x2_recv(j), ss.at[3, ring], rs.at[2, j], to_x)

    def y2_copy(j):
        ring = lax.rem(j, 2)
        return remote(y2_send.at[ring], y2_recv(j), ss.at[4, ring], rs.at[3, j], to_y)

    def z_copy(j, d):
        ring, other = lax.rem(j, 2), lax.rem(me_z + d, 4)
        return remote(
            z_send.at[ring, other],
            z_recv(j, d),
            z_ss.at[ring, d - 1],
            z_rs.at[j, d - 1],
            (dp, me_s, other),
        )

    def place(j):
        return 1 - j // 9, lax.rem(j, 9)

    def local_copy(j):
        layer, i = place(j)
        ring = lax.rem(j, 2)
        return pltpu.make_async_copy(
            div_v.at[ring], out.at[me_s, layer, me_x, me_z, i, me_y], local_sem.at[ring]
        )

    def gz_copy(j, d):
        layer, i = place(j)
        ring, other = lax.rem(j, 2), lax.rem(me_z + d, 4)
        return remote(
            div_v.at[ring],
            out.at[me_s, layer, me_x, me_z, i, me_y],
            gz_ss.at[ring, d - 1],
            gz_rs.at[j, d - 1],
            (dp, me_s, other),
        )

    lower, upper = pl.ds(0, 2), pl.ds(2, 2)

    def spread(j, which, kind, target):
        part = out.at[which]
        return remote(part, part, ss.at[kind, lax.rem(j, 2)], rs.at[kind - 1, j], target)

    def g1y_copy(j):
        layer, i = place(j)
        return spread(j, (me_s, layer, me_x, lower, i, me_y), 5, to_y)

    def g1x_copy(j):
        layer, i = place(j)
        return spread(j, (me_s, layer, me_x, upper, i, me_y), 6, to_x)

    def g2x_copy(j):
        layer, i = place(j)
        return spread(j, (me_s, layer, me_x, lower, i), 7, to_x)

    def g2y_copy(j):
        layer, i = place(j)
        return spread(j, (me_s, layer, pl.ds(0, 2), upper, i, me_y), 8, to_y)

    def gs_copy(j):
        layer, i = place(j)
        return spread(j, (me_s, layer, pl.ds(0, 2), pl.ds(0, 4), i), 9, to_s)

    def products(j, half, store):
        li, i = j // 9, lax.rem(j, 9)
        cols = pl.ds(pl.multiple_of(half * 256, 256), 256)
        for u in range(8):
            x_to = 1 - me_x if u < 4 else me_x
            row = x_to * 2304 + (u % 4) * 576 + 64 * i
            tap = row // 512
            rows = pl.ds(pl.multiple_of(lax.rem(row, 512), 64), 64)
            near = pl.ds(pl.multiple_of((2 - tap // 3) * 16, 16), 128)
            shift = lax.rem(tap, 3) * images
            square = total = None
            for n in range(images):
                p = jnp.dot(
                    at_v[li, rows, n * 128 : (n + 1) * 128],
                    gr_v[shift + n, near, cols],
                    preferred_element_type=full,
                )
                square = p * p if square is None else square + p * p
                total = p if total is None else total + p
            store(u, x_to, u % 4, total, square)

    def at_step(x):
        j = jnp.where(x < 10, x, jnp.where(x < 14, x - 4, x - 5))
        due = ((x >= 0) & (x < 6)) | ((x >= 10) & (x < 13)) | ((x >= 14) & (x < 23))
        return j, due

    def step(k, carry):
        ja, due = at_step(k)

        @pl.when(due & (ja >= 2))
        def _():
            side_copy(ja - 2).wait_send()

        @pl.when(due)
        def _():
            ring = lax.rem(ja, 2)

            def store(u, x_to, z_to, total, square):
                s_send[ring, u, 0] = total.astype(low)
                s_send[ring, u, 1] = square.astype(low)

            products(ja, 1 - me_s, store)
            side_copy(ja).start()

        jb, due = at_step(k - 1)

        @pl.when(due & (jb >= 2))
        def _():
            x1_copy(jb - 2).wait_send()
            y1_copy(jb - 2).wait_send()

        @pl.when(due)
        def _():
            ring, four = lax.rem(jb, 2), lax.rem(jb, 4)
            side_copy(jb).wait_recv()

            def store(u, x_to, z_to, total, square):
                got = s_recv[four, u].astype(full)
                both = (total + got[0], square + got[1])
                for c in range(2):
                    if z_to < 2 and u < 4:
                        x1_send[ring, z_to * 2 + c] = both[c].astype(low)
                    elif z_to < 2:
                        x1_keep[ring, z_to * 2 + c] = both[c]
                    else:
                        at = x_to * 2 + z_to - 2
                        for y_to in range(2):
                            value = both[c][y_to * 32 : y_to * 32 + 32]
                            y1_send[ring, y_to, at, c * 32 : c * 32 + 32, :] = value.astype(low)
                            y1_keep[ring, y_to, at, c * 32 : c * 32 + 32, :] = value

            products(jb, me_s, store)
            x1_copy(jb).start()
            y1_copy(jb).start()

        j7, due = at_step(k - 12)

        @pl.when(due)
        def _():
            @pl.when(j7 >= 2)
            def _():
                gs_copy(j7 - 2).wait_send()

            g2x_copy(j7).wait_recv()
            g2y_copy(j7).wait_recv()
            gs_copy(j7).start()

        j6, due = at_step(k - 10)

        @pl.when(due)
        def _():
            @pl.when(j6 >= 2)
            def _():
                g2y_copy(j6 - 2).wait_send()
                g2x_copy(j6 - 2).wait_send()

            g1y_copy(j6).wait_recv()
            g2x_copy(j6).start()
            g1x_copy(j6).wait_recv()
            g2y_copy(j6).start()

        j5, due = at_step(k - 8)

        @pl.when(due)
        def _():
            @pl.when(j5 >= 2)
            def _():
                g1y_copy(j5 - 2).wait_send()
                g1x_copy(j5 - 2).wait_send()

            local_copy(j5).wait()
            for d in (1, 2, 3):
                gz_copy(j5, d).wait_recv()
            g1y_copy(j5).start()
            g1x_copy(j5).start()

        j4, due = at_step(k - 6)

        @pl.when(due & (j4 == 0))
        def _():
            sc_local.wait()
            sc_remote.wait_recv()

        @pl.when(due)
        def _():
            ring, li, i = lax.rem(j4, 2), j4 // 9, lax.rem(j4, 9)

            @pl.when(j4 >= 2)
            def _():
                for d in (1, 2, 3):
                    gz_copy(j4 - 2, d).wait_send()

            for d in (1, 2, 3):
                z_copy(j4, d).wait_recv()
            both = z_keep[ring, me_z]
            for d in (1, 2, 3):
                both = both + z_recv(j4, d)[...].astype(full)
            scale = DECAY * sc_v[li, i] + (1.0 - DECAY) * both[32:64] / images_all
            ns_v[li, i] = scale
            div_v[ring] = (both[0:32] / total_out[3:4, 0:256] / (scale + DAMPING)).astype(low)
            local_copy(j4).start()
            for d in (1, 2, 3):
                gz_copy(j4, d).start()

        for li in range(2):
            @pl.when(due & (j4 == 9 * li + 8) & (me_y == 1 - li))
            def _():
                pltpu.make_async_copy(ns_v.at[li], ns_out.at[:, me_y], misc_sem.at[3]).start()

            @pl.when(due & (j4 == 9 * li + 8) & (me_y == li))
            def _():
                remote(
                    ns_v.at[li], ns_out.at[:, me_y], misc_sem.at[4], misc_sem.at[5], to_y
                ).start()

        j3, due = at_step(k - 4)

        @pl.when(due)
        def _():
            ring = lax.rem(j3, 2)

            @pl.when(j3 >= 2)
            def _():
                for d in (1, 2, 3):
                    z_copy(j3 - 2, d).wait_send()

            y2_copy(j3).wait_recv()
            x2_copy(j3).wait_recv()
            for z_to in range(4):
                got = y2_recv(j3)[z_to] if z_to < 2 else x2_recv(j3)[z_to - 2]
                both = two_keep[ring, z_to] + got.astype(full)
                z_keep[ring, z_to] = both
                z_send[ring, z_to] = both.astype(low)
            for d in (1, 2, 3):
                z_copy(j3, d).start()

        j2, due = at_step(k - 2)

        @pl.when(due)
        def _():
            ring = lax.rem(j2, 2)

            @pl.when(j2 >= 2)
            def _():
                x2_copy(j2 - 2).wait_send()
                y2_copy(j2 - 2).wait_send()

            x1_copy(j2).wait_recv()
            here = pl.ds(pl.multiple_of(me_y * 32, 32), 32)
            there = pl.ds(pl.multiple_of((1 - me_y) * 32, 32), 32)
            got = x1_recv(j2)
            for z_to in range(2):
                for c in range(2):
                    at, lines = z_to * 2 + c, slice(c * 32, c * 32 + 32)
                    two_keep[ring, z_to, lines, :] = x1_keep[ring, at, here, :] + got[
                        at, here, :
                    ].astype(full)
                    y2_send[ring, z_to, lines, :] = (
                        x1_keep[ring, at, there, :] + got[at, there, :].astype(full)
                    ).astype(low)
            y2_copy(j2).start()
            y1_copy(j2).wait_recv()
            got = y1_recv(j2)
            for z_to in range(2):
                mine_at, other_at = me_x * 2 + z_to, (1 - me_x) * 2 + z_to
                two_keep[ring, 2 + z_to] = y1_keep[ring, me_y, mine_at] + got[mine_at].astype(full)
                x2_send[ring, z_to] = (
                    y1_keep[ring, me_y, other_at] + got[other_at].astype(full)
                ).astype(low)
            x2_copy(j2).start()

        @pl.when((k >= 6) & (k < 9))
        def _():
            lax.fori_loop(0, 3, lambda t, carry: back((k - 6) * 3 + t, carry), 0)

        @pl.when(k == 8)
        def _():
            sum_middle(4, head_one, head_two)

        @pl.when(k == 9)
        def _():
            gammas, betas = lax.fori_loop(0, 8, d_line, (zero, zero))
            put_sums(3, gammas, betas)

        @pl.when(k == 10)
        def _():
            sum_middle(3, small_one.at[3], small_two.at[3])

        @pl.when(k == 25)
        def _():
            head_out[...] = sum_end(4, head_two)

        @pl.when(k == 13)
        def _():
            sum_arrived(3, small_two.at[3])
            bottom()

        return carry

    lax.fori_loop(0, steps + 5 + 12, step, 0)

    def finish(j, carry):
        gs_copy(j).wait_recv()
        return carry

    lax.fori_loop(0, steps, finish, 0)
    sc_remote.wait_send()
    li = 1 - me_y
    pltpu.make_async_copy(ns_v.at[li], ns_out.at[:, me_y], misc_sem.at[3]).wait()
    ns_remote = remote(ns_v.at[0], ns_out.at[:, 0], misc_sem.at[4], misc_sem.at[5], to_y)
    ns_remote.wait_send()
    ns_remote.wait_recv()
    for j in (steps - 2, steps - 1):
        for copy in (side_copy, x1_copy, y1_copy, x2_copy, y2_copy):
            copy(j).wait_send()
        for copy in (g1y_copy, g1x_copy, g2y_copy, g2x_copy, gs_copy):
            copy(j).wait_send()
        for d in (1, 2, 3):
            z_copy(j, d).wait_send()
            gz_copy(j, d).wait_send()
    for n in range(4):
        sum_sent(n, small_one.at[n], small_two.at[n])
    sum_sent(4, head_one, head_two)


def whole_step(
    feats, size_group, labels, class_wt, owners, basis_in, basis_out, master, norm_params, head, scales
):
    count_img, side_len, _, width = feats.shape
    images_all = count_img * lax.axis_size("dp") * lax.axis_size("side") * lax.axis_size("blk")
    low, full, dma = jnp.bfloat16, jnp.float32, pltpu.SemaphoreType.DMA
    vmem, any_spec = pl.BlockSpec(memory_space=pltpu.VMEM), pl.BlockSpec(memory_space=pl.ANY)
    smem = pl.BlockSpec(memory_space=pltpu.SMEM)
    rows = count_img * side_len * side_len
    divided, new_scales, total, norm_sums, head_sums = pl.pallas_call(
        functools.partial(step_kernel, images_all),
        out_shape=[
            jax.ShapeDtypeStruct((2, 2, 2, 4, 9, 2, 32, 256), low),
            jax.ShapeDtypeStruct((9, 2, 32, 256), full),
            jax.ShapeDtypeStruct((4, width), full),
            jax.ShapeDtypeStruct((2, 4, width), full),
            jax.ShapeDtypeStruct((24, width), full),
        ],
        in_specs=[vmem, smem, smem, smem, smem, any_spec, vmem, vmem, vmem, vmem, any_spec],
        out_specs=[any_spec, any_spec, vmem, vmem, vmem],
        scratch_shapes=[
            pltpu.VMEM((18, 2, 4, 64, 512), low),
            pltpu.VMEM((10, 10, 32, 512), low),
            pltpu.VMEM((rows, 512), full),
            pltpu.VMEM((rows, 512), full),
            pltpu.VMEM((2, 512, 4096), low),
            pltpu.VMEM((96, 160, 512), low),
            pltpu.VMEM((32, 512), full),
            pltpu.VMEM((32, 128), full),
            pltpu.VMEM((32, 128), full),
            pltpu.VMEM((10, 64, 512), full),
            pltpu.VMEM((2, 512, 512), low),
            pltpu.VMEM((4, 8, 4, 512), full),
            pltpu.VMEM((4, 4, 4, 512), full),
            pltpu.VMEM((8, 24, 512), full),
            pltpu.VMEM((4, 24, 512), full),
            pltpu.VMEM((2, 9, 32, 256), full),
            pltpu.VMEM((2, 9, 32, 256), full),
            pltpu.VMEM((2, 32, 256), low),
            pltpu.VMEM((2, 8, 2, 64, 256), low),
            pltpu.VMEM((4, 8, 2, 64, 256), low),
            pltpu.VMEM((2, 4, 64, 256), low),
            pltpu.VMEM((2, 4, 64, 256), full),
            pltpu.VMEM((2, 2, 4, 64, 256), low),
            pltpu.VMEM((2, 2, 4, 64, 256), full),
            pltpu.VMEM((2, 2, 64, 256), low),
            pltpu.VMEM((2, 2, 64, 256), low),
            pltpu.VMEM((2, 4, 64, 256), full),
            pltpu.VMEM((2, 4, 64, 256), low),
            pltpu.VMEM((2, 4, 64, 256), full),
            dma((1,)),
            dma((6, 18)),
            dma((6, 18)),
            dma((5, 8)),
            dma((5, 8)),
            dma((5, 4)),
            dma((5, 4)),
            dma((6,)),
            dma((2,)),
            dma((10, 2)),
            dma((2,)),
            dma((4,)),
            dma((9, 18)),
            dma((2, 3)),
            dma((18, 3)),
            dma((2, 3)),
            dma((18, 3)),
        ],
        name="whole_step",
        compiler_params=pltpu.CompilerParams(
            collective_id=0, has_side_effects=True, vmem_limit_bytes=63 * 2**20
        ),
    )(
        feats,
        size_group,
        labels,
        class_wt,
        owners,
        master,
        norm_params,
        head,
        basis_in,
        basis_out,
        scales.reshape(9, 2, 32, 256),
    )
    return (
        divided.reshape(2, 18, 512, 256),
        new_scales.reshape(576, 256),
        total,
        norm_sums,
        head_sums,
    )


def update_kernel(
    owners_ref,
    divided,
    basis_in,
    basis_out,
    w_hbm,
    m_hbm,
    v_hbm,
    total_ref,
    norm_sums,
    head_sums,
    norm_w,
    norm_m,
    norm_v,
    head_w,
    head_m,
    head_v,
    w_out,
    m_out,
    v_out,
    norm_w_out,
    norm_m_out,
    norm_v_out,
    head_w_out,
    head_m_out,
    head_v_out,
    loss_out,
    weight_out,
    matrix,
    p_v,
    rows_v,
    cols_v,
    w_v,
    m_v,
    v_v,
    in_sem,
    out_sem,
):
    low, full = jnp.bfloat16, jnp.float32
    slots, half, width = w_v.shape
    blk, side = lax.axis_index("blk"), lax.axis_index("side")

    def state_in(q):
        return [
            pltpu.make_async_copy(src.at[q], dst.at[q], in_sem.at[n, q])
            for n, (src, dst) in enumerate(((w_hbm, w_v), (m_hbm, m_v), (v_hbm, v_v)))
        ]

    def state_out(q):
        return [
            pltpu.make_async_copy(src.at[q], dst.at[q], out_sem.at[n, q])
            for n, (src, dst) in enumerate(((w_v, w_out), (m_v, m_out), (v_v, v_out)))
        ]

    rows_in = pltpu.make_async_copy(
        basis_in.at[:, pl.ds(pl.multiple_of(side * half, half), half)], rows_v, in_sem.at[4, 0]
    )
    cols_in = pltpu.make_async_copy(basis_out, cols_v, in_sem.at[4, 1])
    rows_in.start()
    cols_in.start()

    for q in range(slots):
        matrix[q] = 0
    count = jnp.zeros((), jnp.int32)
    for m in range(owners_ref.shape[0]):
        mine = owners_ref[m] == blk

        @pl.when(mine)
        def _():
            matrix[count] = m

        count = count + jnp.where(mine, 1, 0)

    def part_in(q):
        return pltpu.make_async_copy(divided.at[:, matrix[q]], p_v.at[q], in_sem.at[3, q])

    for q in range(slots):
        part_in(q).start()
        for copy in state_in(q):
            copy.start()
    weight = total_ref[3:4, 0:1]
    weight_out[0, 0] = total_ref[3, 0]
    loss_out[0, 0] = head_sums[17, 0]
    for layer in range(2):
        norm_w_out[layer], norm_m_out[layer], norm_v_out[layer] = adamw(
            norm_w[layer],
            norm_m[layer],
            norm_v[layer],
            norm_sums[layer, 0:2, :] / weight,
            RATE_NORM,
        )
    classes = head_w.shape[0]
    here = lax.broadcasted_iota(jnp.int32, (classes, classes), 0)
    there = lax.broadcasted_iota(jnp.int32, (classes, classes), 1)
    line = jnp.broadcast_to(head_sums[16:17, 0:classes], (classes, classes))
    bias = jnp.sum(jnp.where(here == there, line, 0.0), axis=1, keepdims=True)
    for at, gradient in (
        (slice(0, width), head_sums[0:classes, :]),
        (slice(width, width + 1), bias),
    ):
        head_w_out[:, at], head_m_out[:, at], head_v_out[:, at] = adamw(
            head_w[:, at], head_m[:, at], head_v[:, at], gradient / weight, RATE_HEAD
        )
    rows_in.wait()
    cols_in.wait()

    def gradient(q):
        layer = matrix[q] // TAPS
        held = jnp.where(q < count, 1.0, 0.0).astype(full)
        both = [
            jnp.dot(rows_v[layer], p_v[q, s], preferred_element_type=full).astype(low)
            for s in range(2)
        ]
        return held * lax.dot_general(
            jnp.concatenate(both, axis=1),
            cols_v[layer],
            (((1,), (1,)), ((), ())),
            preferred_element_type=full,
        )

    def slot(q, carry):
        part_in(q).wait()
        change = gradient(q)
        for copy in state_in(q):
            copy.wait()
        w_v[q], m_v[q], v_v[q] = adamw(w_v[q], m_v[q], v_v[q], change, RATE_CONV)
        for copy in state_out(q):
            copy.start()
        return carry

    lax.fori_loop(0, slots, slot, 0)
    for q in range(slots):
        for copy in state_out(q):
            copy.wait()


def update(
    owners, divided, basis_in, basis_out, states, total, norm_sums, head_sums, norm_states, head_states
):
    full, dma = jnp.float32, pltpu.SemaphoreType.DMA
    slots, half, width = states[0].shape
    vmem, any_spec = pl.BlockSpec(memory_space=pltpu.VMEM), pl.BlockSpec(memory_space=pl.ANY)
    smem = pl.BlockSpec(memory_space=pltpu.SMEM)
    like = [jax.ShapeDtypeStruct(x.shape, full) for x in (*states, *norm_states, *head_states)]
    one = jax.ShapeDtypeStruct((1, 1), full)
    return pl.pallas_call(
        update_kernel,
        out_shape=like + [one, one],
        in_specs=[smem] + [any_spec] * 6 + [vmem] * 9,
        out_specs=[any_spec] * 3 + [vmem] * 6 + [smem] * 2,
        scratch_shapes=[
            pltpu.SMEM((slots,), jnp.int32),
            pltpu.VMEM((slots, 2, width, half), jnp.bfloat16),
            pltpu.VMEM((2, half, width), jnp.bfloat16),
            pltpu.VMEM((2, width, width), jnp.bfloat16),
            pltpu.VMEM(states[0].shape, full),
            pltpu.VMEM(states[0].shape, full),
            pltpu.VMEM(states[0].shape, full),
            dma((5, slots)),
            dma((3, slots)),
        ],
        name="update",
        compiler_params=pltpu.CompilerParams(vmem_limit_bytes=63 * 2**20),
    )(
        owners,
        divided,
        basis_in,
        basis_out,
        *states,
        total,
        norm_sums,
        head_sums,
        *norm_states,
        *head_states,
    )


def shards_general(
    feats,
    size_group,
    labels,
    class_wt,
    owners,
    basis_in,
    basis_out,
    scales,
    master,
    moment1,
    moment2,
    norm_params,
    norm_m,
    norm_v,
    head,
    head_m,
    head_v,
):
    count_img = feats.shape[0]
    side_len = feats.shape[1]
    width = feats.shape[3]
    half = width // 2
    n_dp = lax.axis_size("dp")
    n_side = lax.axis_size("side")
    n_blk = lax.axis_size("blk")
    slots_dev = master.shape[0]
    matrices = owners.shape[0]
    block_rows = scales.shape[0]
    images_all = count_img * n_dp * n_side * n_blk
    index = jnp.arange(matrices)
    earlier = (owners[:, None] == owners[None, :]) & (index[None, :] < index[:, None])
    slot = owners * slots_dev + jnp.sum(earlier.astype(jnp.int32), axis=1)
    pieces = lax.all_gather(master.astype(jnp.bfloat16), ("side", "blk"), axis=0, tiled=True)
    pieces = pieces.reshape(n_side, n_blk * slots_dev, master.shape[1], width)
    pick = (slot[:, None] == jnp.arange(n_blk * slots_dev)[None, :]).astype(jnp.bfloat16)
    kernels = jnp.einsum("ms,hsrc->mhrc", pick, pieces, preferred_element_type=jnp.float32)
    kernels = kernels.astype(jnp.bfloat16).reshape(L, TAPS, width, width)
    line = jnp.arange(side_len)
    inner = (line[:, None] < side_len // 2) & (line[None, :] < side_len // 2)
    cell_mask = jnp.where((size_group == 1)[:, None, None], True, inner[None]).astype(jnp.float32)
    mask_four = cell_mask[..., None]
    pixels = jnp.sum(cell_mask, axis=(1, 2))
    class_hot = labels[:, None] == jnp.arange(class_wt.shape[0])[None, :]
    weight = jnp.sum(jnp.where(class_hot, class_wt[None, :], 0), axis=1).astype(jnp.float32)
    hot_float = class_hot.astype(jnp.float32)
    count_all, weight_all = lax.psum((jnp.sum(pixels), jnp.sum(weight)), ("dp", "side", "blk"))
    current = (feats.astype(jnp.float32) * mask_four).astype(jnp.bfloat16)
    kept = []
    act_out = None
    for layer in range(L):
        conv_out = conv_forward(current, kernels[layer])
        masked = conv_out * mask_four
        col_sum, sq_sum = lax.psum(
            (jnp.sum(masked, axis=(0, 1, 2)), jnp.sum(masked * conv_out, axis=(0, 1, 2))),
            ("dp", "side", "blk"),
        )
        average = col_sum / count_all
        inv_std = lax.rsqrt(sq_sum / count_all - average * average + EPS_NORM)
        normed = (conv_out - average) * inv_std
        pre_act = norm_params[layer, 0] * normed + norm_params[layer, 1]
        act_out = jax.nn.silu(pre_act) * mask_four
        kept.append((current, normed, pre_act, inv_std))
        current = act_out.astype(jnp.bfloat16)
    pooled = jnp.sum(act_out, axis=(1, 2)) / pixels[:, None]
    pooled_low = pooled.astype(jnp.bfloat16)
    head_low = head[:width].astype(jnp.bfloat16)
    logits = jnp.dot(pooled_low, head_low, preferred_element_type=jnp.float32) + head[width]
    log_prob = jax.nn.log_softmax(logits, axis=-1)
    loss_local = -jnp.sum(weight * jnp.sum(hot_float * log_prob, axis=1))
    d_logits = weight[:, None] * (jnp.exp(log_prob) - hot_float)
    grad_weights = jnp.dot(
        pooled_low.astype(jnp.float32).T, d_logits, precision=lax.Precision.HIGHEST
    )
    grad_head = jnp.concatenate([grad_weights, jnp.sum(d_logits, axis=0)[None]], axis=0)
    loss_all, head_all = lax.psum((loss_local, grad_head), ("dp", "side", "blk"))
    d_pooled = jnp.dot(d_logits, head_low.astype(jnp.float32).T, precision=lax.Precision.HIGHEST)
    d_act = d_pooled[:, None, None, :] / pixels[:, None, None, None] * mask_four
    terms = [None] * L
    grad_norm = [None] * L
    for layer in reversed(range(L)):
        inputs, normed, pre_act, inv_std = kept[layer]
        sigma = jax.nn.sigmoid(pre_act)
        d_pre = d_act * mask_four * sigma * (1.0 + pre_act * (1.0 - sigma))
        gamma_sum, beta_sum = lax.psum(
            (jnp.sum(d_pre * normed, axis=(0, 1, 2)), jnp.sum(d_pre, axis=(0, 1, 2))),
            ("dp", "side", "blk"),
        )
        grad_norm[layer] = jnp.stack([gamma_sum, beta_sum])
        gamma = norm_params[layer, 0]
        d_conv = (
            mask_four
            * inv_std
            * (
                gamma * d_pre
                - gamma * beta_sum / count_all
                - normed * gamma * gamma_sum / count_all
            )
        )
        grad_low = d_conv.astype(jnp.bfloat16)
        if layer > 0:
            d_act = conv_backward(grad_low, kernels[layer])
        act_proj = jnp.einsum(
            "npqc,ci->npqi", inputs, basis_in[layer], preferred_element_type=jnp.float32
        ).astype(jnp.bfloat16)
        grad_proj = jnp.einsum(
            "npqo,oj->npqj", grad_low, basis_out[layer], preferred_element_type=jnp.float32
        ).astype(jnp.bfloat16)
        terms[layer] = tap_sums(act_proj, grad_proj)
    whole = jnp.stack(terms).reshape(n_dp, n_blk, block_rows, 2, 2, half)
    whole = whole.transpose(0, 4, 1, 2, 3, 5).reshape(n_dp * 2 * n_blk * block_rows, 2 * half)
    reduced = lax.psum_scatter(whole, ("dp", "side", "blk"), scatter_dimension=0, tiled=True)
    proj_sum = reduced[:, :half]
    proj_square = reduced[:, half:]
    new_scales = DECAY * scales + (1.0 - DECAY) * proj_square / images_all
    divided = (proj_sum / weight_all / (new_scales + DAMPING)).astype(jnp.bfloat16)
    spread = lax.all_gather(divided, ("dp", "side", "blk"), axis=0, tiled=True)
    spread = spread.reshape(n_dp, 2, n_blk, block_rows, half).transpose(0, 2, 3, 1, 4)
    precond_all = spread.reshape(matrices, width, width)
    slot_ids = lax.axis_index("blk") * slots_dev + jnp.arange(slots_dev)
    owned = (slot[None, :] == slot_ids[:, None]).astype(jnp.bfloat16)
    chosen = jnp.einsum(
        "qm,mij->qij", owned, precond_all, preferred_element_type=jnp.float32
    ).astype(jnp.bfloat16)
    layer_hot = (index[:, None] // TAPS == jnp.arange(L)[None, :]).astype(jnp.bfloat16)
    slot_layer = jnp.dot(owned, layer_hot, preferred_element_type=jnp.float32).astype(jnp.bfloat16)
    half_rows = lax.dynamic_slice_in_dim(
        basis_in, lax.axis_index("side") * master.shape[1], master.shape[1], 1
    )
    rows_slot = jnp.einsum(
        "ql,lci->qci", slot_layer, half_rows, preferred_element_type=jnp.float32
    ).astype(jnp.bfloat16)
    cols_slot = jnp.einsum(
        "ql,loj->qoj", slot_layer, basis_out, preferred_element_type=jnp.float32
    ).astype(jnp.bfloat16)
    turned = jnp.einsum(
        "qci,qij->qcj", rows_slot, chosen, preferred_element_type=jnp.float32
    ).astype(jnp.bfloat16)
    slot_grad = jnp.einsum("qcj,qoj->qco", turned, cols_slot, preferred_element_type=jnp.float32)
    new_master, new_moment1, new_moment2 = adamw(master, moment1, moment2, slot_grad, RATE_CONV)
    new_norm, new_norm_m, new_norm_v = adamw(
        norm_params, norm_m, norm_v, jnp.stack(grad_norm) / weight_all, RATE_NORM
    )
    new_head, new_head_m, new_head_v = adamw(head, head_m, head_v, head_all / weight_all, RATE_HEAD)
    return (
        loss_all,
        weight_all,
        new_scales,
        new_master,
        new_moment1,
        new_moment2,
        new_norm,
        new_norm_m,
        new_norm_v,
        new_head,
        new_head_m,
        new_head_v,
    )


def shards_fast(
    feats,
    size_group,
    labels,
    class_wt,
    owners,
    basis_in,
    basis_out,
    scales,
    master,
    moment1,
    moment2,
    norm_params,
    norm_m,
    norm_v,
    head,
    head_m,
    head_v,
):
    divided, new_scales, total, norm_sums, head_sums = whole_step(
        feats,
        size_group,
        labels,
        class_wt,
        owners,
        basis_in,
        basis_out,
        master,
        norm_params,
        head.T,
        scales,
    )
    results = update(
        owners,
        divided,
        basis_in,
        basis_out,
        (master, moment1, moment2),
        total,
        norm_sums,
        head_sums,
        (norm_params, norm_m, norm_v),
        (head.T, head_m.T, head_v.T),
    )
    loss_all, weight_all = results[9][0, 0], results[10][0, 0]
    return (loss_all, weight_all, new_scales, *results[:6], *(x.T for x in results[6:9]))


def shards(*args):
    feats, class_wt, scales, master = args[0], args[3], args[7], args[8]
    mesh_shape = tuple(lax.axis_size(name) for name in ("dp", "side", "blk"))
    fits = (
        mesh_shape == (4, 2, 4)
        and scales.shape == (576, 256)
        and feats.shape == (32, 8, 8, 512)
        and master.shape == (10, 256, 512)
        and class_wt.shape[0] <= 16
    )
    return shards_fast(*args) if fits else shards_general(*args)


def solution(mesh):
    return jax.shard_map(
        shards,
        mesh=mesh,
        in_specs=(
            P(("dp", "side", "blk"), None, None, None),
            P(("dp", "side", "blk")),
            P(("dp", "side", "blk")),
            P(),
            P(),
            P(),
            P(),
            P(("dp", "blk"), "side"),
            P("blk", "side", None),
            P("blk", "side", None),
            P("blk", "side", None),
            P(),
            P(),
            P(),
            P(),
            P(),
            P(),
        ),
        out_specs=(
            P(),
            P(),
            P(("dp", "blk"), "side"),
            P("blk", "side", None),
            P("blk", "side", None),
            P("blk", "side", None),
            P(),
            P(),
            P(),
            P(),
            P(),
            P(),
        ),
        check_vma=False,
    )
```

```python
import functools

import jax
import jax.numpy as jnp
from jax import lax
from jax.experimental import pallas as pl
from jax.experimental.pallas import tpu as pltpu
from jax.sharding import PartitionSpec as P

L = 2
TAPS = 9
STEP = 10


EPS_NORM = 1e-05
DAMPING = 0.001
DECAY = 0.95
BETA_ONE = 0.9
BETA_TWO = 0.999
ADAM_EPS = 1e-08
WEIGHT_DECAY = 0.01
RATE_CONV = 0.01
RATE_NORM = 0.5
RATE_HEAD = 0.02


def adamw(weight_now, first_now, second_now, gradient, rate):
    first_new = BETA_ONE * first_now + (1.0 - BETA_ONE) * gradient
    second_new = BETA_TWO * second_now + (1.0 - BETA_TWO) * gradient * gradient
    first_hat = first_new * (1.0 / (1.0 - BETA_ONE**STEP))
    second_hat = second_new * (1.0 / (1.0 - BETA_TWO**STEP))
    weight_new = weight_now - rate * (
        first_hat / (jnp.sqrt(second_hat) + ADAM_EPS) + WEIGHT_DECAY * weight_now
    )
    return (weight_new, first_new, second_new)


def pad_cells(values):
    return jnp.pad(values, ((0, 0), (1, 1), (1, 1), (0, 0)))


def conv_forward(inputs, kernel):
    side_len = inputs.shape[1]
    padded = pad_cells(inputs)
    total = None
    for tap in range(TAPS):
        shifted = padded[:, tap // 3 : tap // 3 + side_len, tap % 3 : tap % 3 + side_len]
        term = jnp.einsum("npqc,co->npqo", shifted, kernel[tap], preferred_element_type=jnp.float32)
        total = term if total is None else total + term
    return total


def conv_backward(grads, kernel):
    side_len = grads.shape[1]
    total = None
    for tap in range(TAPS):
        offset_row = tap // 3
        offset_col = tap % 3
        term = jnp.einsum("npqo,co->npqc", grads, kernel[tap], preferred_element_type=jnp.float32)
        term = jnp.pad(
            term, ((0, 0), (offset_row, 2 - offset_row), (offset_col, 2 - offset_col), (0, 0))
        )
        total = term if total is None else total + term
    return total[:, 1 : side_len + 1, 1 : side_len + 1]


def tap_sums(act_proj, grad_proj):
    side_len = act_proj.shape[1]
    padded = pad_cells(act_proj)
    firsts, seconds = ([], [])
    for tap in range(TAPS):
        shifted = padded[:, tap // 3 : tap // 3 + side_len, tap % 3 : tap % 3 + side_len]
        each = jnp.einsum("npqi,npqj->nij", shifted, grad_proj, preferred_element_type=jnp.float32)
        firsts.append(jnp.sum(each, axis=0))
        seconds.append(jnp.sum(each * each, axis=0))
    return jnp.concatenate([jnp.stack(firsts), jnp.stack(seconds)], axis=-1)


MESH = pl.DeviceIdType.MESH


def step_kernel(
    images_all,
    feats_hbm,
    image_group,
    labels_ref,
    class_ref,
    owners_ref,
    master_hbm,
    params_ref,
    head_ref,
    basis_in_hbm,
    basis_out_hbm,
    scales_hbm,
    out,
    ns_out,
    total_out,
    norm_out,
    head_out,
    w_full,
    xpad,
    conv_a,
    conv_b,
    at_v,
    gr_v,
    group_ref,
    hot_ref,
    weight_ref,
    piece,
    basis_t,
    small_one,
    small_two,
    head_one,
    head_two,
    sc_v,
    ns_v,
    div_v,
    s_send,
    s_recv,
    x1_send,
    x1_keep,
    y1_send,
    y1_keep,
    x2_send,
    y2_send,
    two_keep,
    z_send,
    z_keep,
    feats_ref,
    basis_in_ref,
    basis_out_ref,
    out_sem,
    g_ss,
    g_rs,
    one_ss,
    one_rs,
    two_ss,
    two_rs,
    misc_sem,
    local_sem,
    ss,
    s_ss,
    s_rs,
    rs,
    z_ss,
    z_rs,
    gz_ss,
    gz_rs,
):
    low, full = jnp.bfloat16, jnp.float32
    highest = lax.Precision.HIGHEST
    dp, me_s, me_z = lax.axis_index("dp"), lax.axis_index("side"), lax.axis_index("blk")
    me_y, me_x = dp // 2, lax.rem(dp, 2)
    to_s = (dp, 1 - me_s, me_z)
    to_x = (me_y * 2 + 1 - me_x, me_s, me_z)
    to_y = ((1 - me_y) * 2 + me_x, me_s, me_z)
    dp_x, dp_y = me_y * 2 + 1 - me_x, (1 - me_y) * 2 + me_x
    dp_xy = (1 - me_y) * 2 + 1 - me_x
    to_right = (dp, me_s, lax.rem(me_z + 1, 4))
    to_left = (dp, me_s, lax.rem(me_z + 3, 4))
    images, width = 32, 512
    matrices = 2 * TAPS
    steps = 2 * 9

    def w_left(m):
        return gr_v.at[m, 0:64]

    def w_right(m):
        return gr_v.at[m, 64:128]

    def w_own(m):
        return gr_v.at[18 + m, 0:64]

    def w_back(m):
        return gr_v.at[18 + m, 64:128]

    first_map = 40

    def remote(src, dst, send, recv, target):
        return pltpu.make_async_remote_copy(
            src_ref=src,
            dst_ref=dst,
            send_sem=send,
            recv_sem=recv,
            device_id=target,
            device_id_type=MESH,
        )

    piece_copy = pltpu.make_async_copy(
        master_hbm.at[:, pl.ds(pl.multiple_of(dp * 64, 64), 64)], piece, out_sem.at[0]
    )
    piece_copy.start()
    feats_in = pltpu.make_async_copy(feats_hbm, feats_ref, out_sem.at[1])
    basis_in_in = pltpu.make_async_copy(basis_in_hbm, basis_in_ref, out_sem.at[2])
    basis_out_in = pltpu.make_async_copy(basis_out_hbm, basis_out_ref, out_sem.at[3])
    feats_in.start()
    basis_in_in.start()
    basis_out_in.start()

    near = [(a, b) for a in range(4) for b in range(2) if a or b]
    barrier = pltpu.get_barrier_semaphore()

    def near_id(a, b):
        return lax.rem(dp + a, 4), lax.rem(me_s + b, 2)

    for a, b in near:
        other, core = near_id(a, b)
        pl.semaphore_signal(barrier, inc=1, device_id=(other, core, me_z), device_id_type=MESH)
    for d in (1, 2, 3):
        pl.semaphore_signal(
            barrier, inc=1, device_id=(dp, me_s, lax.rem(me_z + d, 4)), device_id_type=MESH
        )

    piece_copy.wait()

    mine_is = [jnp.where(owners_ref[m] == me_z, 1, 0) for m in range(matrices)]
    before = jnp.zeros((), jnp.int32)
    for m in range(matrices):
        value = piece[jnp.minimum(before, piece.shape[0] - 1)] * mine_is[m].astype(full)
        w_own(m)[...] = value.astype(low)
        before = before + mine_is[m]

    @pl.when(me_z == 0)
    def _():
        gr_v[0:18, 0:64, :] = jnp.zeros((18, 64, width), low)

    @pl.when(me_z == 3)
    def _():
        gr_v[0:18, 64:128, :] = jnp.zeros((18, 64, width), low)

    pl.semaphore_wait(barrier, 10)

    sc_local = pltpu.make_async_copy(scales_hbm.at[:, me_y], sc_v.at[1 - me_y], misc_sem.at[0])
    sc_remote = remote(
        scales_hbm.at[:, 1 - me_y], sc_v.at[1 - me_y], misc_sem.at[1], misc_sem.at[2], to_y
    )
    sc_local.start()
    sc_remote.start()

    def right_copy(m):
        return remote(w_left(m), w_left(m), g_ss.at[0, m], g_rs.at[0, m], to_right)

    def left_copy(m):
        return remote(w_back(m), w_right(m), g_ss.at[1, m], g_rs.at[1, m], to_left)

    def x_copy(m):
        part = w_full.at[m, me_s, dp]
        return remote(part, part, g_ss.at[2, m], g_rs.at[2, m], to_x)

    def y_copy(m):
        part = w_full.at[m, me_s, dp]
        return remote(part, part, g_ss.at[3, m], g_rs.at[3, m], to_y)

    def even_copy(m):
        part = w_full.at[m, me_s, dp_x]
        return remote(part, part, g_ss.at[4, m], g_rs.at[4, m], to_y)

    def odd_copy(m):
        part = w_full.at[m, me_s, dp_y]
        return remote(part, part, g_ss.at[4, m], g_rs.at[4, m], to_x)

    def core_copy(m):
        part = w_full.at[m, me_s]
        return remote(part, part, g_ss.at[5, m], g_rs.at[5, m], to_s)

    def flow_right(m):
        @pl.when((m >= 0) & (m < matrices))
        def _():
            @pl.when(me_z > 0)
            def _():
                right_copy(m).wait_recv()

            w_left(m)[...] = w_left(m)[...] + w_own(m)[...]

            @pl.when(me_z < 3)
            def _():
                right_copy(m).start()

    def flow_left(m):
        @pl.when((m >= 0) & (m < matrices))
        def _():
            @pl.when(me_z < 3)
            def _():
                left_copy(m).wait_recv()

            w_back(m)[...] = w_right(m)[...] + w_own(m)[...]

            @pl.when(me_z > 0)
            def _():
                left_copy(m).start()

    def gather(t):
        flow_right(t - 2 * me_z)
        flow_left(t - 2 * (3 - me_z))
        m = t - 6

        @pl.when((m >= 0) & (m < matrices))
        def _():
            w_full[m, me_s, dp] = w_left(m)[...] + w_right(m)[...]
            x_copy(m).start()
            y_copy(m).start()

        m4 = t - 8

        @pl.when((m4 >= 0) & (m4 < matrices))
        def _():
            x_copy(m4).wait_recv()
            y_copy(m4).wait_recv()

            @pl.when(lax.rem(m4, 2) == 0)
            def _():
                even_copy(m4).start()

            @pl.when(lax.rem(m4, 2) == 1)
            def _():
                odd_copy(m4).start()

        m6 = t - 11

        @pl.when((m6 >= 0) & (m6 < matrices))
        def _():
            even_copy(m6).wait_recv()
            core_copy(m6).start()

    def weights(m):
        return w_full[m].reshape(width, width)

    def inner(p, q):
        return jnp.where((p < 4) & (q < 4), 1.0, 0.0).astype(full)

    def mask_of(p, q, rows=slice(None)):
        return jnp.maximum(group_ref[rows, :], inner(p, q))

    def cell(i):
        return pl.ds(pl.multiple_of(i * images, images), images)

    def half_cell(i, g):
        return pl.ds(pl.multiple_of(i * images + g * 16, 16), 16)

    def full_map(n):
        return jnp.where(image_group[n] == 1, 1.0, 0.0).astype(full)

    def prepare(t):
        for g in range(2):
            block = feats_ref[g * 16 : g * 16 + 16, t].astype(full)
            turned = jnp.swapaxes(block, 0, 1)
            for q in range(8):
                value = turned[q] * mask_of(t, q, slice(g * 16, g * 16 + 16))
                xpad[t + 1, q + 1, g * 16 : g * 16 + 16, :] = value.astype(low)
        line = lax.broadcasted_iota(jnp.int32, (8, 8, width), 0)
        column = lax.broadcasted_iota(jnp.int32, (8, 8, width), 1)
        core = jnp.where((line < 4) & (column < 4), 1.0, 0.0).astype(full)
        wide = []
        for k in range(4):
            n = t * 4 + k
            value = feats_ref[n].astype(full) * jnp.maximum(core, full_map(n))
            value = jnp.concatenate([value, jnp.zeros_like(value)], axis=1)
            wide.append(value.reshape(128, width).astype(low))
        project(0, t, jnp.concatenate(wide, axis=0))

    def project(layer, t, rows):
        at_v[1 - layer, :, pl.ds(pl.multiple_of(t * 512, 512), 512)] = lax.dot_general(
            basis_t[layer], rows, (((1,), (1,)), ((), ())), preferred_element_type=full
        ).astype(low)

    def conv_tap(tap, m, acc):
        a, b = tap // 3, lax.rem(tap, 3)
        kernel = weights(m)
        for p in range(8):
            rows = xpad[p + a, pl.ds(b, 8)].reshape(8 * images, width)
            acc[p * 256 : p * 256 + 256, :] += jnp.dot(rows, kernel, preferred_element_type=full)

    for t in range(3):
        gather(t)
    xpad[...] = jnp.zeros_like(xpad)
    basis_in_in.wait()
    basis_t[0] = basis_in_ref[0].T
    place = lax.broadcasted_iota(jnp.int32, (1, 128), 1)
    for n in range(images):
        group_ref[n : n + 1, :] = jnp.full((1, width), full_map(n), full)
        hot_ref[n : n + 1, :] = jnp.where(place == labels_ref[n], 1.0, 0.0).astype(full)
        weight_ref[n : n + 1, :] = jnp.full((1, 128), class_ref[labels_ref[n]].astype(full), full)

    feats_in.wait()
    basis_out_in.wait()

    def first(t, carry):
        gather(t)

        @pl.when(t < 11)
        def _():
            prepare(t - 3)

        @pl.when(t == 11)
        def _():
            conv_a[...] = jnp.zeros_like(conv_a)
            conv_b[...] = jnp.zeros_like(conv_b)
            basis_t[1] = basis_in_ref[1].T

        tap = t - 12

        @pl.when(tap >= 0)
        def _():
            core_copy(tap).wait_recv()
            conv_tap(tap, tap, conv_a)

        return carry

    lax.fori_loop(3, 21, first, 0)

    mine = dp * 2 + me_s

    def sum_one(buf, sems, n, a, b):
        other, core = near_id(a, b)
        return remote(
            buf.at[mine], buf.at[mine], sems[0].at[n, a * 2 + b], sems[1].at[n, mine],
            (other, core, me_z),
        )

    def sum_one_wait(buf, n, a, b):
        other, core = near_id(a, b)
        slot = other * 2 + core
        remote(
            buf.at[slot], buf.at[slot], one_ss.at[n, a * 2 + b], one_rs.at[n, slot],
            (other, core, me_z),
        ).wait_recv()

    def sum_two(buf, n, d):
        other = lax.rem(me_z + d, 4)
        return remote(
            buf.at[me_z], buf.at[me_z], two_ss.at[n, d], two_rs.at[n, me_z], (dp, me_s, other)
        )

    def sum_start(n, buf):
        for a, b in near:
            sum_one(buf, (one_ss, one_rs), n, a, b).start()

    def sum_middle(n, buf, buf_two):
        for a, b in near:
            sum_one_wait(buf, n, a, b)
        total = buf[0]
        for slot in range(1, 8):
            total = total + buf[slot]
        buf_two[me_z] = total
        for d in (1, 2, 3):
            sum_two(buf_two, n, d).start()

    def sum_arrived(n, buf_two):
        for d in (1, 2, 3):
            other = lax.rem(me_z + d, 4)
            remote(
                buf_two.at[other], buf_two.at[other], two_ss.at[n, d], two_rs.at[n, other],
                (dp, me_s, other),
            ).wait_recv()

    def sum_total(buf_two):
        return buf_two[0] + buf_two[1] + buf_two[2] + buf_two[3]

    def sum_end(n, buf_two):
        sum_arrived(n, buf_two)
        return sum_total(buf_two)

    def sum_sent(n, buf, buf_two):
        for a, b in near:
            sum_one(buf, (one_ss, one_rs), n, a, b).wait_send()
        for d in (1, 2, 3):
            sum_two(buf_two, n, d).wait_send()

    def column(value):
        return jnp.sum(value, axis=0, keepdims=True)

    zero = jnp.zeros((images, width), full)

    def channel_sums(acc):
        def line(p, carry):
            sums, squares = carry
            for q in range(8):
                value = acc[cell(p * 8 + q), :]
                masked = value * mask_of(p, q)
                sums = sums + masked
                squares = squares + masked * value
            return sums, squares

        sums, squares = lax.fori_loop(0, 8, line, (zero, zero))
        return column(sums), column(squares)

    sums, squares = channel_sums(conv_a)
    group = group_ref[...]
    pixels = 16.0 + 48.0 * group
    small_one[0, mine, 0:1, :] = sums
    small_one[0, mine, 1:2, :] = squares
    small_one[0, mine, 2:3, :] = column(pixels)
    small_one[0, mine, 3:4, :] = jnp.broadcast_to(column(weight_ref[...])[:, 0:1], (1, width))
    sum_start(0, small_one.at[0])

    def later(t, carry):
        gather(t)
        return carry

    lax.fori_loop(21, 23, later, 0)
    sum_middle(0, small_one.at[0], small_two.at[0])
    lax.fori_loop(23, 24, later, 0)
    total = sum_end(0, small_two.at[0])
    total_out[...] = total
    count = total[2:3]

    def moments(total):
        average = total[0:1] / count
        return average, lax.rsqrt(total[1:2] / count - average * average + EPS_NORM)

    average_a, inv_a = moments(total)

    def activation(value, layer, average, inv):
        normed = (value - average) * inv
        pre = params_ref[layer, 0:1, :] * normed + params_ref[layer, 1:2, :]
        return normed, pre, jax.nn.sigmoid(pre)

    def images_first(values):
        return jnp.swapaxes(jnp.stack(values), 0, 1)

    def act_line(p, carry):
        @pl.when(lax.rem(p, 4) == 3)
        def _():
            gather(24 + p // 4)

        for g in range(2):
            acts = []
            for q in range(8):
                value = conv_a[half_cell(p * 8 + q, g), :]
                normed, pre, sigma = activation(value, 0, average_a, inv_a)
                act = pre * sigma * mask_of(p, q, slice(g * 16, g * 16 + 16))
                xpad[p + 1, q + 1, g * 16 : g * 16 + 16, :] = act.astype(low)
                acts.append(act)
            turned = images_first(acts)
            turned = jnp.concatenate([turned, jnp.zeros_like(turned)], axis=1).astype(low)
            gr_v[first_map + g * 16 : first_map + g * 16 + 16, pl.ds(pl.multiple_of(p * 16, 16), 16), :] = turned
        return carry

    lax.fori_loop(0, 8, act_line, 0)

    def second(tap, carry):
        core_copy(TAPS + tap).wait_recv()
        conv_tap(tap, TAPS + tap, conv_b)

        @pl.when(tap < 3)
        def _():
            gather(26 + tap)

        return carry

    lax.fori_loop(0, TAPS, second, 0)
    sums, squares = channel_sums(conv_b)
    small_one[1, mine, 0:1, :] = sums
    small_one[1, mine, 1:2, :] = squares
    small_one[1, mine, 2:4, :] = jnp.zeros((2, width), full)
    sum_start(1, small_one.at[1])

    def project_one(t, carry):
        project(1, t, gr_v[pl.ds(first_map + t * 4, 4), 0:128, :].reshape(512, width))
        return carry

    lax.fori_loop(0, 4, project_one, 0)
    sum_middle(1, small_one.at[1], small_two.at[1])
    lax.fori_loop(4, 8, project_one, 0)
    total = sum_end(1, small_two.at[1])
    average_b, inv_b = moments(total)

    def pool_line(p, carry):
        for q in range(8):
            normed, pre, sigma = activation(conv_b[cell(p * 8 + q), :], 1, average_b, inv_b)
            carry = carry + pre * sigma * mask_of(p, q)
        return carry

    pooled = lax.fori_loop(0, 8, pool_line, zero) / pixels
    pooled_low = pooled.astype(low)
    classes = head_ref.shape[0]
    head_low = head_ref[:, 0:width].astype(low)
    bias = jnp.broadcast_to(head_ref[:, width : width + 1], (classes, classes))
    across = lax.broadcasted_iota(jnp.int32, (classes, classes), 0)
    along = lax.broadcasted_iota(jnp.int32, (classes, classes), 1)
    logits = lax.dot_general(
        pooled_low, head_low, (((1,), (1,)), ((), ())), preferred_element_type=full
    ) + column(jnp.where(across == along, bias, 0.0))
    shifted = logits - jnp.max(logits, axis=1, keepdims=True)
    log_prob = shifted - jnp.log(jnp.sum(jnp.exp(shifted), axis=1, keepdims=True))
    hot = hot_ref[:, 0:classes]
    image_weight = weight_ref[:, 0:classes]
    picked = jnp.sum(hot * log_prob, axis=1, keepdims=True)
    loss = -column(weight_ref[:, 0:1] * picked)
    d_logits = image_weight * (jnp.exp(log_prob) - hot)
    d_pooled = (
        lax.dot_general(
            d_logits,
            head_low.astype(full),
            (((1,), (0,)), ((), ())),
            precision=highest,
            preferred_element_type=full,
        )
        / pixels
    )

    def d_line_top(p, carry):
        gammas, betas = carry
        for q in range(8):
            at = cell(p * 8 + q)
            normed, pre, sigma = activation(conv_b[at, :], 1, average_b, inv_b)
            d_pre = d_pooled * mask_of(p, q) * sigma * (1.0 + pre * (1.0 - sigma))
            gammas = gammas + d_pre * normed
            betas = betas + d_pre
        return gammas, betas

    gammas, betas = lax.fori_loop(0, 8, d_line_top, (zero, zero))

    def put_sums(n, gammas, betas):
        small_one[n, mine, 0:1, :] = column(gammas)
        small_one[n, mine, 1:2, :] = column(betas)
        small_one[n, mine, 2:4, :] = jnp.zeros((2, width), full)
        sum_start(n, small_one.at[n])

    def sent(m, carry):
        @pl.when(me_z < 3)
        def _():
            right_copy(m).wait_send()

        @pl.when(me_z > 0)
        def _():
            left_copy(m).wait_send()

        x_copy(m).wait_send()
        y_copy(m).wait_send()
        even_copy(m).wait_send()
        core_copy(m).wait_send()
        return carry

    lax.fori_loop(0, matrices, sent, 0)
    put_sums(2, gammas, betas)
    grad_head = lax.dot_general(
        d_logits,
        pooled_low.astype(full),
        (((0,), (0,)), ((), ())),
        precision=highest,
        preferred_element_type=full,
    )
    head_one[mine, :, :] = jnp.zeros((24, width), full)
    head_one[mine, 0:classes, :] = grad_head
    head_one[mine, 16:17, 0:classes] = column(d_logits)
    head_one[mine, 17:18, :] = jnp.broadcast_to(loss, (1, width))

    def clear(n, carry):
        gr_v[n, 0:16, :] = jnp.zeros((16, width), low)
        gr_v[n, 144:160, :] = jnp.zeros((16, width), low)
        return carry

    lax.fori_loop(0, 3 * images, clear, 0)

    sum_middle(2, small_one.at[2], small_two.at[2])
    total_b = sum_end(2, small_two.at[2])
    norm_out[1] = total_b
    sum_start(4, head_one)

    def grad_of(layer, normed, d_pre, inv, total):
        gamma = params_ref[layer, 0:1, :]
        return inv * (
            gamma * d_pre
            - gamma * total[1:2] / count
            - normed * (gamma * total[0:1] / count)
        )

    def grad_top(p, carry):
        for q in range(8):
            normed, pre, sigma = activation(conv_b[cell(p * 8 + q), :], 1, average_b, inv_b)
            mask = mask_of(p, q)
            d_pre = d_pooled * mask * sigma * (1.0 + pre * (1.0 - sigma))
            value = mask * grad_of(1, normed, d_pre, inv_b, total_b)
            xpad[p + 1, q + 1, :, :] = value.astype(low)
        return carry

    lax.fori_loop(0, 8, grad_top, 0)
    conv_b[...] = jnp.zeros_like(conv_b)

    def back(tap, carry):
        a, b = tap // 3, lax.rem(tap, 3)
        kernel = weights(TAPS + tap)
        for p in range(8):
            rows = xpad[p + 2 - a, pl.ds(2 - b, 8)].reshape(8 * images, width)
            conv_b[p * 256 : p * 256 + 256, :] += lax.dot_general(
                rows, kernel, (((1,), (1,)), ((), ())), preferred_element_type=full
            )
        return carry

    def d_line(p, carry):
        gammas, betas = carry
        for q in range(8):
            at = cell(p * 8 + q)
            normed, pre, sigma = activation(conv_a[at, :], 0, average_a, inv_a)
            d_pre = conv_b[at, :] * mask_of(p, q) * sigma * (1.0 + pre * (1.0 - sigma))
            conv_b[at, :] = d_pre
            gammas = gammas + d_pre * normed
            betas = betas + d_pre
        return gammas, betas

    def turn_grads(layer):
        def line(p, carry):
            rows = xpad[p + 1, 1:9].reshape(8 * images, width)
            value = jnp.dot(rows, basis_out_ref[layer], preferred_element_type=full)
            value = value.reshape(8, images, width)
            lines = pl.ds(pl.multiple_of(p * 16 + 16, 16), 16)
            gap = jnp.zeros((8, 1, width), full)
            rest = jnp.zeros((8, 8, width), full)
            for g in range(4):
                turned = jnp.swapaxes(value[:, g * 8 : g * 8 + 8], 0, 1)
                shifts = (
                    jnp.concatenate([turned[:, 1:], gap], axis=1),
                    turned,
                    jnp.concatenate([gap, turned[:, :7]], axis=1),
                )
                for b in range(3):
                    wide = jnp.concatenate([shifts[b], rest], axis=1).astype(low)
                    gr_v[b * images + g * 8 : b * images + g * 8 + 8, lines, :] = wide
            return carry

        return line

    lax.fori_loop(0, 8, turn_grads(1), 0)

    def bottom():
        total_a = sum_total(small_two.at[3])
        norm_out[0] = total_a

        def line(p, carry):
            for q in range(8):
                at = cell(p * 8 + q)
                normed = (conv_a[at, :] - average_a) * inv_a
                value = mask_of(p, q) * grad_of(0, normed, conv_b[at, :], inv_a, total_a)
                xpad[p + 1, q + 1, :, :] = value.astype(low)
            return carry

        lax.fori_loop(0, 8, line, 0)
        lax.fori_loop(0, 8, turn_grads(0), 0)

    def x1_recv(j):
        return w_full.at[j, 0, :, :, 0:256]

    def y1_recv(j):
        return w_full.at[j, 0, :, :, 256:512]

    def x2_recv(j):
        return w_full.at[j, 1, 0:2, :, 0:256]

    def y2_recv(j):
        return w_full.at[j, 1, 2:4, :, 0:256]

    def z_recv(j, d):
        return w_full.at[j, 1, d - 1, :, 256:512]

    def side_copy(j):
        ring, four = lax.rem(j, 2), lax.rem(j, 4)
        return remote(s_send.at[ring], s_recv.at[four], s_ss.at[ring], s_rs.at[four], to_s)

    def x1_copy(j):
        ring = lax.rem(j, 2)
        return remote(x1_send.at[ring], x1_recv(j), ss.at[1, ring], rs.at[0, j], to_x)

    def y1_copy(j):
        ring = lax.rem(j, 2)
        return remote(y1_send.at[ring, 1 - me_y], y1_recv(j), ss.at[2, ring], rs.at[1, j], to_y)

    def x2_copy(j):
        ring = lax.rem(j, 2)
        return remote(x2_send.at[ring], x2_recv(j), ss.at[3, ring], rs.at[2, j], to_x)

    def y2_copy(j):
        ring = lax.rem(j, 2)
        return remote(y2_send.at[ring], y2_recv(j), ss.at[4, ring], rs.at[3, j], to_y)

    def z_copy(j, d):
        ring, other = lax.rem(j, 2), lax.rem(me_z + d, 4)
        return remote(
            z_send.at[ring, other],
            z_recv(j, d),
            z_ss.at[ring, d - 1],
            z_rs.at[j, d - 1],
            (dp, me_s, other),
        )

    def place(j):
        return 1 - j // 9, lax.rem(j, 9)

    def local_copy(j):
        layer, i = place(j)
        ring = lax.rem(j, 2)
        return pltpu.make_async_copy(
            div_v.at[ring], out.at[me_s, layer, me_x, me_z, i, me_y], local_sem.at[ring]
        )

    def gz_copy(j, d):
        layer, i = place(j)
        ring, other = lax.rem(j, 2), lax.rem(me_z + d, 4)
        return remote(
            div_v.at[ring],
            out.at[me_s, layer, me_x, me_z, i, me_y],
            gz_ss.at[ring, d - 1],
            gz_rs.at[j, d - 1],
            (dp, me_s, other),
        )

    lower, upper = pl.ds(0, 2), pl.ds(2, 2)

    def spread(j, which, kind, target):
        part = out.at[which]
        return remote(part, part, ss.at[kind, lax.rem(j, 2)], rs.at[kind - 1, j], target)

    def g1y_copy(j):
        layer, i = place(j)
        return spread(j, (me_s, layer, me_x, lower, i, me_y), 5, to_y)

    def g1x_copy(j):
        layer, i = place(j)
        return spread(j, (me_s, layer, me_x, upper, i, me_y), 6, to_x)

    def g2x_copy(j):
        layer, i = place(j)
        return spread(j, (me_s, layer, me_x, lower, i), 7, to_x)

    def g2y_copy(j):
        layer, i = place(j)
        return spread(j, (me_s, layer, pl.ds(0, 2), upper, i, me_y), 8, to_y)

    def gs_copy(j):
        layer, i = place(j)
        return spread(j, (me_s, layer, pl.ds(0, 2), pl.ds(0, 4), i), 9, to_s)

    def products(j, half, store):
        li, i = j // 9, lax.rem(j, 9)
        cols = pl.ds(pl.multiple_of(half * 256, 256), 256)
        for u in range(8):
            x_to = 1 - me_x if u < 4 else me_x
            row = x_to * 2304 + (u % 4) * 576 + 64 * i
            tap = row // 512
            rows = pl.ds(pl.multiple_of(lax.rem(row, 512), 64), 64)
            near = pl.ds(pl.multiple_of((2 - tap // 3) * 16, 16), 128)
            shift = lax.rem(tap, 3) * images
            square = total = None
            for n in range(images):
                p = jnp.dot(
                    at_v[li, rows, n * 128 : (n + 1) * 128],
                    gr_v[shift + n, near, cols],
                    preferred_element_type=full,
                )
                square = p * p if square is None else square + p * p
                total = p if total is None else total + p
            store(u, x_to, u % 4, total, square)

    def at_step(x):
        j = jnp.where(x < 10, x, jnp.where(x < 14, x - 4, x - 5))
        due = ((x >= 0) & (x < 6)) | ((x >= 10) & (x < 13)) | ((x >= 14) & (x < 23))
        return j, due

    def step(k, carry):
        ja, due = at_step(k)

        @pl.when(due & (ja >= 2))
        def _():
            side_copy(ja - 2).wait_send()

        @pl.when(due)
        def _():
            ring = lax.rem(ja, 2)

            def store(u, x_to, z_to, total, square):
                s_send[ring, u, 0] = total.astype(low)
                s_send[ring, u, 1] = square.astype(low)

            products(ja, 1 - me_s, store)
            side_copy(ja).start()

        jb, due = at_step(k - 1)

        @pl.when(due & (jb >= 2))
        def _():
            x1_copy(jb - 2).wait_send()
            y1_copy(jb - 2).wait_send()

        @pl.when(due)
        def _():
            ring, four = lax.rem(jb, 2), lax.rem(jb, 4)
            side_copy(jb).wait_recv()

            def store(u, x_to, z_to, total, square):
                got = s_recv[four, u].astype(full)
                both = (total + got[0], square + got[1])
                for c in range(2):
                    if z_to < 2 and u < 4:
                        x1_send[ring, z_to * 2 + c] = both[c].astype(low)
                    elif z_to < 2:
                        x1_keep[ring, z_to * 2 + c] = both[c]
                    else:
                        at = x_to * 2 + z_to - 2
                        for y_to in range(2):
                            value = both[c][y_to * 32 : y_to * 32 + 32]
                            y1_send[ring, y_to, at, c * 32 : c * 32 + 32, :] = value.astype(low)
                            y1_keep[ring, y_to, at, c * 32 : c * 32 + 32, :] = value

            products(jb, me_s, store)
            x1_copy(jb).start()
            y1_copy(jb).start()

        j7, due = at_step(k - 12)

        @pl.when(due)
        def _():
            @pl.when(j7 >= 2)
            def _():
                gs_copy(j7 - 2).wait_send()

            g2x_copy(j7).wait_recv()
            g2y_copy(j7).wait_recv()
            gs_copy(j7).start()

        j6, due = at_step(k - 10)

        @pl.when(due)
        def _():
            @pl.when(j6 >= 2)
            def _():
                g2y_copy(j6 - 2).wait_send()
                g2x_copy(j6 - 2).wait_send()

            g1y_copy(j6).wait_recv()
            g2x_copy(j6).start()
            g1x_copy(j6).wait_recv()
            g2y_copy(j6).start()

        j5, due = at_step(k - 8)

        @pl.when(due)
        def _():
            @pl.when(j5 >= 2)
            def _():
                g1y_copy(j5 - 2).wait_send()
                g1x_copy(j5 - 2).wait_send()

            local_copy(j5).wait()
            for d in (1, 2, 3):
                gz_copy(j5, d).wait_recv()
            g1y_copy(j5).start()
            g1x_copy(j5).start()

        j4, due = at_step(k - 6)

        @pl.when(due & (j4 == 0))
        def _():
            sc_local.wait()
            sc_remote.wait_recv()

        @pl.when(due)
        def _():
            ring, li, i = lax.rem(j4, 2), j4 // 9, lax.rem(j4, 9)

            @pl.when(j4 >= 2)
            def _():
                for d in (1, 2, 3):
                    gz_copy(j4 - 2, d).wait_send()

            for d in (1, 2, 3):
                z_copy(j4, d).wait_recv()
            both = z_keep[ring, me_z]
            for d in (1, 2, 3):
                both = both + z_recv(j4, d)[...].astype(full)
            scale = DECAY * sc_v[li, i] + (1.0 - DECAY) * both[32:64] / images_all
            ns_v[li, i] = scale
            div_v[ring] = (both[0:32] / total_out[3:4, 0:256] / (scale + DAMPING)).astype(low)
            local_copy(j4).start()
            for d in (1, 2, 3):
                gz_copy(j4, d).start()

        for li in range(2):
            @pl.when(due & (j4 == 9 * li + 8) & (me_y == 1 - li))
            def _():
                pltpu.make_async_copy(ns_v.at[li], ns_out.at[:, me_y], misc_sem.at[3]).start()

            @pl.when(due & (j4 == 9 * li + 8) & (me_y == li))
            def _():
                remote(
                    ns_v.at[li], ns_out.at[:, me_y], misc_sem.at[4], misc_sem.at[5], to_y
                ).start()

        j3, due = at_step(k - 4)

        @pl.when(due)
        def _():
            ring = lax.rem(j3, 2)

            @pl.when(j3 >= 2)
            def _():
                for d in (1, 2, 3):
                    z_copy(j3 - 2, d).wait_send()

            y2_copy(j3).wait_recv()
            x2_copy(j3).wait_recv()
            for z_to in range(4):
                got = y2_recv(j3)[z_to] if z_to < 2 else x2_recv(j3)[z_to - 2]
                both = two_keep[ring, z_to] + got.astype(full)
                z_keep[ring, z_to] = both
                z_send[ring, z_to] = both.astype(low)
            for d in (1, 2, 3):
                z_copy(j3, d).start()

        j2, due = at_step(k - 2)

        @pl.when(due)
        def _():
            ring = lax.rem(j2, 2)

            @pl.when(j2 >= 2)
            def _():
                x2_copy(j2 - 2).wait_send()
                y2_copy(j2 - 2).wait_send()

            x1_copy(j2).wait_recv()
            here = pl.ds(pl.multiple_of(me_y * 32, 32), 32)
            there = pl.ds(pl.multiple_of((1 - me_y) * 32, 32), 32)
            got = x1_recv(j2)
            for z_to in range(2):
                for c in range(2):
                    at, lines = z_to * 2 + c, slice(c * 32, c * 32 + 32)
                    two_keep[ring, z_to, lines, :] = x1_keep[ring, at, here, :] + got[
                        at, here, :
                    ].astype(full)
                    y2_send[ring, z_to, lines, :] = (
                        x1_keep[ring, at, there, :] + got[at, there, :].astype(full)
                    ).astype(low)
            y2_copy(j2).start()
            y1_copy(j2).wait_recv()
            got = y1_recv(j2)
            for z_to in range(2):
                mine_at, other_at = me_x * 2 + z_to, (1 - me_x) * 2 + z_to
                two_keep[ring, 2 + z_to] = y1_keep[ring, me_y, mine_at] + got[mine_at].astype(full)
                x2_send[ring, z_to] = (
                    y1_keep[ring, me_y, other_at] + got[other_at].astype(full)
                ).astype(low)
            x2_copy(j2).start()

        @pl.when((k >= 6) & (k < 9))
        def _():
            lax.fori_loop(0, 3, lambda t, carry: back((k - 6) * 3 + t, carry), 0)

        @pl.when(k == 8)
        def _():
            sum_middle(4, head_one, head_two)

        @pl.when(k == 9)
        def _():
            gammas, betas = lax.fori_loop(0, 8, d_line, (zero, zero))
            put_sums(3, gammas, betas)

        @pl.when(k == 10)
        def _():
            sum_middle(3, small_one.at[3], small_two.at[3])

        @pl.when(k == 25)
        def _():
            head_out[...] = sum_end(4, head_two)

        @pl.when(k == 13)
        def _():
            sum_arrived(3, small_two.at[3])
            bottom()

        return carry

    lax.fori_loop(0, steps + 5 + 12, step, 0)

    def finish(j, carry):
        gs_copy(j).wait_recv()
        return carry

    lax.fori_loop(0, steps, finish, 0)
    sc_remote.wait_send()
    li = 1 - me_y
    pltpu.make_async_copy(ns_v.at[li], ns_out.at[:, me_y], misc_sem.at[3]).wait()
    ns_remote = remote(ns_v.at[0], ns_out.at[:, 0], misc_sem.at[4], misc_sem.at[5], to_y)
    ns_remote.wait_send()
    ns_remote.wait_recv()
    for j in (steps - 2, steps - 1):
        for copy in (side_copy, x1_copy, y1_copy, x2_copy, y2_copy):
            copy(j).wait_send()
        for copy in (g1y_copy, g1x_copy, g2y_copy, g2x_copy, gs_copy):
            copy(j).wait_send()
        for d in (1, 2, 3):
            z_copy(j, d).wait_send()
            gz_copy(j, d).wait_send()
    for n in range(4):
        sum_sent(n, small_one.at[n], small_two.at[n])
    sum_sent(4, head_one, head_two)


def whole_step(
    feats, size_group, labels, class_wt, owners, basis_in, basis_out, master, norm_params, head, scales
):
    count_img, side_len, _, width = feats.shape
    images_all = count_img * lax.axis_size("dp") * lax.axis_size("side") * lax.axis_size("blk")
    low, full, dma = jnp.bfloat16, jnp.float32, pltpu.SemaphoreType.DMA
    vmem, any_spec = pl.BlockSpec(memory_space=pltpu.VMEM), pl.BlockSpec(memory_space=pl.ANY)
    smem = pl.BlockSpec(memory_space=pltpu.SMEM)
    rows = count_img * side_len * side_len
    divided, new_scales, total, norm_sums, head_sums = pl.pallas_call(
        functools.partial(step_kernel, images_all),
        out_shape=[
            jax.ShapeDtypeStruct((2, 2, 2, 4, 9, 2, 32, 256), low),
            jax.ShapeDtypeStruct((9, 2, 32, 256), full),
            jax.ShapeDtypeStruct((4, width), full),
            jax.ShapeDtypeStruct((2, 4, width), full),
            jax.ShapeDtypeStruct((24, width), full),
        ],
        in_specs=[any_spec, smem, smem, smem, smem, any_spec, vmem, vmem, any_spec, any_spec, any_spec],
        out_specs=[any_spec, any_spec, vmem, vmem, vmem],
        scratch_shapes=[
            pltpu.VMEM((18, 2, 4, 64, 512), low),
            pltpu.VMEM((10, 10, 32, 512), low),
            pltpu.VMEM((rows, 512), full),
            pltpu.VMEM((rows, 512), full),
            pltpu.VMEM((2, 512, 4096), low),
            pltpu.VMEM((96, 160, 512), low),
            pltpu.VMEM((32, 512), full),
            pltpu.VMEM((32, 128), full),
            pltpu.VMEM((32, 128), full),
            pltpu.VMEM((10, 64, 512), full),
            pltpu.VMEM((2, 512, 512), low),
            pltpu.VMEM((4, 8, 4, 512), full),
            pltpu.VMEM((4, 4, 4, 512), full),
            pltpu.VMEM((8, 24, 512), full),
            pltpu.VMEM((4, 24, 512), full),
            pltpu.VMEM((2, 9, 32, 256), full),
            pltpu.VMEM((2, 9, 32, 256), full),
            pltpu.VMEM((2, 32, 256), low),
            pltpu.VMEM((2, 8, 2, 64, 256), low),
            pltpu.VMEM((4, 8, 2, 64, 256), low),
            pltpu.VMEM((2, 4, 64, 256), low),
            pltpu.VMEM((2, 4, 64, 256), full),
            pltpu.VMEM((2, 2, 4, 64, 256), low),
            pltpu.VMEM((2, 2, 4, 64, 256), full),
            pltpu.VMEM((2, 2, 64, 256), low),
            pltpu.VMEM((2, 2, 64, 256), low),
            pltpu.VMEM((2, 4, 64, 256), full),
            pltpu.VMEM((2, 4, 64, 256), low),
            pltpu.VMEM((2, 4, 64, 256), full),
            pltpu.VMEM(feats.shape, low),
            pltpu.VMEM(basis_in.shape, low),
            pltpu.VMEM(basis_out.shape, low),
            dma((4,)),
            dma((6, 18)),
            dma((6, 18)),
            dma((5, 8)),
            dma((5, 8)),
            dma((5, 4)),
            dma((5, 4)),
            dma((6,)),
            dma((2,)),
            dma((10, 2)),
            dma((2,)),
            dma((4,)),
            dma((9, 18)),
            dma((2, 3)),
            dma((18, 3)),
            dma((2, 3)),
            dma((18, 3)),
        ],
        name="whole_step",
        compiler_params=pltpu.CompilerParams(
            collective_id=0, has_side_effects=True, vmem_limit_bytes=63 * 2**20
        ),
    )(
        feats,
        size_group,
        labels,
        class_wt,
        owners,
        master,
        norm_params,
        head,
        basis_in,
        basis_out,
        scales.reshape(9, 2, 32, 256),
    )
    return (
        divided.reshape(2, 18, 512, 256),
        new_scales.reshape(576, 256),
        total,
        norm_sums,
        head_sums,
    )


def update_kernel(
    owners_ref,
    divided,
    scales_in,
    basis_in,
    basis_out,
    w_hbm,
    m_hbm,
    v_hbm,
    total_ref,
    norm_sums,
    head_sums,
    norm_w,
    norm_m,
    norm_v,
    head_w,
    head_m,
    head_v,
    w_out,
    m_out,
    v_out,
    norm_w_out,
    norm_m_out,
    norm_v_out,
    head_w_out,
    head_m_out,
    head_v_out,
    loss_out,
    weight_out,
    scales_out,
    matrix,
    p_v,
    rows_v,
    cols_v,
    w_v,
    m_v,
    v_v,
    scales_v,
    in_sem,
    out_sem,
):
    low, full = jnp.bfloat16, jnp.float32
    slots, half, width = w_v.shape
    blk, side = lax.axis_index("blk"), lax.axis_index("side")

    def state_in(q):
        return [
            pltpu.make_async_copy(src.at[q], dst.at[q], in_sem.at[n, q])
            for n, (src, dst) in enumerate(((w_hbm, w_v), (m_hbm, m_v), (v_hbm, v_v)))
        ]

    def state_out(q):
        return [
            pltpu.make_async_copy(src.at[q], dst.at[q], out_sem.at[n, q])
            for n, (src, dst) in enumerate(((w_v, w_out), (m_v, m_out), (v_v, v_out)))
        ]

    rows_in = pltpu.make_async_copy(
        basis_in.at[:, pl.ds(pl.multiple_of(side * half, half), half)], rows_v, in_sem.at[4, 0]
    )
    cols_in = pltpu.make_async_copy(basis_out, cols_v, in_sem.at[4, 1])
    scales_read = pltpu.make_async_copy(scales_in, scales_v, in_sem.at[4, 2])
    scales_write = pltpu.make_async_copy(scales_v, scales_out, in_sem.at[4, 3])
    scales_read.start()
    rows_in.start()
    cols_in.start()

    for q in range(slots):
        matrix[q] = 0
    count = jnp.zeros((), jnp.int32)
    for m in range(owners_ref.shape[0]):
        mine = owners_ref[m] == blk

        @pl.when(mine)
        def _():
            matrix[count] = m

        count = count + jnp.where(mine, 1, 0)

    def part_in(q):
        return pltpu.make_async_copy(divided.at[:, matrix[q]], p_v.at[q], in_sem.at[3, q])

    for q in range(slots):
        part_in(q).start()
        for copy in state_in(q):
            copy.start()
    weight = total_ref[3:4, 0:1]
    weight_out[0, 0] = total_ref[3, 0]
    loss_out[0, 0] = head_sums[17, 0]
    for layer in range(2):
        norm_w_out[layer], norm_m_out[layer], norm_v_out[layer] = adamw(
            norm_w[layer],
            norm_m[layer],
            norm_v[layer],
            norm_sums[layer, 0:2, :] / weight,
            RATE_NORM,
        )
    classes = head_w.shape[0]
    here = lax.broadcasted_iota(jnp.int32, (classes, classes), 0)
    there = lax.broadcasted_iota(jnp.int32, (classes, classes), 1)
    line = jnp.broadcast_to(head_sums[16:17, 0:classes], (classes, classes))
    bias = jnp.sum(jnp.where(here == there, line, 0.0), axis=1, keepdims=True)
    for at, gradient in (
        (slice(0, width), head_sums[0:classes, :]),
        (slice(width, width + 1), bias),
    ):
        head_w_out[:, at], head_m_out[:, at], head_v_out[:, at] = adamw(
            head_w[:, at], head_m[:, at], head_v[:, at], gradient / weight, RATE_HEAD
        )
    rows_in.wait()
    cols_in.wait()

    def gradient(q):
        layer = matrix[q] // TAPS
        held = jnp.where(q < count, 1.0, 0.0).astype(full)
        both = [
            jnp.dot(rows_v[layer], p_v[q, s], preferred_element_type=full).astype(low)
            for s in range(2)
        ]
        return held * lax.dot_general(
            jnp.concatenate(both, axis=1),
            cols_v[layer],
            (((1,), (1,)), ((), ())),
            preferred_element_type=full,
        )

    def slot(q, carry):
        part_in(q).wait()
        change = gradient(q)
        for copy in state_in(q):
            copy.wait()
        w_v[q], m_v[q], v_v[q] = adamw(w_v[q], m_v[q], v_v[q], change, RATE_CONV)
        for copy in state_out(q):
            copy.start()
        return carry

    scales_read.wait()
    scales_write.start()
    lax.fori_loop(0, slots, slot, 0)
    for q in range(slots):
        for copy in state_out(q):
            copy.wait()
    scales_write.wait()


def update(
    owners, divided, scales, basis_in, basis_out, states, total, norm_sums, head_sums, norm_states, head_states
):
    full, dma = jnp.float32, pltpu.SemaphoreType.DMA
    slots, half, width = states[0].shape
    vmem, any_spec = pl.BlockSpec(memory_space=pltpu.VMEM), pl.BlockSpec(memory_space=pl.ANY)
    smem = pl.BlockSpec(memory_space=pltpu.SMEM)
    like = [jax.ShapeDtypeStruct(x.shape, full) for x in (*states, *norm_states, *head_states)]
    one = jax.ShapeDtypeStruct((1, 1), full)
    return pl.pallas_call(
        update_kernel,
        out_shape=like + [one, one, jax.ShapeDtypeStruct(scales.shape, full)],
        in_specs=[smem] + [any_spec] * 7 + [vmem] * 9,
        out_specs=[any_spec] * 3 + [vmem] * 6 + [smem] * 2 + [any_spec],
        scratch_shapes=[
            pltpu.SMEM((slots,), jnp.int32),
            pltpu.VMEM((slots, 2, width, half), jnp.bfloat16),
            pltpu.VMEM((2, half, width), jnp.bfloat16),
            pltpu.VMEM((2, width, width), jnp.bfloat16),
            pltpu.VMEM(states[0].shape, full),
            pltpu.VMEM(states[0].shape, full),
            pltpu.VMEM(states[0].shape, full),
            pltpu.VMEM(scales.shape, full),
            dma((5, slots)),
            dma((3, slots)),
        ],
        name="update",
        compiler_params=pltpu.CompilerParams(vmem_limit_bytes=63 * 2**20),
    )(
        owners,
        divided,
        scales,
        basis_in,
        basis_out,
        *states,
        total,
        norm_sums,
        head_sums,
        *norm_states,
        *head_states,
    )


def shards_general(
    feats,
    size_group,
    labels,
    class_wt,
    owners,
    basis_in,
    basis_out,
    scales,
    master,
    moment1,
    moment2,
    norm_params,
    norm_m,
    norm_v,
    head,
    head_m,
    head_v,
):
    count_img = feats.shape[0]
    side_len = feats.shape[1]
    width = feats.shape[3]
    half = width // 2
    n_dp = lax.axis_size("dp")
    n_side = lax.axis_size("side")
    n_blk = lax.axis_size("blk")
    slots_dev = master.shape[0]
    matrices = owners.shape[0]
    block_rows = scales.shape[0]
    images_all = count_img * n_dp * n_side * n_blk
    index = jnp.arange(matrices)
    earlier = (owners[:, None] == owners[None, :]) & (index[None, :] < index[:, None])
    slot = owners * slots_dev + jnp.sum(earlier.astype(jnp.int32), axis=1)
    pieces = lax.all_gather(master.astype(jnp.bfloat16), ("side", "blk"), axis=0, tiled=True)
    pieces = pieces.reshape(n_side, n_blk * slots_dev, master.shape[1], width)
    pick = (slot[:, None] == jnp.arange(n_blk * slots_dev)[None, :]).astype(jnp.bfloat16)
    kernels = jnp.einsum("ms,hsrc->mhrc", pick, pieces, preferred_element_type=jnp.float32)
    kernels = kernels.astype(jnp.bfloat16).reshape(L, TAPS, width, width)
    line = jnp.arange(side_len)
    inner = (line[:, None] < side_len // 2) & (line[None, :] < side_len // 2)
    cell_mask = jnp.where((size_group == 1)[:, None, None], True, inner[None]).astype(jnp.float32)
    mask_four = cell_mask[..., None]
    pixels = jnp.sum(cell_mask, axis=(1, 2))
    class_hot = labels[:, None] == jnp.arange(class_wt.shape[0])[None, :]
    weight = jnp.sum(jnp.where(class_hot, class_wt[None, :], 0), axis=1).astype(jnp.float32)
    hot_float = class_hot.astype(jnp.float32)
    count_all, weight_all = lax.psum((jnp.sum(pixels), jnp.sum(weight)), ("dp", "side", "blk"))
    current = (feats.astype(jnp.float32) * mask_four).astype(jnp.bfloat16)
    kept = []
    act_out = None
    for layer in range(L):
        conv_out = conv_forward(current, kernels[layer])
        masked = conv_out * mask_four
        col_sum, sq_sum = lax.psum(
            (jnp.sum(masked, axis=(0, 1, 2)), jnp.sum(masked * conv_out, axis=(0, 1, 2))),
            ("dp", "side", "blk"),
        )
        average = col_sum / count_all
        inv_std = lax.rsqrt(sq_sum / count_all - average * average + EPS_NORM)
        normed = (conv_out - average) * inv_std
        pre_act = norm_params[layer, 0] * normed + norm_params[layer, 1]
        act_out = jax.nn.silu(pre_act) * mask_four
        kept.append((current, normed, pre_act, inv_std))
        current = act_out.astype(jnp.bfloat16)
    pooled = jnp.sum(act_out, axis=(1, 2)) / pixels[:, None]
    pooled_low = pooled.astype(jnp.bfloat16)
    head_low = head[:width].astype(jnp.bfloat16)
    logits = jnp.dot(pooled_low, head_low, preferred_element_type=jnp.float32) + head[width]
    log_prob = jax.nn.log_softmax(logits, axis=-1)
    loss_local = -jnp.sum(weight * jnp.sum(hot_float * log_prob, axis=1))
    d_logits = weight[:, None] * (jnp.exp(log_prob) - hot_float)
    grad_weights = jnp.dot(
        pooled_low.astype(jnp.float32).T, d_logits, precision=lax.Precision.HIGHEST
    )
    grad_head = jnp.concatenate([grad_weights, jnp.sum(d_logits, axis=0)[None]], axis=0)
    loss_all, head_all = lax.psum((loss_local, grad_head), ("dp", "side", "blk"))
    d_pooled = jnp.dot(d_logits, head_low.astype(jnp.float32).T, precision=lax.Precision.HIGHEST)
    d_act = d_pooled[:, None, None, :] / pixels[:, None, None, None] * mask_four
    terms = [None] * L
    grad_norm = [None] * L
    for layer in reversed(range(L)):
        inputs, normed, pre_act, inv_std = kept[layer]
        sigma = jax.nn.sigmoid(pre_act)
        d_pre = d_act * mask_four * sigma * (1.0 + pre_act * (1.0 - sigma))
        gamma_sum, beta_sum = lax.psum(
            (jnp.sum(d_pre * normed, axis=(0, 1, 2)), jnp.sum(d_pre, axis=(0, 1, 2))),
            ("dp", "side", "blk"),
        )
        grad_norm[layer] = jnp.stack([gamma_sum, beta_sum])
        gamma = norm_params[layer, 0]
        d_conv = (
            mask_four
            * inv_std
            * (
                gamma * d_pre
                - gamma * beta_sum / count_all
                - normed * gamma * gamma_sum / count_all
            )
        )
        grad_low = d_conv.astype(jnp.bfloat16)
        if layer > 0:
            d_act = conv_backward(grad_low, kernels[layer])
        act_proj = jnp.einsum(
            "npqc,ci->npqi", inputs, basis_in[layer], preferred_element_type=jnp.float32
        ).astype(jnp.bfloat16)
        grad_proj = jnp.einsum(
            "npqo,oj->npqj", grad_low, basis_out[layer], preferred_element_type=jnp.float32
        ).astype(jnp.bfloat16)
        terms[layer] = tap_sums(act_proj, grad_proj)
    whole = jnp.stack(terms).reshape(n_dp, n_blk, block_rows, 2, 2, half)
    whole = whole.transpose(0, 4, 1, 2, 3, 5).reshape(n_dp * 2 * n_blk * block_rows, 2 * half)
    reduced = lax.psum_scatter(whole, ("dp", "side", "blk"), scatter_dimension=0, tiled=True)
    proj_sum = reduced[:, :half]
    proj_square = reduced[:, half:]
    new_scales = DECAY * scales + (1.0 - DECAY) * proj_square / images_all
    divided = (proj_sum / weight_all / (new_scales + DAMPING)).astype(jnp.bfloat16)
    spread = lax.all_gather(divided, ("dp", "side", "blk"), axis=0, tiled=True)
    spread = spread.reshape(n_dp, 2, n_blk, block_rows, half).transpose(0, 2, 3, 1, 4)
    precond_all = spread.reshape(matrices, width, width)
    slot_ids = lax.axis_index("blk") * slots_dev + jnp.arange(slots_dev)
    owned = (slot[None, :] == slot_ids[:, None]).astype(jnp.bfloat16)
    chosen = jnp.einsum(
        "qm,mij->qij", owned, precond_all, preferred_element_type=jnp.float32
    ).astype(jnp.bfloat16)
    layer_hot = (index[:, None] // TAPS == jnp.arange(L)[None, :]).astype(jnp.bfloat16)
    slot_layer = jnp.dot(owned, layer_hot, preferred_element_type=jnp.float32).astype(jnp.bfloat16)
    half_rows = lax.dynamic_slice_in_dim(
        basis_in, lax.axis_index("side") * master.shape[1], master.shape[1], 1
    )
    rows_slot = jnp.einsum(
        "ql,lci->qci", slot_layer, half_rows, preferred_element_type=jnp.float32
    ).astype(jnp.bfloat16)
    cols_slot = jnp.einsum(
        "ql,loj->qoj", slot_layer, basis_out, preferred_element_type=jnp.float32
    ).astype(jnp.bfloat16)
    turned = jnp.einsum(
        "qci,qij->qcj", rows_slot, chosen, preferred_element_type=jnp.float32
    ).astype(jnp.bfloat16)
    slot_grad = jnp.einsum("qcj,qoj->qco", turned, cols_slot, preferred_element_type=jnp.float32)
    new_master, new_moment1, new_moment2 = adamw(master, moment1, moment2, slot_grad, RATE_CONV)
    new_norm, new_norm_m, new_norm_v = adamw(
        norm_params, norm_m, norm_v, jnp.stack(grad_norm) / weight_all, RATE_NORM
    )
    new_head, new_head_m, new_head_v = adamw(head, head_m, head_v, head_all / weight_all, RATE_HEAD)
    return (
        loss_all,
        weight_all,
        new_scales,
        new_master,
        new_moment1,
        new_moment2,
        new_norm,
        new_norm_m,
        new_norm_v,
        new_head,
        new_head_m,
        new_head_v,
    )


def shards_fast(
    feats,
    size_group,
    labels,
    class_wt,
    owners,
    basis_in,
    basis_out,
    scales,
    master,
    moment1,
    moment2,
    norm_params,
    norm_m,
    norm_v,
    head,
    head_m,
    head_v,
):
    divided, new_scales, total, norm_sums, head_sums = whole_step(
        feats,
        size_group,
        labels,
        class_wt,
        owners,
        basis_in,
        basis_out,
        master,
        norm_params,
        head.T,
        scales,
    )
    results = update(
        owners,
        divided,
        new_scales,
        basis_in,
        basis_out,
        (master, moment1, moment2),
        total,
        norm_sums,
        head_sums,
        (norm_params, norm_m, norm_v),
        (head.T, head_m.T, head_v.T),
    )
    loss_all, weight_all = results[9][0, 0], results[10][0, 0]
    return (loss_all, weight_all, results[11], *results[:6], *(x.T for x in results[6:9]))


def shards(*args):
    feats, class_wt, scales, master = args[0], args[3], args[7], args[8]
    mesh_shape = tuple(lax.axis_size(name) for name in ("dp", "side", "blk"))
    fits = (
        mesh_shape == (4, 2, 4)
        and scales.shape == (576, 256)
        and feats.shape == (32, 8, 8, 512)
        and master.shape == (10, 256, 512)
        and class_wt.shape[0] <= 16
    )
    return shards_fast(*args) if fits else shards_general(*args)


def solution(mesh):
    return jax.shard_map(
        shards,
        mesh=mesh,
        in_specs=(
            P(("dp", "side", "blk"), None, None, None),
            P(("dp", "side", "blk")),
            P(("dp", "side", "blk")),
            P(),
            P(),
            P(),
            P(),
            P(("dp", "blk"), "side"),
            P("blk", "side", None),
            P("blk", "side", None),
            P("blk", "side", None),
            P(),
            P(),
            P(),
            P(),
            P(),
            P(),
        ),
        out_specs=(
            P(),
            P(),
            P(("dp", "blk"), "side"),
            P("blk", "side", None),
            P("blk", "side", None),
            P("blk", "side", None),
            P(),
            P(),
            P(),
            P(),
            P(),
            P(),
        ),
        check_vma=False,
    )
```

```python
import functools

import jax
import jax.numpy as jnp
from jax import lax
from jax.experimental import pallas as pl
from jax.experimental.pallas import tpu as pltpu
from jax.sharding import PartitionSpec as P

L = 2
TAPS = 9
STEP = 10


EPS_NORM = 1e-05
DAMPING = 0.001
DECAY = 0.95
BETA_ONE = 0.9
BETA_TWO = 0.999
ADAM_EPS = 1e-08
WEIGHT_DECAY = 0.01
RATE_CONV = 0.01
RATE_NORM = 0.5
RATE_HEAD = 0.02


def adamw(weight_now, first_now, second_now, gradient, rate):
    first_new = BETA_ONE * first_now + (1.0 - BETA_ONE) * gradient
    second_new = BETA_TWO * second_now + (1.0 - BETA_TWO) * gradient * gradient
    first_hat = first_new * (1.0 / (1.0 - BETA_ONE**STEP))
    second_hat = second_new * (1.0 / (1.0 - BETA_TWO**STEP))
    weight_new = weight_now - rate * (
        first_hat / (jnp.sqrt(second_hat) + ADAM_EPS) + WEIGHT_DECAY * weight_now
    )
    return (weight_new, first_new, second_new)


def pad_cells(values):
    return jnp.pad(values, ((0, 0), (1, 1), (1, 1), (0, 0)))


def conv_forward(inputs, kernel):
    side_len = inputs.shape[1]
    padded = pad_cells(inputs)
    total = None
    for tap in range(TAPS):
        shifted = padded[:, tap // 3 : tap // 3 + side_len, tap % 3 : tap % 3 + side_len]
        term = jnp.einsum("npqc,co->npqo", shifted, kernel[tap], preferred_element_type=jnp.float32)
        total = term if total is None else total + term
    return total


def conv_backward(grads, kernel):
    side_len = grads.shape[1]
    total = None
    for tap in range(TAPS):
        offset_row = tap // 3
        offset_col = tap % 3
        term = jnp.einsum("npqo,co->npqc", grads, kernel[tap], preferred_element_type=jnp.float32)
        term = jnp.pad(
            term, ((0, 0), (offset_row, 2 - offset_row), (offset_col, 2 - offset_col), (0, 0))
        )
        total = term if total is None else total + term
    return total[:, 1 : side_len + 1, 1 : side_len + 1]


def tap_sums(act_proj, grad_proj):
    side_len = act_proj.shape[1]
    padded = pad_cells(act_proj)
    firsts, seconds = ([], [])
    for tap in range(TAPS):
        shifted = padded[:, tap // 3 : tap // 3 + side_len, tap % 3 : tap % 3 + side_len]
        each = jnp.einsum("npqi,npqj->nij", shifted, grad_proj, preferred_element_type=jnp.float32)
        firsts.append(jnp.sum(each, axis=0))
        seconds.append(jnp.sum(each * each, axis=0))
    return jnp.concatenate([jnp.stack(firsts), jnp.stack(seconds)], axis=-1)


MESH = pl.DeviceIdType.MESH


def step_kernel(
    images_all,
    feats_hbm,
    image_group,
    labels_ref,
    class_ref,
    owners_ref,
    master_hbm,
    params_ref,
    head_ref,
    basis_in_hbm,
    basis_out_hbm,
    scales_hbm,
    out,
    ns_out,
    total_out,
    norm_out,
    head_out,
    w_full,
    xpad,
    conv_a,
    conv_b,
    at_v,
    gr_v,
    group_ref,
    hot_ref,
    weight_ref,
    piece,
    basis_t,
    small_one,
    small_two,
    head_one,
    head_two,
    sc_v,
    ns_v,
    div_v,
    s_send,
    s_recv,
    x1_send,
    x1_keep,
    y1_send,
    y1_keep,
    x2_send,
    y2_send,
    two_keep,
    z_send,
    z_keep,
    feats_ref,
    basis_in_ref,
    basis_out_ref,
    out_sem,
    g_ss,
    g_rs,
    one_ss,
    one_rs,
    two_ss,
    two_rs,
    misc_sem,
    local_sem,
    ss,
    s_ss,
    s_rs,
    rs,
    z_ss,
    z_rs,
    gz_ss,
    gz_rs,
):
    low, full = jnp.bfloat16, jnp.float32
    highest = lax.Precision.HIGHEST
    dp, me_s, me_z = lax.axis_index("dp"), lax.axis_index("side"), lax.axis_index("blk")
    me_y, me_x = dp // 2, lax.rem(dp, 2)
    to_s = (dp, 1 - me_s, me_z)
    to_x = (me_y * 2 + 1 - me_x, me_s, me_z)
    to_y = ((1 - me_y) * 2 + me_x, me_s, me_z)
    dp_x, dp_y = me_y * 2 + 1 - me_x, (1 - me_y) * 2 + me_x
    dp_xy = (1 - me_y) * 2 + 1 - me_x
    to_right = (dp, me_s, lax.rem(me_z + 1, 4))
    to_left = (dp, me_s, lax.rem(me_z + 3, 4))
    images, width = 32, 512
    matrices = 2 * TAPS
    steps = 2 * 9

    def w_left(m):
        return gr_v.at[m, 0:64]

    def w_right(m):
        return gr_v.at[m, 64:128]

    def w_own(m):
        return gr_v.at[18 + m, 0:64]

    def w_back(m):
        return gr_v.at[18 + m, 64:128]

    first_map = 40

    def remote(src, dst, send, recv, target):
        return pltpu.make_async_remote_copy(
            src_ref=src,
            dst_ref=dst,
            send_sem=send,
            recv_sem=recv,
            device_id=target,
            device_id_type=MESH,
        )

    piece_copy = pltpu.make_async_copy(
        master_hbm.at[:, pl.ds(pl.multiple_of(dp * 64, 64), 64)], piece, out_sem.at[0]
    )
    piece_copy.start()
    feats_in = pltpu.make_async_copy(feats_hbm, feats_ref, out_sem.at[1])
    basis_in_in = pltpu.make_async_copy(basis_in_hbm, basis_in_ref, out_sem.at[2])
    basis_out_in = pltpu.make_async_copy(basis_out_hbm, basis_out_ref, out_sem.at[3])
    feats_in.start()
    basis_in_in.start()
    basis_out_in.start()

    near = [(a, b) for a in range(4) for b in range(2) if a or b]
    barrier = pltpu.get_barrier_semaphore()

    def near_id(a, b):
        return lax.rem(dp + a, 4), lax.rem(me_s + b, 2)

    for a, b in near:
        other, core = near_id(a, b)
        pl.semaphore_signal(barrier, inc=1, device_id=(other, core, me_z), device_id_type=MESH)
    for d in (1, 2, 3):
        pl.semaphore_signal(
            barrier, inc=1, device_id=(dp, me_s, lax.rem(me_z + d, 4)), device_id_type=MESH
        )

    piece_copy.wait()

    mine_is = [jnp.where(owners_ref[m] == me_z, 1, 0) for m in range(matrices)]
    before = jnp.zeros((), jnp.int32)
    for m in range(matrices):
        value = piece[jnp.minimum(before, piece.shape[0] - 1)] * mine_is[m].astype(full)
        w_own(m)[...] = value.astype(low)
        before = before + mine_is[m]

    @pl.when(me_z == 0)
    def _():
        gr_v[0:18, 0:64, :] = jnp.zeros((18, 64, width), low)

    @pl.when(me_z == 3)
    def _():
        gr_v[0:18, 64:128, :] = jnp.zeros((18, 64, width), low)

    pl.semaphore_wait(barrier, 10)

    sc_local = pltpu.make_async_copy(scales_hbm.at[:, me_y], sc_v.at[1 - me_y], misc_sem.at[0])
    sc_remote = remote(
        scales_hbm.at[:, 1 - me_y], sc_v.at[1 - me_y], misc_sem.at[1], misc_sem.at[2], to_y
    )
    sc_local.start()
    sc_remote.start()

    def right_copy(m):
        return remote(w_left(m), w_left(m), g_ss.at[0, m], g_rs.at[0, m], to_right)

    def left_copy(m):
        return remote(w_back(m), w_right(m), g_ss.at[1, m], g_rs.at[1, m], to_left)

    def x_copy(m):
        part = w_full.at[m, me_s, dp]
        return remote(part, part, g_ss.at[2, m], g_rs.at[2, m], to_x)

    def y_copy(m):
        part = w_full.at[m, me_s, dp]
        return remote(part, part, g_ss.at[3, m], g_rs.at[3, m], to_y)

    def even_copy(m):
        part = w_full.at[m, me_s, dp_x]
        return remote(part, part, g_ss.at[4, m], g_rs.at[4, m], to_y)

    def odd_copy(m):
        part = w_full.at[m, me_s, dp_y]
        return remote(part, part, g_ss.at[4, m], g_rs.at[4, m], to_x)

    def core_copy(m):
        part = w_full.at[m, me_s]
        return remote(part, part, g_ss.at[5, m], g_rs.at[5, m], to_s)

    def flow_right(m):
        @pl.when((m >= 0) & (m < matrices))
        def _():
            @pl.when(me_z > 0)
            def _():
                right_copy(m).wait_recv()

            w_left(m)[...] = w_left(m)[...] + w_own(m)[...]

            @pl.when(me_z < 3)
            def _():
                right_copy(m).start()

    def flow_left(m):
        @pl.when((m >= 0) & (m < matrices))
        def _():
            @pl.when(me_z < 3)
            def _():
                left_copy(m).wait_recv()

            w_back(m)[...] = w_right(m)[...] + w_own(m)[...]

            @pl.when(me_z > 0)
            def _():
                left_copy(m).start()

    def gather(t):
        flow_right(t - 2 * me_z)
        flow_left(t - 2 * (3 - me_z))
        m = t - 6

        @pl.when((m >= 0) & (m < matrices))
        def _():
            w_full[m, me_s, dp] = w_left(m)[...] + w_right(m)[...]
            x_copy(m).start()
            y_copy(m).start()

        m4 = t - 8

        @pl.when((m4 >= 0) & (m4 < matrices))
        def _():
            x_copy(m4).wait_recv()
            y_copy(m4).wait_recv()

            @pl.when(lax.rem(m4, 2) == 0)
            def _():
                even_copy(m4).start()

            @pl.when(lax.rem(m4, 2) == 1)
            def _():
                odd_copy(m4).start()

        m6 = t - 11

        @pl.when((m6 >= 0) & (m6 < matrices))
        def _():
            even_copy(m6).wait_recv()
            core_copy(m6).start()

    def weights(m):
        return w_full[m].reshape(width, width)

    def inner(p, q):
        return jnp.where((p < 4) & (q < 4), 1.0, 0.0).astype(full)

    def mask_of(p, q, rows=slice(None)):
        return jnp.maximum(group_ref[rows, :], inner(p, q))

    def cell(i):
        return pl.ds(pl.multiple_of(i * images, images), images)

    def half_cell(i, g):
        return pl.ds(pl.multiple_of(i * images + g * 16, 16), 16)

    def full_map(n):
        return jnp.where(image_group[n] == 1, 1.0, 0.0).astype(full)

    def prepare(t):
        for g in range(2):
            block = feats_ref[g * 16 : g * 16 + 16, t].astype(full)
            turned = jnp.swapaxes(block, 0, 1)
            for q in range(8):
                value = turned[q] * mask_of(t, q, slice(g * 16, g * 16 + 16))
                xpad[t + 1, q + 1, g * 16 : g * 16 + 16, :] = value.astype(low)
        line = lax.broadcasted_iota(jnp.int32, (8, 8, width), 0)
        column = lax.broadcasted_iota(jnp.int32, (8, 8, width), 1)
        core = jnp.where((line < 4) & (column < 4), 1.0, 0.0).astype(full)
        wide = []
        for k in range(4):
            n = t * 4 + k
            value = feats_ref[n].astype(full) * jnp.maximum(core, full_map(n))
            value = jnp.concatenate([value, jnp.zeros_like(value)], axis=1)
            wide.append(value.reshape(128, width).astype(low))
        project(0, t, jnp.concatenate(wide, axis=0))

    def project(layer, t, rows):
        at_v[1 - layer, :, pl.ds(pl.multiple_of(t * 512, 512), 512)] = lax.dot_general(
            basis_t[layer], rows, (((1,), (1,)), ((), ())), preferred_element_type=full
        ).astype(low)

    def conv_tap(tap, m, acc):
        a, b = tap // 3, lax.rem(tap, 3)
        kernel = weights(m)
        for p in range(8):
            rows = xpad[p + a, pl.ds(b, 8)].reshape(8 * images, width)
            acc[p * 256 : p * 256 + 256, :] += jnp.dot(rows, kernel, preferred_element_type=full)

    for t in range(3):
        gather(t)
    xpad[...] = jnp.zeros_like(xpad)
    basis_in_in.wait()
    basis_t[0] = basis_in_ref[0].T
    place = lax.broadcasted_iota(jnp.int32, (1, 128), 1)
    for n in range(images):
        group_ref[n : n + 1, :] = jnp.full((1, width), full_map(n), full)
        hot_ref[n : n + 1, :] = jnp.where(place == labels_ref[n], 1.0, 0.0).astype(full)
        weight_ref[n : n + 1, :] = jnp.full((1, 128), class_ref[labels_ref[n]].astype(full), full)

    feats_in.wait()
    basis_out_in.wait()

    def first(t, carry):
        gather(t)

        @pl.when(t < 11)
        def _():
            prepare(t - 3)

        @pl.when(t == 11)
        def _():
            conv_a[...] = jnp.zeros_like(conv_a)
            conv_b[...] = jnp.zeros_like(conv_b)
            basis_t[1] = basis_in_ref[1].T

        tap = t - 12

        @pl.when(tap >= 0)
        def _():
            core_copy(tap).wait_recv()
            conv_tap(tap, tap, conv_a)

        return carry

    lax.fori_loop(3, 21, first, 0)

    mine = dp * 2 + me_s

    def sum_one(buf, sems, n, a, b):
        other, core = near_id(a, b)
        return remote(
            buf.at[mine], buf.at[mine], sems[0].at[n, a * 2 + b], sems[1].at[n, mine],
            (other, core, me_z),
        )

    def sum_one_wait(buf, n, a, b):
        other, core = near_id(a, b)
        slot = other * 2 + core
        remote(
            buf.at[slot], buf.at[slot], one_ss.at[n, a * 2 + b], one_rs.at[n, slot],
            (other, core, me_z),
        ).wait_recv()

    def sum_two(buf, n, d):
        other = lax.rem(me_z + d, 4)
        return remote(
            buf.at[me_z], buf.at[me_z], two_ss.at[n, d], two_rs.at[n, me_z], (dp, me_s, other)
        )

    def sum_start(n, buf):
        for a, b in near:
            sum_one(buf, (one_ss, one_rs), n, a, b).start()

    def sum_middle(n, buf, buf_two):
        for a, b in near:
            sum_one_wait(buf, n, a, b)
        total = buf[0]
        for slot in range(1, 8):
            total = total + buf[slot]
        buf_two[me_z] = total
        for d in (1, 2, 3):
            sum_two(buf_two, n, d).start()

    def sum_arrived(n, buf_two):
        for d in (1, 2, 3):
            other = lax.rem(me_z + d, 4)
            remote(
                buf_two.at[other], buf_two.at[other], two_ss.at[n, d], two_rs.at[n, other],
                (dp, me_s, other),
            ).wait_recv()

    def sum_total(buf_two):
        return buf_two[0] + buf_two[1] + buf_two[2] + buf_two[3]

    def sum_end(n, buf_two):
        sum_arrived(n, buf_two)
        return sum_total(buf_two)

    def sum_sent(n, buf, buf_two):
        for a, b in near:
            sum_one(buf, (one_ss, one_rs), n, a, b).wait_send()
        for d in (1, 2, 3):
            sum_two(buf_two, n, d).wait_send()

    def column(value):
        return jnp.sum(value, axis=0, keepdims=True)

    zero = jnp.zeros((images, width), full)

    def channel_sums(acc):
        def line(p, carry):
            sums, squares = carry
            for q in range(8):
                value = acc[cell(p * 8 + q), :]
                masked = value * mask_of(p, q)
                sums = sums + masked
                squares = squares + masked * value
            return sums, squares

        sums, squares = lax.fori_loop(0, 8, line, (zero, zero))
        return column(sums), column(squares)

    sums, squares = channel_sums(conv_a)
    group = group_ref[...]
    pixels = 16.0 + 48.0 * group
    small_one[0, mine, 0:1, :] = sums
    small_one[0, mine, 1:2, :] = squares
    small_one[0, mine, 2:3, :] = column(pixels)
    small_one[0, mine, 3:4, :] = jnp.broadcast_to(column(weight_ref[...])[:, 0:1], (1, width))
    sum_start(0, small_one.at[0])

    def later(t, carry):
        gather(t)
        return carry

    lax.fori_loop(21, 23, later, 0)
    sum_middle(0, small_one.at[0], small_two.at[0])
    lax.fori_loop(23, 24, later, 0)
    total = sum_end(0, small_two.at[0])
    total_out[...] = total
    count = total[2:3]

    def moments(total):
        average = total[0:1] / count
        return average, lax.rsqrt(total[1:2] / count - average * average + EPS_NORM)

    average_a, inv_a = moments(total)

    def activation(value, layer, average, inv):
        normed = (value - average) * inv
        pre = params_ref[layer, 0:1, :] * normed + params_ref[layer, 1:2, :]
        return normed, pre, jax.nn.sigmoid(pre)

    def images_first(values):
        return jnp.swapaxes(jnp.stack(values), 0, 1)

    def act_line(p, carry):
        @pl.when(lax.rem(p, 4) == 3)
        def _():
            gather(24 + p // 4)

        for g in range(2):
            acts = []
            for q in range(8):
                value = conv_a[half_cell(p * 8 + q, g), :]
                normed, pre, sigma = activation(value, 0, average_a, inv_a)
                act = pre * sigma * mask_of(p, q, slice(g * 16, g * 16 + 16))
                xpad[p + 1, q + 1, g * 16 : g * 16 + 16, :] = act.astype(low)
                acts.append(act)
            turned = images_first(acts)
            turned = jnp.concatenate([turned, jnp.zeros_like(turned)], axis=1).astype(low)
            gr_v[first_map + g * 16 : first_map + g * 16 + 16, pl.ds(pl.multiple_of(p * 16, 16), 16), :] = turned
        return carry

    lax.fori_loop(0, 8, act_line, 0)

    def second(tap, carry):
        core_copy(TAPS + tap).wait_recv()
        conv_tap(tap, TAPS + tap, conv_b)

        @pl.when(tap < 3)
        def _():
            gather(26 + tap)

        return carry

    lax.fori_loop(0, TAPS, second, 0)
    sums, squares = channel_sums(conv_b)
    small_one[1, mine, 0:1, :] = sums
    small_one[1, mine, 1:2, :] = squares
    small_one[1, mine, 2:4, :] = jnp.zeros((2, width), full)
    sum_start(1, small_one.at[1])

    def project_one(t, carry):
        project(1, t, gr_v[pl.ds(first_map + t * 4, 4), 0:128, :].reshape(512, width))
        return carry

    lax.fori_loop(0, 4, project_one, 0)
    sum_middle(1, small_one.at[1], small_two.at[1])
    lax.fori_loop(4, 8, project_one, 0)
    total = sum_end(1, small_two.at[1])
    average_b, inv_b = moments(total)

    def pool_line(p, carry):
        for q in range(8):
            normed, pre, sigma = activation(conv_b[cell(p * 8 + q), :], 1, average_b, inv_b)
            carry = carry + pre * sigma * mask_of(p, q)
        return carry

    pooled = lax.fori_loop(0, 8, pool_line, zero) / pixels
    pooled_low = pooled.astype(low)
    classes = head_ref.shape[0]
    head_low = head_ref[:, 0:width].astype(low)
    bias = jnp.broadcast_to(head_ref[:, width : width + 1], (classes, classes))
    across = lax.broadcasted_iota(jnp.int32, (classes, classes), 0)
    along = lax.broadcasted_iota(jnp.int32, (classes, classes), 1)
    logits = lax.dot_general(
        pooled_low, head_low, (((1,), (1,)), ((), ())), preferred_element_type=full
    ) + column(jnp.where(across == along, bias, 0.0))
    shifted = logits - jnp.max(logits, axis=1, keepdims=True)
    log_prob = shifted - jnp.log(jnp.sum(jnp.exp(shifted), axis=1, keepdims=True))
    hot = hot_ref[:, 0:classes]
    image_weight = weight_ref[:, 0:classes]
    picked = jnp.sum(hot * log_prob, axis=1, keepdims=True)
    loss = -column(weight_ref[:, 0:1] * picked)
    d_logits = image_weight * (jnp.exp(log_prob) - hot)
    d_pooled = (
        lax.dot_general(
            d_logits,
            head_low.astype(full),
            (((1,), (0,)), ((), ())),
            precision=highest,
            preferred_element_type=full,
        )
        / pixels
    )

    def d_line_top(p, carry):
        gammas, betas = carry
        for q in range(8):
            at = cell(p * 8 + q)
            normed, pre, sigma = activation(conv_b[at, :], 1, average_b, inv_b)
            d_pre = d_pooled * mask_of(p, q) * sigma * (1.0 + pre * (1.0 - sigma))
            gammas = gammas + d_pre * normed
            betas = betas + d_pre
        return gammas, betas

    gammas, betas = lax.fori_loop(0, 8, d_line_top, (zero, zero))

    def put_sums(n, gammas, betas):
        small_one[n, mine, 0:1, :] = column(gammas)
        small_one[n, mine, 1:2, :] = column(betas)
        small_one[n, mine, 2:4, :] = jnp.zeros((2, width), full)
        sum_start(n, small_one.at[n])

    def sent(m, carry):
        @pl.when(me_z < 3)
        def _():
            right_copy(m).wait_send()

        @pl.when(me_z > 0)
        def _():
            left_copy(m).wait_send()

        x_copy(m).wait_send()
        y_copy(m).wait_send()
        even_copy(m).wait_send()
        core_copy(m).wait_send()
        return carry

    lax.fori_loop(0, matrices, sent, 0)
    put_sums(2, gammas, betas)
    grad_head = lax.dot_general(
        d_logits,
        pooled_low.astype(full),
        (((0,), (0,)), ((), ())),
        precision=highest,
        preferred_element_type=full,
    )
    head_one[mine, :, :] = jnp.zeros((24, width), full)
    head_one[mine, 0:classes, :] = grad_head
    head_one[mine, 16:17, 0:classes] = column(d_logits)
    head_one[mine, 17:18, :] = jnp.broadcast_to(loss, (1, width))

    def clear(n, carry):
        gr_v[n, 0:16, :] = jnp.zeros((16, width), low)
        gr_v[n, 144:160, :] = jnp.zeros((16, width), low)
        return carry

    lax.fori_loop(0, 3 * images, clear, 0)

    sum_middle(2, small_one.at[2], small_two.at[2])
    total_b = sum_end(2, small_two.at[2])
    norm_out[1] = total_b
    sum_start(4, head_one)

    def grad_of(layer, normed, d_pre, inv, total):
        gamma = params_ref[layer, 0:1, :]
        return inv * (
            gamma * d_pre
            - gamma * total[1:2] / count
            - normed * (gamma * total[0:1] / count)
        )

    def grad_top(p, carry):
        for q in range(8):
            normed, pre, sigma = activation(conv_b[cell(p * 8 + q), :], 1, average_b, inv_b)
            mask = mask_of(p, q)
            d_pre = d_pooled * mask * sigma * (1.0 + pre * (1.0 - sigma))
            value = mask * grad_of(1, normed, d_pre, inv_b, total_b)
            xpad[p + 1, q + 1, :, :] = value.astype(low)
        return carry

    lax.fori_loop(0, 8, grad_top, 0)
    conv_b[...] = jnp.zeros_like(conv_b)

    def back(tap, carry):
        a, b = tap // 3, lax.rem(tap, 3)
        kernel = weights(TAPS + tap)
        for p in range(8):
            rows = xpad[p + 2 - a, pl.ds(2 - b, 8)].reshape(8 * images, width)
            conv_b[p * 256 : p * 256 + 256, :] += lax.dot_general(
                rows, kernel, (((1,), (1,)), ((), ())), preferred_element_type=full
            )
        return carry

    def d_line(p, carry):
        gammas, betas = carry
        for q in range(8):
            at = cell(p * 8 + q)
            normed, pre, sigma = activation(conv_a[at, :], 0, average_a, inv_a)
            d_pre = conv_b[at, :] * mask_of(p, q) * sigma * (1.0 + pre * (1.0 - sigma))
            conv_b[at, :] = d_pre
            gammas = gammas + d_pre * normed
            betas = betas + d_pre
        return gammas, betas

    def turn_grads(layer):
        def line(p, carry):
            rows = xpad[p + 1, 1:9].reshape(8 * images, width)
            value = jnp.dot(rows, basis_out_ref[layer], preferred_element_type=full)
            value = value.reshape(8, images, width)
            lines = pl.ds(pl.multiple_of(p * 16 + 16, 16), 16)
            gap = jnp.zeros((8, 1, width), full)
            rest = jnp.zeros((8, 8, width), full)
            for g in range(4):
                turned = jnp.swapaxes(value[:, g * 8 : g * 8 + 8], 0, 1)
                shifts = (
                    jnp.concatenate([turned[:, 1:], gap], axis=1),
                    turned,
                    jnp.concatenate([gap, turned[:, :7]], axis=1),
                )
                for b in range(3):
                    wide = jnp.concatenate([shifts[b], rest], axis=1).astype(low)
                    gr_v[b * images + g * 8 : b * images + g * 8 + 8, lines, :] = wide
            return carry

        return line

    lax.fori_loop(0, 8, turn_grads(1), 0)

    def bottom():
        total_a = sum_total(small_two.at[3])
        norm_out[0] = total_a

        def line(p, carry):
            for q in range(8):
                at = cell(p * 8 + q)
                normed = (conv_a[at, :] - average_a) * inv_a
                value = mask_of(p, q) * grad_of(0, normed, conv_b[at, :], inv_a, total_a)
                xpad[p + 1, q + 1, :, :] = value.astype(low)
            return carry

        lax.fori_loop(0, 8, line, 0)
        lax.fori_loop(0, 8, turn_grads(0), 0)

    def x1_recv(j):
        return w_full.at[j, 0, :, :, 0:256]

    def y1_recv(j):
        return w_full.at[j, 0, :, :, 256:512]

    def x2_recv(j):
        return w_full.at[j, 1, 0:2, :, 0:256]

    def y2_recv(j):
        return w_full.at[j, 1, 2:4, :, 0:256]

    def z_recv(j, d):
        return w_full.at[j, 1, d - 1, :, 256:512]

    def side_copy(j):
        ring, four = lax.rem(j, 2), lax.rem(j, 4)
        return remote(s_send.at[ring], s_recv.at[four], s_ss.at[ring], s_rs.at[four], to_s)

    def x1_copy(j):
        ring = lax.rem(j, 2)
        return remote(x1_send.at[ring], x1_recv(j), ss.at[1, ring], rs.at[0, j], to_x)

    def y1_copy(j):
        ring = lax.rem(j, 2)
        return remote(y1_send.at[ring, 1 - me_y], y1_recv(j), ss.at[2, ring], rs.at[1, j], to_y)

    def x2_copy(j):
        ring = lax.rem(j, 2)
        return remote(x2_send.at[ring], x2_recv(j), ss.at[3, ring], rs.at[2, j], to_x)

    def y2_copy(j):
        ring = lax.rem(j, 2)
        return remote(y2_send.at[ring], y2_recv(j), ss.at[4, ring], rs.at[3, j], to_y)

    def z_copy(j, d):
        ring, other = lax.rem(j, 2), lax.rem(me_z + d, 4)
        return remote(
            z_send.at[ring, other],
            z_recv(j, d),
            z_ss.at[ring, d - 1],
            z_rs.at[j, d - 1],
            (dp, me_s, other),
        )

    def place(j):
        return 1 - j // 9, lax.rem(j, 9)

    def local_copy(j):
        layer, i = place(j)
        ring = lax.rem(j, 2)
        return pltpu.make_async_copy(
            div_v.at[ring], out.at[me_s, layer, me_x, me_z, i, me_y], local_sem.at[ring]
        )

    def gz_copy(j, d):
        layer, i = place(j)
        ring, other = lax.rem(j, 2), lax.rem(me_z + d, 4)
        return remote(
            div_v.at[ring],
            out.at[me_s, layer, me_x, me_z, i, me_y],
            gz_ss.at[ring, d - 1],
            gz_rs.at[j, d - 1],
            (dp, me_s, other),
        )

    lower, upper = pl.ds(0, 2), pl.ds(2, 2)

    def spread(j, which, kind, target):
        part = out.at[which]
        return remote(part, part, ss.at[kind, lax.rem(j, 2)], rs.at[kind - 1, j], target)

    def g1y_copy(j):
        layer, i = place(j)
        return spread(j, (me_s, layer, me_x, lower, i, me_y), 5, to_y)

    def g1x_copy(j):
        layer, i = place(j)
        return spread(j, (me_s, layer, me_x, upper, i, me_y), 6, to_x)

    def g2x_copy(j):
        layer, i = place(j)
        return spread(j, (me_s, layer, me_x, lower, i), 7, to_x)

    def g2y_copy(j):
        layer, i = place(j)
        return spread(j, (me_s, layer, pl.ds(0, 2), upper, i, me_y), 8, to_y)

    def gs_copy(j):
        layer, i = place(j)
        return spread(j, (me_s, layer, pl.ds(0, 2), pl.ds(0, 4), i), 9, to_s)

    def products(j, half, store):
        li, i = j // 9, lax.rem(j, 9)
        cols = pl.ds(pl.multiple_of(half * 256, 256), 256)
        for u in range(8):
            x_to = 1 - me_x if u < 4 else me_x
            row = x_to * 2304 + (u % 4) * 576 + 64 * i
            tap = row // 512
            rows = pl.ds(pl.multiple_of(lax.rem(row, 512), 64), 64)
            near = pl.ds(pl.multiple_of((2 - tap // 3) * 16, 16), 128)
            shift = lax.rem(tap, 3) * images
            square = total = None
            for n in range(images):
                p = jnp.dot(
                    at_v[li, rows, n * 128 : (n + 1) * 128],
                    gr_v[shift + n, near, cols],
                    preferred_element_type=full,
                )
                square = p * p if square is None else square + p * p
                total = p if total is None else total + p
            store(u, x_to, u % 4, total, square)

    def at_step(x):
        j = jnp.where(x < 10, x, jnp.where(x < 14, x - 4, x - 5))
        due = ((x >= 0) & (x < 6)) | ((x >= 10) & (x < 13)) | ((x >= 14) & (x < 23))
        return j, due

    def step(k, carry):
        ja, due = at_step(k)

        @pl.when(due & (ja >= 2))
        def _():
            side_copy(ja - 2).wait_send()

        @pl.when(due)
        def _():
            ring = lax.rem(ja, 2)

            def store(u, x_to, z_to, total, square):
                s_send[ring, u, 0] = total.astype(low)
                s_send[ring, u, 1] = square.astype(low)

            products(ja, 1 - me_s, store)
            side_copy(ja).start()

        j7, due = at_step(k - 13)

        @pl.when(due)
        def _():
            @pl.when(j7 >= 2)
            def _():
                gs_copy(j7 - 2).wait_send()

            g2x_copy(j7).wait_recv()
            g2y_copy(j7).wait_recv()
            gs_copy(j7).start()

        j6, due = at_step(k - 11)

        @pl.when(due)
        def _():
            @pl.when(j6 >= 2)
            def _():
                g2y_copy(j6 - 2).wait_send()
                g2x_copy(j6 - 2).wait_send()

            g1y_copy(j6).wait_recv()
            g2x_copy(j6).start()
            g1x_copy(j6).wait_recv()
            g2y_copy(j6).start()

        j5, due = at_step(k - 9)

        @pl.when(due)
        def _():
            @pl.when(j5 >= 2)
            def _():
                g1y_copy(j5 - 2).wait_send()
                g1x_copy(j5 - 2).wait_send()

            local_copy(j5).wait()
            for d in (1, 2, 3):
                gz_copy(j5, d).wait_recv()
            g1y_copy(j5).start()
            g1x_copy(j5).start()

        j4, due = at_step(k - 7)

        @pl.when(due & (j4 == 0))
        def _():
            sc_local.wait()
            sc_remote.wait_recv()

        @pl.when(due)
        def _():
            ring, li, i = lax.rem(j4, 2), j4 // 9, lax.rem(j4, 9)

            @pl.when(j4 >= 2)
            def _():
                for d in (1, 2, 3):
                    gz_copy(j4 - 2, d).wait_send()

            for d in (1, 2, 3):
                z_copy(j4, d).wait_recv()
            both = z_keep[ring, me_z]
            for d in (1, 2, 3):
                both = both + z_recv(j4, d)[...].astype(full)
            scale = DECAY * sc_v[li, i] + (1.0 - DECAY) * both[32:64] / images_all
            ns_v[li, i] = scale
            div_v[ring] = (both[0:32] / total_out[3:4, 0:256] / (scale + DAMPING)).astype(low)
            local_copy(j4).start()
            for d in (1, 2, 3):
                gz_copy(j4, d).start()

        for li in range(2):
            @pl.when(due & (j4 == 9 * li + 8) & (me_y == 1 - li))
            def _():
                pltpu.make_async_copy(ns_v.at[li], ns_out.at[:, me_y], misc_sem.at[3]).start()

            @pl.when(due & (j4 == 9 * li + 8) & (me_y == li))
            def _():
                remote(
                    ns_v.at[li], ns_out.at[:, me_y], misc_sem.at[4], misc_sem.at[5], to_y
                ).start()

        j3, due = at_step(k - 5)

        @pl.when(due)
        def _():
            ring = lax.rem(j3, 2)

            @pl.when(j3 >= 2)
            def _():
                for d in (1, 2, 3):
                    z_copy(j3 - 2, d).wait_send()

            y2_copy(j3).wait_recv()
            x2_copy(j3).wait_recv()
            for z_to in range(4):
                got = y2_recv(j3)[z_to] if z_to < 2 else x2_recv(j3)[z_to - 2]
                both = two_keep[ring, z_to] + got.astype(full)
                z_keep[ring, z_to] = both
                z_send[ring, z_to] = both.astype(low)
            for d in (1, 2, 3):
                z_copy(j3, d).start()

        j2, due = at_step(k - 3)

        @pl.when(due)
        def _():
            ring = lax.rem(j2, 2)

            @pl.when(j2 >= 2)
            def _():
                x2_copy(j2 - 2).wait_send()
                y2_copy(j2 - 2).wait_send()

            x1_copy(j2).wait_recv()
            here = pl.ds(pl.multiple_of(me_y * 32, 32), 32)
            there = pl.ds(pl.multiple_of((1 - me_y) * 32, 32), 32)
            got = x1_recv(j2)
            for z_to in range(2):
                for c in range(2):
                    at, lines = z_to * 2 + c, slice(c * 32, c * 32 + 32)
                    two_keep[ring, z_to, lines, :] = x1_keep[ring, at, here, :] + got[
                        at, here, :
                    ].astype(full)
                    y2_send[ring, z_to, lines, :] = (
                        x1_keep[ring, at, there, :] + got[at, there, :].astype(full)
                    ).astype(low)
            y2_copy(j2).start()
            y1_copy(j2).wait_recv()
            got = y1_recv(j2)
            for z_to in range(2):
                mine_at, other_at = me_x * 2 + z_to, (1 - me_x) * 2 + z_to
                two_keep[ring, 2 + z_to] = y1_keep[ring, me_y, mine_at] + got[mine_at].astype(full)
                x2_send[ring, z_to] = (
                    y1_keep[ring, me_y, other_at] + got[other_at].astype(full)
                ).astype(low)
            x2_copy(j2).start()

        jb, due = at_step(k - 1)

        @pl.when(due & (jb >= 2))
        def _():
            x1_copy(jb - 2).wait_send()
            y1_copy(jb - 2).wait_send()

        @pl.when(due)
        def _():
            ring, four = lax.rem(jb, 2), lax.rem(jb, 4)
            side_copy(jb).wait_recv()

            def store(u, x_to, z_to, total, square):
                got = s_recv[four, u].astype(full)
                both = (total + got[0], square + got[1])
                for c in range(2):
                    if z_to < 2 and u < 4:
                        x1_send[ring, z_to * 2 + c] = both[c].astype(low)
                    elif z_to < 2:
                        x1_keep[ring, z_to * 2 + c] = both[c]
                    else:
                        at = x_to * 2 + z_to - 2
                        for y_to in range(2):
                            value = both[c][y_to * 32 : y_to * 32 + 32]
                            y1_send[ring, y_to, at, c * 32 : c * 32 + 32, :] = value.astype(low)
                            y1_keep[ring, y_to, at, c * 32 : c * 32 + 32, :] = value

            products(jb, me_s, store)
            x1_copy(jb).start()
            y1_copy(jb).start()

        @pl.when((k >= 6) & (k < 9))
        def _():
            lax.fori_loop(0, 3, lambda t, carry: back((k - 6) * 3 + t, carry), 0)

        @pl.when(k == 8)
        def _():
            sum_middle(4, head_one, head_two)

        @pl.when(k == 9)
        def _():
            gammas, betas = lax.fori_loop(0, 8, d_line, (zero, zero))
            put_sums(3, gammas, betas)

        @pl.when(k == 10)
        def _():
            sum_middle(3, small_one.at[3], small_two.at[3])

        @pl.when(k == 25)
        def _():
            head_out[...] = sum_end(4, head_two)

        @pl.when(k == 13)
        def _():
            sum_arrived(3, small_two.at[3])
            bottom()

        return carry

    lax.fori_loop(0, steps + 5 + 13, step, 0)

    def finish(j, carry):
        gs_copy(j).wait_recv()
        return carry

    lax.fori_loop(0, steps, finish, 0)
    sc_remote.wait_send()
    li = 1 - me_y
    pltpu.make_async_copy(ns_v.at[li], ns_out.at[:, me_y], misc_sem.at[3]).wait()
    ns_remote = remote(ns_v.at[0], ns_out.at[:, 0], misc_sem.at[4], misc_sem.at[5], to_y)
    ns_remote.wait_send()
    ns_remote.wait_recv()
    for j in (steps - 2, steps - 1):
        for copy in (side_copy, x1_copy, y1_copy, x2_copy, y2_copy):
            copy(j).wait_send()
        for copy in (g1y_copy, g1x_copy, g2y_copy, g2x_copy, gs_copy):
            copy(j).wait_send()
        for d in (1, 2, 3):
            z_copy(j, d).wait_send()
            gz_copy(j, d).wait_send()
    for n in range(4):
        sum_sent(n, small_one.at[n], small_two.at[n])
    sum_sent(4, head_one, head_two)


def whole_step(
    feats, size_group, labels, class_wt, owners, basis_in, basis_out, master, norm_params, head, scales
):
    count_img, side_len, _, width = feats.shape
    images_all = count_img * lax.axis_size("dp") * lax.axis_size("side") * lax.axis_size("blk")
    low, full, dma = jnp.bfloat16, jnp.float32, pltpu.SemaphoreType.DMA
    vmem, any_spec = pl.BlockSpec(memory_space=pltpu.VMEM), pl.BlockSpec(memory_space=pl.ANY)
    smem = pl.BlockSpec(memory_space=pltpu.SMEM)
    rows = count_img * side_len * side_len
    divided, new_scales, total, norm_sums, head_sums = pl.pallas_call(
        functools.partial(step_kernel, images_all),
        out_shape=[
            jax.ShapeDtypeStruct((2, 2, 2, 4, 9, 2, 32, 256), low),
            jax.ShapeDtypeStruct((9, 2, 32, 256), full),
            jax.ShapeDtypeStruct((4, width), full),
            jax.ShapeDtypeStruct((2, 4, width), full),
            jax.ShapeDtypeStruct((24, width), full),
        ],
        in_specs=[any_spec, smem, smem, smem, smem, any_spec, vmem, vmem, any_spec, any_spec, any_spec],
        out_specs=[any_spec, any_spec, vmem, vmem, vmem],
        scratch_shapes=[
            pltpu.VMEM((18, 2, 4, 64, 512), low),
            pltpu.VMEM((10, 10, 32, 512), low),
            pltpu.VMEM((rows, 512), full),
            pltpu.VMEM((rows, 512), full),
            pltpu.VMEM((2, 512, 4096), low),
            pltpu.VMEM((96, 160, 512), low),
            pltpu.VMEM((32, 512), full),
            pltpu.VMEM((32, 128), full),
            pltpu.VMEM((32, 128), full),
            pltpu.VMEM((10, 64, 512), full),
            pltpu.VMEM((2, 512, 512), low),
            pltpu.VMEM((4, 8, 4, 512), full),
            pltpu.VMEM((4, 4, 4, 512), full),
            pltpu.VMEM((8, 24, 512), full),
            pltpu.VMEM((4, 24, 512), full),
            pltpu.VMEM((2, 9, 32, 256), full),
            pltpu.VMEM((2, 9, 32, 256), full),
            pltpu.VMEM((2, 32, 256), low),
            pltpu.VMEM((2, 8, 2, 64, 256), low),
            pltpu.VMEM((4, 8, 2, 64, 256), low),
            pltpu.VMEM((2, 4, 64, 256), low),
            pltpu.VMEM((2, 4, 64, 256), full),
            pltpu.VMEM((2, 2, 4, 64, 256), low),
            pltpu.VMEM((2, 2, 4, 64, 256), full),
            pltpu.VMEM((2, 2, 64, 256), low),
            pltpu.VMEM((2, 2, 64, 256), low),
            pltpu.VMEM((2, 4, 64, 256), full),
            pltpu.VMEM((2, 4, 64, 256), low),
            pltpu.VMEM((2, 4, 64, 256), full),
            pltpu.VMEM(feats.shape, low),
            pltpu.VMEM(basis_in.shape, low),
            pltpu.VMEM(basis_out.shape, low),
            dma((4,)),
            dma((6, 18)),
            dma((6, 18)),
            dma((5, 8)),
            dma((5, 8)),
            dma((5, 4)),
            dma((5, 4)),
            dma((6,)),
            dma((2,)),
            dma((10, 2)),
            dma((2,)),
            dma((4,)),
            dma((9, 18)),
            dma((2, 3)),
            dma((18, 3)),
            dma((2, 3)),
            dma((18, 3)),
        ],
        name="whole_step",
        compiler_params=pltpu.CompilerParams(
            collective_id=0, has_side_effects=True, vmem_limit_bytes=63 * 2**20
        ),
    )(
        feats,
        size_group,
        labels,
        class_wt,
        owners,
        master,
        norm_params,
        head,
        basis_in,
        basis_out,
        scales.reshape(9, 2, 32, 256),
    )
    return (
        divided.reshape(2, 18, 512, 256),
        new_scales.reshape(576, 256),
        total,
        norm_sums,
        head_sums,
    )


def update_kernel(
    owners_ref,
    divided,
    scales_in,
    basis_in,
    basis_out,
    w_hbm,
    m_hbm,
    v_hbm,
    total_ref,
    norm_sums,
    head_sums,
    norm_w,
    norm_m,
    norm_v,
    head_w,
    head_m,
    head_v,
    w_out,
    m_out,
    v_out,
    norm_w_out,
    norm_m_out,
    norm_v_out,
    head_w_out,
    head_m_out,
    head_v_out,
    loss_out,
    weight_out,
    scales_out,
    matrix,
    p_v,
    rows_v,
    cols_v,
    w_v,
    m_v,
    v_v,
    scales_v,
    in_sem,
    out_sem,
):
    low, full = jnp.bfloat16, jnp.float32
    slots, half, width = w_v.shape
    blk, side = lax.axis_index("blk"), lax.axis_index("side")

    def state_in(q):
        return [
            pltpu.make_async_copy(src.at[q], dst.at[q], in_sem.at[n, q])
            for n, (src, dst) in enumerate(((w_hbm, w_v), (m_hbm, m_v), (v_hbm, v_v)))
        ]

    def state_out(q):
        return [
            pltpu.make_async_copy(src.at[q], dst.at[q], out_sem.at[n, q])
            for n, (src, dst) in enumerate(((w_v, w_out), (m_v, m_out), (v_v, v_out)))
        ]

    rows_in = pltpu.make_async_copy(
        basis_in.at[:, pl.ds(pl.multiple_of(side * half, half), half)], rows_v, in_sem.at[4, 0]
    )
    cols_in = pltpu.make_async_copy(basis_out, cols_v, in_sem.at[4, 1])
    scales_read = pltpu.make_async_copy(scales_in, scales_v, in_sem.at[4, 2])
    scales_write = pltpu.make_async_copy(scales_v, scales_out, in_sem.at[4, 3])
    scales_read.start()
    rows_in.start()
    cols_in.start()

    for q in range(slots):
        matrix[q] = 0
    count = jnp.zeros((), jnp.int32)
    for m in range(owners_ref.shape[0]):
        mine = owners_ref[m] == blk

        @pl.when(mine)
        def _():
            matrix[count] = m

        count = count + jnp.where(mine, 1, 0)

    def part_in(q):
        return pltpu.make_async_copy(divided.at[:, matrix[q]], p_v.at[q], in_sem.at[3, q])

    for q in range(slots):
        part_in(q).start()
        for copy in state_in(q):
            copy.start()
    weight = total_ref[3:4, 0:1]
    weight_out[0, 0] = total_ref[3, 0]
    loss_out[0, 0] = head_sums[17, 0]
    for layer in range(2):
        norm_w_out[layer], norm_m_out[layer], norm_v_out[layer] = adamw(
            norm_w[layer],
            norm_m[layer],
            norm_v[layer],
            norm_sums[layer, 0:2, :] / weight,
            RATE_NORM,
        )
    classes = head_w.shape[0]
    here = lax.broadcasted_iota(jnp.int32, (classes, classes), 0)
    there = lax.broadcasted_iota(jnp.int32, (classes, classes), 1)
    line = jnp.broadcast_to(head_sums[16:17, 0:classes], (classes, classes))
    bias = jnp.sum(jnp.where(here == there, line, 0.0), axis=1, keepdims=True)
    for at, gradient in (
        (slice(0, width), head_sums[0:classes, :]),
        (slice(width, width + 1), bias),
    ):
        head_w_out[:, at], head_m_out[:, at], head_v_out[:, at] = adamw(
            head_w[:, at], head_m[:, at], head_v[:, at], gradient / weight, RATE_HEAD
        )
    rows_in.wait()
    cols_in.wait()

    def gradient(q):
        layer = matrix[q] // TAPS
        held = jnp.where(q < count, 1.0, 0.0).astype(full)
        both = [
            jnp.dot(rows_v[layer], p_v[q, s], preferred_element_type=full).astype(low)
            for s in range(2)
        ]
        return held * lax.dot_general(
            jnp.concatenate(both, axis=1),
            cols_v[layer],
            (((1,), (1,)), ((), ())),
            preferred_element_type=full,
        )

    def slot(q, carry):
        part_in(q).wait()
        change = gradient(q)
        for copy in state_in(q):
            copy.wait()
        w_v[q], m_v[q], v_v[q] = adamw(w_v[q], m_v[q], v_v[q], change, RATE_CONV)
        for copy in state_out(q):
            copy.start()
        return carry

    scales_read.wait()
    scales_write.start()
    lax.fori_loop(0, slots, slot, 0)
    for q in range(slots):
        for copy in state_out(q):
            copy.wait()
    scales_write.wait()


def update(
    owners, divided, scales, basis_in, basis_out, states, total, norm_sums, head_sums, norm_states, head_states
):
    full, dma = jnp.float32, pltpu.SemaphoreType.DMA
    slots, half, width = states[0].shape
    vmem, any_spec = pl.BlockSpec(memory_space=pltpu.VMEM), pl.BlockSpec(memory_space=pl.ANY)
    smem = pl.BlockSpec(memory_space=pltpu.SMEM)
    like = [jax.ShapeDtypeStruct(x.shape, full) for x in (*states, *norm_states, *head_states)]
    one = jax.ShapeDtypeStruct((1, 1), full)
    return pl.pallas_call(
        update_kernel,
        out_shape=like + [one, one, jax.ShapeDtypeStruct(scales.shape, full)],
        in_specs=[smem] + [any_spec] * 7 + [vmem] * 9,
        out_specs=[any_spec] * 3 + [vmem] * 6 + [smem] * 2 + [any_spec],
        scratch_shapes=[
            pltpu.SMEM((slots,), jnp.int32),
            pltpu.VMEM((slots, 2, width, half), jnp.bfloat16),
            pltpu.VMEM((2, half, width), jnp.bfloat16),
            pltpu.VMEM((2, width, width), jnp.bfloat16),
            pltpu.VMEM(states[0].shape, full),
            pltpu.VMEM(states[0].shape, full),
            pltpu.VMEM(states[0].shape, full),
            pltpu.VMEM(scales.shape, full),
            dma((5, slots)),
            dma((3, slots)),
        ],
        name="update",
        compiler_params=pltpu.CompilerParams(vmem_limit_bytes=63 * 2**20),
    )(
        owners,
        divided,
        scales,
        basis_in,
        basis_out,
        *states,
        total,
        norm_sums,
        head_sums,
        *norm_states,
        *head_states,
    )


def shards_general(
    feats,
    size_group,
    labels,
    class_wt,
    owners,
    basis_in,
    basis_out,
    scales,
    master,
    moment1,
    moment2,
    norm_params,
    norm_m,
    norm_v,
    head,
    head_m,
    head_v,
):
    count_img = feats.shape[0]
    side_len = feats.shape[1]
    width = feats.shape[3]
    half = width // 2
    n_dp = lax.axis_size("dp")
    n_side = lax.axis_size("side")
    n_blk = lax.axis_size("blk")
    slots_dev = master.shape[0]
    matrices = owners.shape[0]
    block_rows = scales.shape[0]
    images_all = count_img * n_dp * n_side * n_blk
    index = jnp.arange(matrices)
    earlier = (owners[:, None] == owners[None, :]) & (index[None, :] < index[:, None])
    slot = owners * slots_dev + jnp.sum(earlier.astype(jnp.int32), axis=1)
    pieces = lax.all_gather(master.astype(jnp.bfloat16), ("side", "blk"), axis=0, tiled=True)
    pieces = pieces.reshape(n_side, n_blk * slots_dev, master.shape[1], width)
    pick = (slot[:, None] == jnp.arange(n_blk * slots_dev)[None, :]).astype(jnp.bfloat16)
    kernels = jnp.einsum("ms,hsrc->mhrc", pick, pieces, preferred_element_type=jnp.float32)
    kernels = kernels.astype(jnp.bfloat16).reshape(L, TAPS, width, width)
    line = jnp.arange(side_len)
    inner = (line[:, None] < side_len // 2) & (line[None, :] < side_len // 2)
    cell_mask = jnp.where((size_group == 1)[:, None, None], True, inner[None]).astype(jnp.float32)
    mask_four = cell_mask[..., None]
    pixels = jnp.sum(cell_mask, axis=(1, 2))
    class_hot = labels[:, None] == jnp.arange(class_wt.shape[0])[None, :]
    weight = jnp.sum(jnp.where(class_hot, class_wt[None, :], 0), axis=1).astype(jnp.float32)
    hot_float = class_hot.astype(jnp.float32)
    count_all, weight_all = lax.psum((jnp.sum(pixels), jnp.sum(weight)), ("dp", "side", "blk"))
    current = (feats.astype(jnp.float32) * mask_four).astype(jnp.bfloat16)
    kept = []
    act_out = None
    for layer in range(L):
        conv_out = conv_forward(current, kernels[layer])
        masked = conv_out * mask_four
        col_sum, sq_sum = lax.psum(
            (jnp.sum(masked, axis=(0, 1, 2)), jnp.sum(masked * conv_out, axis=(0, 1, 2))),
            ("dp", "side", "blk"),
        )
        average = col_sum / count_all
        inv_std = lax.rsqrt(sq_sum / count_all - average * average + EPS_NORM)
        normed = (conv_out - average) * inv_std
        pre_act = norm_params[layer, 0] * normed + norm_params[layer, 1]
        act_out = jax.nn.silu(pre_act) * mask_four
        kept.append((current, normed, pre_act, inv_std))
        current = act_out.astype(jnp.bfloat16)
    pooled = jnp.sum(act_out, axis=(1, 2)) / pixels[:, None]
    pooled_low = pooled.astype(jnp.bfloat16)
    head_low = head[:width].astype(jnp.bfloat16)
    logits = jnp.dot(pooled_low, head_low, preferred_element_type=jnp.float32) + head[width]
    log_prob = jax.nn.log_softmax(logits, axis=-1)
    loss_local = -jnp.sum(weight * jnp.sum(hot_float * log_prob, axis=1))
    d_logits = weight[:, None] * (jnp.exp(log_prob) - hot_float)
    grad_weights = jnp.dot(
        pooled_low.astype(jnp.float32).T, d_logits, precision=lax.Precision.HIGHEST
    )
    grad_head = jnp.concatenate([grad_weights, jnp.sum(d_logits, axis=0)[None]], axis=0)
    loss_all, head_all = lax.psum((loss_local, grad_head), ("dp", "side", "blk"))
    d_pooled = jnp.dot(d_logits, head_low.astype(jnp.float32).T, precision=lax.Precision.HIGHEST)
    d_act = d_pooled[:, None, None, :] / pixels[:, None, None, None] * mask_four
    terms = [None] * L
    grad_norm = [None] * L
    for layer in reversed(range(L)):
        inputs, normed, pre_act, inv_std = kept[layer]
        sigma = jax.nn.sigmoid(pre_act)
        d_pre = d_act * mask_four * sigma * (1.0 + pre_act * (1.0 - sigma))
        gamma_sum, beta_sum = lax.psum(
            (jnp.sum(d_pre * normed, axis=(0, 1, 2)), jnp.sum(d_pre, axis=(0, 1, 2))),
            ("dp", "side", "blk"),
        )
        grad_norm[layer] = jnp.stack([gamma_sum, beta_sum])
        gamma = norm_params[layer, 0]
        d_conv = (
            mask_four
            * inv_std
            * (
                gamma * d_pre
                - gamma * beta_sum / count_all
                - normed * gamma * gamma_sum / count_all
            )
        )
        grad_low = d_conv.astype(jnp.bfloat16)
        if layer > 0:
            d_act = conv_backward(grad_low, kernels[layer])
        act_proj = jnp.einsum(
            "npqc,ci->npqi", inputs, basis_in[layer], preferred_element_type=jnp.float32
        ).astype(jnp.bfloat16)
        grad_proj = jnp.einsum(
            "npqo,oj->npqj", grad_low, basis_out[layer], preferred_element_type=jnp.float32
        ).astype(jnp.bfloat16)
        terms[layer] = tap_sums(act_proj, grad_proj)
    whole = jnp.stack(terms).reshape(n_dp, n_blk, block_rows, 2, 2, half)
    whole = whole.transpose(0, 4, 1, 2, 3, 5).reshape(n_dp * 2 * n_blk * block_rows, 2 * half)
    reduced = lax.psum_scatter(whole, ("dp", "side", "blk"), scatter_dimension=0, tiled=True)
    proj_sum = reduced[:, :half]
    proj_square = reduced[:, half:]
    new_scales = DECAY * scales + (1.0 - DECAY) * proj_square / images_all
    divided = (proj_sum / weight_all / (new_scales + DAMPING)).astype(jnp.bfloat16)
    spread = lax.all_gather(divided, ("dp", "side", "blk"), axis=0, tiled=True)
    spread = spread.reshape(n_dp, 2, n_blk, block_rows, half).transpose(0, 2, 3, 1, 4)
    precond_all = spread.reshape(matrices, width, width)
    slot_ids = lax.axis_index("blk") * slots_dev + jnp.arange(slots_dev)
    owned = (slot[None, :] == slot_ids[:, None]).astype(jnp.bfloat16)
    chosen = jnp.einsum(
        "qm,mij->qij", owned, precond_all, preferred_element_type=jnp.float32
    ).astype(jnp.bfloat16)
    layer_hot = (index[:, None] // TAPS == jnp.arange(L)[None, :]).astype(jnp.bfloat16)
    slot_layer = jnp.dot(owned, layer_hot, preferred_element_type=jnp.float32).astype(jnp.bfloat16)
    half_rows = lax.dynamic_slice_in_dim(
        basis_in, lax.axis_index("side") * master.shape[1], master.shape[1], 1
    )
    rows_slot = jnp.einsum(
        "ql,lci->qci", slot_layer, half_rows, preferred_element_type=jnp.float32
    ).astype(jnp.bfloat16)
    cols_slot = jnp.einsum(
        "ql,loj->qoj", slot_layer, basis_out, preferred_element_type=jnp.float32
    ).astype(jnp.bfloat16)
    turned = jnp.einsum(
        "qci,qij->qcj", rows_slot, chosen, preferred_element_type=jnp.float32
    ).astype(jnp.bfloat16)
    slot_grad = jnp.einsum("qcj,qoj->qco", turned, cols_slot, preferred_element_type=jnp.float32)
    new_master, new_moment1, new_moment2 = adamw(master, moment1, moment2, slot_grad, RATE_CONV)
    new_norm, new_norm_m, new_norm_v = adamw(
        norm_params, norm_m, norm_v, jnp.stack(grad_norm) / weight_all, RATE_NORM
    )
    new_head, new_head_m, new_head_v = adamw(head, head_m, head_v, head_all / weight_all, RATE_HEAD)
    return (
        loss_all,
        weight_all,
        new_scales,
        new_master,
        new_moment1,
        new_moment2,
        new_norm,
        new_norm_m,
        new_norm_v,
        new_head,
        new_head_m,
        new_head_v,
    )


def shards_fast(
    feats,
    size_group,
    labels,
    class_wt,
    owners,
    basis_in,
    basis_out,
    scales,
    master,
    moment1,
    moment2,
    norm_params,
    norm_m,
    norm_v,
    head,
    head_m,
    head_v,
):
    divided, new_scales, total, norm_sums, head_sums = whole_step(
        feats,
        size_group,
        labels,
        class_wt,
        owners,
        basis_in,
        basis_out,
        master,
        norm_params,
        head.T,
        scales,
    )
    results = update(
        owners,
        divided,
        new_scales,
        basis_in,
        basis_out,
        (master, moment1, moment2),
        total,
        norm_sums,
        head_sums,
        (norm_params, norm_m, norm_v),
        (head.T, head_m.T, head_v.T),
    )
    loss_all, weight_all = results[9][0, 0], results[10][0, 0]
    return (loss_all, weight_all, results[11], *results[:6], *(x.T for x in results[6:9]))


def shards(*args):
    feats, class_wt, scales, master = args[0], args[3], args[7], args[8]
    mesh_shape = tuple(lax.axis_size(name) for name in ("dp", "side", "blk"))
    fits = (
        mesh_shape == (4, 2, 4)
        and scales.shape == (576, 256)
        and feats.shape == (32, 8, 8, 512)
        and master.shape == (10, 256, 512)
        and class_wt.shape[0] <= 16
    )
    return shards_fast(*args) if fits else shards_general(*args)


def solution(mesh):
    return jax.shard_map(
        shards,
        mesh=mesh,
        in_specs=(
            P(("dp", "side", "blk"), None, None, None),
            P(("dp", "side", "blk")),
            P(("dp", "side", "blk")),
            P(),
            P(),
            P(),
            P(),
            P(("dp", "blk"), "side"),
            P("blk", "side", None),
            P("blk", "side", None),
            P("blk", "side", None),
            P(),
            P(),
            P(),
            P(),
            P(),
            P(),
        ),
        out_specs=(
            P(),
            P(),
            P(("dp", "blk"), "side"),
            P("blk", "side", None),
            P("blk", "side", None),
            P("blk", "side", None),
            P(),
            P(),
            P(),
            P(),
            P(),
            P(),
        ),
        check_vma=False,
    )
```
